32 devices in a mesh: seq: 8 (over z, y), head: 4 (over x, core).
Axes of the slice: x: 2, y: 2, z: 4, core: 2. Of those that a mesh axis runs over, the one named last changes fastest.
Arguments:
- queries: bfloat16 [4096, 2048], P('seq', 'head'), may hold values from -4 to 4
- keys: bfloat16 [4096, 2048], P('seq', 'head'), may hold values from -4 to 4
- values: bfloat16 [4096, 2048], P('seq', 'head'), may hold values from -6 to 6
- rates: float32 [4096, 4], P('seq', 'head'), may hold values from 0.02 to 0.3
- fast: bfloat16 [4, 3, 512, 512], P('head'), may hold values from -0.25 to 0.25
- momentum: float32 [4, 3, 512, 512], P('head', None, 'seq'), may hold values from -0.24 to 0.24
- out_proj: bfloat16 [2048, 2048], P('seq', 'head'), may hold values from -0.125 to 0.125
Outputs:
- mixed: bfloat16 [4096, 2048], P('seq', 'head')
- new_momentum: float32 [4, 3, 512, 512], P('head', None, 'seq')
The draws below stay inside these ranges and needn't reach their ends.
All inputs are finite; a program needn't handle non-finite values.
Results may differ from the reference program's by a relative error of at most 0.0094.
Values may be sent and summed in bfloat16 or wider, within the bound.
No kernel may reach another device: no remote copies, remote signals or barrier semaphores. Data moves between devices by JAX's collectives and lax.ppermute only.
A program may use at most 64 MiB of HBM per device.

```python
import math
import jax
import jax.numpy as jnp
from jax import lax

HD = 512
HEADS = 4
D = 2048
WINDOW = 512
TOKENS = 4096


def draw_queries(key, part):
    drawn = jnp.clip(jax.random.normal(jax.random.fold_in(key, 11), (TOKENS, D), jnp.float32), -4.0, 4.0)
    return drawn.astype(jnp.bfloat16)


def draw_keys(key, part):
    drawn = jnp.clip(jax.random.normal(jax.random.fold_in(key, 12), (TOKENS, D), jnp.float32), -4.0, 4.0)
    return drawn.astype(jnp.bfloat16)


def block_levels(own_key, shape, cuts, smallest, top_value):
    level = 1.0
    for position, blocks in cuts:
        heights = jax.random.uniform(jax.random.fold_in(jax.random.fold_in(own_key, 6), position), (blocks,), jnp.float32, smallest / len(cuts), top_value / len(cuts))
        level = level * jnp.repeat(jnp.exp(heights), shape[position] // blocks).reshape((-1,) + (1,) * (len(shape) - 1 - position))
    return level


def normal_values(key, extent, spread, bound, split=(), dtype=jnp.bfloat16):
    array = spread * jax.random.normal(key, extent, jnp.float32)
    if split:
        array = array * block_levels(key, extent, split, -0.22, 0.18)
    return jnp.clip(array, -bound, bound).astype(dtype)


def setup_inputs(seed: int = 0) -> dict:
    arg_keys = jax.random.split(jax.random.key(seed), 8)
    queries = draw_queries(jax.random.fold_in(arg_keys[7], 71), 0)
    keys = draw_keys(jax.random.fold_in(arg_keys[7], 71), 0)
    values = normal_values(arg_keys[2], (TOKENS, D), 1.0, 6.0, ((0, 8), (1, 4)))
    rates = jnp.clip(jnp.exp(math.log(0.3) - 2.7080503 * jax.random.uniform(arg_keys[3], (TOKENS, HEADS), jnp.float32) ** block_levels(arg_keys[3], (TOKENS, HEADS), ((0, 8), (1, 4)), -0.2, 0.2)), 0.02, 0.3)
    fast = normal_values(arg_keys[4], (HEADS, 3, HD, HD), HD ** -0.5, 0.25, ((0, 4),))
    momentum = normal_values(arg_keys[5], (HEADS, 3, HD, HD), 0.04, 0.24, ((0, 4), (2, 8)), jnp.float32)
    out_proj = normal_values(arg_keys[6], (D, D), D ** -0.5, 0.125, ((0, 8), (1, 4)))
    return dict(queries=queries, keys=keys, values=values, rates=rates, fast=fast, momentum=momentum, out_proj=out_proj)


MOMENTUM_DECAY = 0.9
NORM_EPS = 1e-06
NEG_LARGE = -1e+30

def times_transposed(left, right):
    return lax.dot_general(left, right, (((1,), (1,)), ((), ())), preferred_element_type=jnp.float32)

def contract_rows(left, right):
    return lax.dot_general(left, right, (((0,), (0,)), ((), ())), preferred_element_type=jnp.float32)

def fast_gradients(keys_head, values_head, rates_head, weights, grad_scale):
    h_gate = times_transposed(keys_head, weights[0])
    h_up = times_transposed(keys_head, weights[1])
    sigma = jax.nn.sigmoid(h_gate)
    gated = (h_gate * sigma * h_up).astype(jnp.bfloat16)
    errors = (-grad_scale * rates_head * values_head.astype(jnp.float32)).astype(jnp.bfloat16)
    grad_down = contract_rows(errors, gated)
    back = jnp.dot(errors, weights[2], preferred_element_type=jnp.float32)
    d_gate = (back * h_up * sigma * (1.0 + h_gate * (1.0 - sigma))).astype(jnp.bfloat16)
    d_up = (back * h_gate * sigma).astype(jnp.bfloat16)
    grad_gate = contract_rows(d_gate, keys_head)
    grad_up = contract_rows(d_up, keys_head)
    return jnp.stack([grad_gate, grad_up, grad_down])

def renormalize(base, moment):
    updated = base - moment
    base_rms = jnp.sqrt(lax.optimization_barrier(jnp.mean(base * base, axis=-1, keepdims=True)) + NORM_EPS)
    new_rms = jnp.sqrt(lax.optimization_barrier(jnp.mean(updated * updated, axis=-1, keepdims=True)) + NORM_EPS)
    return (updated * (base_rms / new_rms)).astype(jnp.bfloat16)

def fast_output(queries_head, renewed):
    h_gate = times_transposed(queries_head, renewed[0])
    h_up = times_transposed(queries_head, renewed[1])
    fast_in = (h_gate * jax.nn.sigmoid(h_gate) * h_up).astype(jnp.bfloat16)
    return times_transposed(fast_in, renewed[2])

def window_attention(queries_head, keys_head, values_head):
    total = queries_head.shape[0]
    block = math.gcd(512, total)
    padding = jnp.zeros((WINDOW, HD), jnp.bfloat16)
    padded_keys = jnp.concatenate([padding, keys_head], axis=0)
    padded_values = jnp.concatenate([padding, values_head], axis=0)

    def one_block(start):
        q_block = lax.dynamic_slice_in_dim(queries_head, start, block, 0)
        k_block = lax.dynamic_slice_in_dim(padded_keys, start, block + WINDOW, 0)
        v_block = lax.dynamic_slice_in_dim(padded_values, start, block + WINDOW, 0)
        q_pos = start + jnp.arange(block).astype(jnp.int32)
        k_pos = start - WINDOW + jnp.arange(block + WINDOW).astype(jnp.int32)
        spacing = q_pos[:, None] - k_pos[None, :]
        allowed = (spacing >= 0) & (spacing < WINDOW) & (k_pos[None, :] >= 0)
        scores = times_transposed(q_block, k_block) * (1.0 / math.sqrt(HD))
        scores = jnp.where(allowed, scores, NEG_LARGE)
        highest = lax.optimization_barrier(jnp.max(scores, axis=1, keepdims=True))
        expo = jnp.exp(scores - highest)
        probs = (expo / lax.optimization_barrier(jnp.sum(expo, axis=1, keepdims=True))).astype(jnp.bfloat16)
        return jnp.dot(probs, v_block, preferred_element_type=jnp.float32)
    starts = (jnp.arange(total // block) * block).astype(jnp.int32)
    return lax.map(one_block, starts).reshape(total, HD)

def reference(queries, keys, values, rates, fast, momentum, out_proj):
    grad_scale = 1.0 / math.sqrt(TOKENS)
    pieces = []
    moments = []
    for head_number in range(HEADS):
        first = head_number * HD
        q_head = queries[:, first:first + HD]
        k_head = keys[:, first:first + HD]
        v_head = values[:, first:first + HD]
        grads = fast_gradients(k_head, v_head, rates[:, head_number:head_number + 1], fast[head_number], grad_scale)
        moment = MOMENTUM_DECAY * momentum[head_number] + grads
        renewed = renormalize(fast[head_number].astype(jnp.float32), moment)
        fast_out = fast_output(q_head, renewed)
        attended = window_attention(q_head, k_head, v_head)
        pieces.append((attended + fast_out).astype(jnp.bfloat16))
        moments.append(moment)
    combined = jnp.concatenate(pieces, axis=1)
    mixed = jnp.dot(combined, out_proj, preferred_element_type=jnp.float32).astype(jnp.bfloat16)
    return (mixed, jnp.stack(moments))
```

```python
import math

import jax
import jax.numpy as jnp
from jax import lax
from jax.sharding import PartitionSpec as P

HD = 512
WINDOW = 512

MOMENTUM_DECAY = 0.9
NORM_EPS = 1e-06
NEG_LARGE = -1e30


def times_transposed(left, right):
    return lax.dot_general(
        left, right, (((1,), (1,)), ((), ())), preferred_element_type=jnp.float32
    )


def contract_rows(left, right):
    return lax.dot_general(
        left, right, (((0,), (0,)), ((), ())), preferred_element_type=jnp.float32
    )


def swap(array, axis, mask):
    devices = lax.axis_size(axis)
    return lax.ppermute(array, axis, [(i, i ^ mask) for i in range(devices)])


def scatter_rows(grads, position, ranks):
    count, rows, width = grads.shape
    own = rows // ranks
    if ranks != 8:
        return lax.psum_scatter(grads, "seq", scatter_dimension=1, tiled=True).astype(jnp.float32)
    outer, inner = ranks // 2, 2
    z, y = position // inner, position % inner
    parts = grads.reshape(count, outer, inner, own, width)
    mine = lax.dynamic_index_in_dim(parts, y, 2, keepdims=False)
    other = lax.dynamic_index_in_dim(parts, 1 - y, 2, keepdims=False)
    both = mine.astype(jnp.float32) + swap(other, "seq", 1).astype(jnp.float32)
    total = lax.dynamic_index_in_dim(both, z, 1, keepdims=False)
    for step in range(1, outer):
        piece = lax.dynamic_index_in_dim(both, z ^ step, 1, keepdims=False).astype(jnp.bfloat16)
        total = total + swap(piece, "seq", step * inner).astype(jnp.float32)
    return total


def gather_rows(rows, position, ranks):
    if ranks != 8:
        return lax.all_gather(rows, "seq", axis=1, tiled=True)
    count, own, width = rows.shape
    outer, inner = ranks // 2, 2
    z, y = position // inner, position % inner
    near = [rows] + [swap(rows, "seq", step * inner) for step in range(1, outer)]
    far = [swap(piece, "seq", 1) for piece in near]
    whole = jnp.zeros((count, outer, inner, own, width), rows.dtype)
    for step in range(outer):
        for side, pieces in ((y, near), (1 - y, far)):
            whole = lax.dynamic_update_slice(
                whole, pieces[step][:, None, None], (0, z ^ step, side, 0, 0)
            )
    return whole.reshape(count, own * ranks, width)


def renormalize(base, moment):
    updated = base - moment
    base_rms = jnp.sqrt(jnp.mean(base * base, axis=-1, keepdims=True) + NORM_EPS)
    new_rms = jnp.sqrt(jnp.mean(updated * updated, axis=-1, keepdims=True) + NORM_EPS)
    return (updated * (base_rms / new_rms)).astype(jnp.bfloat16)


def shards(queries, keys, values, rates, fast, momentum, out_proj):
    tok_rows = queries.shape[0]
    ranks = lax.axis_size("seq")
    heads = lax.axis_size("head")
    position = lax.axis_index("seq")
    own_rows = momentum.shape[2]
    grad_scale = 1.0 / math.sqrt(tok_rows * ranks)
    projection = lax.all_gather(out_proj, "seq", axis=0, tiled=True)

    weights = fast[0]
    h_gate = times_transposed(keys, weights[0])
    h_up = times_transposed(keys, weights[1])
    sigma = jax.nn.sigmoid(h_gate)
    gated = (h_gate * sigma * h_up).astype(jnp.bfloat16)
    errors = (-grad_scale * rates * values.astype(jnp.float32)).astype(jnp.bfloat16)
    grad_down = contract_rows(errors, gated)
    back = jnp.dot(errors, weights[2], preferred_element_type=jnp.float32)
    d_gate = (back * h_up * sigma * (1.0 + h_gate * (1.0 - sigma))).astype(jnp.bfloat16)
    d_up = (back * h_gate * sigma).astype(jnp.bfloat16)
    grad_gate = contract_rows(d_gate, keys)
    grad_up = contract_rows(d_up, keys)
    grads = jnp.stack([grad_gate, grad_up, grad_down]).astype(jnp.bfloat16)

    reach = (WINDOW + tok_rows - 2) // tok_rows
    behind = [(i, i + 1) for i in range(ranks - 1)]
    early_keys = lax.ppermute(keys, "seq", behind)
    early_values = lax.ppermute(values, "seq", behind)

    summed_rows = scatter_rows(grads, position, ranks)
    moment_own = MOMENTUM_DECAY * momentum[0] + summed_rows
    base_rows = lax.dynamic_slice_in_dim(weights, position * own_rows, own_rows, 1).astype(jnp.float32)
    renewed = gather_rows(renormalize(base_rows, moment_own), position, ranks)

    all_keys = jnp.concatenate([early_keys, keys], axis=0)
    all_values = jnp.concatenate([early_values, values], axis=0)
    key_pos = (position - reach) * tok_rows + jnp.arange(all_keys.shape[0])
    query_pos = position * tok_rows + jnp.arange(tok_rows)
    spacing = query_pos[:, None] - key_pos[None, :]
    allowed = (spacing >= 0) & (spacing < WINDOW) & (key_pos[None, :] >= 0)
    scores = times_transposed(queries, all_keys) * (1.0 / math.sqrt(HD))
    scores = jnp.where(allowed, scores, NEG_LARGE)
    highest = jnp.max(scores, axis=1, keepdims=True)
    expo = jnp.exp(scores - highest)
    probs = (expo / jnp.sum(expo, axis=1, keepdims=True)).astype(jnp.bfloat16)
    attended = jnp.dot(probs, all_values, preferred_element_type=jnp.float32)

    q_gate = times_transposed(queries, renewed[0])
    q_up = times_transposed(queries, renewed[1])
    fast_in = (q_gate * jax.nn.sigmoid(q_gate) * q_up).astype(jnp.bfloat16)
    fast_out = times_transposed(fast_in, renewed[2])
    combined = (attended + fast_out).astype(jnp.bfloat16)

    head = lax.axis_index("head")

    def projected(block, owner):
        rows = lax.dynamic_slice_in_dim(projection, owner * HD, HD, 0)
        return jnp.dot(block, rows, preferred_element_type=jnp.float32)

    blocks = [(combined, 0)]
    mask = heads // 2
    while mask:
        blocks = blocks + [(swap(block, "head", mask), tag ^ mask) for block, tag in blocks]
        mask //= 2
    mixed = sum(projected(block, head ^ tag) for block, tag in blocks)
    return (mixed.astype(jnp.bfloat16), moment_own[None])


def solution(mesh):
    return jax.shard_map(
        shards,
        mesh=mesh,
        in_specs=(
            P("seq", "head"),
            P("seq", "head"),
            P("seq", "head"),
            P("seq", "head"),
            P("head", None, None, None),
            P("head", None, "seq", None),
            P("seq", "head"),
        ),
        out_specs=(P("seq", "head"), P("head", None, "seq", None)),
        check_vma=False,
    )
```

```python
import functools
import math

import jax
import jax.numpy as jnp
import numpy as np
from jax import lax
from jax.experimental import pallas as pl
from jax.experimental.pallas import tpu as pltpu
from jax.sharding import PartitionSpec as P

HD = 512
WINDOW = 512

MOMENTUM_DECAY = 0.9
NORM_EPS = 1e-06
NEG_LARGE = -1e30
VMEM_LIMIT = 48 * 1024 * 1024


def times_transposed(left, right):
    return lax.dot_general(
        left, right, (((1,), (1,)), ((), ())), preferred_element_type=jnp.float32
    )


def contract_rows(left, right):
    return lax.dot_general(
        left, right, (((0,), (0,)), ((), ())), preferred_element_type=jnp.float32
    )


def matmul(left, right):
    return jnp.dot(left, right, preferred_element_type=jnp.float32)


def swap(array, axis, mask):
    devices = lax.axis_size(axis)
    return lax.ppermute(array, axis, [(i, i ^ mask) for i in range(devices)])


def params(**more):
    return pltpu.CompilerParams(vmem_limit_bytes=VMEM_LIMIT, **more)


def whole_spec():
    return pl.BlockSpec(memory_space=pltpu.VMEM)


def gradient_rows(outer, scale, side, k, v, r, w, eye, hg_s, hu_s, err_s, dg_s, du_s):
    tokens, hidden = k.shape
    own = hidden // (2 * outer)
    hg = times_transposed(w[0], k)
    hu = times_transposed(w[1], k)
    hg_s[...] = hg
    hu_s[...] = hu
    gated = (hg * jax.nn.sigmoid(hg) * hu).astype(jnp.bfloat16)
    turned = times_transposed(eye, v)
    err_s[...] = (-scale * r * turned).astype(jnp.bfloat16)
    down_t = times_transposed(eye, w[2]).astype(jnp.bfloat16)
    back = matmul(down_t, err_s[...])
    dg_s[2] = back
    errors = []
    for z in range(outer):
        rows = pl.ds(pl.multiple_of((2 * z + side) * own, own), own)
        to = pl.ds(z * own, own)
        g, u, b = hg_s[rows], hu_s[rows], dg_s[2, rows]
        s = jax.nn.sigmoid(g)
        du_s[0, to] = (b * u * s * (1.0 + g * (1.0 - s))).astype(jnp.bfloat16)
        du_s[1, to] = (b * g * s).astype(jnp.bfloat16)
        du_s[2, to] = err_s[rows]
    return (
        matmul(du_s[0], k),
        matmul(du_s[1], k),
        times_transposed(du_s[2], gated),
    )


def identity(size):
    rows = lax.broadcasted_iota(jnp.int32, (size, size), 0)
    columns = lax.broadcasted_iota(jnp.int32, (size, size), 1)
    return jnp.where(rows == columns, 1.0, 0.0).astype(jnp.bfloat16)


def own_kernel(outer, scale, place, k, v, r, w, acc, *scratch):
    eye = identity(v.shape[1])
    parts = gradient_rows(outer, scale, place[0], k[...], v[...], r[...], w[0], eye, *scratch)
    own = acc.shape[2]
    for i, part in enumerate(parts):
        acc[:, i] = part.reshape(outer, own, part.shape[1])


def both_kernel(outer, scale, place, k, v, r, w, acc, mine, *rest):
    sent, scratch = rest[: outer - 1], rest[outer - 1 :]
    eye = identity(v.shape[1])
    parts = gradient_rows(outer, scale, place[0], k[...], v[...], r[...], w[0], eye, *scratch)
    own = acc.shape[2]
    total = scratch[1]
    for i, part in enumerate(parts):
        total[pl.ds(0, outer * own), :] = part + acc[:, i].reshape(outer * own, part.shape[1])
        mine[i] = total[pl.ds(pl.multiple_of(place[1] * own, own), own), :]
        for step in range(1, outer):
            other = place[1] ^ step
            block = total[pl.ds(pl.multiple_of(other * own, own), own), :]
            sent[step - 1][i] = block.astype(jnp.bfloat16)


def gradient_scratch(tokens, hidden):
    return [
        pltpu.VMEM((hidden, tokens), jnp.float32),
        pltpu.VMEM((hidden, tokens), jnp.float32),
        pltpu.VMEM((hidden, tokens), jnp.bfloat16),
        pltpu.VMEM((3, hidden, tokens), jnp.float32),
        pltpu.VMEM((3, hidden // 2, tokens), jnp.bfloat16),
    ]


def gradient_cost(tokens, hidden):
    return pl.CostEstimate(
        flops=12 * tokens * hidden * hidden, bytes_accessed=4_000_000, transcendentals=0
    )


def own_gradients(place, k, v, r, w, outer, scale):
    tokens, hidden = k.shape
    own = hidden // (2 * outer)
    return pl.pallas_call(
        functools.partial(own_kernel, outer, scale),
        out_shape=jax.ShapeDtypeStruct((outer, 3, own, hidden), jnp.float32),
        in_specs=[pl.BlockSpec(memory_space=pltpu.SMEM)] + [whole_spec()] * 4,
        out_specs=whole_spec(),
        scratch_shapes=gradient_scratch(tokens, hidden),
        compiler_params=params(),
        cost_estimate=gradient_cost(tokens, hidden),
        name="own_gradients",
    )(place, k, v, r, w)


def both_gradients(place, k, v, r, w, acc, outer, scale):
    tokens, hidden = k.shape
    own = hidden // (2 * outer)
    return pl.pallas_call(
        functools.partial(both_kernel, outer, scale),
        out_shape=[jax.ShapeDtypeStruct((3, own, hidden), jnp.float32)]
        + [jax.ShapeDtypeStruct((3, own, hidden), jnp.bfloat16)] * (outer - 1),
        in_specs=[pl.BlockSpec(memory_space=pltpu.SMEM)] + [whole_spec()] * 5,
        out_specs=[whole_spec()] * outer,
        scratch_shapes=gradient_scratch(tokens, hidden),
        compiler_params=params(),
        cost_estimate=gradient_cost(tokens, hidden),
        name="both_gradients",
    )(place, k, v, r, w, acc)


def apply_kernel(count, origin, q, attended, *rest):
    units, combined, full = rest[:count], rest[count], rest[count + 1]
    own = units[0].shape[1]
    for i in range(count):
        rows = pl.ds(pl.multiple_of(origin[i] * own, own), own)
        full[:, rows, :] = units[i][...]
    b1 = times_transposed(q[...], full[0])
    b3 = times_transposed(q[...], full[1])
    fast_in = (b1 * jax.nn.sigmoid(b1) * b3).astype(jnp.bfloat16)
    out = times_transposed(fast_in, full[2])
    combined[...] = (attended[...] + out).astype(jnp.bfloat16)


def apply_fast(origin, q, attended, units):
    tokens, hidden = q.shape
    return pl.pallas_call(
        functools.partial(apply_kernel, len(units)),
        out_shape=jax.ShapeDtypeStruct((tokens, hidden), jnp.bfloat16),
        in_specs=[pl.BlockSpec(memory_space=pltpu.SMEM)] + [whole_spec()] * (2 + len(units)),
        out_specs=whole_spec(),
        scratch_shapes=[pltpu.VMEM((3, hidden, hidden), jnp.bfloat16)],
        compiler_params=params(),
        cost_estimate=pl.CostEstimate(
            flops=6 * tokens * hidden * hidden, bytes_accessed=4_000_000, transcendentals=0
        ),
        name="apply_fast",
    )(origin, q, attended, *units)


def project_kernel(count, blocks_in, origin, *rest):
    blocks, units = rest[:blocks_in], rest[blocks_in : blocks_in + count]
    mixed, full = rest[blocks_in + count :]
    rows_in = units[0].shape[0]
    for i in range(count):
        rows = pl.ds(pl.multiple_of(origin[i] * rows_in, rows_in), rows_in)
        full[rows, :] = units[i][...]
    width = blocks[0].shape[1]
    total = None
    for i in range(blocks_in):
        rows = pl.ds(pl.multiple_of(origin[count + i] * width, width), width)
        part = matmul(blocks[i][...], full[rows, :])
        total = part if total is None else total + part
    mixed[...] = total.astype(jnp.bfloat16)


def project(origin, blocks, units):
    tokens = blocks[0].shape[0]
    rows_in, width = units[0].shape
    return pl.pallas_call(
        functools.partial(project_kernel, len(units), len(blocks)),
        out_shape=jax.ShapeDtypeStruct((tokens, width), jnp.bfloat16),
        in_specs=[pl.BlockSpec(memory_space=pltpu.SMEM)]
        + [whole_spec()] * (len(units) + len(blocks)),
        out_specs=whole_spec(),
        scratch_shapes=[pltpu.VMEM((rows_in * len(units), width), jnp.bfloat16)],
        compiler_params=params(),
        cost_estimate=pl.CostEstimate(
            flops=2 * tokens * rows_in * len(units) * width,
            bytes_accessed=5_000_000,
            transcendentals=0,
        ),
        name="project",
    )(origin, *blocks, *units)


def ring_order(outer):
    return [0] + list(range(1, outer, 2)) + list(range(outer - 2 + outer % 2, 0, -2))


def ring_step(unit, outer):
    order = ring_order(outer)
    pairs = []
    for place, z in enumerate(order):
        to = order[(place + 1) % outer]
        pairs += [(2 * z + y, 2 * to + y) for y in range(2)]
    return lax.ppermute(unit, "seq", pairs)


def both_ways(near, far, outer):
    along, across = ring_step(near[-1], outer), swap(near[-1], "seq", 1)
    along, across = lax.optimization_barrier((along, across))
    near.append(along)
    far.append(across)


def after(array, *others):
    return lax.optimization_barrier((array,) + others)[0]


def ring_origins(outer):
    order = ring_order(outer)
    table = []
    for s in range(2 * outer):
        place = order.index(s // 2)
        sources = [order[(place - step) % outer] for step in range(outer)]
        table.append([2 * z + s % 2 for z in sources] + [2 * z + 1 - s % 2 for z in sources])
    return np.array(table, np.int32)


def renormalize(base, moment):
    updated = base - moment
    base_rms = jnp.sqrt(jnp.mean(base * base, axis=-1, keepdims=True) + NORM_EPS)
    new_rms = jnp.sqrt(jnp.mean(updated * updated, axis=-1, keepdims=True) + NORM_EPS)
    return (updated * (base_rms / new_rms)).astype(jnp.bfloat16)


def attention(queries, keys, values, early_keys, early_values, position):
    tok_rows = queries.shape[0]
    all_keys = jnp.concatenate([early_keys, keys], axis=0)
    all_values = jnp.concatenate([early_values, values], axis=0)
    key_pos = (position - 1) * tok_rows + jnp.arange(all_keys.shape[0])
    query_pos = position * tok_rows + jnp.arange(tok_rows)
    spacing = query_pos[:, None] - key_pos[None, :]
    allowed = (spacing >= 0) & (spacing < WINDOW) & (key_pos[None, :] >= 0)
    scores = times_transposed(queries, all_keys) * (1.0 / math.sqrt(HD))
    scores = jnp.where(allowed, scores, NEG_LARGE)
    highest = jnp.max(scores, axis=1, keepdims=True)
    expo = jnp.exp(scores - highest)
    probs = (expo / jnp.sum(expo, axis=1, keepdims=True)).astype(jnp.bfloat16)
    return jnp.dot(probs, all_values, preferred_element_type=jnp.float32)


def head_blocks(combined, heads):
    blocks = [(combined, 0)]
    mask = heads // 2
    while mask:
        blocks = blocks + [(swap(block, "head", mask), tag ^ mask) for block, tag in blocks]
        mask //= 2
    return blocks


def shards(queries, keys, values, rates, fast, momentum, out_proj):
    tok_rows = queries.shape[0]
    ranks = lax.axis_size("seq")
    heads = lax.axis_size("head")
    position = lax.axis_index("seq")
    head = lax.axis_index("head")
    own_rows = momentum.shape[2]
    if own_rows % 16 or ranks % 2:
        return plain(queries, keys, values, rates, fast, momentum, out_proj)
    outer = ranks // 2
    grad_scale = 1.0 / math.sqrt(tok_rows * ranks)
    place = jnp.stack([position % 2, position // 2]).astype(jnp.int32)
    origins = jnp.asarray(ring_origins(outer))[position]

    behind = [(i, (i + 1) % ranks) for i in range(ranks)]
    rates_row = rates.reshape(1, tok_rows)
    early_keys = lax.ppermute(keys, "seq", behind)
    early_values = lax.ppermute(values, "seq", behind)
    early_rates = lax.ppermute(rates_row, "seq", behind)

    acc = own_gradients(place, keys, values, rates_row, fast, outer, grad_scale)
    summed = both_gradients(
        place, early_keys, early_values, early_rates, fast, acc, outer, grad_scale
    )
    wide, wide_far = [after(out_proj, early_values)], []
    both_ways(wide, wide_far, outer)
    arrived = [swap(summed[step], "seq", step * 2) for step in range(1, outer)]
    arrived[0] = after(arrived[0], wide[1], wide_far[0])
    total = summed[0]
    for piece in arrived:
        total = total + piece.astype(jnp.float32)
    moment_own = MOMENTUM_DECAY * momentum[0] + total
    base_rows = lax.dynamic_slice_in_dim(fast[0], position * own_rows, own_rows, 1).astype(jnp.float32)
    near = [renormalize(base_rows, moment_own)]
    far = []
    for step in range(1, outer):
        both_ways(near, far, outer)
        if step + 2 < outer:
            both_ways(wide, wide_far, outer)
            near[-1] = after(near[-1], wide[-1], wide_far[-1])
    far.append(swap(near[-1], "seq", 1))
    while len(wide) < outer:
        both_ways(wide, wide_far, outer)
    wide_far.append(swap(wide[-1], "seq", 1))

    attended = attention(queries, keys, values, early_keys, early_values, position)
    combined = apply_fast(origins, queries, attended, near + far)

    blocks = head_blocks(combined, heads)
    tags = jnp.stack([head ^ tag for _, tag in blocks]).astype(jnp.int32)
    mixed = project(
        jnp.concatenate([origins, tags]), [block for block, _ in blocks], wide + wide_far
    )
    return (mixed, moment_own[None])


def plain(queries, keys, values, rates, fast, momentum, out_proj):
    tok_rows = queries.shape[0]
    ranks = lax.axis_size("seq")
    position = lax.axis_index("seq")
    own_rows = momentum.shape[2]
    grad_scale = 1.0 / math.sqrt(tok_rows * ranks)
    weights = fast[0]
    h_gate = times_transposed(keys, weights[0])
    h_up = times_transposed(keys, weights[1])
    sigma = jax.nn.sigmoid(h_gate)
    gated = (h_gate * sigma * h_up).astype(jnp.bfloat16)
    errors = (-grad_scale * rates * values.astype(jnp.float32)).astype(jnp.bfloat16)
    grad_down = contract_rows(errors, gated)
    back = matmul(errors, weights[2])
    d_gate = (back * h_up * sigma * (1.0 + h_gate * (1.0 - sigma))).astype(jnp.bfloat16)
    d_up = (back * h_gate * sigma).astype(jnp.bfloat16)
    grads = jnp.stack([contract_rows(d_gate, keys), contract_rows(d_up, keys), grad_down])
    summed_rows = lax.psum_scatter(grads, "seq", scatter_dimension=1, tiled=True)
    moment_own = MOMENTUM_DECAY * momentum[0] + summed_rows
    base_rows = lax.dynamic_slice_in_dim(weights, position * own_rows, own_rows, 1).astype(jnp.float32)
    renewed = lax.all_gather(renormalize(base_rows, moment_own), "seq", axis=1, tiled=True)
    q_gate = times_transposed(queries, renewed[0])
    q_up = times_transposed(queries, renewed[1])
    fast_in = (q_gate * jax.nn.sigmoid(q_gate) * q_up).astype(jnp.bfloat16)
    fast_out = times_transposed(fast_in, renewed[2])
    behind = [(i, i + 1) for i in range(ranks - 1)]
    early_keys = lax.ppermute(keys, "seq", behind)
    early_values = lax.ppermute(values, "seq", behind)
    attended = attention(queries, keys, values, early_keys, early_values, position)
    combined = (attended + fast_out).astype(jnp.bfloat16)
    all_heads = lax.all_gather(combined, "head", axis=1, tiled=True)
    projection = lax.all_gather(out_proj, "seq", axis=0, tiled=True)
    return (matmul(all_heads, projection).astype(jnp.bfloat16), moment_own[None])


def solution(mesh):
    return jax.shard_map(
        shards,
        mesh=mesh,
        in_specs=(
            P("seq", "head"),
            P("seq", "head"),
            P("seq", "head"),
            P("seq", "head"),
            P("head", None, None, None),
            P("head", None, "seq", None),
            P("seq", "head"),
        ),
        out_specs=(P("seq", "head"), P("head", None, "seq", None)),
        check_vma=False,
    )
```

```python
import functools
import math

import jax
import jax.numpy as jnp
import numpy as np
from jax import lax
from jax.experimental import pallas as pl
from jax.experimental.pallas import tpu as pltpu
from jax.sharding import PartitionSpec as P

HD = 512
WINDOW = 512

MOMENTUM_DECAY = 0.9
NORM_EPS = 1e-06
NEG_LARGE = -1e30
MIB = 1024 * 1024


def times_transposed(left, right):
    return lax.dot_general(
        left, right, (((1,), (1,)), ((), ())), preferred_element_type=jnp.float32
    )


def contract_rows(left, right):
    return lax.dot_general(
        left, right, (((0,), (0,)), ((), ())), preferred_element_type=jnp.float32
    )


def matmul(left, right):
    return jnp.dot(left, right, preferred_element_type=jnp.float32)


def swap(array, axis, mask):
    devices = lax.axis_size(axis)
    return lax.ppermute(array, axis, [(i, i ^ mask) for i in range(devices)])


def params(mib):
    return pltpu.CompilerParams(vmem_limit_bytes=mib * MIB)


def whole_spec():
    return pl.BlockSpec(memory_space=pltpu.VMEM)


def gradient_rows(outer, scale, side, k, v, r, w, eye, hg_s, hu_s, err_s, dg_s, du_s):
    tokens, hidden = k.shape
    own = hidden // (2 * outer)
    hg = times_transposed(w[0], k)
    hu = times_transposed(w[1], k)
    hg_s[...] = hg
    hu_s[...] = hu
    gated = (hg * jax.nn.sigmoid(hg) * hu).astype(jnp.bfloat16)
    turned = times_transposed(eye, v)
    err_s[...] = (-scale * r * turned).astype(jnp.bfloat16)
    down_t = times_transposed(eye, w[2]).astype(jnp.bfloat16)
    back = matmul(down_t, err_s[...])
    dg_s[2] = back
    errors = []
    for z in range(outer):
        rows = pl.ds(pl.multiple_of((2 * z + side) * own, own), own)
        to = pl.ds(z * own, own)
        g, u, b = hg_s[rows], hu_s[rows], dg_s[2, rows]
        s = jax.nn.sigmoid(g)
        du_s[0, to] = (b * u * s * (1.0 + g * (1.0 - s))).astype(jnp.bfloat16)
        du_s[1, to] = (b * g * s).astype(jnp.bfloat16)
        du_s[2, to] = err_s[rows]
    return (
        matmul(du_s[0], k),
        matmul(du_s[1], k),
        times_transposed(du_s[2], gated),
    )


def identity(size):
    rows = lax.broadcasted_iota(jnp.int32, (size, size), 0)
    columns = lax.broadcasted_iota(jnp.int32, (size, size), 1)
    return jnp.where(rows == columns, 1.0, 0.0).astype(jnp.bfloat16)


def own_kernel(outer, scale, place, k, v, r, w, acc, *scratch):
    eye = identity(v.shape[1])
    parts = gradient_rows(outer, scale, place[0], k[...], v[...], r[...], w[0], eye, *scratch)
    own = acc.shape[2]
    for i, part in enumerate(parts):
        acc[:, i] = part.reshape(outer, own, part.shape[1])


def both_kernel(outer, scale, place, k, v, r, w, acc, mine, *rest):
    sent, scratch = rest[: outer - 1], rest[outer - 1 :]
    eye = identity(v.shape[1])
    parts = gradient_rows(outer, scale, place[0], k[...], v[...], r[...], w[0], eye, *scratch)
    own = acc.shape[2]
    total = scratch[1]
    for i, part in enumerate(parts):
        total[pl.ds(0, outer * own), :] = part + acc[:, i].reshape(outer * own, part.shape[1])
        mine[i] = total[pl.ds(pl.multiple_of(place[1] * own, own), own), :]
        for step in range(1, outer):
            other = place[1] ^ step
            block = total[pl.ds(pl.multiple_of(other * own, own), own), :]
            sent[step - 1][i] = block.astype(jnp.bfloat16)


def gradient_scratch(tokens, hidden):
    return [
        pltpu.VMEM((hidden, tokens), jnp.float32),
        pltpu.VMEM((hidden, tokens), jnp.float32),
        pltpu.VMEM((hidden, tokens), jnp.bfloat16),
        pltpu.VMEM((3, hidden, tokens), jnp.float32),
        pltpu.VMEM((3, hidden // 2, tokens), jnp.bfloat16),
    ]


def gradient_cost(tokens, hidden):
    return pl.CostEstimate(
        flops=12 * tokens * hidden * hidden, bytes_accessed=4_000_000, transcendentals=0
    )


def own_gradients(place, k, v, r, w, outer, scale):
    tokens, hidden = k.shape
    own = hidden // (2 * outer)
    return pl.pallas_call(
        functools.partial(own_kernel, outer, scale),
        out_shape=jax.ShapeDtypeStruct((outer, 3, own, hidden), jnp.float32),
        in_specs=[pl.BlockSpec(memory_space=pltpu.SMEM)] + [whole_spec()] * 4,
        out_specs=whole_spec(),
        scratch_shapes=gradient_scratch(tokens, hidden),
        compiler_params=params(20),
        cost_estimate=gradient_cost(tokens, hidden),
        name="own_gradients",
    )(place, k, v, r, w)


def both_gradients(place, k, v, r, w, acc, outer, scale):
    tokens, hidden = k.shape
    own = hidden // (2 * outer)
    return pl.pallas_call(
        functools.partial(both_kernel, outer, scale),
        out_shape=[jax.ShapeDtypeStruct((3, own, hidden), jnp.float32)]
        + [jax.ShapeDtypeStruct((3, own, hidden), jnp.bfloat16)] * (outer - 1),
        in_specs=[pl.BlockSpec(memory_space=pltpu.SMEM)] + [whole_spec()] * 5,
        out_specs=[whole_spec()] * outer,
        scratch_shapes=gradient_scratch(tokens, hidden),
        compiler_params=params(20),
        cost_estimate=gradient_cost(tokens, hidden),
        name="both_gradients",
    )(place, k, v, r, w, acc)


def apply_kernel(count, origin, q, attended, *rest):
    units, combined, full = rest[:count], rest[count], rest[count + 1]
    own = units[0].shape[1]
    for i in range(count):
        rows = pl.ds(pl.multiple_of(origin[i] * own, own), own)
        full[:, rows, :] = units[i][...]
    b1 = times_transposed(q[...], full[0])
    b3 = times_transposed(q[...], full[1])
    fast_in = (b1 * jax.nn.sigmoid(b1) * b3).astype(jnp.bfloat16)
    out = times_transposed(fast_in, full[2])
    combined[...] = (attended[...] + out).astype(jnp.bfloat16)


def apply_fast(origin, q, attended, units):
    tokens, hidden = q.shape
    return pl.pallas_call(
        functools.partial(apply_kernel, len(units)),
        out_shape=jax.ShapeDtypeStruct((tokens, hidden), jnp.bfloat16),
        in_specs=[pl.BlockSpec(memory_space=pltpu.SMEM)] + [whole_spec()] * (2 + len(units)),
        out_specs=whole_spec(),
        scratch_shapes=[pltpu.VMEM((3, hidden, hidden), jnp.bfloat16)],
        compiler_params=params(14),
        cost_estimate=pl.CostEstimate(
            flops=6 * tokens * hidden * hidden, bytes_accessed=4_000_000, transcendentals=0
        ),
        name="apply_fast",
    )(origin, q, attended, *units)


def project_kernel(count, tags, blocks_in, last, origin, *rest):
    blocks, units = rest[:blocks_in], rest[blocks_in : blocks_in + 4]
    before = None if not last else rest[blocks_in + 4]
    total, full = rest[-2:]
    steps = count // 2
    rows_in = units[0].shape[0] * 2 // steps
    for i in range(count):
        part, at = divmod(i % steps, steps // 2)
        rows = pl.ds(pl.multiple_of(origin[i] * rows_in, rows_in), rows_in)
        full[rows, :] = units[2 * (i // steps) + part][pl.ds(at * rows_in, rows_in), :]
    width = blocks[0].shape[1]
    value = before[...] if last else None
    for block, tag in zip(blocks, tags):
        rows = pl.ds(pl.multiple_of((origin[count] ^ tag) * width, width), width)
        part = matmul(block[...], full[rows, :])
        value = part if value is None else value + part
    total[...] = value.astype(total.dtype)


def project(origin, blocks, tags, units, before=None):
    tokens = blocks[0].shape[0]
    count = origin.shape[0] - 1
    rows_in, width = sum(unit.shape[0] for unit in units), units[0].shape[1]
    last = before is not None
    return pl.pallas_call(
        functools.partial(project_kernel, count, tags, len(blocks), last),
        out_shape=jax.ShapeDtypeStruct((tokens, width), jnp.bfloat16 if last else jnp.float32),
        in_specs=[pl.BlockSpec(memory_space=pltpu.SMEM)]
        + [whole_spec()] * (4 + len(blocks) + last),
        out_specs=whole_spec(),
        scratch_shapes=[pltpu.VMEM((rows_in, width), jnp.bfloat16)],
        compiler_params=params(14),
        cost_estimate=pl.CostEstimate(
            flops=2 * tokens * HD * len(blocks) * width,
            bytes_accessed=4_000_000,
            transcendentals=0,
        ),
        name="project",
    )(origin, *blocks, *units, *([before] if last else []))


def ring_order(outer):
    return [0] + list(range(1, outer, 2)) + list(range(outer - 2 + outer % 2, 0, -2))


def ring_step(unit, outer):
    order = ring_order(outer)
    pairs = []
    for place, z in enumerate(order):
        to = order[(place + 1) % outer]
        pairs += [(2 * z + y, 2 * to + y) for y in range(2)]
    return lax.ppermute(unit, "seq", pairs)


def after(array, *others):
    return lax.optimization_barrier((array,) + others)[0]


def ring_origins(outer):
    order = ring_order(outer)
    table = []
    for s in range(2 * outer):
        place = order.index(s // 2)
        sources = [order[(place - step) % outer] for step in range(outer)]
        table.append([2 * z + s % 2 for z in sources] + [2 * z + 1 - s % 2 for z in sources])
    return np.array(table, np.int32)


def renormalize(base, moment):
    updated = base - moment
    base_rms = jnp.sqrt(jnp.mean(base * base, axis=-1, keepdims=True) + NORM_EPS)
    new_rms = jnp.sqrt(jnp.mean(updated * updated, axis=-1, keepdims=True) + NORM_EPS)
    return (updated * (base_rms / new_rms)).astype(jnp.bfloat16)


def attention(queries, keys, values, early_keys, early_values, position):
    tok_rows = queries.shape[0]
    all_keys = jnp.concatenate([early_keys, keys], axis=0)
    all_values = jnp.concatenate([early_values, values], axis=0)
    key_pos = (position - 1) * tok_rows + jnp.arange(all_keys.shape[0])
    query_pos = position * tok_rows + jnp.arange(tok_rows)
    spacing = query_pos[:, None] - key_pos[None, :]
    allowed = (spacing >= 0) & (spacing < WINDOW) & (key_pos[None, :] >= 0)
    scores = times_transposed(queries, all_keys) * (1.0 / math.sqrt(HD))
    scores = jnp.where(allowed, scores, NEG_LARGE)
    highest = jnp.max(scores, axis=1, keepdims=True)
    expo = jnp.exp(scores - highest)
    probs = (expo / jnp.sum(expo, axis=1, keepdims=True)).astype(jnp.bfloat16)
    return jnp.dot(probs, all_values, preferred_element_type=jnp.float32)


def shards(queries, keys, values, rates, fast, momentum, out_proj):
    tok_rows = queries.shape[0]
    ranks = lax.axis_size("seq")
    heads = lax.axis_size("head")
    position = lax.axis_index("seq")
    head = lax.axis_index("head")
    own_rows = momentum.shape[2]
    if own_rows % 16 or ranks % 4 or heads % 2:
        return plain(queries, keys, values, rates, fast, momentum, out_proj)
    outer = ranks // 2
    grad_scale = 1.0 / math.sqrt(tok_rows * ranks)
    place = jnp.stack([position % 2, position // 2]).astype(jnp.int32)
    origins = jnp.asarray(ring_origins(outer))[position]

    behind = [(i, (i + 1) % ranks) for i in range(ranks)]
    rates_row = rates.reshape(1, tok_rows)
    early_keys = lax.ppermute(keys, "seq", behind)
    early_values = lax.ppermute(values, "seq", behind)
    early_rates = lax.ppermute(rates_row, "seq", behind)

    acc = own_gradients(place, keys, values, rates_row, fast, outer, grad_scale)
    wide = [after(out_proj, acc)]
    for _ in range(1, outer):
        wide.append(ring_step(wide[-1], outer))
    half = outer // 2
    near_half = [jnp.concatenate(wide[:half]), jnp.concatenate(wide[half:])]
    early_keys = after(early_keys, wide[-2])
    far_half = [swap(unit, "seq", 1) for unit in near_half]

    summed = both_gradients(
        place, early_keys, early_values, early_rates, fast, acc, outer, grad_scale
    )
    arrived = [swap(summed[step], "seq", step * 2) for step in range(1, outer)]
    arrived[0] = after(arrived[0], far_half[0])
    total = summed[0]
    for piece in arrived:
        total = total + piece.astype(jnp.float32)
    moment_own = MOMENTUM_DECAY * momentum[0] + total
    base_rows = lax.dynamic_slice_in_dim(fast[0], position * own_rows, own_rows, 1).astype(jnp.float32)
    near = [renormalize(base_rows, moment_own)]
    far = [swap(near[0], "seq", 1)]
    for step in range(1, outer):
        near.append(ring_step(near[-1], outer))
        if step == 2:
            near[-1] = after(near[-1], far_half[1])
        if step > 1:
            near[-1] = after(near[-1], far[step - 2])
        far.append(swap(near[-1], "seq", 1))

    attended = attention(queries, keys, values, early_keys, early_values, position)
    combined = apply_fast(origins, queries, attended, near + far)

    blocks = [(combined, 0)]
    mask = heads // 2
    while mask:
        blocks = blocks + [(swap(block, "head", mask), tag ^ mask) for block, tag in blocks]
        mask //= 2
    origins = jnp.concatenate([origins, head[None].astype(jnp.int32)])
    early = [pair for pair in blocks if pair[1] <= 1]
    late = [pair for pair in blocks if pair[1] > 1]
    mixed = None
    for group in (early, late):
        mixed = project(
            origins, [b for b, _ in group], [t for _, t in group], near_half + far_half, mixed
        )
    return (mixed, moment_own[None])


def plain(queries, keys, values, rates, fast, momentum, out_proj):
    tok_rows = queries.shape[0]
    ranks = lax.axis_size("seq")
    position = lax.axis_index("seq")
    own_rows = momentum.shape[2]
    grad_scale = 1.0 / math.sqrt(tok_rows * ranks)
    weights = fast[0]
    h_gate = times_transposed(keys, weights[0])
    h_up = times_transposed(keys, weights[1])
    sigma = jax.nn.sigmoid(h_gate)
    gated = (h_gate * sigma * h_up).astype(jnp.bfloat16)
    errors = (-grad_scale * rates * values.astype(jnp.float32)).astype(jnp.bfloat16)
    grad_down = contract_rows(errors, gated)
    back = matmul(errors, weights[2])
    d_gate = (back * h_up * sigma * (1.0 + h_gate * (1.0 - sigma))).astype(jnp.bfloat16)
    d_up = (back * h_gate * sigma).astype(jnp.bfloat16)
    grads = jnp.stack([contract_rows(d_gate, keys), contract_rows(d_up, keys), grad_down])
    summed_rows = lax.psum_scatter(grads, "seq", scatter_dimension=1, tiled=True)
    moment_own = MOMENTUM_DECAY * momentum[0] + summed_rows
    base_rows = lax.dynamic_slice_in_dim(weights, position * own_rows, own_rows, 1).astype(jnp.float32)
    renewed = lax.all_gather(renormalize(base_rows, moment_own), "seq", axis=1, tiled=True)
    q_gate = times_transposed(queries, renewed[0])
    q_up = times_transposed(queries, renewed[1])
    fast_in = (q_gate * jax.nn.sigmoid(q_gate) * q_up).astype(jnp.bfloat16)
    fast_out = times_transposed(fast_in, renewed[2])
    behind = [(i, i + 1) for i in range(ranks - 1)]
    early_keys = lax.ppermute(keys, "seq", behind)
    early_values = lax.ppermute(values, "seq", behind)
    attended = attention(queries, keys, values, early_keys, early_values, position)
    combined = (attended + fast_out).astype(jnp.bfloat16)
    all_heads = lax.all_gather(combined, "head", axis=1, tiled=True)
    projection = lax.all_gather(out_proj, "seq", axis=0, tiled=True)
    return (matmul(all_heads, projection).astype(jnp.bfloat16), moment_own[None])


def solution(mesh):
    return jax.shard_map(
        shards,
        mesh=mesh,
        in_specs=(
            P("seq", "head"),
            P("seq", "head"),
            P("seq", "head"),
            P("seq", "head"),
            P("head", None, None, None),
            P("head", None, "seq", None),
            P("seq", "head"),
        ),
        out_specs=(P("seq", "head"), P("head", None, "seq", None)),
        check_vma=False,
    )
```

```python
import functools
import math

import jax
import jax.numpy as jnp
import numpy as np
from jax import lax
from jax.experimental import pallas as pl
from jax.experimental.pallas import tpu as pltpu
from jax.sharding import PartitionSpec as P

HD = 512
WINDOW = 512

MOMENTUM_DECAY = 0.9
NORM_EPS = 1e-06
NEG_LARGE = -1e30
MIB = 1024 * 1024


def times_transposed(left, right):
    return lax.dot_general(
        left, right, (((1,), (1,)), ((), ())), preferred_element_type=jnp.float32
    )


def contract_rows(left, right):
    return lax.dot_general(
        left, right, (((0,), (0,)), ((), ())), preferred_element_type=jnp.float32
    )


def matmul(left, right):
    return jnp.dot(left, right, preferred_element_type=jnp.float32)


def swap(array, axis, mask):
    devices = lax.axis_size(axis)
    return lax.ppermute(array, axis, [(i, i ^ mask) for i in range(devices)])


def params(mib):
    return pltpu.CompilerParams(vmem_limit_bytes=mib * MIB)


def whole_spec():
    return pl.BlockSpec(memory_space=pltpu.VMEM)


def gradient_rows(outer, scale, side, k, v, r, w, eye, hg_s, hu_s, err_s, dg_s, du_s):
    tokens, hidden = k.shape
    own = hidden // (2 * outer)
    hg = times_transposed(w[0], k)
    hu = times_transposed(w[1], k)
    hg_s[...] = hg
    hu_s[...] = hu
    gated = (hg * jax.nn.sigmoid(hg) * hu).astype(jnp.bfloat16)
    turned = times_transposed(eye, v)
    err_s[...] = (-scale * r * turned).astype(jnp.bfloat16)
    down_t = times_transposed(eye, w[2]).astype(jnp.bfloat16)
    back = matmul(down_t, err_s[...])
    dg_s[2] = back
    errors = []
    for z in range(outer):
        rows = pl.ds(pl.multiple_of((2 * z + side) * own, own), own)
        to = pl.ds(z * own, own)
        g, u, b = hg_s[rows], hu_s[rows], dg_s[2, rows]
        s = jax.nn.sigmoid(g)
        du_s[0, to] = (b * u * s * (1.0 + g * (1.0 - s))).astype(jnp.bfloat16)
        du_s[1, to] = (b * g * s).astype(jnp.bfloat16)
        du_s[2, to] = err_s[rows]
    return (
        matmul(du_s[0], k),
        matmul(du_s[1], k),
        times_transposed(du_s[2], gated),
    )


def identity(size):
    rows = lax.broadcasted_iota(jnp.int32, (size, size), 0)
    columns = lax.broadcasted_iota(jnp.int32, (size, size), 1)
    return jnp.where(rows == columns, 1.0, 0.0).astype(jnp.bfloat16)


def own_kernel(outer, scale, place, k, v, r, w, acc, *scratch):
    eye = identity(v.shape[1])
    parts = gradient_rows(outer, scale, place[0], k[...], v[...], r[...], w[0], eye, *scratch)
    own = acc.shape[2]
    for i, part in enumerate(parts):
        acc[:, i] = part.reshape(outer, own, part.shape[1])


def both_kernel(outer, scale, place, k, v, r, w, acc, mine, *rest):
    sent, scratch = rest[: outer - 1], rest[outer - 1 :]
    eye = identity(v.shape[1])
    parts = gradient_rows(outer, scale, place[0], k[...], v[...], r[...], w[0], eye, *scratch)
    own = acc.shape[2]
    total = scratch[1]
    for i, part in enumerate(parts):
        total[pl.ds(0, outer * own), :] = part + acc[:, i].reshape(outer * own, part.shape[1])
        mine[i] = total[pl.ds(pl.multiple_of(place[1] * own, own), own), :]
        for step in range(1, outer):
            other = place[1] ^ step
            block = total[pl.ds(pl.multiple_of(other * own, own), own), :]
            sent[step - 1][i] = block.astype(jnp.bfloat16)


def gradient_scratch(tokens, hidden):
    return [
        pltpu.VMEM((hidden, tokens), jnp.float32),
        pltpu.VMEM((hidden, tokens), jnp.float32),
        pltpu.VMEM((hidden, tokens), jnp.bfloat16),
        pltpu.VMEM((3, hidden, tokens), jnp.float32),
        pltpu.VMEM((3, hidden // 2, tokens), jnp.bfloat16),
    ]


def gradient_cost(tokens, hidden):
    return pl.CostEstimate(
        flops=12 * tokens * hidden * hidden, bytes_accessed=4_000_000, transcendentals=0
    )


def own_gradients(place, k, v, r, w, outer, scale):
    tokens, hidden = k.shape
    own = hidden // (2 * outer)
    return pl.pallas_call(
        functools.partial(own_kernel, outer, scale),
        out_shape=jax.ShapeDtypeStruct((outer, 3, own, hidden), jnp.float32),
        in_specs=[pl.BlockSpec(memory_space=pltpu.SMEM)] + [whole_spec()] * 4,
        out_specs=whole_spec(),
        scratch_shapes=gradient_scratch(tokens, hidden),
        compiler_params=params(20),
        cost_estimate=gradient_cost(tokens, hidden),
        name="own_gradients",
    )(place, k, v, r, w)


def both_gradients(place, k, v, r, w, acc, outer, scale):
    tokens, hidden = k.shape
    own = hidden // (2 * outer)
    return pl.pallas_call(
        functools.partial(both_kernel, outer, scale),
        out_shape=[jax.ShapeDtypeStruct((3, own, hidden), jnp.float32)]
        + [jax.ShapeDtypeStruct((3, own, hidden), jnp.bfloat16)] * (outer - 1),
        in_specs=[pl.BlockSpec(memory_space=pltpu.SMEM)] + [whole_spec()] * 5,
        out_specs=[whole_spec()] * outer,
        scratch_shapes=gradient_scratch(tokens, hidden),
        compiler_params=params(20),
        cost_estimate=gradient_cost(tokens, hidden),
        name="both_gradients",
    )(place, k, v, r, w, acc)


def apply_kernel(count, origin, q, attended, *rest):
    units, combined, full = rest[:count], rest[count], rest[count + 1]
    own = units[0].shape[1]
    for i in range(count):
        rows = pl.ds(pl.multiple_of(origin[i] * own, own), own)
        full[:, rows, :] = units[i][...]
    b1 = times_transposed(q[...], full[0])
    b3 = times_transposed(q[...], full[1])
    fast_in = (b1 * jax.nn.sigmoid(b1) * b3).astype(jnp.bfloat16)
    out = times_transposed(fast_in, full[2])
    combined[...] = (attended[...] + out).astype(jnp.bfloat16)


def apply_fast(origin, q, attended, units):
    tokens, hidden = q.shape
    return pl.pallas_call(
        functools.partial(apply_kernel, len(units)),
        out_shape=jax.ShapeDtypeStruct((tokens, hidden), jnp.bfloat16),
        in_specs=[pl.BlockSpec(memory_space=pltpu.SMEM)] + [whole_spec()] * (2 + len(units)),
        out_specs=whole_spec(),
        scratch_shapes=[pltpu.VMEM((3, hidden, hidden), jnp.bfloat16)],
        compiler_params=params(14),
        cost_estimate=pl.CostEstimate(
            flops=6 * tokens * hidden * hidden, bytes_accessed=4_000_000, transcendentals=0
        ),
        name="apply_fast",
    )(origin, q, attended, *units)


def project_kernel(count, tags, origin, *rest):
    blocks, units = rest[: len(tags)], rest[len(tags) : len(tags) + 4]
    total, full = rest[-2:]
    steps = count // 2
    rows_in = units[0].shape[0] * 2 // steps
    for i in range(count):
        part, at = divmod(i % steps, steps // 2)
        rows = pl.ds(pl.multiple_of(origin[i] * rows_in, rows_in), rows_in)
        full[rows, :] = units[2 * (i // steps) + part][pl.ds(at * rows_in, rows_in), :]
    width = blocks[0].shape[1]
    value = None
    for block, tag in zip(blocks, tags):
        rows = pl.ds(pl.multiple_of((origin[count] ^ tag) * width, width), width)
        part = matmul(block[...], full[rows, :])
        value = part if value is None else value + part
    total[...] = value.astype(total.dtype)


def project(origin, blocks, tags, units):
    tokens = blocks[0].shape[0]
    count = origin.shape[0] - 1
    rows_in, width = sum(unit.shape[0] for unit in units), units[0].shape[1]
    return pl.pallas_call(
        functools.partial(project_kernel, count, tags),
        out_shape=jax.ShapeDtypeStruct((tokens, width), jnp.bfloat16),
        in_specs=[pl.BlockSpec(memory_space=pltpu.SMEM)]
        + [whole_spec()] * (4 + len(blocks)),
        out_specs=whole_spec(),
        scratch_shapes=[pltpu.VMEM((rows_in, width), jnp.bfloat16)],
        compiler_params=params(14),
        cost_estimate=pl.CostEstimate(
            flops=2 * tokens * HD * len(blocks) * width,
            bytes_accessed=4_000_000,
            transcendentals=0,
        ),
        name="project",
    )(origin, *blocks, *units)


def ring_order(outer):
    return [0] + list(range(1, outer, 2)) + list(range(outer - 2 + outer % 2, 0, -2))


def ring_step(unit, outer):
    order = ring_order(outer)
    pairs = []
    for place, z in enumerate(order):
        to = order[(place + 1) % outer]
        pairs += [(2 * z + y, 2 * to + y) for y in range(2)]
    return lax.ppermute(unit, "seq", pairs)


def after(array, *others):
    return lax.optimization_barrier((array,) + others)[0]


def ring_origins(outer):
    order = ring_order(outer)
    table = []
    for s in range(2 * outer):
        place = order.index(s // 2)
        sources = [order[(place - step) % outer] for step in range(outer)]
        table.append([2 * z + s % 2 for z in sources] + [2 * z + 1 - s % 2 for z in sources])
    return np.array(table, np.int32)


def renormalize(base, moment):
    updated = base - moment
    base_rms = jnp.sqrt(jnp.mean(base * base, axis=-1, keepdims=True) + NORM_EPS)
    new_rms = jnp.sqrt(jnp.mean(updated * updated, axis=-1, keepdims=True) + NORM_EPS)
    return (updated * (base_rms / new_rms)).astype(jnp.bfloat16)


def attention(queries, keys, values, early_keys, early_values, position):
    tok_rows = queries.shape[0]
    all_keys = jnp.concatenate([early_keys, keys], axis=0)
    all_values = jnp.concatenate([early_values, values], axis=0)
    key_pos = (position - 1) * tok_rows + jnp.arange(all_keys.shape[0])
    query_pos = position * tok_rows + jnp.arange(tok_rows)
    spacing = query_pos[:, None] - key_pos[None, :]
    allowed = (spacing >= 0) & (spacing < WINDOW) & (key_pos[None, :] >= 0)
    scores = times_transposed(queries, all_keys) * (1.0 / math.sqrt(HD))
    scores = jnp.where(allowed, scores, NEG_LARGE)
    highest = jnp.max(scores, axis=1, keepdims=True)
    expo = jnp.exp(scores - highest)
    probs = (expo / jnp.sum(expo, axis=1, keepdims=True)).astype(jnp.bfloat16)
    return jnp.dot(probs, all_values, preferred_element_type=jnp.float32)


def shards(queries, keys, values, rates, fast, momentum, out_proj):
    tok_rows = queries.shape[0]
    ranks = lax.axis_size("seq")
    heads = lax.axis_size("head")
    position = lax.axis_index("seq")
    head = lax.axis_index("head")
    own_rows = momentum.shape[2]
    if own_rows % 16 or ranks % 4 or heads % 2:
        return plain(queries, keys, values, rates, fast, momentum, out_proj)
    outer = ranks // 2
    grad_scale = 1.0 / math.sqrt(tok_rows * ranks)
    place = jnp.stack([position % 2, position // 2]).astype(jnp.int32)
    origins = jnp.asarray(ring_origins(outer))[position]

    behind = [(i, (i + 1) % ranks) for i in range(ranks)]
    rates_row = rates.reshape(1, tok_rows)
    early_rates = lax.ppermute(rates_row, "seq", behind)
    early_keys = lax.ppermute(keys, "seq", behind)
    early_values = lax.ppermute(after(values, early_rates), "seq", behind)

    acc = own_gradients(place, keys, values, rates_row, fast, outer, grad_scale)
    wide = [after(out_proj, early_rates)]
    for _ in range(1, outer):
        wide.append(ring_step(wide[-1], outer))
    half = outer // 2
    near_half = [jnp.concatenate(wide[:half]), jnp.concatenate(wide[half:])]
    early_values = after(early_values, *near_half)
    far_half = [swap(after(near_half[0], early_keys, early_values), "seq", 1)]

    summed = both_gradients(
        place, early_keys, early_values, early_rates, fast, acc, outer, grad_scale
    )
    arrived = [swap(summed[step], "seq", step * 2) for step in range(1, outer)]
    arrived[0] = after(arrived[0], far_half[0])
    total = summed[0]
    for piece in arrived:
        total = total + piece.astype(jnp.float32)
    attended = attention(queries, keys, values, early_keys, early_values, position)
    total = after(total, attended)
    moment_own = MOMENTUM_DECAY * momentum[0] + total
    base_rows = lax.dynamic_slice_in_dim(fast[0], position * own_rows, own_rows, 1).astype(jnp.float32)
    near = [renormalize(base_rows, moment_own)]
    far = [swap(near[0], "seq", 1)]
    for step in range(1, outer):
        near.append(ring_step(near[-1], outer))
        if step > 1:
            near[-1] = after(near[-1], far[step - 2])
        far.append(swap(near[-1], "seq", 1))
    far_half.append(swap(after(near_half[1], far[-2]), "seq", 1))

    combined = apply_fast(origins, queries, attended, near + far)

    blocks = [(combined, 0)]
    mask = heads // 2
    while mask:
        blocks = blocks + [(swap(block, "head", mask), tag ^ mask) for block, tag in blocks]
        mask //= 2
    origins = jnp.concatenate([origins, head[None].astype(jnp.int32)])
    mixed = project(
        origins, [b for b, _ in blocks], [t for _, t in blocks], near_half + far_half
    )
    return (mixed, moment_own[None])


def plain(queries, keys, values, rates, fast, momentum, out_proj):
    tok_rows = queries.shape[0]
    ranks = lax.axis_size("seq")
    position = lax.axis_index("seq")
    own_rows = momentum.shape[2]
    grad_scale = 1.0 / math.sqrt(tok_rows * ranks)
    weights = fast[0]
    h_gate = times_transposed(keys, weights[0])
    h_up = times_transposed(keys, weights[1])
    sigma = jax.nn.sigmoid(h_gate)
    gated = (h_gate * sigma * h_up).astype(jnp.bfloat16)
    errors = (-grad_scale * rates * values.astype(jnp.float32)).astype(jnp.bfloat16)
    grad_down = contract_rows(errors, gated)
    back = matmul(errors, weights[2])
    d_gate = (back * h_up * sigma * (1.0 + h_gate * (1.0 - sigma))).astype(jnp.bfloat16)
    d_up = (back * h_gate * sigma).astype(jnp.bfloat16)
    grads = jnp.stack([contract_rows(d_gate, keys), contract_rows(d_up, keys), grad_down])
    summed_rows = lax.psum_scatter(grads, "seq", scatter_dimension=1, tiled=True)
    moment_own = MOMENTUM_DECAY * momentum[0] + summed_rows
    base_rows = lax.dynamic_slice_in_dim(weights, position * own_rows, own_rows, 1).astype(jnp.float32)
    renewed = lax.all_gather(renormalize(base_rows, moment_own), "seq", axis=1, tiled=True)
    q_gate = times_transposed(queries, renewed[0])
    q_up = times_transposed(queries, renewed[1])
    fast_in = (q_gate * jax.nn.sigmoid(q_gate) * q_up).astype(jnp.bfloat16)
    fast_out = times_transposed(fast_in, renewed[2])
    behind = [(i, i + 1) for i in range(ranks - 1)]
    early_keys = lax.ppermute(keys, "seq", behind)
    early_values = lax.ppermute(values, "seq", behind)
    attended = attention(queries, keys, values, early_keys, early_values, position)
    combined = (attended + fast_out).astype(jnp.bfloat16)
    all_heads = lax.all_gather(combined, "head", axis=1, tiled=True)
    projection = lax.all_gather(out_proj, "seq", axis=0, tiled=True)
    return (matmul(all_heads, projection).astype(jnp.bfloat16), moment_own[None])


def solution(mesh):
    return jax.shard_map(
        shards,
        mesh=mesh,
        in_specs=(
            P("seq", "head"),
            P("seq", "head"),
            P("seq", "head"),
            P("seq", "head"),
            P("head", None, None, None),
            P("head", None, "seq", None),
            P("seq", "head"),
        ),
        out_specs=(P("seq", "head"), P("head", None, "seq", None)),
        check_vma=False,
    )
```

```python
import functools
import math

import jax
import jax.numpy as jnp
import numpy as np
from jax import lax
from jax.experimental import pallas as pl
from jax.experimental.pallas import tpu as pltpu
from jax.sharding import PartitionSpec as P

HD = 512
WINDOW = 512

MOMENTUM_DECAY = 0.9
NORM_EPS = 1e-06
NEG_LARGE = -1e30
MIB = 1024 * 1024
ORIGINS = 4


def times_transposed(left, right):
    return lax.dot_general(
        left, right, (((1,), (1,)), ((), ())), preferred_element_type=jnp.float32
    )


def contract_rows(left, right):
    return lax.dot_general(
        left, right, (((0,), (0,)), ((), ())), preferred_element_type=jnp.float32
    )


def matmul(left, right):
    return jnp.dot(left, right, preferred_element_type=jnp.float32)


def swap(array, axis, mask):
    devices = lax.axis_size(axis)
    return lax.ppermute(array, axis, [(i, i ^ mask) for i in range(devices)])


def params(mib):
    return pltpu.CompilerParams(vmem_limit_bytes=mib * MIB)


def whole_spec():
    return pl.BlockSpec(memory_space=pltpu.VMEM)


def gradient_rows(outer, scale, side, k, v, r, w, eye, hg_s, hu_s, err_s, dg_s, du_s):
    tokens, hidden = k.shape
    own = hidden // (2 * outer)
    hg = times_transposed(w[0], k)
    hu = times_transposed(w[1], k)
    hg_s[...] = hg
    hu_s[...] = hu
    gated = (hg * jax.nn.sigmoid(hg) * hu).astype(jnp.bfloat16)
    turned = times_transposed(eye, v)
    err_s[...] = (-scale * r * turned).astype(jnp.bfloat16)
    down_t = times_transposed(eye, w[2]).astype(jnp.bfloat16)
    back = matmul(down_t, err_s[...])
    dg_s[2] = back
    errors = []
    for z in range(outer):
        rows = pl.ds(pl.multiple_of((2 * z + side) * own, own), own)
        to = pl.ds(z * own, own)
        g, u, b = hg_s[rows], hu_s[rows], dg_s[2, rows]
        s = jax.nn.sigmoid(g)
        du_s[0, to] = (b * u * s * (1.0 + g * (1.0 - s))).astype(jnp.bfloat16)
        du_s[1, to] = (b * g * s).astype(jnp.bfloat16)
        du_s[2, to] = err_s[rows]
    return (
        matmul(du_s[0], k),
        matmul(du_s[1], k),
        times_transposed(du_s[2], gated),
    )


def identity(size):
    rows = lax.broadcasted_iota(jnp.int32, (size, size), 0)
    columns = lax.broadcasted_iota(jnp.int32, (size, size), 1)
    return jnp.where(rows == columns, 1.0, 0.0).astype(jnp.bfloat16)


def own_kernel(outer, scale, place, k, v, r, w, acc, *scratch):
    eye = identity(v.shape[1])
    parts = gradient_rows(outer, scale, place[0], k[...], v[...], r[...], w[0], eye, *scratch)
    own = acc.shape[2]
    for i, part in enumerate(parts):
        acc[:, i] = part.reshape(outer, own, part.shape[1])


def both_kernel(outer, scale, place, k, v, r, w, acc, mine, *rest):
    sent, scratch = rest[: outer - 1], rest[outer - 1 :]
    eye = identity(v.shape[1])
    parts = gradient_rows(outer, scale, place[0], k[...], v[...], r[...], w[0], eye, *scratch)
    own = acc.shape[2]
    total = scratch[1]
    for i, part in enumerate(parts):
        total[pl.ds(0, outer * own), :] = part + acc[:, i].reshape(outer * own, part.shape[1])
        mine[i] = total[pl.ds(pl.multiple_of(place[1] * own, own), own), :]
        for step in range(1, outer):
            other = place[1] ^ step
            block = total[pl.ds(pl.multiple_of(other * own, own), own), :]
            sent[step - 1][i] = block.astype(jnp.bfloat16)


def gradient_scratch(tokens, hidden):
    return [
        pltpu.VMEM((hidden, tokens), jnp.float32),
        pltpu.VMEM((hidden, tokens), jnp.float32),
        pltpu.VMEM((hidden, tokens), jnp.bfloat16),
        pltpu.VMEM((3, hidden, tokens), jnp.float32),
        pltpu.VMEM((3, hidden // 2, tokens), jnp.bfloat16),
    ]


def gradient_cost(tokens, hidden):
    return pl.CostEstimate(
        flops=12 * tokens * hidden * hidden, bytes_accessed=4_000_000, transcendentals=0
    )


def own_gradients(place, k, v, r, w, outer, scale):
    tokens, hidden = k.shape
    own = hidden // (2 * outer)
    return pl.pallas_call(
        functools.partial(own_kernel, outer, scale),
        out_shape=jax.ShapeDtypeStruct((outer, 3, own, hidden), jnp.float32),
        in_specs=[pl.BlockSpec(memory_space=pltpu.SMEM)] + [whole_spec()] * 4,
        out_specs=whole_spec(),
        scratch_shapes=gradient_scratch(tokens, hidden),
        compiler_params=params(12),
        cost_estimate=gradient_cost(tokens, hidden),
        name="own_gradients",
    )(place, k, v, r, w)


def both_gradients(place, k, v, r, w, acc, outer, scale):
    tokens, hidden = k.shape
    own = hidden // (2 * outer)
    return pl.pallas_call(
        functools.partial(both_kernel, outer, scale),
        out_shape=[jax.ShapeDtypeStruct((3, own, hidden), jnp.float32)]
        + [jax.ShapeDtypeStruct((3, own, hidden), jnp.bfloat16)] * (outer - 1),
        in_specs=[pl.BlockSpec(memory_space=pltpu.SMEM)] + [whole_spec()] * 5,
        out_specs=[whole_spec()] * outer,
        scratch_shapes=gradient_scratch(tokens, hidden),
        compiler_params=params(12),
        cost_estimate=gradient_cost(tokens, hidden),
        name="both_gradients",
    )(place, k, v, r, w, acc)


def attend_kernel(blocks, place, q, k, v, early_k, early_v, out):
    tokens = q.shape[0]
    rows = tokens // blocks
    scale = 1.0 / math.sqrt(q.shape[1])
    for b in range(blocks):
        first, last = b * rows, (b + 1) * rows
        own = times_transposed(q[first:last], k[:last]) * scale
        old = times_transposed(q[first:last], early_k[first:]) * scale
        row = first + lax.broadcasted_iota(jnp.int32, own.shape, 0)
        column = lax.broadcasted_iota(jnp.int32, own.shape, 1)
        own = jnp.where(column <= row, own, NEG_LARGE)
        row = first + lax.broadcasted_iota(jnp.int32, old.shape, 0)
        column = first + lax.broadcasted_iota(jnp.int32, old.shape, 1)
        old = jnp.where((column > row) & (place[2] > 0), old, NEG_LARGE)
        highest = jnp.maximum(
            jnp.max(own, axis=1, keepdims=True), jnp.max(old, axis=1, keepdims=True)
        )
        own, old = jnp.exp(own - highest), jnp.exp(old - highest)
        total = jnp.sum(own, axis=1, keepdims=True) + jnp.sum(old, axis=1, keepdims=True)
        own = (own / total).astype(jnp.bfloat16)
        old = (old / total).astype(jnp.bfloat16)
        out[first:last] = matmul(own, v[:last]) + matmul(old, early_v[first:])


def window_attention(place, q, k, v, early_k, early_v):
    tokens, hidden = q.shape
    return pl.pallas_call(
        functools.partial(attend_kernel, 2),
        out_shape=jax.ShapeDtypeStruct((tokens, hidden), jnp.float32),
        in_specs=[pl.BlockSpec(memory_space=pltpu.SMEM)] + [whole_spec()] * 5,
        out_specs=whole_spec(),
        compiler_params=params(12),
        cost_estimate=pl.CostEstimate(
            flops=6 * tokens * tokens * hidden, bytes_accessed=4_000_000, transcendentals=0
        ),
        name="window_attention",
    )(place, q, k, v, early_k, early_v)


def renew_kernel(place, w, momentum, mine, *rest):
    pieces, (moment, renewed) = rest[:-2], rest[-2:]
    own = mine.shape[1]
    total = mine[...]
    for piece in pieces:
        total = total + piece[...].astype(jnp.float32)
    new = MOMENTUM_DECAY * momentum[0] + total
    moment[0] = new
    rows = pl.ds(pl.multiple_of(place[2] * own, own), own)
    for i in range(w.shape[1]):
        base = w[0, i, rows, :].astype(jnp.float32)
        renewed[i] = renormalize(base, new[i])


def renew(place, w, momentum, mine, pieces):
    return pl.pallas_call(
        renew_kernel,
        out_shape=[
            jax.ShapeDtypeStruct(momentum.shape, jnp.float32),
            jax.ShapeDtypeStruct(mine.shape, jnp.bfloat16),
        ],
        in_specs=[pl.BlockSpec(memory_space=pltpu.SMEM)] + [whole_spec()] * (3 + len(pieces)),
        out_specs=[whole_spec()] * 2,
        compiler_params=params(12),
        cost_estimate=pl.CostEstimate(flops=2_000_000, bytes_accessed=2_000_000, transcendentals=0),
        name="renew",
    )(place, w, momentum, mine, *pieces)


def apply_kernel(count, place, q, attended, *rest):
    units, combined, full = rest[:count], rest[count], rest[count + 1]
    own = units[0].shape[1]
    for i in range(count):
        rows = pl.ds(pl.multiple_of(place[ORIGINS + i] * own, own), own)
        full[:, rows, :] = units[i][...]
    b1 = times_transposed(q[...], full[0])
    b3 = times_transposed(q[...], full[1])
    fast_in = (b1 * jax.nn.sigmoid(b1) * b3).astype(jnp.bfloat16)
    out = times_transposed(fast_in, full[2])
    combined[...] = (attended[...] + out).astype(jnp.bfloat16)


def apply_fast(place, q, attended, units):
    tokens, hidden = q.shape
    return pl.pallas_call(
        functools.partial(apply_kernel, len(units)),
        out_shape=jax.ShapeDtypeStruct((tokens, hidden), jnp.bfloat16),
        in_specs=[pl.BlockSpec(memory_space=pltpu.SMEM)] + [whole_spec()] * (2 + len(units)),
        out_specs=whole_spec(),
        scratch_shapes=[pltpu.VMEM((3, hidden, hidden), jnp.bfloat16)],
        compiler_params=params(12),
        cost_estimate=pl.CostEstimate(
            flops=6 * tokens * hidden * hidden, bytes_accessed=4_000_000, transcendentals=0
        ),
        name="apply_fast",
    )(place, q, attended, *units)


def project_kernel(tags, place, *rest):
    blocks, units = rest[: len(tags)], rest[len(tags) : -2]
    mixed, full = rest[-2:]
    rows_in = units[0].shape[0]
    at = 0
    for unit in units:
        for part in range(unit.shape[0] // rows_in):
            rows = pl.ds(pl.multiple_of(place[ORIGINS + at] * rows_in, rows_in), rows_in)
            full[rows, :] = unit[part * rows_in : (part + 1) * rows_in, :]
            at += 1
    width = blocks[0].shape[1]
    value = None
    for block, tag in zip(blocks, tags):
        rows = pl.ds(pl.multiple_of((place[3] ^ tag) * width, width), width)
        part = matmul(block[...], full[rows, :])
        value = part if value is None else value + part
    mixed[...] = value.astype(mixed.dtype)


def project(place, blocks, tags, near, far):
    tokens = blocks[0].shape[0]
    units = near + far
    rows_in, width = sum(unit.shape[0] for unit in units), units[0].shape[1]
    return pl.pallas_call(
        functools.partial(project_kernel, tags),
        out_shape=jax.ShapeDtypeStruct((tokens, width), jnp.bfloat16),
        in_specs=[pl.BlockSpec(memory_space=pltpu.SMEM)]
        + [whole_spec()] * (len(units) + len(blocks)),
        out_specs=whole_spec(),
        scratch_shapes=[pltpu.VMEM((rows_in, width), jnp.bfloat16)],
        compiler_params=params(12),
        cost_estimate=pl.CostEstimate(
            flops=2 * tokens * rows_in * width, bytes_accessed=4_000_000, transcendentals=0
        ),
        name="project",
    )(place, *blocks, *units)


def ring_order(outer):
    return [0] + list(range(1, outer, 2)) + list(range(outer - 2 + outer % 2, 0, -2))


def ring_step(unit, outer):
    order = ring_order(outer)
    pairs = []
    for place, z in enumerate(order):
        to = order[(place + 1) % outer]
        pairs += [(2 * z + y, 2 * to + y) for y in range(2)]
    return lax.ppermute(unit, "seq", pairs)


def after(array, *others):
    return lax.optimization_barrier((array,) + others)[0]


def place_table(outer, heads):
    order = ring_order(outer)
    table = []
    for s in range(2 * outer):
        place = order.index(s // 2)
        sources = [order[(place - step) % outer] for step in range(outer)]
        near = [2 * z + s % 2 for z in sources]
        far = [2 * z + 1 - s % 2 for z in sources]
        table += [[s % 2, s // 2, s, head] + near + far for head in range(heads)]
    return np.array(table, np.int32)


def renormalize(base, moment):
    updated = base - moment
    base_rms = jnp.sqrt(jnp.mean(base * base, axis=-1, keepdims=True) + NORM_EPS)
    new_rms = jnp.sqrt(jnp.mean(updated * updated, axis=-1, keepdims=True) + NORM_EPS)
    return (updated * (base_rms / new_rms)).astype(jnp.bfloat16)


def attention(queries, keys, values, early_keys, early_values, position):
    tok_rows = queries.shape[0]
    all_keys = jnp.concatenate([early_keys, keys], axis=0)
    all_values = jnp.concatenate([early_values, values], axis=0)
    key_pos = (position - 1) * tok_rows + jnp.arange(all_keys.shape[0])
    query_pos = position * tok_rows + jnp.arange(tok_rows)
    spacing = query_pos[:, None] - key_pos[None, :]
    allowed = (spacing >= 0) & (spacing < WINDOW) & (key_pos[None, :] >= 0)
    scores = times_transposed(queries, all_keys) * (1.0 / math.sqrt(HD))
    scores = jnp.where(allowed, scores, NEG_LARGE)
    highest = jnp.max(scores, axis=1, keepdims=True)
    expo = jnp.exp(scores - highest)
    probs = (expo / jnp.sum(expo, axis=1, keepdims=True)).astype(jnp.bfloat16)
    return jnp.dot(probs, all_values, preferred_element_type=jnp.float32)


def shards(queries, keys, values, rates, fast, momentum, out_proj):
    tok_rows = queries.shape[0]
    ranks = lax.axis_size("seq")
    heads = lax.axis_size("head")
    own_rows = momentum.shape[2]
    if own_rows % 16 or ranks % 4 or heads % 2 or tok_rows != WINDOW:
        return plain(queries, keys, values, rates, fast, momentum, out_proj)
    outer = ranks // 2
    grad_scale = 1.0 / math.sqrt(tok_rows * ranks)
    index = lax.axis_index("seq") * heads + lax.axis_index("head")
    place = lax.dynamic_index_in_dim(jnp.asarray(place_table(outer, heads)), index, 0, False)

    behind = [(i, (i + 1) % ranks) for i in range(ranks)]
    rates_row = rates.reshape(1, tok_rows)
    early_rates = lax.ppermute(rates_row, "seq", behind)
    early_keys = lax.ppermute(keys, "seq", behind)
    early_values = lax.ppermute(after(values, early_rates), "seq", behind)

    acc = own_gradients(place, keys, values, rates_row, fast, outer, grad_scale)
    summed = both_gradients(
        place, early_keys, early_values, early_rates, fast, acc, outer, grad_scale
    )
    attended = window_attention(place, queries, keys, values, early_keys, early_values)
    wide = [after(out_proj, attended)]
    wide.append(ring_step(wide[0], outer))
    wide_far = [swap(wide[0], "seq", 1)]
    pieces = [swap(summed[step], "seq", step * 2) for step in range(1, outer)]
    pieces[0] = after(pieces[0], attended, wide[-1], wide_far[-1])
    moment, renewed = renew(place, fast, momentum, summed[0], pieces)

    near, far = [renewed], [swap(renewed, "seq", 1)]
    for step in range(1, outer):
        near.append(ring_step(near[-1], outer))
        if step > 1:
            wide.append(ring_step(wide[-1], outer))
            near[-1] = after(near[-1], far[step - 2], wide[-1])
        if step == 2:
            wide_far.append(swap(wide[1], "seq", 1))
        if step == 3:
            near[-1] = after(near[-1], wide_far[-1])
        far.append(swap(near[-1], "seq", 1))
    rest = jnp.concatenate(wide[2:])
    wide_far.append(swap(after(rest, far[-2]), "seq", 1))
    combined = apply_fast(place, queries, attended, near + far)

    blocks = [(combined, 0)]
    mask = heads // 2
    while mask:
        blocks = blocks + [(swap(block, "head", mask), tag ^ mask) for block, tag in blocks]
        mask //= 2
    mixed = project(
        place, [b for b, _ in blocks], [t for _, t in blocks], wide, wide_far
    )
    return (mixed, moment)


def plain(queries, keys, values, rates, fast, momentum, out_proj):
    tok_rows = queries.shape[0]
    ranks = lax.axis_size("seq")
    position = lax.axis_index("seq")
    own_rows = momentum.shape[2]
    grad_scale = 1.0 / math.sqrt(tok_rows * ranks)
    weights = fast[0]
    h_gate = times_transposed(keys, weights[0])
    h_up = times_transposed(keys, weights[1])
    sigma = jax.nn.sigmoid(h_gate)
    gated = (h_gate * sigma * h_up).astype(jnp.bfloat16)
    errors = (-grad_scale * rates * values.astype(jnp.float32)).astype(jnp.bfloat16)
    grad_down = contract_rows(errors, gated)
    back = matmul(errors, weights[2])
    d_gate = (back * h_up * sigma * (1.0 + h_gate * (1.0 - sigma))).astype(jnp.bfloat16)
    d_up = (back * h_gate * sigma).astype(jnp.bfloat16)
    grads = jnp.stack([contract_rows(d_gate, keys), contract_rows(d_up, keys), grad_down])
    summed_rows = lax.psum_scatter(grads, "seq", scatter_dimension=1, tiled=True)
    moment_own = MOMENTUM_DECAY * momentum[0] + summed_rows
    base_rows = lax.dynamic_slice_in_dim(weights, position * own_rows, own_rows, 1).astype(jnp.float32)
    renewed = lax.all_gather(renormalize(base_rows, moment_own), "seq", axis=1, tiled=True)
    q_gate = times_transposed(queries, renewed[0])
    q_up = times_transposed(queries, renewed[1])
    fast_in = (q_gate * jax.nn.sigmoid(q_gate) * q_up).astype(jnp.bfloat16)
    fast_out = times_transposed(fast_in, renewed[2])
    behind = [(i, i + 1) for i in range(ranks - 1)]
    early_keys = lax.ppermute(keys, "seq", behind)
    early_values = lax.ppermute(values, "seq", behind)
    attended = attention(queries, keys, values, early_keys, early_values, position)
    combined = (attended + fast_out).astype(jnp.bfloat16)
    all_heads = lax.all_gather(combined, "head", axis=1, tiled=True)
    projection = lax.all_gather(out_proj, "seq", axis=0, tiled=True)
    return (matmul(all_heads, projection).astype(jnp.bfloat16), moment_own[None])


def solution(mesh):
    return jax.shard_map(
        shards,
        mesh=mesh,
        in_specs=(
            P("seq", "head"),
            P("seq", "head"),
            P("seq", "head"),
            P("seq", "head"),
            P("head", None, None, None),
            P("head", None, "seq", None),
            P("seq", "head"),
        ),
        out_specs=(P("seq", "head"), P("head", None, "seq", None)),
        check_vma=False,
    )
```

```python
import functools
import math

import jax
import jax.numpy as jnp
import numpy as np
from jax import lax
from jax.experimental import pallas as pl
from jax.experimental.pallas import tpu as pltpu
from jax.sharding import PartitionSpec as P

HD = 512
WINDOW = 512

MOMENTUM_DECAY = 0.9
NORM_EPS = 1e-06
NEG_LARGE = -1e30
MIB = 1024 * 1024
ORIGINS = 4


def times_transposed(left, right):
    return lax.dot_general(
        left, right, (((1,), (1,)), ((), ())), preferred_element_type=jnp.float32
    )


def contract_rows(left, right):
    return lax.dot_general(
        left, right, (((0,), (0,)), ((), ())), preferred_element_type=jnp.float32
    )


def matmul(left, right):
    return jnp.dot(left, right, preferred_element_type=jnp.float32)


def swap(array, axis, mask):
    devices = lax.axis_size(axis)
    return lax.ppermute(array, axis, [(i, i ^ mask) for i in range(devices)])


def params(mib):
    return pltpu.CompilerParams(vmem_limit_bytes=mib * MIB)


def whole_spec():
    return pl.BlockSpec(memory_space=pltpu.VMEM)


def gradient_rows(outer, scale, side, k, v, r, w, eye, hg_s, hu_s, err_s, dg_s, du_s):
    tokens, hidden = k.shape
    own = hidden // (2 * outer)
    hg = times_transposed(w[0], k)
    hu = times_transposed(w[1], k)
    hg_s[...] = hg
    hu_s[...] = hu
    gated = (hg * jax.nn.sigmoid(hg) * hu).astype(jnp.bfloat16)
    turned = times_transposed(eye, v)
    err_s[...] = (-scale * r * turned).astype(jnp.bfloat16)
    down_t = times_transposed(eye, w[2]).astype(jnp.bfloat16)
    back = matmul(down_t, err_s[...])
    dg_s[2] = back
    errors = []
    for z in range(outer):
        rows = pl.ds(pl.multiple_of((2 * z + side) * own, own), own)
        to = pl.ds(z * own, own)
        g, u, b = hg_s[rows], hu_s[rows], dg_s[2, rows]
        s = jax.nn.sigmoid(g)
        du_s[0, to] = (b * u * s * (1.0 + g * (1.0 - s))).astype(jnp.bfloat16)
        du_s[1, to] = (b * g * s).astype(jnp.bfloat16)
        du_s[2, to] = err_s[rows]
    return (
        matmul(du_s[0], k),
        matmul(du_s[1], k),
        times_transposed(du_s[2], gated),
    )


def identity(size):
    rows = lax.broadcasted_iota(jnp.int32, (size, size), 0)
    columns = lax.broadcasted_iota(jnp.int32, (size, size), 1)
    return jnp.where(rows == columns, 1.0, 0.0).astype(jnp.bfloat16)


def own_kernel(outer, scale, place, k, v, r, w, acc, *scratch):
    eye = identity(v.shape[1])
    parts = gradient_rows(outer, scale, place[0], k[...], v[...], r[...], w[0], eye, *scratch)
    own = acc.shape[2]
    for i, part in enumerate(parts):
        acc[:, i] = part.reshape(outer, own, part.shape[1])


def both_kernel(outer, scale, place, k, v, r, w, acc, mine, *rest):
    sent, scratch = rest[: outer - 1], rest[outer - 1 :]
    eye = identity(v.shape[1])
    parts = gradient_rows(outer, scale, place[0], k[...], v[...], r[...], w[0], eye, *scratch)
    own = acc.shape[2]
    total = scratch[1]
    for i, part in enumerate(parts):
        total[pl.ds(0, outer * own), :] = part + acc[:, i].reshape(outer * own, part.shape[1])
        mine[i] = total[pl.ds(pl.multiple_of(place[1] * own, own), own), :]
        for step in range(1, outer):
            other = place[1] ^ step
            block = total[pl.ds(pl.multiple_of(other * own, own), own), :]
            sent[step - 1][i] = block.astype(jnp.bfloat16)


def gradient_scratch(tokens, hidden):
    return [
        pltpu.VMEM((hidden, tokens), jnp.float32),
        pltpu.VMEM((hidden, tokens), jnp.float32),
        pltpu.VMEM((hidden, tokens), jnp.bfloat16),
        pltpu.VMEM((3, hidden, tokens), jnp.float32),
        pltpu.VMEM((3, hidden // 2, tokens), jnp.bfloat16),
    ]


def gradient_cost(tokens, hidden):
    return pl.CostEstimate(
        flops=12 * tokens * hidden * hidden, bytes_accessed=4_000_000, transcendentals=0
    )


def own_gradients(place, k, v, r, w, outer, scale):
    tokens, hidden = k.shape
    own = hidden // (2 * outer)
    return pl.pallas_call(
        functools.partial(own_kernel, outer, scale),
        out_shape=jax.ShapeDtypeStruct((outer, 3, own, hidden), jnp.float32),
        in_specs=[pl.BlockSpec(memory_space=pltpu.SMEM)] + [whole_spec()] * 4,
        out_specs=whole_spec(),
        scratch_shapes=gradient_scratch(tokens, hidden),
        compiler_params=params(12),
        cost_estimate=gradient_cost(tokens, hidden),
        name="own_gradients",
    )(place, k, v, r, w)


def both_gradients(place, k, v, r, w, acc, outer, scale):
    tokens, hidden = k.shape
    own = hidden // (2 * outer)
    return pl.pallas_call(
        functools.partial(both_kernel, outer, scale),
        out_shape=[jax.ShapeDtypeStruct((3, own, hidden), jnp.float32)]
        + [jax.ShapeDtypeStruct((3, own, hidden), jnp.bfloat16)] * (outer - 1),
        in_specs=[pl.BlockSpec(memory_space=pltpu.SMEM)] + [whole_spec()] * 5,
        out_specs=[whole_spec()] * outer,
        scratch_shapes=gradient_scratch(tokens, hidden),
        compiler_params=params(12),
        cost_estimate=gradient_cost(tokens, hidden),
        name="both_gradients",
    )(place, k, v, r, w, acc)


def attend_kernel(blocks, place, q, k, v, pair_k, pair_v, up_k, up_v, out):
    even = place[0] == 0
    early_k = jnp.where(even, up_k[...], pair_k[...])
    early_v = jnp.where(even, up_v[...], pair_v[...])
    early_v = jnp.where(place[2] > 0, early_v, jnp.zeros_like(early_v))
    tokens = q.shape[0]
    rows = tokens // blocks
    scale = 1.0 / math.sqrt(q.shape[1])
    for b in range(blocks):
        first, last = b * rows, (b + 1) * rows
        own = times_transposed(q[first:last], k[:last]) * scale
        old = times_transposed(q[first:last], early_k[first:]) * scale
        row = first + lax.broadcasted_iota(jnp.int32, own.shape, 0)
        column = lax.broadcasted_iota(jnp.int32, own.shape, 1)
        own = jnp.where(column <= row, own, NEG_LARGE)
        row = first + lax.broadcasted_iota(jnp.int32, old.shape, 0)
        column = first + lax.broadcasted_iota(jnp.int32, old.shape, 1)
        old = jnp.where((column > row) & (place[2] > 0), old, NEG_LARGE)
        highest = jnp.maximum(
            jnp.max(own, axis=1, keepdims=True), jnp.max(old, axis=1, keepdims=True)
        )
        own, old = jnp.exp(own - highest), jnp.exp(old - highest)
        total = jnp.sum(own, axis=1, keepdims=True) + jnp.sum(old, axis=1, keepdims=True)
        own = (own / total).astype(jnp.bfloat16)
        old = (old / total).astype(jnp.bfloat16)
        out[first:last] = matmul(own, v[:last]) + matmul(old, early_v[first:])


def window_attention(place, q, k, v, *early):
    tokens, hidden = q.shape
    return pl.pallas_call(
        functools.partial(attend_kernel, 2),
        out_shape=jax.ShapeDtypeStruct((tokens, hidden), jnp.float32),
        in_specs=[pl.BlockSpec(memory_space=pltpu.SMEM)] + [whole_spec()] * 7,
        out_specs=whole_spec(),
        compiler_params=params(12),
        cost_estimate=pl.CostEstimate(
            flops=6 * tokens * tokens * hidden, bytes_accessed=4_000_000, transcendentals=0
        ),
        name="window_attention",
    )(place, q, k, v, *early)


def renew_kernel(place, w, momentum, mine, *rest):
    pieces, (moment, renewed) = rest[:-2], rest[-2:]
    own = mine.shape[1]
    total = mine[...]
    for piece in pieces:
        total = total + piece[...].astype(jnp.float32)
    new = MOMENTUM_DECAY * momentum[0] + total
    moment[0] = new
    rows = pl.ds(pl.multiple_of(place[2] * own, own), own)
    for i in range(w.shape[1]):
        base = w[0, i, rows, :].astype(jnp.float32)
        renewed[i] = renormalize(base, new[i])


def renew(place, w, momentum, mine, pieces):
    return pl.pallas_call(
        renew_kernel,
        out_shape=[
            jax.ShapeDtypeStruct(momentum.shape, jnp.float32),
            jax.ShapeDtypeStruct(mine.shape, jnp.bfloat16),
        ],
        in_specs=[pl.BlockSpec(memory_space=pltpu.SMEM)] + [whole_spec()] * (3 + len(pieces)),
        out_specs=[whole_spec()] * 2,
        compiler_params=params(12),
        cost_estimate=pl.CostEstimate(flops=2_000_000, bytes_accessed=2_000_000, transcendentals=0),
        name="renew",
    )(place, w, momentum, mine, *pieces)


def apply_kernel(count, place, q, attended, *rest):
    units, combined, full = rest[:count], rest[count], rest[count + 1]
    own = units[0].shape[1]
    for i in range(count):
        rows = pl.ds(pl.multiple_of(place[ORIGINS + i] * own, own), own)
        full[:, rows, :] = units[i][...]
    b1 = times_transposed(q[...], full[0])
    b3 = times_transposed(q[...], full[1])
    fast_in = (b1 * jax.nn.sigmoid(b1) * b3).astype(jnp.bfloat16)
    out = times_transposed(fast_in, full[2])
    combined[...] = (attended[...] + out).astype(jnp.bfloat16)


def apply_fast(place, q, attended, units):
    tokens, hidden = q.shape
    return pl.pallas_call(
        functools.partial(apply_kernel, len(units)),
        out_shape=jax.ShapeDtypeStruct((tokens, hidden), jnp.bfloat16),
        in_specs=[pl.BlockSpec(memory_space=pltpu.SMEM)] + [whole_spec()] * (2 + len(units)),
        out_specs=whole_spec(),
        scratch_shapes=[pltpu.VMEM((3, hidden, hidden), jnp.bfloat16)],
        compiler_params=params(12),
        cost_estimate=pl.CostEstimate(
            flops=6 * tokens * hidden * hidden, bytes_accessed=4_000_000, transcendentals=0
        ),
        name="apply_fast",
    )(place, q, attended, *units)


def project_kernel(tags, rows_in, place, *rest):
    blocks, units = rest[: len(tags)], rest[len(tags) : -2]
    mixed, full = rest[-2:]
    at = 0
    for unit in units:
        for part in range(unit.shape[0] // rows_in):
            rows = pl.ds(pl.multiple_of(place[ORIGINS + at] * rows_in, rows_in), rows_in)
            full[rows, :] = unit[part * rows_in : (part + 1) * rows_in, :]
            at += 1
    width = blocks[0].shape[1]
    value = None
    for block, tag in zip(blocks, tags):
        rows = pl.ds(pl.multiple_of((place[3] ^ tag) * width, width), width)
        part = matmul(block[...], full[rows, :])
        value = part if value is None else value + part
    mixed[...] = value.astype(mixed.dtype)


def project(place, blocks, tags, near, far, rows_in):
    tokens = blocks[0].shape[0]
    units = near + far
    depth, width = sum(unit.shape[0] for unit in units), units[0].shape[1]
    return pl.pallas_call(
        functools.partial(project_kernel, tags, rows_in),
        out_shape=jax.ShapeDtypeStruct((tokens, width), jnp.bfloat16),
        in_specs=[pl.BlockSpec(memory_space=pltpu.SMEM)]
        + [whole_spec()] * (len(units) + len(blocks)),
        out_specs=whole_spec(),
        scratch_shapes=[pltpu.VMEM((depth, width), jnp.bfloat16)],
        compiler_params=params(12),
        cost_estimate=pl.CostEstimate(
            flops=2 * tokens * depth * width, bytes_accessed=4_000_000, transcendentals=0
        ),
        name="project",
    )(place, *blocks, *units)


def ring_order(outer):
    return [0] + list(range(1, outer, 2)) + list(range(outer - 2 + outer % 2, 0, -2))


def ring_step(unit, outer):
    order = ring_order(outer)
    pairs = []
    for place, z in enumerate(order):
        to = order[(place + 1) % outer]
        pairs += [(2 * z + y, 2 * to + y) for y in range(2)]
    return lax.ppermute(unit, "seq", pairs)


def after(array, *others):
    return lax.optimization_barrier((array,) + others)[0]


def place_table(outer, heads):
    order = ring_order(outer)
    table = []
    for s in range(2 * outer):
        place = order.index(s // 2)
        sources = [order[(place - step) % outer] for step in range(outer)]
        near = [2 * z + s % 2 for z in sources]
        far = [2 * z + 1 - s % 2 for z in sources]
        table += [[s % 2, s // 2, s, head] + near + far for head in range(heads)]
    return np.array(table, np.int32)


def renormalize(base, moment):
    updated = base - moment
    base_rms = jnp.sqrt(jnp.mean(base * base, axis=-1, keepdims=True) + NORM_EPS)
    new_rms = jnp.sqrt(jnp.mean(updated * updated, axis=-1, keepdims=True) + NORM_EPS)
    return (updated * (base_rms / new_rms)).astype(jnp.bfloat16)


def attention(queries, keys, values, early_keys, early_values, position):
    tok_rows = queries.shape[0]
    all_keys = jnp.concatenate([early_keys, keys], axis=0)
    all_values = jnp.concatenate([early_values, values], axis=0)
    key_pos = (position - 1) * tok_rows + jnp.arange(all_keys.shape[0])
    query_pos = position * tok_rows + jnp.arange(tok_rows)
    spacing = query_pos[:, None] - key_pos[None, :]
    allowed = (spacing >= 0) & (spacing < WINDOW) & (key_pos[None, :] >= 0)
    scores = times_transposed(queries, all_keys) * (1.0 / math.sqrt(HD))
    scores = jnp.where(allowed, scores, NEG_LARGE)
    highest = jnp.max(scores, axis=1, keepdims=True)
    expo = jnp.exp(scores - highest)
    probs = (expo / jnp.sum(expo, axis=1, keepdims=True)).astype(jnp.bfloat16)
    return jnp.dot(probs, all_values, preferred_element_type=jnp.float32)


def shards(queries, keys, values, rates, fast, momentum, out_proj):
    tok_rows = queries.shape[0]
    ranks = lax.axis_size("seq")
    heads = lax.axis_size("head")
    own_rows = momentum.shape[2]
    if own_rows % 16 or ranks % 4 or heads % 2 or tok_rows != WINDOW:
        return plain(queries, keys, values, rates, fast, momentum, out_proj)
    outer = ranks // 2
    grad_scale = 1.0 / math.sqrt(tok_rows * ranks)
    index = lax.axis_index("seq") * heads + lax.axis_index("head")
    place = lax.dynamic_index_in_dim(jnp.asarray(place_table(outer, heads)), index, 0, False)

    rates_row = rates.reshape(1, tok_rows)
    pair_rates = swap(rates_row, "seq", 1)
    pair_keys = swap(keys, "seq", 1)
    values = after(values, pair_rates)
    pair_values = swap(values, "seq", 1)

    up_values = lax.ppermute(values, "seq", [(s, s + 2) for s in range(1, ranks - 2, 2)])
    up_keys = lax.ppermute(pair_keys, "seq", [(s, s + 2) for s in range(0, ranks - 2, 2)])
    up_values = lax.ppermute(up_values, "seq", [(s, s - 1) for s in range(1, ranks, 2)])

    wide = [after(out_proj, pair_rates)]
    for _ in range(1, outer):
        wide.append(ring_step(wide[-1], outer))
    half = outer // 2
    wide = [jnp.concatenate(wide[:half]), jnp.concatenate(wide[half:])]
    wide_far = [swap(wide[0], "seq", 1)]

    acc = own_gradients(place, keys, values, rates_row, fast, outer, grad_scale)
    summed = both_gradients(
        place, pair_keys, after(pair_values, *wide), pair_rates, fast, acc, outer, grad_scale
    )
    pieces = [swap(summed[step], "seq", step * 2) for step in range(1, outer)]
    attended = window_attention(
        place, queries, keys, values, pair_keys, pair_values, up_keys, up_values
    )
    pieces[0] = after(pieces[0], attended, wide_far[0])
    moment, renewed = renew(place, fast, momentum, summed[0], pieces)

    near, far = [renewed], [swap(renewed, "seq", 1)]
    for step in range(1, outer):
        near.append(ring_step(near[-1], outer))
        if step > 1:
            near[-1] = after(near[-1], far[step - 2])
        far.append(swap(near[-1], "seq", 1))
    wide_far.append(swap(after(wide[1], far[-2]), "seq", 1))
    combined = apply_fast(place, queries, attended, near + far)

    blocks = [(combined, 0)]
    mask = heads // 2
    while mask:
        blocks = blocks + [(swap(block, "head", mask), tag ^ mask) for block, tag in blocks]
        mask //= 2
    mixed = project(
        place, [b for b, _ in blocks], [t for _, t in blocks], wide, wide_far, out_proj.shape[0]
    )
    return (mixed, moment)


def plain(queries, keys, values, rates, fast, momentum, out_proj):
    tok_rows = queries.shape[0]
    ranks = lax.axis_size("seq")
    position = lax.axis_index("seq")
    own_rows = momentum.shape[2]
    grad_scale = 1.0 / math.sqrt(tok_rows * ranks)
    weights = fast[0]
    h_gate = times_transposed(keys, weights[0])
    h_up = times_transposed(keys, weights[1])
    sigma = jax.nn.sigmoid(h_gate)
    gated = (h_gate * sigma * h_up).astype(jnp.bfloat16)
    errors = (-grad_scale * rates * values.astype(jnp.float32)).astype(jnp.bfloat16)
    grad_down = contract_rows(errors, gated)
    back = matmul(errors, weights[2])
    d_gate = (back * h_up * sigma * (1.0 + h_gate * (1.0 - sigma))).astype(jnp.bfloat16)
    d_up = (back * h_gate * sigma).astype(jnp.bfloat16)
    grads = jnp.stack([contract_rows(d_gate, keys), contract_rows(d_up, keys), grad_down])
    summed_rows = lax.psum_scatter(grads, "seq", scatter_dimension=1, tiled=True)
    moment_own = MOMENTUM_DECAY * momentum[0] + summed_rows
    base_rows = lax.dynamic_slice_in_dim(weights, position * own_rows, own_rows, 1).astype(jnp.float32)
    renewed = lax.all_gather(renormalize(base_rows, moment_own), "seq", axis=1, tiled=True)
    q_gate = times_transposed(queries, renewed[0])
    q_up = times_transposed(queries, renewed[1])
    fast_in = (q_gate * jax.nn.sigmoid(q_gate) * q_up).astype(jnp.bfloat16)
    fast_out = times_transposed(fast_in, renewed[2])
    behind = [(i, i + 1) for i in range(ranks - 1)]
    early_keys = lax.ppermute(keys, "seq", behind)
    early_values = lax.ppermute(values, "seq", behind)
    attended = attention(queries, keys, values, early_keys, early_values, position)
    combined = (attended + fast_out).astype(jnp.bfloat16)
    all_heads = lax.all_gather(combined, "head", axis=1, tiled=True)
    projection = lax.all_gather(out_proj, "seq", axis=0, tiled=True)
    return (matmul(all_heads, projection).astype(jnp.bfloat16), moment_own[None])


def solution(mesh):
    return jax.shard_map(
        shards,
        mesh=mesh,
        in_specs=(
            P("seq", "head"),
            P("seq", "head"),
            P("seq", "head"),
            P("seq", "head"),
            P("head", None, None, None),
            P("head", None, "seq", None),
            P("seq", "head"),
        ),
        out_specs=(P("seq", "head"), P("head", None, "seq", None)),
        check_vma=False,
    )
```

```python
import functools
import math

import jax
import jax.numpy as jnp
import numpy as np
from jax import lax
from jax.experimental import pallas as pl
from jax.experimental.pallas import tpu as pltpu
from jax.sharding import PartitionSpec as P

HD = 512
WINDOW = 512

MOMENTUM_DECAY = 0.9
NORM_EPS = 1e-06
NEG_LARGE = -1e30
MIB = 1024 * 1024
ORIGINS = 4
BRIEF = pl.CostEstimate(flops=1, bytes_accessed=1, transcendentals=0)


def times_transposed(left, right):
    return lax.dot_general(
        left, right, (((1,), (1,)), ((), ())), preferred_element_type=jnp.float32
    )


def contract_rows(left, right):
    return lax.dot_general(
        left, right, (((0,), (0,)), ((), ())), preferred_element_type=jnp.float32
    )


def matmul(left, right):
    return jnp.dot(left, right, preferred_element_type=jnp.float32)


def swap(array, axis, mask):
    devices = lax.axis_size(axis)
    return lax.ppermute(array, axis, [(i, i ^ mask) for i in range(devices)])


def params(mib):
    return pltpu.CompilerParams(vmem_limit_bytes=mib * MIB)


def whole_spec():
    return pl.BlockSpec(memory_space=pltpu.VMEM)


def gradient_rows(outer, side, k, e, w, eye, hg_s, hu_s, err_s, dg_s, du_s):
    tokens, hidden = k.shape
    own = hidden // (2 * outer)
    hg = times_transposed(w[0], k)
    hu = times_transposed(w[1], k)
    hg_s[...] = hg
    hu_s[...] = hu
    gated = (hg * jax.nn.sigmoid(hg) * hu).astype(jnp.bfloat16)
    err_s[...] = times_transposed(eye, e).astype(jnp.bfloat16)
    down_t = times_transposed(eye, w[2]).astype(jnp.bfloat16)
    back = matmul(down_t, err_s[...])
    dg_s[2] = back
    errors = []
    for z in range(outer):
        rows = pl.ds(pl.multiple_of((2 * z + side) * own, own), own)
        to = pl.ds(z * own, own)
        g, u, b = hg_s[rows], hu_s[rows], dg_s[2, rows]
        s = jax.nn.sigmoid(g)
        du_s[0, to] = (b * u * s * (1.0 + g * (1.0 - s))).astype(jnp.bfloat16)
        du_s[1, to] = (b * g * s).astype(jnp.bfloat16)
        du_s[2, to] = err_s[rows]
    return (
        matmul(du_s[0], k),
        matmul(du_s[1], k),
        times_transposed(du_s[2], gated),
    )


def identity(size):
    rows = lax.broadcasted_iota(jnp.int32, (size, size), 0)
    columns = lax.broadcasted_iota(jnp.int32, (size, size), 1)
    return jnp.where(rows == columns, 1.0, 0.0).astype(jnp.bfloat16)


def own_kernel(outer, place, k, e, w, acc, *scratch):
    eye = identity(e.shape[1])
    parts = gradient_rows(outer, place[0], k[...], e[...], w[0], eye, *scratch)
    own = acc.shape[2]
    for i, part in enumerate(parts):
        acc[:, i] = part.reshape(outer, own, part.shape[1])


def both_kernel(outer, place, k, e, w, acc, mine, *rest):
    sent, scratch = rest[: outer - 1], rest[outer - 1 :]
    eye = identity(e.shape[1])
    parts = gradient_rows(outer, place[0], k[...], e[...], w[0], eye, *scratch)
    own = acc.shape[2]
    total = scratch[1]
    for i, part in enumerate(parts):
        total[pl.ds(0, outer * own), :] = part + acc[:, i].reshape(outer * own, part.shape[1])
        mine[i] = total[pl.ds(pl.multiple_of(place[1] * own, own), own), :]
        for step in range(1, outer):
            other = place[1] ^ step
            block = total[pl.ds(pl.multiple_of(other * own, own), own), :]
            sent[step - 1][i] = block.astype(jnp.bfloat16)


def gradient_scratch(tokens, hidden):
    return [
        pltpu.VMEM((hidden, tokens), jnp.float32),
        pltpu.VMEM((hidden, tokens), jnp.float32),
        pltpu.VMEM((hidden, tokens), jnp.bfloat16),
        pltpu.VMEM((3, hidden, tokens), jnp.float32),
        pltpu.VMEM((3, hidden // 2, tokens), jnp.bfloat16),
    ]


def own_gradients(place, k, e, w, outer):
    tokens, hidden = k.shape
    own = hidden // (2 * outer)
    return pl.pallas_call(
        functools.partial(own_kernel, outer),
        out_shape=jax.ShapeDtypeStruct((outer, 3, own, hidden), jnp.float32),
        in_specs=[pl.BlockSpec(memory_space=pltpu.SMEM)] + [whole_spec()] * 3,
        out_specs=whole_spec(),
        scratch_shapes=gradient_scratch(tokens, hidden),
        compiler_params=params(12),
        cost_estimate=BRIEF,
        name="own_gradients",
    )(place, k, e, w)


def both_gradients(place, k, e, w, acc, outer):
    tokens, hidden = k.shape
    own = hidden // (2 * outer)
    return pl.pallas_call(
        functools.partial(both_kernel, outer),
        out_shape=[jax.ShapeDtypeStruct((3, own, hidden), jnp.float32)]
        + [jax.ShapeDtypeStruct((3, own, hidden), jnp.bfloat16)] * (outer - 1),
        in_specs=[pl.BlockSpec(memory_space=pltpu.SMEM)] + [whole_spec()] * 4,
        out_specs=[whole_spec()] * outer,
        scratch_shapes=gradient_scratch(tokens, hidden),
        compiler_params=params(12),
        cost_estimate=BRIEF,
        name="both_gradients",
    )(place, k, e, w, acc)


def attend_kernel(blocks, place, q, k, v, pair_k, up_k, early_v, out):
    early_k = jnp.where(place[0] == 0, up_k[...], pair_k[...])
    early_v = early_v[...]
    early_v = jnp.where(place[2] > 0, early_v, jnp.zeros_like(early_v))
    tokens = q.shape[0]
    rows = tokens // blocks
    scale = 1.0 / math.sqrt(q.shape[1])
    for b in range(blocks):
        first, last = b * rows, (b + 1) * rows
        own = times_transposed(q[first:last], k[:last]) * scale
        old = times_transposed(q[first:last], early_k[first:]) * scale
        row = first + lax.broadcasted_iota(jnp.int32, own.shape, 0)
        column = lax.broadcasted_iota(jnp.int32, own.shape, 1)
        own = jnp.where(column <= row, own, NEG_LARGE)
        row = first + lax.broadcasted_iota(jnp.int32, old.shape, 0)
        column = first + lax.broadcasted_iota(jnp.int32, old.shape, 1)
        old = jnp.where((column > row) & (place[2] > 0), old, NEG_LARGE)
        highest = jnp.maximum(
            jnp.max(own, axis=1, keepdims=True), jnp.max(old, axis=1, keepdims=True)
        )
        own, old = jnp.exp(own - highest), jnp.exp(old - highest)
        total = jnp.sum(own, axis=1, keepdims=True) + jnp.sum(old, axis=1, keepdims=True)
        own = (own / total).astype(jnp.bfloat16)
        old = (old / total).astype(jnp.bfloat16)
        out[first:last] = matmul(own, v[:last]) + matmul(old, early_v[first:])


def window_attention(place, q, k, v, *early):
    tokens, hidden = q.shape
    return pl.pallas_call(
        functools.partial(attend_kernel, 2),
        out_shape=jax.ShapeDtypeStruct((tokens, hidden), jnp.float32),
        in_specs=[pl.BlockSpec(memory_space=pltpu.SMEM)] + [whole_spec()] * 6,
        out_specs=whole_spec(),
        compiler_params=params(12),
        cost_estimate=BRIEF,
        name="window_attention",
    )(place, q, k, v, *early)


def pick_kernel(place, even, odd, out):
    @pl.when(place[0] == 0)
    def _():
        out[...] = even[...]

    @pl.when(place[0] == 1)
    def _():
        out[...] = odd[...]


def pick(place, even, odd):
    return pl.pallas_call(
        pick_kernel,
        out_shape=jax.ShapeDtypeStruct(even.shape, even.dtype),
        in_specs=[pl.BlockSpec(memory_space=pltpu.SMEM)] + [whole_spec()] * 2,
        out_specs=whole_spec(),
        compiler_params=params(12),
        cost_estimate=BRIEF,
        name="pick",
    )(place, even, odd)


def renew_kernel(place, w, momentum, mine, *rest):
    pieces, (moment, renewed) = rest[:-2], rest[-2:]
    own = mine.shape[1]
    total = mine[...]
    for piece in pieces:
        total = total + piece[...].astype(jnp.float32)
    new = MOMENTUM_DECAY * momentum[0] + total
    moment[0] = new
    rows = pl.ds(pl.multiple_of(place[2] * own, own), own)
    for i in range(w.shape[1]):
        base = w[0, i, rows, :].astype(jnp.float32)
        renewed[i] = renormalize(base, new[i])


def renew(place, w, momentum, mine, pieces):
    return pl.pallas_call(
        renew_kernel,
        out_shape=[
            jax.ShapeDtypeStruct(momentum.shape, jnp.float32),
            jax.ShapeDtypeStruct(mine.shape, jnp.bfloat16),
        ],
        in_specs=[pl.BlockSpec(memory_space=pltpu.SMEM)] + [whole_spec()] * (3 + len(pieces)),
        out_specs=[whole_spec()] * 2,
        compiler_params=params(12),
        cost_estimate=BRIEF,
        name="renew",
    )(place, w, momentum, mine, *pieces)


def apply_kernel(count, place, q, attended, *rest):
    units, combined, full = rest[:count], rest[count], rest[count + 1]
    own = units[0].shape[1]
    for i in range(count):
        rows = pl.ds(pl.multiple_of(place[ORIGINS + i] * own, own), own)
        full[:, rows, :] = units[i][...]
    b1 = times_transposed(q[...], full[0])
    b3 = times_transposed(q[...], full[1])
    fast_in = (b1 * jax.nn.sigmoid(b1) * b3).astype(jnp.bfloat16)
    out = times_transposed(fast_in, full[2])
    combined[...] = (attended[...] + out).astype(jnp.bfloat16)


def apply_fast(place, q, attended, units):
    tokens, hidden = q.shape
    return pl.pallas_call(
        functools.partial(apply_kernel, len(units)),
        out_shape=jax.ShapeDtypeStruct((tokens, hidden), jnp.bfloat16),
        in_specs=[pl.BlockSpec(memory_space=pltpu.SMEM)] + [whole_spec()] * (2 + len(units)),
        out_specs=whole_spec(),
        scratch_shapes=[pltpu.VMEM((3, hidden, hidden), jnp.bfloat16)],
        compiler_params=params(12),
        cost_estimate=BRIEF,
        name="apply_fast",
    )(place, q, attended, *units)


def project_kernel(tags, rows_in, place, *rest):
    blocks, units = rest[: len(tags)], rest[len(tags) : -2]
    mixed, full = rest[-2:]
    at = 0
    for unit in units:
        for part in range(unit.shape[0] // rows_in):
            rows = pl.ds(pl.multiple_of(place[ORIGINS + at] * rows_in, rows_in), rows_in)
            full[rows, :] = unit[part * rows_in : (part + 1) * rows_in, :]
            at += 1
    width = blocks[0].shape[1]
    value = None
    for block, tag in zip(blocks, tags):
        rows = pl.ds(pl.multiple_of((place[3] ^ tag) * width, width), width)
        part = matmul(block[...], full[rows, :])
        value = part if value is None else value + part
    mixed[...] = value.astype(mixed.dtype)


def project(place, blocks, tags, near, far, rows_in):
    tokens = blocks[0].shape[0]
    units = near + far
    depth, width = sum(unit.shape[0] for unit in units), units[0].shape[1]
    return pl.pallas_call(
        functools.partial(project_kernel, tags, rows_in),
        out_shape=jax.ShapeDtypeStruct((tokens, width), jnp.bfloat16),
        in_specs=[pl.BlockSpec(memory_space=pltpu.SMEM)]
        + [whole_spec()] * (len(units) + len(blocks)),
        out_specs=whole_spec(),
        scratch_shapes=[pltpu.VMEM((depth, width), jnp.bfloat16)],
        compiler_params=params(12),
        cost_estimate=BRIEF,
        name="project",
    )(place, *blocks, *units)


def ring_order(outer):
    return [0] + list(range(1, outer, 2)) + list(range(outer - 2 + outer % 2, 0, -2))


def ring_step(unit, outer):
    order = ring_order(outer)
    pairs = []
    for place, z in enumerate(order):
        to = order[(place + 1) % outer]
        pairs += [(2 * z + y, 2 * to + y) for y in range(2)]
    return lax.ppermute(unit, "seq", pairs)


def after(array, *others):
    return lax.optimization_barrier((array,) + others)[0]


def place_table(outer, heads):
    order = ring_order(outer)
    table = []
    for s in range(2 * outer):
        place = order.index(s // 2)
        sources = [order[(place - step) % outer] for step in range(outer)]
        near = [2 * z + s % 2 for z in sources]
        far = [2 * z + 1 - s % 2 for z in sources]
        table += [[s % 2, s // 2, s, head] + near + far for head in range(heads)]
    return np.array(table, np.int32)


def renormalize(base, moment):
    updated = base - moment
    base_rms = jnp.sqrt(jnp.mean(base * base, axis=-1, keepdims=True) + NORM_EPS)
    new_rms = jnp.sqrt(jnp.mean(updated * updated, axis=-1, keepdims=True) + NORM_EPS)
    return (updated * (base_rms / new_rms)).astype(jnp.bfloat16)


def attention(queries, keys, values, early_keys, early_values, position):
    tok_rows = queries.shape[0]
    all_keys = jnp.concatenate([early_keys, keys], axis=0)
    all_values = jnp.concatenate([early_values, values], axis=0)
    key_pos = (position - 1) * tok_rows + jnp.arange(all_keys.shape[0])
    query_pos = position * tok_rows + jnp.arange(tok_rows)
    spacing = query_pos[:, None] - key_pos[None, :]
    allowed = (spacing >= 0) & (spacing < WINDOW) & (key_pos[None, :] >= 0)
    scores = times_transposed(queries, all_keys) * (1.0 / math.sqrt(HD))
    scores = jnp.where(allowed, scores, NEG_LARGE)
    highest = jnp.max(scores, axis=1, keepdims=True)
    expo = jnp.exp(scores - highest)
    probs = (expo / jnp.sum(expo, axis=1, keepdims=True)).astype(jnp.bfloat16)
    return jnp.dot(probs, all_values, preferred_element_type=jnp.float32)


def shards(queries, keys, values, rates, fast, momentum, out_proj):
    tok_rows = queries.shape[0]
    ranks = lax.axis_size("seq")
    heads = lax.axis_size("head")
    own_rows = momentum.shape[2]
    if own_rows % 16 or ranks != 8 or heads % 2 or tok_rows != WINDOW:
        return plain(queries, keys, values, rates, fast, momentum, out_proj)
    outer = ranks // 2
    grad_scale = 1.0 / math.sqrt(tok_rows * ranks)
    index = lax.axis_index("seq") * heads + lax.axis_index("head")
    place = lax.dynamic_index_in_dim(jnp.asarray(place_table(outer, heads)), index, 0, False)

    pair_keys = swap(keys, "seq", 1)
    errors = (-grad_scale * rates * values.astype(jnp.float32)).astype(jnp.bfloat16)
    pair_errors = swap(errors, "seq", 1)

    up_values = lax.ppermute(values, "seq", [(s, s + 2) for s in range(1, ranks - 2, 2)])
    up_keys = lax.ppermute(pair_keys, "seq", [(s, s + 2) for s in range(0, ranks - 2, 2)])

    wide = [after(out_proj, errors)]
    for _ in range(2, outer):
        wide.append(ring_step(wide[-1], outer))

    acc = own_gradients(place, keys, errors, fast, outer)
    across = pick(place, values, up_values)
    pair_errors = after(pair_errors, up_keys, wide[-1], across)
    summed = both_gradients(place, pair_keys, pair_errors, fast, acc, outer)
    pieces = [swap(summed[step], "seq", step * 2) for step in range(1, outer)]
    early_values = swap(after(across, summed[1]), "seq", 1)
    pieces[2] = after(pieces[2], early_values)
    moment, renewed = renew(place, fast, momentum, summed[0], pieces)

    wide_far = [swap(after(wide[0], pieces[1]), "seq", 1)]
    wide.append(ring_step(after(wide[-1], renewed), outer))

    near, far = [renewed], [swap(renewed, "seq", 1)]
    for step in range(1, outer):
        near.append(ring_step(near[-1], outer))
        if step == 2:
            near[-1] = after(near[-1], far[0], wide[-1], wide_far[0])
            wide_far.append(swap(after(wide[1], near[-2]), "seq", 1))
            attended = window_attention(
                place, queries, keys, values, pair_keys, up_keys, early_values
            )
        if step == 3:
            near[-1] = after(near[-1], far[1], attended, wide_far[1])
        far.append(swap(near[-1], "seq", 1))
    rest = jnp.concatenate(wide[2:])
    wide_far.append(swap(after(rest, far[-2]), "seq", 1))
    combined = apply_fast(place, queries, attended, near + far)

    blocks = [(combined, 0)]
    mask = heads // 2
    while mask:
        blocks = blocks + [(swap(block, "head", mask), tag ^ mask) for block, tag in blocks]
        mask //= 2
    mixed = project(
        place, [b for b, _ in blocks], [t for _, t in blocks], wide, wide_far, out_proj.shape[0]
    )
    return (mixed, moment)


def plain(queries, keys, values, rates, fast, momentum, out_proj):
    tok_rows = queries.shape[0]
    ranks = lax.axis_size("seq")
    position = lax.axis_index("seq")
    own_rows = momentum.shape[2]
    grad_scale = 1.0 / math.sqrt(tok_rows * ranks)
    weights = fast[0]
    h_gate = times_transposed(keys, weights[0])
    h_up = times_transposed(keys, weights[1])
    sigma = jax.nn.sigmoid(h_gate)
    gated = (h_gate * sigma * h_up).astype(jnp.bfloat16)
    errors = (-grad_scale * rates * values.astype(jnp.float32)).astype(jnp.bfloat16)
    grad_down = contract_rows(errors, gated)
    back = matmul(errors, weights[2])
    d_gate = (back * h_up * sigma * (1.0 + h_gate * (1.0 - sigma))).astype(jnp.bfloat16)
    d_up = (back * h_gate * sigma).astype(jnp.bfloat16)
    grads = jnp.stack([contract_rows(d_gate, keys), contract_rows(d_up, keys), grad_down])
    summed_rows = lax.psum_scatter(grads, "seq", scatter_dimension=1, tiled=True)
    moment_own = MOMENTUM_DECAY * momentum[0] + summed_rows
    base_rows = lax.dynamic_slice_in_dim(weights, position * own_rows, own_rows, 1).astype(jnp.float32)
    renewed = lax.all_gather(renormalize(base_rows, moment_own), "seq", axis=1, tiled=True)
    q_gate = times_transposed(queries, renewed[0])
    q_up = times_transposed(queries, renewed[1])
    fast_in = (q_gate * jax.nn.sigmoid(q_gate) * q_up).astype(jnp.bfloat16)
    fast_out = times_transposed(fast_in, renewed[2])
    behind = [(i, i + 1) for i in range(ranks - 1)]
    early_keys = lax.ppermute(keys, "seq", behind)
    early_values = lax.ppermute(values, "seq", behind)
    attended = attention(queries, keys, values, early_keys, early_values, position)
    combined = (attended + fast_out).astype(jnp.bfloat16)
    all_heads = lax.all_gather(combined, "head", axis=1, tiled=True)
    projection = lax.all_gather(out_proj, "seq", axis=0, tiled=True)
    return (matmul(all_heads, projection).astype(jnp.bfloat16), moment_own[None])


def solution(mesh):
    return jax.shard_map(
        shards,
        mesh=mesh,
        in_specs=(
            P("seq", "head"),
            P("seq", "head"),
            P("seq", "head"),
            P("seq", "head"),
            P("head", None, None, None),
            P("head", None, "seq", None),
            P("seq", "head"),
        ),
        out_specs=(P("seq", "head"), P("head", None, "seq", None)),
        check_vma=False,
    )
```

```python
import functools
import math

import jax
import jax.numpy as jnp
import numpy as np
from jax import lax
from jax.experimental import pallas as pl
from jax.experimental.pallas import tpu as pltpu
from jax.sharding import PartitionSpec as P

HD = 512
WINDOW = 512

MOMENTUM_DECAY = 0.9
NORM_EPS = 1e-06
NEG_LARGE = -1e30
MIB = 1024 * 1024
ORIGINS = 4
BRIEF = pl.CostEstimate(flops=1, bytes_accessed=1, transcendentals=0)


def times_transposed(left, right):
    return lax.dot_general(
        left, right, (((1,), (1,)), ((), ())), preferred_element_type=jnp.float32
    )


def contract_rows(left, right):
    return lax.dot_general(
        left, right, (((0,), (0,)), ((), ())), preferred_element_type=jnp.float32
    )


def matmul(left, right):
    return jnp.dot(left, right, preferred_element_type=jnp.float32)


def swap(array, axis, mask):
    devices = lax.axis_size(axis)
    return lax.ppermute(array, axis, [(i, i ^ mask) for i in range(devices)])


def params(mib):
    return pltpu.CompilerParams(vmem_limit_bytes=mib * MIB)


def whole_spec():
    return pl.BlockSpec(memory_space=pltpu.VMEM)


def gradient_rows(outer, side, k, e, w, eye, hg_s, hu_s, err_s, dg_s, du_s):
    tokens, hidden = k.shape
    own = hidden // (2 * outer)
    hg = times_transposed(w[0], k)
    hu = times_transposed(w[1], k)
    hg_s[...] = hg
    hu_s[...] = hu
    gated = (hg * jax.nn.sigmoid(hg) * hu).astype(jnp.bfloat16)
    err_s[...] = times_transposed(eye, e).astype(jnp.bfloat16)
    down_t = times_transposed(eye, w[2]).astype(jnp.bfloat16)
    back = matmul(down_t, err_s[...])
    dg_s[2] = back
    errors = []
    for z in range(outer):
        rows = pl.ds(pl.multiple_of((2 * z + side) * own, own), own)
        to = pl.ds(z * own, own)
        g, u, b = hg_s[rows], hu_s[rows], dg_s[2, rows]
        s = jax.nn.sigmoid(g)
        du_s[0, to] = (b * u * s * (1.0 + g * (1.0 - s))).astype(jnp.bfloat16)
        du_s[1, to] = (b * g * s).astype(jnp.bfloat16)
        du_s[2, to] = err_s[rows]
    return (
        matmul(du_s[0], k),
        matmul(du_s[1], k),
        times_transposed(du_s[2], gated),
    )


def identity(size):
    rows = lax.broadcasted_iota(jnp.int32, (size, size), 0)
    columns = lax.broadcasted_iota(jnp.int32, (size, size), 1)
    return jnp.where(rows == columns, 1.0, 0.0).astype(jnp.bfloat16)


def own_kernel(outer, place, k, e, w, acc, *scratch):
    eye = identity(e.shape[1])
    parts = gradient_rows(outer, place[0], k[...], e[...], w[0], eye, *scratch)
    own = acc.shape[2]
    for i, part in enumerate(parts):
        acc[:, i] = part.reshape(outer, own, part.shape[1])


def both_kernel(outer, place, k, e, w, acc, mine, *rest):
    sent, scratch = rest[: outer - 1], rest[outer - 1 :]
    eye = identity(e.shape[1])
    parts = gradient_rows(outer, place[0], k[...], e[...], w[0], eye, *scratch)
    own = acc.shape[2]
    total = scratch[1]
    for i, part in enumerate(parts):
        total[pl.ds(0, outer * own), :] = part + acc[:, i].reshape(outer * own, part.shape[1])
        mine[i] = total[pl.ds(pl.multiple_of(place[1] * own, own), own), :]
        for step in range(1, outer):
            other = place[1] ^ step
            block = total[pl.ds(pl.multiple_of(other * own, own), own), :]
            sent[step - 1][i] = block.astype(jnp.bfloat16)


def gradient_scratch(tokens, hidden):
    return [
        pltpu.VMEM((hidden, tokens), jnp.float32),
        pltpu.VMEM((hidden, tokens), jnp.float32),
        pltpu.VMEM((hidden, tokens), jnp.bfloat16),
        pltpu.VMEM((3, hidden, tokens), jnp.float32),
        pltpu.VMEM((3, hidden // 2, tokens), jnp.bfloat16),
    ]


def own_gradients(place, k, e, w, outer):
    tokens, hidden = k.shape
    own = hidden // (2 * outer)
    return pl.pallas_call(
        functools.partial(own_kernel, outer),
        out_shape=jax.ShapeDtypeStruct((outer, 3, own, hidden), jnp.float32),
        in_specs=[pl.BlockSpec(memory_space=pltpu.SMEM)] + [whole_spec()] * 3,
        out_specs=whole_spec(),
        scratch_shapes=gradient_scratch(tokens, hidden),
        compiler_params=params(12),
        cost_estimate=BRIEF,
        name="own_gradients",
    )(place, k, e, w)


def both_gradients(place, k, e, w, acc, outer):
    tokens, hidden = k.shape
    own = hidden // (2 * outer)
    return pl.pallas_call(
        functools.partial(both_kernel, outer),
        out_shape=[jax.ShapeDtypeStruct((3, own, hidden), jnp.float32)]
        + [jax.ShapeDtypeStruct((3, own, hidden), jnp.bfloat16)] * (outer - 1),
        in_specs=[pl.BlockSpec(memory_space=pltpu.SMEM)] + [whole_spec()] * 4,
        out_specs=[whole_spec()] * outer,
        scratch_shapes=gradient_scratch(tokens, hidden),
        compiler_params=params(12),
        cost_estimate=BRIEF,
        name="both_gradients",
    )(place, k, e, w, acc)


def attend_kernel(blocks, place, q, k, v, pair_k, up_k, early_v, out):
    early_k = jnp.where(place[0] == 0, up_k[...], pair_k[...])
    early_v = early_v[: v.shape[0]]
    early_v = jnp.where(place[2] > 0, early_v, jnp.zeros_like(early_v))
    tokens = q.shape[0]
    rows = tokens // blocks
    scale = 1.0 / math.sqrt(q.shape[1])
    for b in range(blocks):
        first, last = b * rows, (b + 1) * rows
        own = times_transposed(q[first:last], k[:last]) * scale
        old = times_transposed(q[first:last], early_k[first:]) * scale
        row = first + lax.broadcasted_iota(jnp.int32, own.shape, 0)
        column = lax.broadcasted_iota(jnp.int32, own.shape, 1)
        own = jnp.where(column <= row, own, NEG_LARGE)
        row = first + lax.broadcasted_iota(jnp.int32, old.shape, 0)
        column = first + lax.broadcasted_iota(jnp.int32, old.shape, 1)
        old = jnp.where((column > row) & (place[2] > 0), old, NEG_LARGE)
        highest = jnp.maximum(
            jnp.max(own, axis=1, keepdims=True), jnp.max(old, axis=1, keepdims=True)
        )
        own, old = jnp.exp(own - highest), jnp.exp(old - highest)
        total = jnp.sum(own, axis=1, keepdims=True) + jnp.sum(old, axis=1, keepdims=True)
        own = (own / total).astype(jnp.bfloat16)
        old = (old / total).astype(jnp.bfloat16)
        out[first:last] = matmul(own, v[:last]) + matmul(old, early_v[first:])


def window_attention(place, q, k, v, *early):
    tokens, hidden = q.shape
    return pl.pallas_call(
        functools.partial(attend_kernel, 2),
        out_shape=jax.ShapeDtypeStruct((tokens, hidden), jnp.float32),
        in_specs=[pl.BlockSpec(memory_space=pltpu.SMEM)] + [whole_spec()] * 6,
        out_specs=whole_spec(),
        compiler_params=params(12),
        cost_estimate=BRIEF,
        name="window_attention",
    )(place, q, k, v, *early)


def crossing_kernel(place, even, odd, rows, out):
    tokens = even.shape[0]

    @pl.when(place[0] == 0)
    def _():
        out[:tokens] = even[...]

    @pl.when(place[0] == 1)
    def _():
        out[:tokens] = odd[...]

    out[tokens:] = rows[...]


def crossing(place, even, odd, rows):
    shape = (even.shape[0] + rows.shape[0], even.shape[1])
    return pl.pallas_call(
        crossing_kernel,
        out_shape=jax.ShapeDtypeStruct(shape, even.dtype),
        in_specs=[pl.BlockSpec(memory_space=pltpu.SMEM)] + [whole_spec()] * 3,
        out_specs=whole_spec(),
        compiler_params=params(12),
        cost_estimate=BRIEF,
        name="crossing",
    )(place, even, odd, rows)


def renew_kernel(place, w, momentum, mine, *rest):
    pieces, (moment, renewed) = rest[:-2], rest[-2:]
    own = mine.shape[1]
    total = mine[...]
    for piece in pieces:
        total = total + piece[...].astype(jnp.float32)
    new = MOMENTUM_DECAY * momentum[0] + total
    moment[0] = new
    rows = pl.ds(pl.multiple_of(place[2] * own, own), own)
    for i in range(w.shape[1]):
        base = w[0, i, rows, :].astype(jnp.float32)
        renewed[i] = renormalize(base, new[i])


def renew(place, w, momentum, mine, pieces):
    return pl.pallas_call(
        renew_kernel,
        out_shape=[
            jax.ShapeDtypeStruct(momentum.shape, jnp.float32),
            jax.ShapeDtypeStruct(mine.shape, jnp.bfloat16),
        ],
        in_specs=[pl.BlockSpec(memory_space=pltpu.SMEM)] + [whole_spec()] * (3 + len(pieces)),
        out_specs=[whole_spec()] * 2,
        compiler_params=params(12),
        cost_estimate=BRIEF,
        name="renew",
    )(place, w, momentum, mine, *pieces)


def apply_kernel(count, place, q, attended, *rest):
    units, combined, full = rest[:count], rest[count], rest[count + 1]
    own = units[0].shape[1]
    for i in range(count):
        step, across = i % (count // 2), i // (count // 2)
        rows = pl.ds(pl.multiple_of((place[2] ^ (2 * step + across)) * own, own), own)
        full[:, rows, :] = units[i][...]
    b1 = times_transposed(q[...], full[0])
    b3 = times_transposed(q[...], full[1])
    fast_in = (b1 * jax.nn.sigmoid(b1) * b3).astype(jnp.bfloat16)
    out = times_transposed(fast_in, full[2])
    combined[...] = (attended[...] + out).astype(jnp.bfloat16)


def apply_fast(place, q, attended, units):
    tokens, hidden = q.shape
    return pl.pallas_call(
        functools.partial(apply_kernel, len(units)),
        out_shape=jax.ShapeDtypeStruct((tokens, hidden), jnp.bfloat16),
        in_specs=[pl.BlockSpec(memory_space=pltpu.SMEM)] + [whole_spec()] * (2 + len(units)),
        out_specs=whole_spec(),
        scratch_shapes=[pltpu.VMEM((3, hidden, hidden), jnp.bfloat16)],
        compiler_params=params(12),
        cost_estimate=BRIEF,
        name="apply_fast",
    )(place, q, attended, *units)


def project_kernel(tags, rows_in, place, *rest):
    blocks, units = rest[: len(tags)], rest[len(tags) : -2]
    mixed, full = rest[-2:]
    for at, unit in enumerate(units):
        rows = pl.ds(pl.multiple_of(place[ORIGINS + at] * rows_in, rows_in), rows_in)
        full[rows, :] = unit[unit.shape[0] - rows_in :, :]
    width = blocks[0].shape[1]
    value = None
    for block, tag in zip(blocks, tags):
        rows = pl.ds(pl.multiple_of((place[3] ^ tag) * width, width), width)
        part = matmul(block[...], full[rows, :])
        value = part if value is None else value + part
    mixed[...] = value.astype(mixed.dtype)


def project(place, blocks, tags, near, far, rows_in):
    tokens = blocks[0].shape[0]
    units = near + far
    depth, width = rows_in * len(units), units[0].shape[1]
    return pl.pallas_call(
        functools.partial(project_kernel, tags, rows_in),
        out_shape=jax.ShapeDtypeStruct((tokens, width), jnp.bfloat16),
        in_specs=[pl.BlockSpec(memory_space=pltpu.SMEM)]
        + [whole_spec()] * (len(units) + len(blocks)),
        out_specs=whole_spec(),
        scratch_shapes=[pltpu.VMEM((depth, width), jnp.bfloat16)],
        compiler_params=params(12),
        cost_estimate=BRIEF,
        name="project",
    )(place, *blocks, *units)


def ring_order(outer):
    return [0] + list(range(1, outer, 2)) + list(range(outer - 2 + outer % 2, 0, -2))


def ring_step(unit, outer):
    order = ring_order(outer)
    pairs = []
    for place, z in enumerate(order):
        to = order[(place + 1) % outer]
        pairs += [(2 * z + y, 2 * to + y) for y in range(2)]
    return lax.ppermute(unit, "seq", pairs)


def after(array, *others):
    return lax.optimization_barrier((array,) + others)[0]


def place_table(outer, heads):
    order = ring_order(outer)
    table = []
    for s in range(2 * outer):
        place = order.index(s // 2)
        sources = [order[(place - step) % outer] for step in range(outer)]
        near = [2 * z + s % 2 for z in sources]
        far = [2 * z + 1 - s % 2 for z in sources]
        table += [[s % 2, s // 2, s, head] + near + far for head in range(heads)]
    return np.array(table, np.int32)


def renormalize(base, moment):
    updated = base - moment
    base_rms = jnp.sqrt(jnp.mean(base * base, axis=-1, keepdims=True) + NORM_EPS)
    new_rms = jnp.sqrt(jnp.mean(updated * updated, axis=-1, keepdims=True) + NORM_EPS)
    return (updated * (base_rms / new_rms)).astype(jnp.bfloat16)


def attention(queries, keys, values, early_keys, early_values, position):
    tok_rows = queries.shape[0]
    all_keys = jnp.concatenate([early_keys, keys], axis=0)
    all_values = jnp.concatenate([early_values, values], axis=0)
    key_pos = (position - 1) * tok_rows + jnp.arange(all_keys.shape[0])
    query_pos = position * tok_rows + jnp.arange(tok_rows)
    spacing = query_pos[:, None] - key_pos[None, :]
    allowed = (spacing >= 0) & (spacing < WINDOW) & (key_pos[None, :] >= 0)
    scores = times_transposed(queries, all_keys) * (1.0 / math.sqrt(HD))
    scores = jnp.where(allowed, scores, NEG_LARGE)
    highest = jnp.max(scores, axis=1, keepdims=True)
    expo = jnp.exp(scores - highest)
    probs = (expo / jnp.sum(expo, axis=1, keepdims=True)).astype(jnp.bfloat16)
    return jnp.dot(probs, all_values, preferred_element_type=jnp.float32)


def shards(queries, keys, values, rates, fast, momentum, out_proj):
    tok_rows = queries.shape[0]
    ranks = lax.axis_size("seq")
    heads = lax.axis_size("head")
    own_rows = momentum.shape[2]
    if own_rows % 16 or ranks != 8 or heads % 2 or tok_rows != WINDOW:
        return plain(queries, keys, values, rates, fast, momentum, out_proj)
    outer = ranks // 2
    grad_scale = 1.0 / math.sqrt(tok_rows * ranks)
    index = lax.axis_index("seq") * heads + lax.axis_index("head")
    place = lax.dynamic_index_in_dim(jnp.asarray(place_table(outer, heads)), index, 0, False)

    pair_keys = swap(keys, "seq", 1)
    errors = (-grad_scale * rates * values.astype(jnp.float32)).astype(jnp.bfloat16)
    pair_errors = swap(errors, "seq", 1)

    up_values = lax.ppermute(values, "seq", [(s, s + 2) for s in range(1, ranks - 2, 2)])

    wide = [after(out_proj, errors)]
    wide.append(ring_step(wide[-1], outer))
    up_keys = after(pair_keys, wide[-1])
    up_keys = lax.ppermute(up_keys, "seq", [(s, s + 2) for s in range(0, ranks - 2, 2)])
    wide.append(ring_step(wide[-1], outer))

    acc = own_gradients(place, keys, errors, fast, outer)
    across = crossing(place, values, up_values, wide[0])
    pair_errors = after(pair_errors, up_keys, wide[-1], across)
    summed = both_gradients(place, pair_keys, pair_errors, fast, acc, outer)
    pieces = [swap(summed[step], "seq", step * 2) for step in range(1, outer)]
    crossed = swap(after(across, summed[1]), "seq", 1)
    pieces[2] = after(pieces[2], crossed)
    moment, renewed = renew(place, fast, momentum, summed[0], pieces)

    near = [renewed]
    for step in range(1, outer):
        near.append(swap(renewed, "seq", step * 2))
    far = [swap(renewed, "seq", 1)]
    near[1] = after(near[1], far[0])
    far += [swap(unit, "seq", 1) for unit in near[1:]]
    attended = window_attention(
        place, queries, keys, values, pair_keys, up_keys, after(crossed, near[1])
    )
    far[1] = after(far[1], attended)
    wide_far = [crossed, swap(after(wide[1], near[1]), "seq", 1)]
    wide.append(ring_step(after(wide[2], near[1], near[2]), outer))
    far[-1] = after(far[-1], wide_far[1], wide[3])
    wide_far += [swap(after(unit, far[1]), "seq", 1) for unit in wide[2:]]
    combined = apply_fast(place, queries, attended, near + far)

    blocks = [(combined, 0)]
    mask = heads // 2
    while mask:
        moved = [(swap(block, "head", mask), tag ^ mask) for block, tag in blocks]
        if mask > 1:
            moved = [(after(block, *wide_far[2:]), tag) for block, tag in moved]
        blocks = blocks + moved
        mask //= 2
    mixed = project(
        place, [b for b, _ in blocks], [t for _, t in blocks], wide, wide_far, out_proj.shape[0]
    )
    return (mixed, moment)


def plain(queries, keys, values, rates, fast, momentum, out_proj):
    tok_rows = queries.shape[0]
    ranks = lax.axis_size("seq")
    position = lax.axis_index("seq")
    own_rows = momentum.shape[2]
    grad_scale = 1.0 / math.sqrt(tok_rows * ranks)
    weights = fast[0]
    h_gate = times_transposed(keys, weights[0])
    h_up = times_transposed(keys, weights[1])
    sigma = jax.nn.sigmoid(h_gate)
    gated = (h_gate * sigma * h_up).astype(jnp.bfloat16)
    errors = (-grad_scale * rates * values.astype(jnp.float32)).astype(jnp.bfloat16)
    grad_down = contract_rows(errors, gated)
    back = matmul(errors, weights[2])
    d_gate = (back * h_up * sigma * (1.0 + h_gate * (1.0 - sigma))).astype(jnp.bfloat16)
    d_up = (back * h_gate * sigma).astype(jnp.bfloat16)
    grads = jnp.stack([contract_rows(d_gate, keys), contract_rows(d_up, keys), grad_down])
    summed_rows = lax.psum_scatter(grads, "seq", scatter_dimension=1, tiled=True)
    moment_own = MOMENTUM_DECAY * momentum[0] + summed_rows
    base_rows = lax.dynamic_slice_in_dim(weights, position * own_rows, own_rows, 1).astype(jnp.float32)
    renewed = lax.all_gather(renormalize(base_rows, moment_own), "seq", axis=1, tiled=True)
    q_gate = times_transposed(queries, renewed[0])
    q_up = times_transposed(queries, renewed[1])
    fast_in = (q_gate * jax.nn.sigmoid(q_gate) * q_up).astype(jnp.bfloat16)
    fast_out = times_transposed(fast_in, renewed[2])
    behind = [(i, i + 1) for i in range(ranks - 1)]
    early_keys = lax.ppermute(keys, "seq", behind)
    early_values = lax.ppermute(values, "seq", behind)
    attended = attention(queries, keys, values, early_keys, early_values, position)
    combined = (attended + fast_out).astype(jnp.bfloat16)
    all_heads = lax.all_gather(combined, "head", axis=1, tiled=True)
    projection = lax.all_gather(out_proj, "seq", axis=0, tiled=True)
    return (matmul(all_heads, projection).astype(jnp.bfloat16), moment_own[None])


def solution(mesh):
    return jax.shard_map(
        shards,
        mesh=mesh,
        in_specs=(
            P("seq", "head"),
            P("seq", "head"),
            P("seq", "head"),
            P("seq", "head"),
            P("head", None, None, None),
            P("head", None, "seq", None),
            P("seq", "head"),
        ),
        out_specs=(P("seq", "head"), P("head", None, "seq", None)),
        check_vma=False,
    )
```

```python
import functools
import math

import jax
import jax.numpy as jnp
import numpy as np
from jax import lax
from jax.experimental import pallas as pl
from jax.experimental.pallas import tpu as pltpu
from jax.sharding import PartitionSpec as P

HD = 512
WINDOW = 512

MOMENTUM_DECAY = 0.9
NORM_EPS = 1e-06
NEG_LARGE = -1e30
MIB = 1024 * 1024
ORIGINS = 4
BRIEF = pl.CostEstimate(flops=1, bytes_accessed=1, transcendentals=0)


def times_transposed(left, right):
    return lax.dot_general(
        left, right, (((1,), (1,)), ((), ())), preferred_element_type=jnp.float32
    )


def contract_rows(left, right):
    return lax.dot_general(
        left, right, (((0,), (0,)), ((), ())), preferred_element_type=jnp.float32
    )


def matmul(left, right):
    return jnp.dot(left, right, preferred_element_type=jnp.float32)


def swap(array, axis, mask):
    devices = lax.axis_size(axis)
    return lax.ppermute(array, axis, [(i, i ^ mask) for i in range(devices)])


def params(mib):
    return pltpu.CompilerParams(vmem_limit_bytes=mib * MIB)


def whole_spec():
    return pl.BlockSpec(memory_space=pltpu.VMEM)


def gradient_rows(outer, side, k, e, w, eye, hg_s, hu_s, err_s, dg_s, du_s):
    tokens, hidden = k.shape
    own = hidden // (2 * outer)
    hg = times_transposed(w[0], k)
    hu = times_transposed(w[1], k)
    hg_s[...] = hg
    hu_s[...] = hu
    gated = (hg * jax.nn.sigmoid(hg) * hu).astype(jnp.bfloat16)
    err_s[...] = times_transposed(eye, e).astype(jnp.bfloat16)
    down_t = times_transposed(eye, w[2]).astype(jnp.bfloat16)
    back = matmul(down_t, err_s[...])
    dg_s[2] = back
    errors = []
    for z in range(outer):
        rows = pl.ds(pl.multiple_of((2 * z + side) * own, own), own)
        to = pl.ds(z * own, own)
        g, u, b = hg_s[rows], hu_s[rows], dg_s[2, rows]
        s = jax.nn.sigmoid(g)
        du_s[0, to] = (b * u * s * (1.0 + g * (1.0 - s))).astype(jnp.bfloat16)
        du_s[1, to] = (b * g * s).astype(jnp.bfloat16)
        du_s[2, to] = err_s[rows]
    return (
        matmul(du_s[0], k),
        matmul(du_s[1], k),
        times_transposed(du_s[2], gated),
    )


def identity(size):
    rows = lax.broadcasted_iota(jnp.int32, (size, size), 0)
    columns = lax.broadcasted_iota(jnp.int32, (size, size), 1)
    return jnp.where(rows == columns, 1.0, 0.0).astype(jnp.bfloat16)


def own_kernel(outer, place, k, e, w, acc, *scratch):
    eye = identity(e.shape[1])
    parts = gradient_rows(outer, place[0], k[...], e[...], w[0], eye, *scratch)
    own = acc.shape[2]
    for i, part in enumerate(parts):
        acc[:, i] = part.reshape(outer, own, part.shape[1])


def both_kernel(outer, place, k, e, w, acc, mine, *rest):
    sent, scratch = rest[: outer - 1], rest[outer - 1 :]
    eye = identity(e.shape[1])
    parts = gradient_rows(outer, place[0], k[...], e[...], w[0], eye, *scratch)
    own = acc.shape[2]
    total = scratch[1]
    for i, part in enumerate(parts):
        total[pl.ds(0, outer * own), :] = part + acc[:, i].reshape(outer * own, part.shape[1])
        mine[i] = total[pl.ds(pl.multiple_of(place[1] * own, own), own), :]
        for step in range(1, outer):
            other = place[1] ^ step
            block = total[pl.ds(pl.multiple_of(other * own, own), own), :]
            sent[step - 1][i] = block.astype(jnp.bfloat16)


def gradient_scratch(tokens, hidden):
    return [
        pltpu.VMEM((hidden, tokens), jnp.float32),
        pltpu.VMEM((hidden, tokens), jnp.float32),
        pltpu.VMEM((hidden, tokens), jnp.bfloat16),
        pltpu.VMEM((3, hidden, tokens), jnp.float32),
        pltpu.VMEM((3, hidden // 2, tokens), jnp.bfloat16),
    ]


def own_gradients(place, k, e, w, outer):
    tokens, hidden = k.shape
    own = hidden // (2 * outer)
    return pl.pallas_call(
        functools.partial(own_kernel, outer),
        out_shape=jax.ShapeDtypeStruct((outer, 3, own, hidden), jnp.float32),
        in_specs=[pl.BlockSpec(memory_space=pltpu.SMEM)] + [whole_spec()] * 3,
        out_specs=whole_spec(),
        scratch_shapes=gradient_scratch(tokens, hidden),
        compiler_params=params(12),
        cost_estimate=BRIEF,
        name="own_gradients",
    )(place, k, e, w)


def both_gradients(place, k, e, w, acc, outer):
    tokens, hidden = k.shape
    own = hidden // (2 * outer)
    return pl.pallas_call(
        functools.partial(both_kernel, outer),
        out_shape=[jax.ShapeDtypeStruct((3, own, hidden), jnp.float32)]
        + [jax.ShapeDtypeStruct((3, own, hidden), jnp.bfloat16)] * (outer - 1),
        in_specs=[pl.BlockSpec(memory_space=pltpu.SMEM)] + [whole_spec()] * 4,
        out_specs=[whole_spec()] * outer,
        scratch_shapes=gradient_scratch(tokens, hidden),
        compiler_params=params(12),
        cost_estimate=BRIEF,
        name="both_gradients",
    )(place, k, e, w, acc)


def attend_kernel(blocks, place, q, k, v, pair_k, up_k, early_v, out):
    early_k = jnp.where(place[0] == 0, up_k[...], pair_k[...])
    early_v = early_v[: v.shape[0]]
    early_v = jnp.where(place[2] > 0, early_v, jnp.zeros_like(early_v))
    tokens = q.shape[0]
    rows = tokens // blocks
    scale = 1.0 / math.sqrt(q.shape[1])
    for b in range(blocks):
        first, last = b * rows, (b + 1) * rows
        own = times_transposed(q[first:last], k[:last]) * scale
        old = times_transposed(q[first:last], early_k[first:]) * scale
        row = first + lax.broadcasted_iota(jnp.int32, own.shape, 0)
        column = lax.broadcasted_iota(jnp.int32, own.shape, 1)
        own = jnp.where(column <= row, own, NEG_LARGE)
        row = first + lax.broadcasted_iota(jnp.int32, old.shape, 0)
        column = first + lax.broadcasted_iota(jnp.int32, old.shape, 1)
        old = jnp.where((column > row) & (place[2] > 0), old, NEG_LARGE)
        highest = jnp.maximum(
            jnp.max(own, axis=1, keepdims=True), jnp.max(old, axis=1, keepdims=True)
        )
        own, old = jnp.exp(own - highest), jnp.exp(old - highest)
        total = jnp.sum(own, axis=1, keepdims=True) + jnp.sum(old, axis=1, keepdims=True)
        own = (own / total).astype(jnp.bfloat16)
        old = (old / total).astype(jnp.bfloat16)
        out[first:last] = matmul(own, v[:last]) + matmul(old, early_v[first:])


def window_attention(place, q, k, v, *early):
    tokens, hidden = q.shape
    return pl.pallas_call(
        functools.partial(attend_kernel, 2),
        out_shape=jax.ShapeDtypeStruct((tokens, hidden), jnp.float32),
        in_specs=[pl.BlockSpec(memory_space=pltpu.SMEM)] + [whole_spec()] * 6,
        out_specs=whole_spec(),
        compiler_params=params(12),
        cost_estimate=BRIEF,
        name="window_attention",
    )(place, q, k, v, *early)


def crossing_kernel(place, even, odd, rows, out):
    tokens = even.shape[0]

    @pl.when(place[0] == 0)
    def _():
        out[:tokens] = even[...]

    @pl.when(place[0] == 1)
    def _():
        out[:tokens] = odd[...]

    out[tokens:] = rows[...]


def crossing(place, even, odd, rows):
    shape = (even.shape[0] + rows.shape[0], even.shape[1])
    return pl.pallas_call(
        crossing_kernel,
        out_shape=jax.ShapeDtypeStruct(shape, even.dtype),
        in_specs=[pl.BlockSpec(memory_space=pltpu.SMEM)] + [whole_spec()] * 3,
        out_specs=whole_spec(),
        compiler_params=params(12),
        cost_estimate=BRIEF,
        name="crossing",
    )(place, even, odd, rows)


def renew_kernel(place, w, momentum, mine, *rest):
    pieces, (moment, renewed) = rest[:-2], rest[-2:]
    own = mine.shape[1]
    total = mine[...]
    for piece in pieces:
        total = total + piece[...].astype(jnp.float32)
    new = MOMENTUM_DECAY * momentum[0] + total
    moment[0] = new
    rows = pl.ds(pl.multiple_of(place[2] * own, own), own)
    for i in range(w.shape[1]):
        base = w[0, i, rows, :].astype(jnp.float32)
        renewed[i] = renormalize(base, new[i])


def renew(place, w, momentum, mine, pieces):
    return pl.pallas_call(
        renew_kernel,
        out_shape=[
            jax.ShapeDtypeStruct(momentum.shape, jnp.float32),
            jax.ShapeDtypeStruct(mine.shape, jnp.bfloat16),
        ],
        in_specs=[pl.BlockSpec(memory_space=pltpu.SMEM)] + [whole_spec()] * (3 + len(pieces)),
        out_specs=[whole_spec()] * 2,
        compiler_params=params(12),
        cost_estimate=BRIEF,
        name="renew",
    )(place, w, momentum, mine, *pieces)


def apply_kernel(count, place, q, attended, *rest):
    units, combined, full = rest[:count], rest[count], rest[count + 1]
    own = units[0].shape[1]
    for i in range(count):
        step, across = i % (count // 2), i // (count // 2)
        rows = pl.ds(pl.multiple_of((place[2] ^ (2 * step + across)) * own, own), own)
        full[:, rows, :] = units[i][...]
    b1 = times_transposed(q[...], full[0])
    b3 = times_transposed(q[...], full[1])
    fast_in = (b1 * jax.nn.sigmoid(b1) * b3).astype(jnp.bfloat16)
    out = times_transposed(fast_in, full[2])
    combined[...] = (attended[...] + out).astype(jnp.bfloat16)


def apply_fast(place, q, attended, units):
    tokens, hidden = q.shape
    return pl.pallas_call(
        functools.partial(apply_kernel, len(units)),
        out_shape=jax.ShapeDtypeStruct((tokens, hidden), jnp.bfloat16),
        in_specs=[pl.BlockSpec(memory_space=pltpu.SMEM)] + [whole_spec()] * (2 + len(units)),
        out_specs=whole_spec(),
        scratch_shapes=[pltpu.VMEM((3, hidden, hidden), jnp.bfloat16)],
        compiler_params=params(12),
        cost_estimate=BRIEF,
        name="apply_fast",
    )(place, q, attended, *units)


def project_kernel(tags, rows_in, place, *rest):
    blocks, units = rest[: len(tags)], rest[len(tags) : -2]
    mixed, full = rest[-2:]
    for at, unit in enumerate(units):
        rows = pl.ds(pl.multiple_of(place[ORIGINS + at] * rows_in, rows_in), rows_in)
        full[rows, :] = unit[unit.shape[0] - rows_in :, :]
    width = blocks[0].shape[1]
    value = None
    for block, tag in zip(blocks, tags):
        rows = pl.ds(pl.multiple_of((place[3] ^ tag) * width, width), width)
        part = matmul(block[...], full[rows, :])
        value = part if value is None else value + part
    mixed[...] = value.astype(mixed.dtype)


def project(place, blocks, tags, near, far, rows_in):
    tokens = blocks[0].shape[0]
    units = near + far
    depth, width = rows_in * len(units), units[0].shape[1]
    return pl.pallas_call(
        functools.partial(project_kernel, tags, rows_in),
        out_shape=jax.ShapeDtypeStruct((tokens, width), jnp.bfloat16),
        in_specs=[pl.BlockSpec(memory_space=pltpu.SMEM)]
        + [whole_spec()] * (len(units) + len(blocks)),
        out_specs=whole_spec(),
        scratch_shapes=[pltpu.VMEM((depth, width), jnp.bfloat16)],
        compiler_params=params(12),
        cost_estimate=BRIEF,
        name="project",
    )(place, *blocks, *units)


def ring_order(outer):
    return [0] + list(range(1, outer, 2)) + list(range(outer - 2 + outer % 2, 0, -2))


def ring_step(unit, outer):
    order = ring_order(outer)
    pairs = []
    for place, z in enumerate(order):
        to = order[(place + 1) % outer]
        pairs += [(2 * z + y, 2 * to + y) for y in range(2)]
    return lax.ppermute(unit, "seq", pairs)


def after(array, *others):
    return lax.optimization_barrier((array,) + others)[0]


def place_table(outer, heads):
    order = ring_order(outer)
    table = []
    for s in range(2 * outer):
        place = order.index(s // 2)
        sources = [order[(place - step) % outer] for step in range(outer)]
        near = [2 * z + s % 2 for z in sources]
        far = [2 * z + 1 - s % 2 for z in sources]
        table += [[s % 2, s // 2, s, head] + near + far for head in range(heads)]
    return np.array(table, np.int32)


def renormalize(base, moment):
    updated = base - moment
    base_rms = jnp.sqrt(jnp.mean(base * base, axis=-1, keepdims=True) + NORM_EPS)
    new_rms = jnp.sqrt(jnp.mean(updated * updated, axis=-1, keepdims=True) + NORM_EPS)
    return (updated * (base_rms / new_rms)).astype(jnp.bfloat16)


def attention(queries, keys, values, early_keys, early_values, position):
    tok_rows = queries.shape[0]
    all_keys = jnp.concatenate([early_keys, keys], axis=0)
    all_values = jnp.concatenate([early_values, values], axis=0)
    key_pos = (position - 1) * tok_rows + jnp.arange(all_keys.shape[0])
    query_pos = position * tok_rows + jnp.arange(tok_rows)
    spacing = query_pos[:, None] - key_pos[None, :]
    allowed = (spacing >= 0) & (spacing < WINDOW) & (key_pos[None, :] >= 0)
    scores = times_transposed(queries, all_keys) * (1.0 / math.sqrt(HD))
    scores = jnp.where(allowed, scores, NEG_LARGE)
    highest = jnp.max(scores, axis=1, keepdims=True)
    expo = jnp.exp(scores - highest)
    probs = (expo / jnp.sum(expo, axis=1, keepdims=True)).astype(jnp.bfloat16)
    return jnp.dot(probs, all_values, preferred_element_type=jnp.float32)


def shards(queries, keys, values, rates, fast, momentum, out_proj):
    tok_rows = queries.shape[0]
    ranks = lax.axis_size("seq")
    heads = lax.axis_size("head")
    own_rows = momentum.shape[2]
    if own_rows % 16 or ranks != 8 or heads % 2 or tok_rows != WINDOW:
        return plain(queries, keys, values, rates, fast, momentum, out_proj)
    outer = ranks // 2
    grad_scale = 1.0 / math.sqrt(tok_rows * ranks)
    index = lax.axis_index("seq") * heads + lax.axis_index("head")
    place = lax.dynamic_index_in_dim(jnp.asarray(place_table(outer, heads)), index, 0, False)

    pair_keys = swap(keys, "seq", 1)
    errors = (-grad_scale * rates * values.astype(jnp.float32)).astype(jnp.bfloat16)
    pair_errors = swap(errors, "seq", 1)

    up_values = lax.ppermute(values, "seq", [(s, s + 2) for s in range(1, ranks - 2, 2)])

    wide = [out_proj]
    for _ in range(2):
        wide.append(ring_step(wide[-1], outer))
    up_keys = after(pair_keys, wide[-1])
    up_keys = lax.ppermute(up_keys, "seq", [(s, s + 2) for s in range(0, ranks - 2, 2)])

    acc = own_gradients(place, keys, errors, fast, outer)
    across = crossing(place, values, up_values, wide[0])
    pair_errors = after(pair_errors, up_keys, across)
    summed = both_gradients(place, pair_keys, pair_errors, fast, acc, outer)
    pieces = [swap(summed[step], "seq", step * 2) for step in range(1, outer)]
    crossed = swap(after(across, summed[1]), "seq", 1)
    pieces[2] = after(pieces[2], crossed)
    moment, renewed = renew(place, fast, momentum, summed[0], pieces)

    near = [renewed]
    for step in range(1, outer):
        near.append(swap(renewed, "seq", step * 2))
    far = [swap(renewed, "seq", 1)]
    near[1] = after(near[1], far[0])
    far.append(swap(near[1], "seq", 1))
    near[2] = after(near[2], far[1])
    far += [swap(unit, "seq", 1) for unit in near[2:]]
    attended = window_attention(
        place, queries, keys, values, pair_keys, up_keys, after(crossed, near[1])
    )
    far[2] = after(far[2], attended)
    wide_far = [crossed, swap(after(wide[1], near[1]), "seq", 1)]
    wide.append(ring_step(after(wide[2], near[1], near[2]), outer))
    far[-1] = after(far[-1], wide_far[1], wide[3])
    wide_far += [swap(after(unit, far[1]), "seq", 1) for unit in wide[2:]]
    combined = apply_fast(place, queries, attended, near + far)

    blocks = [(combined, 0)]
    mask = heads // 2
    while mask:
        moved = [(swap(block, "head", mask), tag ^ mask) for block, tag in blocks]
        if mask > 1:
            moved = [(after(block, *wide_far[2:]), tag) for block, tag in moved]
        blocks = blocks + moved
        mask //= 2
    mixed = project(
        place, [b for b, _ in blocks], [t for _, t in blocks], wide, wide_far, out_proj.shape[0]
    )
    return (mixed, moment)


def plain(queries, keys, values, rates, fast, momentum, out_proj):
    tok_rows = queries.shape[0]
    ranks = lax.axis_size("seq")
    position = lax.axis_index("seq")
    own_rows = momentum.shape[2]
    grad_scale = 1.0 / math.sqrt(tok_rows * ranks)
    weights = fast[0]
    h_gate = times_transposed(keys, weights[0])
    h_up = times_transposed(keys, weights[1])
    sigma = jax.nn.sigmoid(h_gate)
    gated = (h_gate * sigma * h_up).astype(jnp.bfloat16)
    errors = (-grad_scale * rates * values.astype(jnp.float32)).astype(jnp.bfloat16)
    grad_down = contract_rows(errors, gated)
    back = matmul(errors, weights[2])
    d_gate = (back * h_up * sigma * (1.0 + h_gate * (1.0 - sigma))).astype(jnp.bfloat16)
    d_up = (back * h_gate * sigma).astype(jnp.bfloat16)
    grads = jnp.stack([contract_rows(d_gate, keys), contract_rows(d_up, keys), grad_down])
    summed_rows = lax.psum_scatter(grads, "seq", scatter_dimension=1, tiled=True)
    moment_own = MOMENTUM_DECAY * momentum[0] + summed_rows
    base_rows = lax.dynamic_slice_in_dim(weights, position * own_rows, own_rows, 1).astype(jnp.float32)
    renewed = lax.all_gather(renormalize(base_rows, moment_own), "seq", axis=1, tiled=True)
    q_gate = times_transposed(queries, renewed[0])
    q_up = times_transposed(queries, renewed[1])
    fast_in = (q_gate * jax.nn.sigmoid(q_gate) * q_up).astype(jnp.bfloat16)
    fast_out = times_transposed(fast_in, renewed[2])
    behind = [(i, i + 1) for i in range(ranks - 1)]
    early_keys = lax.ppermute(keys, "seq", behind)
    early_values = lax.ppermute(values, "seq", behind)
    attended = attention(queries, keys, values, early_keys, early_values, position)
    combined = (attended + fast_out).astype(jnp.bfloat16)
    all_heads = lax.all_gather(combined, "head", axis=1, tiled=True)
    projection = lax.all_gather(out_proj, "seq", axis=0, tiled=True)
    return (matmul(all_heads, projection).astype(jnp.bfloat16), moment_own[None])


def solution(mesh):
    return jax.shard_map(
        shards,
        mesh=mesh,
        in_specs=(
            P("seq", "head"),
            P("seq", "head"),
            P("seq", "head"),
            P("seq", "head"),
            P("head", None, None, None),
            P("head", None, "seq", None),
            P("seq", "head"),
        ),
        out_specs=(P("seq", "head"), P("head", None, "seq", None)),
        check_vma=False,
    )
```

```python
import functools
import math

import jax
import jax.numpy as jnp
import numpy as np
from jax import lax
from jax.experimental import pallas as pl
from jax.experimental.pallas import tpu as pltpu
from jax.sharding import PartitionSpec as P

HD = 512
WINDOW = 512

MOMENTUM_DECAY = 0.9
NORM_EPS = 1e-06
NEG_LARGE = -1e30
MIB = 1024 * 1024
ORIGINS = 4
BRIEF = pl.CostEstimate(flops=1, bytes_accessed=1, transcendentals=0)


def times_transposed(left, right):
    return lax.dot_general(
        left, right, (((1,), (1,)), ((), ())), preferred_element_type=jnp.float32
    )


def contract_rows(left, right):
    return lax.dot_general(
        left, right, (((0,), (0,)), ((), ())), preferred_element_type=jnp.float32
    )


def matmul(left, right):
    return jnp.dot(left, right, preferred_element_type=jnp.float32)


def swap(array, axis, mask):
    devices = lax.axis_size(axis)
    return lax.ppermute(array, axis, [(i, i ^ mask) for i in range(devices)])


def params(mib):
    return pltpu.CompilerParams(vmem_limit_bytes=mib * MIB)


def whole_spec():
    return pl.BlockSpec(memory_space=pltpu.VMEM)


def gradient_rows(outer, side, k, e, w, eye, hg_s, hu_s, err_s, dg_s, du_s):
    tokens, hidden = k.shape
    own = hidden // (2 * outer)
    hg = times_transposed(w[0], k)
    hu = times_transposed(w[1], k)
    hg_s[...] = hg
    hu_s[...] = hu
    gated = (hg * jax.nn.sigmoid(hg) * hu).astype(jnp.bfloat16)
    err_s[...] = times_transposed(eye, e).astype(jnp.bfloat16)
    down_t = times_transposed(eye, w[2]).astype(jnp.bfloat16)
    back = matmul(down_t, err_s[...])
    dg_s[2] = back
    errors = []
    for z in range(outer):
        rows = pl.ds(pl.multiple_of((2 * z + side) * own, own), own)
        to = pl.ds(z * own, own)
        g, u, b = hg_s[rows], hu_s[rows], dg_s[2, rows]
        s = jax.nn.sigmoid(g)
        du_s[0, to] = (b * u * s * (1.0 + g * (1.0 - s))).astype(jnp.bfloat16)
        du_s[1, to] = (b * g * s).astype(jnp.bfloat16)
        du_s[2, to] = err_s[rows]
    return (
        matmul(du_s[0], k),
        matmul(du_s[1], k),
        times_transposed(du_s[2], gated),
    )


def identity(size):
    rows = lax.broadcasted_iota(jnp.int32, (size, size), 0)
    columns = lax.broadcasted_iota(jnp.int32, (size, size), 1)
    return jnp.where(rows == columns, 1.0, 0.0).astype(jnp.bfloat16)


def own_kernel(outer, place, k, e, w, acc, *scratch):
    eye = identity(e.shape[1])
    parts = gradient_rows(outer, place[0], k[...], e[...], w[0], eye, *scratch)
    own = acc.shape[2]
    for i, part in enumerate(parts):
        acc[:, i] = part.reshape(outer, own, part.shape[1])


def both_kernel(outer, place, k, e, w, acc, mine, *rest):
    sent, scratch = rest[: outer - 1], rest[outer - 1 :]
    eye = identity(e.shape[1])
    parts = gradient_rows(outer, place[0], k[...], e[...], w[0], eye, *scratch)
    own = acc.shape[2]
    total = scratch[1]
    for i, part in enumerate(parts):
        total[pl.ds(0, outer * own), :] = part + acc[:, i].reshape(outer * own, part.shape[1])
        mine[i] = total[pl.ds(pl.multiple_of(place[1] * own, own), own), :]
        for step in range(1, outer):
            other = place[1] ^ step
            block = total[pl.ds(pl.multiple_of(other * own, own), own), :]
            sent[step - 1][i] = block.astype(jnp.bfloat16)


def gradient_scratch(tokens, hidden):
    return [
        pltpu.VMEM((hidden, tokens), jnp.float32),
        pltpu.VMEM((hidden, tokens), jnp.float32),
        pltpu.VMEM((hidden, tokens), jnp.bfloat16),
        pltpu.VMEM((3, hidden, tokens), jnp.float32),
        pltpu.VMEM((3, hidden // 2, tokens), jnp.bfloat16),
    ]


def own_gradients(place, k, e, w, outer):
    tokens, hidden = k.shape
    own = hidden // (2 * outer)
    return pl.pallas_call(
        functools.partial(own_kernel, outer),
        out_shape=jax.ShapeDtypeStruct((outer, 3, own, hidden), jnp.float32),
        in_specs=[pl.BlockSpec(memory_space=pltpu.SMEM)] + [whole_spec()] * 3,
        out_specs=whole_spec(),
        scratch_shapes=gradient_scratch(tokens, hidden),
        compiler_params=params(12),
        cost_estimate=BRIEF,
        name="own_gradients",
    )(place, k, e, w)


def both_gradients(place, k, e, w, acc, outer):
    tokens, hidden = k.shape
    own = hidden // (2 * outer)
    return pl.pallas_call(
        functools.partial(both_kernel, outer),
        out_shape=[jax.ShapeDtypeStruct((3, own, hidden), jnp.float32)]
        + [jax.ShapeDtypeStruct((3, own, hidden), jnp.bfloat16)] * (outer - 1),
        in_specs=[pl.BlockSpec(memory_space=pltpu.SMEM)] + [whole_spec()] * 4,
        out_specs=[whole_spec()] * outer,
        scratch_shapes=gradient_scratch(tokens, hidden),
        compiler_params=params(12),
        cost_estimate=BRIEF,
        name="both_gradients",
    )(place, k, e, w, acc)


def attend_kernel(blocks, place, q, k, v, pair_k, up_k, early_v, out):
    early_k = jnp.where(place[0] == 0, up_k[...], pair_k[...])
    early_v = early_v[: v.shape[0]]
    early_v = jnp.where(place[2] > 0, early_v, jnp.zeros_like(early_v))
    tokens = q.shape[0]
    rows = tokens // blocks
    scale = 1.0 / math.sqrt(q.shape[1])
    for b in range(blocks):
        first, last = b * rows, (b + 1) * rows
        own = times_transposed(q[first:last], k[:last]) * scale
        old = times_transposed(q[first:last], early_k[first:]) * scale
        row = first + lax.broadcasted_iota(jnp.int32, own.shape, 0)
        column = lax.broadcasted_iota(jnp.int32, own.shape, 1)
        own = jnp.where(column <= row, own, NEG_LARGE)
        row = first + lax.broadcasted_iota(jnp.int32, old.shape, 0)
        column = first + lax.broadcasted_iota(jnp.int32, old.shape, 1)
        old = jnp.where((column > row) & (place[2] > 0), old, NEG_LARGE)
        highest = jnp.maximum(
            jnp.max(own, axis=1, keepdims=True), jnp.max(old, axis=1, keepdims=True)
        )
        own, old = jnp.exp(own - highest), jnp.exp(old - highest)
        total = jnp.sum(own, axis=1, keepdims=True) + jnp.sum(old, axis=1, keepdims=True)
        own = (own / total).astype(jnp.bfloat16)
        old = (old / total).astype(jnp.bfloat16)
        out[first:last] = matmul(own, v[:last]) + matmul(old, early_v[first:])


def window_attention(place, q, k, v, *early):
    tokens, hidden = q.shape
    return pl.pallas_call(
        functools.partial(attend_kernel, 2),
        out_shape=jax.ShapeDtypeStruct((tokens, hidden), jnp.float32),
        in_specs=[pl.BlockSpec(memory_space=pltpu.SMEM)] + [whole_spec()] * 6,
        out_specs=whole_spec(),
        compiler_params=params(12),
        cost_estimate=BRIEF,
        name="window_attention",
    )(place, q, k, v, *early)


def pick_kernel(place, even, odd, out):
    @pl.when(place[0] == 0)
    def _():
        out[...] = even[...]

    @pl.when(place[0] == 1)
    def _():
        out[...] = odd[...]


def pick(place, even, odd):
    return pl.pallas_call(
        pick_kernel,
        out_shape=jax.ShapeDtypeStruct(even.shape, even.dtype),
        in_specs=[pl.BlockSpec(memory_space=pltpu.SMEM)] + [whole_spec()] * 2,
        out_specs=whole_spec(),
        compiler_params=params(12),
        cost_estimate=BRIEF,
        name="pick",
    )(place, even, odd)


def crossing_kernel(place, even, odd, rows, out):
    tokens = even.shape[0]

    @pl.when(place[0] == 0)
    def _():
        out[:tokens] = even[...]

    @pl.when(place[0] == 1)
    def _():
        out[:tokens] = odd[...]

    out[tokens:] = rows[...]


def crossing(place, even, odd, rows):
    shape = (even.shape[0] + rows.shape[0], even.shape[1])
    return pl.pallas_call(
        crossing_kernel,
        out_shape=jax.ShapeDtypeStruct(shape, even.dtype),
        in_specs=[pl.BlockSpec(memory_space=pltpu.SMEM)] + [whole_spec()] * 3,
        out_specs=whole_spec(),
        compiler_params=params(12),
        cost_estimate=BRIEF,
        name="crossing",
    )(place, even, odd, rows)


def renew_kernel(place, w, momentum, mine, *rest):
    pieces, (moment, renewed) = rest[:-2], rest[-2:]
    own = mine.shape[1]
    total = mine[...]
    for piece in pieces:
        total = total + piece[...].astype(jnp.float32)
    new = MOMENTUM_DECAY * momentum[0] + total
    moment[0] = new
    rows = pl.ds(pl.multiple_of(place[2] * own, own), own)
    for i in range(w.shape[1]):
        base = w[0, i, rows, :].astype(jnp.float32)
        renewed[i] = renormalize(base, new[i])


def renew(place, w, momentum, mine, pieces):
    return pl.pallas_call(
        renew_kernel,
        out_shape=[
            jax.ShapeDtypeStruct(momentum.shape, jnp.float32),
            jax.ShapeDtypeStruct(mine.shape, jnp.bfloat16),
        ],
        in_specs=[pl.BlockSpec(memory_space=pltpu.SMEM)] + [whole_spec()] * (3 + len(pieces)),
        out_specs=[whole_spec()] * 2,
        compiler_params=params(12),
        cost_estimate=BRIEF,
        name="renew",
    )(place, w, momentum, mine, *pieces)


def apply_kernel(count, place, q, attended, *rest):
    units, combined, full = rest[:count], rest[count], rest[count + 1]
    own = units[0].shape[1]
    for i in range(count):
        step, across = i % (count // 2), i // (count // 2)
        rows = pl.ds(pl.multiple_of((place[2] ^ (2 * step + across)) * own, own), own)
        full[:, rows, :] = units[i][...]
    b1 = times_transposed(q[...], full[0])
    b3 = times_transposed(q[...], full[1])
    fast_in = (b1 * jax.nn.sigmoid(b1) * b3).astype(jnp.bfloat16)
    out = times_transposed(fast_in, full[2])
    combined[...] = (attended[...] + out).astype(jnp.bfloat16)


def apply_fast(place, q, attended, units):
    tokens, hidden = q.shape
    return pl.pallas_call(
        functools.partial(apply_kernel, len(units)),
        out_shape=jax.ShapeDtypeStruct((tokens, hidden), jnp.bfloat16),
        in_specs=[pl.BlockSpec(memory_space=pltpu.SMEM)] + [whole_spec()] * (2 + len(units)),
        out_specs=whole_spec(),
        scratch_shapes=[pltpu.VMEM((3, hidden, hidden), jnp.bfloat16)],
        compiler_params=params(12),
        cost_estimate=BRIEF,
        name="apply_fast",
    )(place, q, attended, *units)


def project_kernel(tags, rows_in, place, *rest):
    blocks, units = rest[: len(tags)], rest[len(tags) : -2]
    mixed, full = rest[-2:]
    for at, unit in enumerate(units):
        rows = pl.ds(pl.multiple_of(place[ORIGINS + at] * rows_in, rows_in), rows_in)
        full[rows, :] = unit[unit.shape[0] - rows_in :, :]
    width = blocks[0].shape[1]
    value = None
    for block, tag in zip(blocks, tags):
        rows = pl.ds(pl.multiple_of((place[3] ^ tag) * width, width), width)
        part = matmul(block[...], full[rows, :])
        value = part if value is None else value + part
    mixed[...] = value.astype(mixed.dtype)


def project(place, blocks, tags, near, far, rows_in):
    tokens = blocks[0].shape[0]
    units = near + far
    depth, width = rows_in * len(units), units[0].shape[1]
    return pl.pallas_call(
        functools.partial(project_kernel, tags, rows_in),
        out_shape=jax.ShapeDtypeStruct((tokens, width), jnp.bfloat16),
        in_specs=[pl.BlockSpec(memory_space=pltpu.SMEM)]
        + [whole_spec()] * (len(units) + len(blocks)),
        out_specs=whole_spec(),
        scratch_shapes=[pltpu.VMEM((depth, width), jnp.bfloat16)],
        compiler_params=params(12),
        cost_estimate=BRIEF,
        name="project",
    )(place, *blocks, *units)


def ring_order(outer):
    return [0] + list(range(1, outer, 2)) + list(range(outer - 2 + outer % 2, 0, -2))


def ring_step(unit, outer):
    order = ring_order(outer)
    pairs = []
    for place, z in enumerate(order):
        to = order[(place + 1) % outer]
        pairs += [(2 * z + y, 2 * to + y) for y in range(2)]
    return lax.ppermute(unit, "seq", pairs)


def after(array, *others):
    return lax.optimization_barrier((array,) + others)[0]


def place_table(outer, heads):
    order = ring_order(outer)
    table = []
    for s in range(2 * outer):
        place = order.index(s // 2)
        sources = [order[(place - step) % outer] for step in range(outer)]
        near = [2 * z + s % 2 for z in sources]
        far = [2 * z + 1 - s % 2 for z in sources]
        table += [[s % 2, s // 2, s, head] + near + far for head in range(heads)]
    return np.array(table, np.int32)


def renormalize(base, moment):
    updated = base - moment
    base_rms = jnp.sqrt(jnp.mean(base * base, axis=-1, keepdims=True) + NORM_EPS)
    new_rms = jnp.sqrt(jnp.mean(updated * updated, axis=-1, keepdims=True) + NORM_EPS)
    return (updated * (base_rms / new_rms)).astype(jnp.bfloat16)


def attention(queries, keys, values, early_keys, early_values, position):
    tok_rows = queries.shape[0]
    all_keys = jnp.concatenate([early_keys, keys], axis=0)
    all_values = jnp.concatenate([early_values, values], axis=0)
    key_pos = (position - 1) * tok_rows + jnp.arange(all_keys.shape[0])
    query_pos = position * tok_rows + jnp.arange(tok_rows)
    spacing = query_pos[:, None] - key_pos[None, :]
    allowed = (spacing >= 0) & (spacing < WINDOW) & (key_pos[None, :] >= 0)
    scores = times_transposed(queries, all_keys) * (1.0 / math.sqrt(HD))
    scores = jnp.where(allowed, scores, NEG_LARGE)
    highest = jnp.max(scores, axis=1, keepdims=True)
    expo = jnp.exp(scores - highest)
    probs = (expo / jnp.sum(expo, axis=1, keepdims=True)).astype(jnp.bfloat16)
    return jnp.dot(probs, all_values, preferred_element_type=jnp.float32)


def shards(queries, keys, values, rates, fast, momentum, out_proj):
    tok_rows = queries.shape[0]
    ranks = lax.axis_size("seq")
    heads = lax.axis_size("head")
    own_rows = momentum.shape[2]
    if own_rows % 16 or ranks != 8 or heads % 2 or tok_rows != WINDOW:
        return plain(queries, keys, values, rates, fast, momentum, out_proj)
    outer = ranks // 2
    grad_scale = 1.0 / math.sqrt(tok_rows * ranks)
    index = lax.axis_index("seq") * heads + lax.axis_index("head")
    place = lax.dynamic_index_in_dim(jnp.asarray(place_table(outer, heads)), index, 0, False)

    pair_keys = swap(keys, "seq", 1)
    errors = (-grad_scale * rates * values.astype(jnp.float32)).astype(jnp.bfloat16)
    pair_errors = swap(errors, "seq", 1)

    wide = [out_proj]
    for _ in range(2):
        wide.append(ring_step(wide[-1], outer))

    up = pick(place, after(pair_keys, wide[-1]), values)
    up = lax.ppermute(up, "seq", [(s, s + 2) for s in range(ranks - 2)])

    acc = own_gradients(place, keys, errors, fast, outer)
    across = crossing(place, values, up, wide[0])
    pair_errors = after(pair_errors, up)
    summed = both_gradients(place, pair_keys, pair_errors, fast, acc, outer)
    pieces = [swap(summed[step], "seq", step * 2) for step in range(1, outer)]
    crossed = swap(after(across, summed[1]), "seq", 1)
    pieces[2] = after(pieces[2], crossed)
    moment, renewed = renew(place, fast, momentum, summed[0], pieces)

    near = [renewed]
    for step in range(1, outer):
        near.append(swap(renewed, "seq", step * 2))
    far = [swap(renewed, "seq", 1)]
    near[1] = after(near[1], far[0])
    far.append(swap(near[1], "seq", 1))
    near[2] = after(near[2], far[1])
    far += [swap(unit, "seq", 1) for unit in near[2:]]
    attended = window_attention(
        place, queries, keys, values, pair_keys, up, after(crossed, near[1])
    )
    far[2] = after(far[2], attended)
    wide_far = [crossed] + [swap(after(unit, near[1]), "seq", 1) for unit in wide[1:]]
    wide.append(ring_step(after(wide[2], near[1], near[2]), outer))
    far[-1] = after(far[-1], wide_far[1], wide_far[2], wide[3])
    wide_far.append(swap(wide[3], "seq", 1))
    combined = apply_fast(place, queries, attended, near + far)

    blocks = [(combined, 0)]
    mask = heads // 2
    while mask:
        moved = [(swap(block, "head", mask), tag ^ mask) for block, tag in blocks]
        if mask > 1:
            moved = [(after(block, wide_far[3]), tag) for block, tag in moved]
        blocks = blocks + moved
        mask //= 2
    mixed = project(
        place, [b for b, _ in blocks], [t for _, t in blocks], wide, wide_far, out_proj.shape[0]
    )
    return (mixed, moment)


def plain(queries, keys, values, rates, fast, momentum, out_proj):
    tok_rows = queries.shape[0]
    ranks = lax.axis_size("seq")
    position = lax.axis_index("seq")
    own_rows = momentum.shape[2]
    grad_scale = 1.0 / math.sqrt(tok_rows * ranks)
    weights = fast[0]
    h_gate = times_transposed(keys, weights[0])
    h_up = times_transposed(keys, weights[1])
    sigma = jax.nn.sigmoid(h_gate)
    gated = (h_gate * sigma * h_up).astype(jnp.bfloat16)
    errors = (-grad_scale * rates * values.astype(jnp.float32)).astype(jnp.bfloat16)
    grad_down = contract_rows(errors, gated)
    back = matmul(errors, weights[2])
    d_gate = (back * h_up * sigma * (1.0 + h_gate * (1.0 - sigma))).astype(jnp.bfloat16)
    d_up = (back * h_gate * sigma).astype(jnp.bfloat16)
    grads = jnp.stack([contract_rows(d_gate, keys), contract_rows(d_up, keys), grad_down])
    summed_rows = lax.psum_scatter(grads, "seq", scatter_dimension=1, tiled=True)
    moment_own = MOMENTUM_DECAY * momentum[0] + summed_rows
    base_rows = lax.dynamic_slice_in_dim(weights, position * own_rows, own_rows, 1).astype(jnp.float32)
    renewed = lax.all_gather(renormalize(base_rows, moment_own), "seq", axis=1, tiled=True)
    q_gate = times_transposed(queries, renewed[0])
    q_up = times_transposed(queries, renewed[1])
    fast_in = (q_gate * jax.nn.sigmoid(q_gate) * q_up).astype(jnp.bfloat16)
    fast_out = times_transposed(fast_in, renewed[2])
    behind = [(i, i + 1) for i in range(ranks - 1)]
    early_keys = lax.ppermute(keys, "seq", behind)
    early_values = lax.ppermute(values, "seq", behind)
    attended = attention(queries, keys, values, early_keys, early_values, position)
    combined = (attended + fast_out).astype(jnp.bfloat16)
    all_heads = lax.all_gather(combined, "head", axis=1, tiled=True)
    projection = lax.all_gather(out_proj, "seq", axis=0, tiled=True)
    return (matmul(all_heads, projection).astype(jnp.bfloat16), moment_own[None])


def solution(mesh):
    return jax.shard_map(
        shards,
        mesh=mesh,
        in_specs=(
            P("seq", "head"),
            P("seq", "head"),
            P("seq", "head"),
            P("seq", "head"),
            P("head", None, None, None),
            P("head", None, "seq", None),
            P("seq", "head"),
        ),
        out_specs=(P("seq", "head"), P("head", None, "seq", None)),
        check_vma=False,
    )
```

```python
import functools
import math

import jax
import jax.numpy as jnp
import numpy as np
from jax import lax
from jax.experimental import pallas as pl
from jax.experimental.pallas import tpu as pltpu
from jax.sharding import PartitionSpec as P

HD = 512
WINDOW = 512

MOMENTUM_DECAY = 0.9
NORM_EPS = 1e-06
NEG_LARGE = -1e30
MIB = 1024 * 1024
BRIEF = pl.CostEstimate(flops=1, bytes_accessed=1, transcendentals=0)


def times_transposed(left, right):
    return lax.dot_general(
        left, right, (((1,), (1,)), ((), ())), preferred_element_type=jnp.float32
    )


def contract_rows(left, right):
    return lax.dot_general(
        left, right, (((0,), (0,)), ((), ())), preferred_element_type=jnp.float32
    )


def matmul(left, right):
    return jnp.dot(left, right, preferred_element_type=jnp.float32)


def swap(array, axis, mask):
    devices = lax.axis_size(axis)
    return lax.ppermute(array, axis, [(i, i ^ mask) for i in range(devices)])


def params(mib):
    return pltpu.CompilerParams(vmem_limit_bytes=mib * MIB)


def whole_spec():
    return pl.BlockSpec(memory_space=pltpu.VMEM)


def gradient_rows(outer, side, k, e, w, eye, hg_s, hu_s, err_s, dg_s, du_s):
    tokens, hidden = k.shape
    own = hidden // (2 * outer)
    hg = times_transposed(w[0], k)
    hu = times_transposed(w[1], k)
    hg_s[...] = hg
    hu_s[...] = hu
    gated = (hg * jax.nn.sigmoid(hg) * hu).astype(jnp.bfloat16)
    err_s[...] = times_transposed(eye, e).astype(jnp.bfloat16)
    down_t = times_transposed(eye, w[2]).astype(jnp.bfloat16)
    back = matmul(down_t, err_s[...])
    dg_s[2] = back
    errors = []
    for z in range(outer):
        rows = pl.ds(pl.multiple_of((2 * z + side) * own, own), own)
        to = pl.ds(z * own, own)
        g, u, b = hg_s[rows], hu_s[rows], dg_s[2, rows]
        s = jax.nn.sigmoid(g)
        du_s[0, to] = (b * u * s * (1.0 + g * (1.0 - s))).astype(jnp.bfloat16)
        du_s[1, to] = (b * g * s).astype(jnp.bfloat16)
        du_s[2, to] = err_s[rows]
    return (
        matmul(du_s[0], k),
        matmul(du_s[1], k),
        times_transposed(du_s[2], gated),
    )


def identity(size):
    rows = lax.broadcasted_iota(jnp.int32, (size, size), 0)
    columns = lax.broadcasted_iota(jnp.int32, (size, size), 1)
    return jnp.where(rows == columns, 1.0, 0.0).astype(jnp.bfloat16)


def own_kernel(outer, place, k, e, w, acc, *scratch):
    eye = identity(e.shape[1])
    parts = gradient_rows(outer, place[0], k[...], e[...], w[0], eye, *scratch)
    own = acc.shape[2]
    for i, part in enumerate(parts):
        acc[:, i] = part.reshape(outer, own, part.shape[1])


def both_kernel(outer, place, k, e, w, acc, mine, *rest):
    sent, scratch = rest[: outer - 1], rest[outer - 1 :]
    eye = identity(e.shape[1])
    parts = gradient_rows(outer, place[0], k[...], e[...], w[0], eye, *scratch)
    own = acc.shape[2]
    total = scratch[1]
    for i, part in enumerate(parts):
        total[pl.ds(0, outer * own), :] = part + acc[:, i].reshape(outer * own, part.shape[1])
        mine[i] = total[pl.ds(pl.multiple_of(place[1] * own, own), own), :]
        for step in range(1, outer):
            other = place[1] ^ step
            block = total[pl.ds(pl.multiple_of(other * own, own), own), :]
            sent[step - 1][i] = block.astype(jnp.bfloat16)


def gradient_scratch(tokens, hidden):
    return [
        pltpu.VMEM((hidden, tokens), jnp.float32),
        pltpu.VMEM((hidden, tokens), jnp.float32),
        pltpu.VMEM((hidden, tokens), jnp.bfloat16),
        pltpu.VMEM((3, hidden, tokens), jnp.float32),
        pltpu.VMEM((3, hidden // 2, tokens), jnp.bfloat16),
    ]


def own_gradients(place, k, e, w, outer):
    tokens, hidden = k.shape
    own = hidden // (2 * outer)
    return pl.pallas_call(
        functools.partial(own_kernel, outer),
        out_shape=jax.ShapeDtypeStruct((outer, 3, own, hidden), jnp.float32),
        in_specs=[pl.BlockSpec(memory_space=pltpu.SMEM)] + [whole_spec()] * 3,
        out_specs=whole_spec(),
        scratch_shapes=gradient_scratch(tokens, hidden),
        compiler_params=params(12),
        cost_estimate=BRIEF,
        name="own_gradients",
    )(place, k, e, w)


def both_gradients(place, k, e, w, acc, outer):
    tokens, hidden = k.shape
    own = hidden // (2 * outer)
    return pl.pallas_call(
        functools.partial(both_kernel, outer),
        out_shape=[jax.ShapeDtypeStruct((3, own, hidden), jnp.float32)]
        + [jax.ShapeDtypeStruct((3, own, hidden), jnp.bfloat16)] * (outer - 1),
        in_specs=[pl.BlockSpec(memory_space=pltpu.SMEM)] + [whole_spec()] * 4,
        out_specs=[whole_spec()] * outer,
        scratch_shapes=gradient_scratch(tokens, hidden),
        compiler_params=params(12),
        cost_estimate=BRIEF,
        name="both_gradients",
    )(place, k, e, w, acc)


def attend_kernel(blocks, place, q, k, v, pair_k, up_k, early_v, out):
    early_k = jnp.where(place[0] == 0, up_k[...], pair_k[...])
    early_v = early_v[: v.shape[0]]
    early_v = jnp.where(place[2] > 0, early_v, jnp.zeros_like(early_v))
    tokens = q.shape[0]
    rows = tokens // blocks
    scale = 1.0 / math.sqrt(q.shape[1])
    for b in range(blocks):
        first, last = b * rows, (b + 1) * rows
        own = times_transposed(q[first:last], k[:last]) * scale
        old = times_transposed(q[first:last], early_k[first:]) * scale
        row = first + lax.broadcasted_iota(jnp.int32, own.shape, 0)
        column = lax.broadcasted_iota(jnp.int32, own.shape, 1)
        own = jnp.where(column <= row, own, NEG_LARGE)
        row = first + lax.broadcasted_iota(jnp.int32, old.shape, 0)
        column = first + lax.broadcasted_iota(jnp.int32, old.shape, 1)
        old = jnp.where((column > row) & (place[2] > 0), old, NEG_LARGE)
        highest = jnp.maximum(
            jnp.max(own, axis=1, keepdims=True), jnp.max(old, axis=1, keepdims=True)
        )
        own, old = jnp.exp(own - highest), jnp.exp(old - highest)
        total = jnp.sum(own, axis=1, keepdims=True) + jnp.sum(old, axis=1, keepdims=True)
        own = (own / total).astype(jnp.bfloat16)
        old = (old / total).astype(jnp.bfloat16)
        out[first:last] = matmul(own, v[:last]) + matmul(old, early_v[first:])


def window_attention(place, q, k, v, *early):
    tokens, hidden = q.shape
    return pl.pallas_call(
        functools.partial(attend_kernel, 2),
        out_shape=jax.ShapeDtypeStruct((tokens, hidden), jnp.float32),
        in_specs=[pl.BlockSpec(memory_space=pltpu.SMEM)] + [whole_spec()] * 6,
        out_specs=whole_spec(),
        compiler_params=params(12),
        cost_estimate=BRIEF,
        name="window_attention",
    )(place, q, k, v, *early)


def crossing_kernel(place, even, odd, rows, out):
    tokens = even.shape[0]

    @pl.when(place[0] == 0)
    def _():
        out[:tokens] = even[...]

    @pl.when(place[0] == 1)
    def _():
        out[:tokens] = odd[...]

    out[tokens:] = rows[...]


def crossing(place, even, odd, rows):
    shape = (even.shape[0] + rows.shape[0], even.shape[1])
    return pl.pallas_call(
        crossing_kernel,
        out_shape=jax.ShapeDtypeStruct(shape, even.dtype),
        in_specs=[pl.BlockSpec(memory_space=pltpu.SMEM)] + [whole_spec()] * 3,
        out_specs=whole_spec(),
        compiler_params=params(12),
        cost_estimate=BRIEF,
        name="crossing",
    )(place, even, odd, rows)


def parts_kernel(place, column, *outs):
    rows_in = outs[0].shape[0]
    for step, out in enumerate(outs, 1):
        rows = pl.ds(pl.multiple_of((place[1] ^ step) * rows_in, rows_in), rows_in)
        out[...] = column[rows, :]


def parts(place, column, outer):
    shape = (column.shape[0] // outer, column.shape[1])
    return pl.pallas_call(
        parts_kernel,
        out_shape=[jax.ShapeDtypeStruct(shape, column.dtype)] * (outer - 1),
        in_specs=[pl.BlockSpec(memory_space=pltpu.SMEM), whole_spec()],
        out_specs=[whole_spec()] * (outer - 1),
        compiler_params=params(12),
        cost_estimate=BRIEF,
        name="parts",
    )(place, column)


def renew_kernel(place, w, momentum, mine, *rest):
    pieces, (moment, renewed) = rest[:-2], rest[-2:]
    own = mine.shape[1]
    total = mine[...]
    for piece in pieces:
        total = total + piece[...].astype(jnp.float32)
    new = MOMENTUM_DECAY * momentum[0] + total
    moment[0] = new
    rows = pl.ds(pl.multiple_of(place[2] * own, own), own)
    for i in range(w.shape[1]):
        base = w[0, i, rows, :].astype(jnp.float32)
        renewed[i] = renormalize(base, new[i])


def renew(place, w, momentum, mine, pieces):
    return pl.pallas_call(
        renew_kernel,
        out_shape=[
            jax.ShapeDtypeStruct(momentum.shape, jnp.float32),
            jax.ShapeDtypeStruct(mine.shape, jnp.bfloat16),
        ],
        in_specs=[pl.BlockSpec(memory_space=pltpu.SMEM)] + [whole_spec()] * (3 + len(pieces)),
        out_specs=[whole_spec()] * 2,
        compiler_params=params(12),
        cost_estimate=BRIEF,
        name="renew",
    )(place, w, momentum, mine, *pieces)


def apply_kernel(count, place, q, attended, *rest):
    units, combined, full = rest[:count], rest[count], rest[count + 1]
    own = units[0].shape[1]
    for i in range(count):
        step, across = i % (count // 2), i // (count // 2)
        rows = pl.ds(pl.multiple_of((place[2] ^ (2 * step + across)) * own, own), own)
        full[:, rows, :] = units[i][...]
    b1 = times_transposed(q[...], full[0])
    b3 = times_transposed(q[...], full[1])
    fast_in = (b1 * jax.nn.sigmoid(b1) * b3).astype(jnp.bfloat16)
    out = times_transposed(fast_in, full[2])
    combined[...] = (attended[...] + out).astype(jnp.bfloat16)


def apply_fast(place, q, attended, units):
    tokens, hidden = q.shape
    return pl.pallas_call(
        functools.partial(apply_kernel, len(units)),
        out_shape=jax.ShapeDtypeStruct((tokens, hidden), jnp.bfloat16),
        in_specs=[pl.BlockSpec(memory_space=pltpu.SMEM)] + [whole_spec()] * (2 + len(units)),
        out_specs=whole_spec(),
        scratch_shapes=[pltpu.VMEM((3, hidden, hidden), jnp.bfloat16)],
        compiler_params=params(12),
        cost_estimate=BRIEF,
        name="apply_fast",
    )(place, q, attended, *units)


def project_kernel(tags, rows_in, place, *rest):
    blocks, units = rest[: len(tags)], rest[len(tags) : -2]
    mixed, full = rest[-2:]
    column, others = units[0], units[1:]
    for step, other in enumerate(others):
        rows = pl.ds(pl.multiple_of((2 * step + place[0]) * rows_in, rows_in), rows_in)
        full[rows, :] = column[step * rows_in : (step + 1) * rows_in, :]
        rows = pl.ds(pl.multiple_of((place[2] ^ (2 * step + 1)) * rows_in, rows_in), rows_in)
        full[rows, :] = other[other.shape[0] - rows_in :, :]
    width = blocks[0].shape[1]
    value = None
    for block, tag in zip(blocks, tags):
        rows = pl.ds(pl.multiple_of((place[3] ^ tag) * width, width), width)
        part = matmul(block[...], full[rows, :])
        value = part if value is None else value + part
    mixed[...] = value.astype(mixed.dtype)


def project(place, blocks, tags, column, others, rows_in):
    tokens = blocks[0].shape[0]
    units = [column] + others
    depth, width = 2 * column.shape[0], column.shape[1]
    return pl.pallas_call(
        functools.partial(project_kernel, tags, rows_in),
        out_shape=jax.ShapeDtypeStruct((tokens, width), jnp.bfloat16),
        in_specs=[pl.BlockSpec(memory_space=pltpu.SMEM)]
        + [whole_spec()] * (len(units) + len(blocks)),
        out_specs=whole_spec(),
        scratch_shapes=[pltpu.VMEM((depth, width), jnp.bfloat16)],
        compiler_params=params(12),
        cost_estimate=BRIEF,
        name="project",
    )(place, *blocks, *units)


def after(array, *others):
    return lax.optimization_barrier((array,) + others)[0]


def place_table(outer, heads):
    table = [[s % 2, s // 2, s, head] for s in range(2 * outer) for head in range(heads)]
    return np.array(table, np.int32)


def renormalize(base, moment):
    updated = base - moment
    base_rms = jnp.sqrt(jnp.mean(base * base, axis=-1, keepdims=True) + NORM_EPS)
    new_rms = jnp.sqrt(jnp.mean(updated * updated, axis=-1, keepdims=True) + NORM_EPS)
    return (updated * (base_rms / new_rms)).astype(jnp.bfloat16)


def attention(queries, keys, values, early_keys, early_values, position):
    tok_rows = queries.shape[0]
    all_keys = jnp.concatenate([early_keys, keys], axis=0)
    all_values = jnp.concatenate([early_values, values], axis=0)
    key_pos = (position - 1) * tok_rows + jnp.arange(all_keys.shape[0])
    query_pos = position * tok_rows + jnp.arange(tok_rows)
    spacing = query_pos[:, None] - key_pos[None, :]
    allowed = (spacing >= 0) & (spacing < WINDOW) & (key_pos[None, :] >= 0)
    scores = times_transposed(queries, all_keys) * (1.0 / math.sqrt(HD))
    scores = jnp.where(allowed, scores, NEG_LARGE)
    highest = jnp.max(scores, axis=1, keepdims=True)
    expo = jnp.exp(scores - highest)
    probs = (expo / jnp.sum(expo, axis=1, keepdims=True)).astype(jnp.bfloat16)
    return jnp.dot(probs, all_values, preferred_element_type=jnp.float32)


def shards(queries, keys, values, rates, fast, momentum, out_proj):
    tok_rows = queries.shape[0]
    ranks = lax.axis_size("seq")
    heads = lax.axis_size("head")
    own_rows = momentum.shape[2]
    if own_rows % 16 or ranks != 8 or heads % 2 or tok_rows != WINDOW:
        return plain(queries, keys, values, rates, fast, momentum, out_proj)
    outer = ranks // 2
    grad_scale = 1.0 / math.sqrt(tok_rows * ranks)
    index = lax.axis_index("seq") * heads + lax.axis_index("head")
    place = lax.dynamic_index_in_dim(jnp.asarray(place_table(outer, heads)), index, 0, False)

    pair_keys = swap(keys, "seq", 1)
    errors = (-grad_scale * rates * values.astype(jnp.float32)).astype(jnp.bfloat16)
    pair_errors = swap(errors, "seq", 1)

    up_values = lax.ppermute(values, "seq", [(s, s + 2) for s in range(1, ranks - 2, 2)])

    column = lax.all_gather(
        out_proj,
        "seq",
        axis=0,
        tiled=True,
        axis_index_groups=[list(range(y, ranks, 2)) for y in range(2)],
    )
    up_keys = lax.ppermute(pair_keys, "seq", [(s, s + 2) for s in range(0, ranks - 2, 2)])

    acc = own_gradients(place, keys, errors, fast, outer)
    across = crossing(place, values, up_values, out_proj)
    pair_errors = after(pair_errors, up_keys, column)
    summed = both_gradients(place, pair_keys, pair_errors, fast, acc, outer)
    pieces = [swap(summed[step], "seq", step * 2) for step in range(1, outer)]
    crossed = swap(after(across, summed[1]), "seq", 1)
    pieces[2] = after(pieces[2], crossed)
    moment, renewed = renew(place, fast, momentum, summed[0], pieces)

    near = [renewed]
    for step in range(1, outer):
        near.append(swap(renewed, "seq", step * 2))
    far = [swap(renewed, "seq", 1)]
    near[1] = after(near[1], far[0])
    far += [swap(unit, "seq", 1) for unit in near[1:]]
    attended = window_attention(
        place, queries, keys, values, pair_keys, up_keys, after(crossed, near[1])
    )
    far[1] = after(far[1], attended)
    wide = parts(place, after(column, near[1]), outer)
    wide_far = [crossed, swap(wide[0], "seq", 1)]
    far[-1] = after(far[-1], wide_far[1])
    wide_far += [swap(after(unit, far[1]), "seq", 1) for unit in wide[1:]]
    combined = apply_fast(place, queries, attended, near + far)

    blocks = [(combined, 0)]
    mask = heads // 2
    while mask:
        moved = [(swap(block, "head", mask), tag ^ mask) for block, tag in blocks]
        if mask > 1:
            moved = [(after(block, *wide_far[2:]), tag) for block, tag in moved]
        blocks = blocks + moved
        mask //= 2
    mixed = project(
        place, [b for b, _ in blocks], [t for _, t in blocks], column, wide_far, out_proj.shape[0]
    )
    return (mixed, moment)


def plain(queries, keys, values, rates, fast, momentum, out_proj):
    tok_rows = queries.shape[0]
    ranks = lax.axis_size("seq")
    position = lax.axis_index("seq")
    own_rows = momentum.shape[2]
    grad_scale = 1.0 / math.sqrt(tok_rows * ranks)
    weights = fast[0]
    h_gate = times_transposed(keys, weights[0])
    h_up = times_transposed(keys, weights[1])
    sigma = jax.nn.sigmoid(h_gate)
    gated = (h_gate * sigma * h_up).astype(jnp.bfloat16)
    errors = (-grad_scale * rates * values.astype(jnp.float32)).astype(jnp.bfloat16)
    grad_down = contract_rows(errors, gated)
    back = matmul(errors, weights[2])
    d_gate = (back * h_up * sigma * (1.0 + h_gate * (1.0 - sigma))).astype(jnp.bfloat16)
    d_up = (back * h_gate * sigma).astype(jnp.bfloat16)
    grads = jnp.stack([contract_rows(d_gate, keys), contract_rows(d_up, keys), grad_down])
    summed_rows = lax.psum_scatter(grads, "seq", scatter_dimension=1, tiled=True)
    moment_own = MOMENTUM_DECAY * momentum[0] + summed_rows
    base_rows = lax.dynamic_slice_in_dim(weights, position * own_rows, own_rows, 1).astype(jnp.float32)
    renewed = lax.all_gather(renormalize(base_rows, moment_own), "seq", axis=1, tiled=True)
    q_gate = times_transposed(queries, renewed[0])
    q_up = times_transposed(queries, renewed[1])
    fast_in = (q_gate * jax.nn.sigmoid(q_gate) * q_up).astype(jnp.bfloat16)
    fast_out = times_transposed(fast_in, renewed[2])
    behind = [(i, i + 1) for i in range(ranks - 1)]
    early_keys = lax.ppermute(keys, "seq", behind)
    early_values = lax.ppermute(values, "seq", behind)
    attended = attention(queries, keys, values, early_keys, early_values, position)
    combined = (attended + fast_out).astype(jnp.bfloat16)
    all_heads = lax.all_gather(combined, "head", axis=1, tiled=True)
    projection = lax.all_gather(out_proj, "seq", axis=0, tiled=True)
    return (matmul(all_heads, projection).astype(jnp.bfloat16), moment_own[None])


def solution(mesh):
    return jax.shard_map(
        shards,
        mesh=mesh,
        in_specs=(
            P("seq", "head"),
            P("seq", "head"),
            P("seq", "head"),
            P("seq", "head"),
            P("head", None, None, None),
            P("head", None, "seq", None),
            P("seq", "head"),
        ),
        out_specs=(P("seq", "head"), P("head", None, "seq", None)),
        check_vma=False,
    )
```

```python
import functools
import math

import jax
import jax.numpy as jnp
import numpy as np
from jax import lax
from jax.experimental import pallas as pl
from jax.experimental.pallas import tpu as pltpu
from jax.sharding import PartitionSpec as P

HD = 512
WINDOW = 512

MOMENTUM_DECAY = 0.9
NORM_EPS = 1e-06
NEG_LARGE = -1e30
MIB = 1024 * 1024
ORIGINS = 4
BRIEF = pl.CostEstimate(flops=1, bytes_accessed=1, transcendentals=0)


def times_transposed(left, right):
    return lax.dot_general(
        left, right, (((1,), (1,)), ((), ())), preferred_element_type=jnp.float32
    )


def contract_rows(left, right):
    return lax.dot_general(
        left, right, (((0,), (0,)), ((), ())), preferred_element_type=jnp.float32
    )


def matmul(left, right):
    return jnp.dot(left, right, preferred_element_type=jnp.float32)


def swap(array, axis, mask):
    devices = lax.axis_size(axis)
    return lax.ppermute(array, axis, [(i, i ^ mask) for i in range(devices)])


def params(mib):
    return pltpu.CompilerParams(vmem_limit_bytes=mib * MIB)


def whole_spec():
    return pl.BlockSpec(memory_space=pltpu.VMEM)


def gradient_rows(outer, side, k, e, w, eye, hg_s, hu_s, err_s, dg_s, du_s):
    tokens, hidden = k.shape
    own = hidden // (2 * outer)
    hg = times_transposed(w[0], k)
    hu = times_transposed(w[1], k)
    hg_s[...] = hg
    hu_s[...] = hu
    gated = (hg * jax.nn.sigmoid(hg) * hu).astype(jnp.bfloat16)
    err_s[...] = times_transposed(eye, e).astype(jnp.bfloat16)
    down_t = times_transposed(eye, w[2]).astype(jnp.bfloat16)
    back = matmul(down_t, err_s[...])
    dg_s[2] = back
    errors = []
    for z in range(outer):
        rows = pl.ds(pl.multiple_of((2 * z + side) * own, own), own)
        to = pl.ds(z * own, own)
        g, u, b = hg_s[rows], hu_s[rows], dg_s[2, rows]
        s = jax.nn.sigmoid(g)
        du_s[0, to] = (b * u * s * (1.0 + g * (1.0 - s))).astype(jnp.bfloat16)
        du_s[1, to] = (b * g * s).astype(jnp.bfloat16)
        du_s[2, to] = err_s[rows]
    return (
        matmul(du_s[0], k),
        matmul(du_s[1], k),
        times_transposed(du_s[2], gated),
    )


def identity(size):
    rows = lax.broadcasted_iota(jnp.int32, (size, size), 0)
    columns = lax.broadcasted_iota(jnp.int32, (size, size), 1)
    return jnp.where(rows == columns, 1.0, 0.0).astype(jnp.bfloat16)


def own_kernel(outer, place, k, e, w, acc, *scratch):
    eye = identity(e.shape[1])
    parts = gradient_rows(outer, place[0], k[...], e[...], w[0], eye, *scratch)
    own = acc.shape[2]
    for i, part in enumerate(parts):
        acc[:, i] = part.reshape(outer, own, part.shape[1])


def both_kernel(outer, place, k, e, w, acc, mine, *rest):
    sent, scratch = rest[: outer - 1], rest[outer - 1 :]
    eye = identity(e.shape[1])
    parts = gradient_rows(outer, place[0], k[...], e[...], w[0], eye, *scratch)
    own = acc.shape[2]
    total = scratch[1]
    for i, part in enumerate(parts):
        total[pl.ds(0, outer * own), :] = part + acc[:, i].reshape(outer * own, part.shape[1])
        mine[i] = total[pl.ds(pl.multiple_of(place[1] * own, own), own), :]
        for step in range(1, outer):
            other = place[1] ^ step
            block = total[pl.ds(pl.multiple_of(other * own, own), own), :]
            sent[step - 1][i] = block.astype(jnp.bfloat16)


def gradient_scratch(tokens, hidden):
    return [
        pltpu.VMEM((hidden, tokens), jnp.float32),
        pltpu.VMEM((hidden, tokens), jnp.float32),
        pltpu.VMEM((hidden, tokens), jnp.bfloat16),
        pltpu.VMEM((3, hidden, tokens), jnp.float32),
        pltpu.VMEM((3, hidden // 2, tokens), jnp.bfloat16),
    ]


def own_gradients(place, k, e, w, outer):
    tokens, hidden = k.shape
    own = hidden // (2 * outer)
    return pl.pallas_call(
        functools.partial(own_kernel, outer),
        out_shape=jax.ShapeDtypeStruct((outer, 3, own, hidden), jnp.float32),
        in_specs=[pl.BlockSpec(memory_space=pltpu.SMEM)] + [whole_spec()] * 3,
        out_specs=whole_spec(),
        scratch_shapes=gradient_scratch(tokens, hidden),
        compiler_params=params(12),
        cost_estimate=BRIEF,
        name="own_gradients",
    )(place, k, e, w)


def both_gradients(place, k, e, w, acc, outer):
    tokens, hidden = k.shape
    own = hidden // (2 * outer)
    return pl.pallas_call(
        functools.partial(both_kernel, outer),
        out_shape=[jax.ShapeDtypeStruct((3, own, hidden), jnp.float32)]
        + [jax.ShapeDtypeStruct((3, own, hidden), jnp.bfloat16)] * (outer - 1),
        in_specs=[pl.BlockSpec(memory_space=pltpu.SMEM)] + [whole_spec()] * 4,
        out_specs=[whole_spec()] * outer,
        scratch_shapes=gradient_scratch(tokens, hidden),
        compiler_params=params(12),
        cost_estimate=BRIEF,
        name="both_gradients",
    )(place, k, e, w, acc)


def attend_kernel(blocks, place, q, k, v, pair_k, up_k, early_v, out):
    early_k = jnp.where(place[0] == 0, up_k[...], pair_k[...])
    early_v = early_v[: v.shape[0]]
    early_v = jnp.where(place[2] > 0, early_v, jnp.zeros_like(early_v))
    tokens = q.shape[0]
    rows = tokens // blocks
    scale = 1.0 / math.sqrt(q.shape[1])
    for b in range(blocks):
        first, last = b * rows, (b + 1) * rows
        own = times_transposed(q[first:last], k[:last]) * scale
        old = times_transposed(q[first:last], early_k[first:]) * scale
        row = first + lax.broadcasted_iota(jnp.int32, own.shape, 0)
        column = lax.broadcasted_iota(jnp.int32, own.shape, 1)
        own = jnp.where(column <= row, own, NEG_LARGE)
        row = first + lax.broadcasted_iota(jnp.int32, old.shape, 0)
        column = first + lax.broadcasted_iota(jnp.int32, old.shape, 1)
        old = jnp.where((column > row) & (place[2] > 0), old, NEG_LARGE)
        highest = jnp.maximum(
            jnp.max(own, axis=1, keepdims=True), jnp.max(old, axis=1, keepdims=True)
        )
        own, old = jnp.exp(own - highest), jnp.exp(old - highest)
        total = jnp.sum(own, axis=1, keepdims=True) + jnp.sum(old, axis=1, keepdims=True)
        own = (own / total).astype(jnp.bfloat16)
        old = (old / total).astype(jnp.bfloat16)
        out[first:last] = matmul(own, v[:last]) + matmul(old, early_v[first:])


def window_attention(place, q, k, v, *early):
    tokens, hidden = q.shape
    return pl.pallas_call(
        functools.partial(attend_kernel, 2),
        out_shape=jax.ShapeDtypeStruct((tokens, hidden), jnp.float32),
        in_specs=[pl.BlockSpec(memory_space=pltpu.SMEM)] + [whole_spec()] * 6,
        out_specs=whole_spec(),
        compiler_params=params(12),
        cost_estimate=BRIEF,
        name="window_attention",
    )(place, q, k, v, *early)


def crossing_kernel(place, even, odd, rows, out):
    tokens = even.shape[0]

    @pl.when(place[0] == 0)
    def _():
        out[:tokens] = even[...]

    @pl.when(place[0] == 1)
    def _():
        out[:tokens] = odd[...]

    out[tokens:] = rows[...]


def crossing(place, even, odd, rows):
    shape = (even.shape[0] + rows.shape[0], even.shape[1])
    return pl.pallas_call(
        crossing_kernel,
        out_shape=jax.ShapeDtypeStruct(shape, even.dtype),
        in_specs=[pl.BlockSpec(memory_space=pltpu.SMEM)] + [whole_spec()] * 3,
        out_specs=whole_spec(),
        compiler_params=params(12),
        cost_estimate=BRIEF,
        name="crossing",
    )(place, even, odd, rows)


def renew_kernel(place, w, momentum, mine, *rest):
    pieces, (moment, renewed) = rest[:-2], rest[-2:]
    own = mine.shape[1]
    total = mine[...]
    for piece in pieces:
        total = total + piece[...].astype(jnp.float32)
    new = MOMENTUM_DECAY * momentum[0] + total
    moment[0] = new
    rows = pl.ds(pl.multiple_of(place[2] * own, own), own)
    for i in range(w.shape[1]):
        base = w[0, i, rows, :].astype(jnp.float32)
        renewed[i] = renormalize(base, new[i])


def renew(place, w, momentum, mine, pieces):
    return pl.pallas_call(
        renew_kernel,
        out_shape=[
            jax.ShapeDtypeStruct(momentum.shape, jnp.float32),
            jax.ShapeDtypeStruct(mine.shape, jnp.bfloat16),
        ],
        in_specs=[pl.BlockSpec(memory_space=pltpu.SMEM)] + [whole_spec()] * (3 + len(pieces)),
        out_specs=[whole_spec()] * 2,
        compiler_params=params(12),
        cost_estimate=BRIEF,
        name="renew",
    )(place, w, momentum, mine, *pieces)


def apply_kernel(count, place, q, attended, *rest):
    units, combined, full = rest[:count], rest[count], rest[count + 1]
    own = units[0].shape[1]
    for i in range(count):
        step, across = i % (count // 2), i // (count // 2)
        rows = pl.ds(pl.multiple_of((place[2] ^ (2 * step + across)) * own, own), own)
        full[:, rows, :] = units[i][...]
    b1 = times_transposed(q[...], full[0])
    b3 = times_transposed(q[...], full[1])
    fast_in = (b1 * jax.nn.sigmoid(b1) * b3).astype(jnp.bfloat16)
    out = times_transposed(fast_in, full[2])
    combined[...] = (attended[...] + out).astype(jnp.bfloat16)


def apply_fast(place, q, attended, units):
    tokens, hidden = q.shape
    return pl.pallas_call(
        functools.partial(apply_kernel, len(units)),
        out_shape=jax.ShapeDtypeStruct((tokens, hidden), jnp.bfloat16),
        in_specs=[pl.BlockSpec(memory_space=pltpu.SMEM)] + [whole_spec()] * (2 + len(units)),
        out_specs=whole_spec(),
        scratch_shapes=[pltpu.VMEM((3, hidden, hidden), jnp.bfloat16)],
        compiler_params=params(12),
        cost_estimate=BRIEF,
        name="apply_fast",
    )(place, q, attended, *units)


def project_kernel(tags, rows_in, place, *rest):
    blocks, units = rest[: len(tags)], rest[len(tags) : -2]
    mixed, full = rest[-2:]
    for at, unit in enumerate(units):
        rows = pl.ds(pl.multiple_of(place[ORIGINS + at] * rows_in, rows_in), rows_in)
        full[rows, :] = unit[unit.shape[0] - rows_in :, :]
    width = blocks[0].shape[1]
    value = None
    for block, tag in zip(blocks, tags):
        rows = pl.ds(pl.multiple_of((place[3] ^ tag) * width, width), width)
        part = matmul(block[...], full[rows, :])
        value = part if value is None else value + part
    mixed[...] = value.astype(mixed.dtype)


def project(place, blocks, tags, near, far, rows_in):
    tokens = blocks[0].shape[0]
    units = near + far
    depth, width = rows_in * len(units), units[0].shape[1]
    return pl.pallas_call(
        functools.partial(project_kernel, tags, rows_in),
        out_shape=jax.ShapeDtypeStruct((tokens, width), jnp.bfloat16),
        in_specs=[pl.BlockSpec(memory_space=pltpu.SMEM)]
        + [whole_spec()] * (len(units) + len(blocks)),
        out_specs=whole_spec(),
        scratch_shapes=[pltpu.VMEM((depth, width), jnp.bfloat16)],
        compiler_params=params(12),
        cost_estimate=BRIEF,
        name="project",
    )(place, *blocks, *units)


def ring_order(outer):
    return [0] + list(range(1, outer, 2)) + list(range(outer - 2 + outer % 2, 0, -2))


def ring_step(unit, outer):
    order = ring_order(outer)
    pairs = []
    for place, z in enumerate(order):
        to = order[(place + 1) % outer]
        pairs += [(2 * z + y, 2 * to + y) for y in range(2)]
    return lax.ppermute(unit, "seq", pairs)


def after(array, *others):
    return lax.optimization_barrier((array,) + others)[0]


def place_table(outer, heads):
    order = ring_order(outer)
    table = []
    for s in range(2 * outer):
        place = order.index(s // 2)
        sources = [order[(place - step) % outer] for step in range(outer)]
        near = [2 * z + s % 2 for z in sources]
        far = [2 * z + 1 - s % 2 for z in sources]
        table += [[s % 2, s // 2, s, head] + near + far for head in range(heads)]
    return np.array(table, np.int32)


def renormalize(base, moment):
    updated = base - moment
    base_rms = jnp.sqrt(jnp.mean(base * base, axis=-1, keepdims=True) + NORM_EPS)
    new_rms = jnp.sqrt(jnp.mean(updated * updated, axis=-1, keepdims=True) + NORM_EPS)
    return (updated * (base_rms / new_rms)).astype(jnp.bfloat16)


def attention(queries, keys, values, early_keys, early_values, position):
    tok_rows = queries.shape[0]
    all_keys = jnp.concatenate([early_keys, keys], axis=0)
    all_values = jnp.concatenate([early_values, values], axis=0)
    key_pos = (position - 1) * tok_rows + jnp.arange(all_keys.shape[0])
    query_pos = position * tok_rows + jnp.arange(tok_rows)
    spacing = query_pos[:, None] - key_pos[None, :]
    allowed = (spacing >= 0) & (spacing < WINDOW) & (key_pos[None, :] >= 0)
    scores = times_transposed(queries, all_keys) * (1.0 / math.sqrt(HD))
    scores = jnp.where(allowed, scores, NEG_LARGE)
    highest = jnp.max(scores, axis=1, keepdims=True)
    expo = jnp.exp(scores - highest)
    probs = (expo / jnp.sum(expo, axis=1, keepdims=True)).astype(jnp.bfloat16)
    return jnp.dot(probs, all_values, preferred_element_type=jnp.float32)


def shards(queries, keys, values, rates, fast, momentum, out_proj):
    tok_rows = queries.shape[0]
    ranks = lax.axis_size("seq")
    heads = lax.axis_size("head")
    own_rows = momentum.shape[2]
    if own_rows % 16 or ranks != 8 or heads % 2 or tok_rows != WINDOW:
        return plain(queries, keys, values, rates, fast, momentum, out_proj)
    outer = ranks // 2
    grad_scale = 1.0 / math.sqrt(tok_rows * ranks)
    index = lax.axis_index("seq") * heads + lax.axis_index("head")
    place = lax.dynamic_index_in_dim(jnp.asarray(place_table(outer, heads)), index, 0, False)

    pair_keys = swap(keys, "seq", 1)
    errors = (-grad_scale * rates * values.astype(jnp.float32)).astype(jnp.bfloat16)
    pair_errors = swap(errors, "seq", 1)

    wide = [out_proj]
    for _ in range(2):
        wide.append(ring_step(wide[-1], outer))

    up_values = after(values, wide[1])
    up_values = lax.ppermute(up_values, "seq", [(s, s + 2) for s in range(1, ranks - 2, 2)])
    up_keys = after(pair_keys, wide[2])
    up_keys = lax.ppermute(up_keys, "seq", [(s, s + 2) for s in range(0, ranks - 2, 2)])

    acc = own_gradients(place, keys, errors, fast, outer)
    across = crossing(place, values, up_values, wide[0])
    pair_errors = after(pair_errors, up_keys, across)
    summed = both_gradients(place, pair_keys, pair_errors, fast, acc, outer)
    pieces = [swap(summed[step], "seq", step * 2) for step in range(1, outer)]
    crossed = swap(after(across, summed[1]), "seq", 1)
    pieces[2] = after(pieces[2], crossed)
    moment, renewed = renew(place, fast, momentum, summed[0], pieces)

    near = [renewed]
    for step in range(1, outer):
        near.append(swap(renewed, "seq", step * 2))
    far = [swap(renewed, "seq", 1)]
    near[1] = after(near[1], far[0])
    far += [swap(unit, "seq", 1) for unit in near[1:]]
    attended = window_attention(
        place, queries, keys, values, pair_keys, up_keys, after(crossed, near[1])
    )
    far[1] = after(far[1], attended)
    wide_far = [crossed, swap(after(wide[1], near[1]), "seq", 1)]
    wide.append(ring_step(after(wide[2], near[1], near[2]), outer))
    far[-1] = after(far[-1], wide_far[1], wide[3])
    wide_far += [swap(after(unit, far[1]), "seq", 1) for unit in wide[2:]]
    combined = apply_fast(place, queries, attended, near + far)

    blocks = [(combined, 0)]
    mask = heads // 2
    while mask:
        moved = [(swap(block, "head", mask), tag ^ mask) for block, tag in blocks]
        if mask > 1:
            moved = [(after(block, *wide_far[2:]), tag) for block, tag in moved]
        blocks = blocks + moved
        mask //= 2
    mixed = project(
        place, [b for b, _ in blocks], [t for _, t in blocks], wide, wide_far, out_proj.shape[0]
    )
    return (mixed, moment)


def plain(queries, keys, values, rates, fast, momentum, out_proj):
    tok_rows = queries.shape[0]
    ranks = lax.axis_size("seq")
    position = lax.axis_index("seq")
    own_rows = momentum.shape[2]
    grad_scale = 1.0 / math.sqrt(tok_rows * ranks)
    weights = fast[0]
    h_gate = times_transposed(keys, weights[0])
    h_up = times_transposed(keys, weights[1])
    sigma = jax.nn.sigmoid(h_gate)
    gated = (h_gate * sigma * h_up).astype(jnp.bfloat16)
    errors = (-grad_scale * rates * values.astype(jnp.float32)).astype(jnp.bfloat16)
    grad_down = contract_rows(errors, gated)
    back = matmul(errors, weights[2])
    d_gate = (back * h_up * sigma * (1.0 + h_gate * (1.0 - sigma))).astype(jnp.bfloat16)
    d_up = (back * h_gate * sigma).astype(jnp.bfloat16)
    grads = jnp.stack([contract_rows(d_gate, keys), contract_rows(d_up, keys), grad_down])
    summed_rows = lax.psum_scatter(grads, "seq", scatter_dimension=1, tiled=True)
    moment_own = MOMENTUM_DECAY * momentum[0] + summed_rows
    base_rows = lax.dynamic_slice_in_dim(weights, position * own_rows, own_rows, 1).astype(jnp.float32)
    renewed = lax.all_gather(renormalize(base_rows, moment_own), "seq", axis=1, tiled=True)
    q_gate = times_transposed(queries, renewed[0])
    q_up = times_transposed(queries, renewed[1])
    fast_in = (q_gate * jax.nn.sigmoid(q_gate) * q_up).astype(jnp.bfloat16)
    fast_out = times_transposed(fast_in, renewed[2])
    behind = [(i, i + 1) for i in range(ranks - 1)]
    early_keys = lax.ppermute(keys, "seq", behind)
    early_values = lax.ppermute(values, "seq", behind)
    attended = attention(queries, keys, values, early_keys, early_values, position)
    combined = (attended + fast_out).astype(jnp.bfloat16)
    all_heads = lax.all_gather(combined, "head", axis=1, tiled=True)
    projection = lax.all_gather(out_proj, "seq", axis=0, tiled=True)
    return (matmul(all_heads, projection).astype(jnp.bfloat16), moment_own[None])


def solution(mesh):
    return jax.shard_map(
        shards,
        mesh=mesh,
        in_specs=(
            P("seq", "head"),
            P("seq", "head"),
            P("seq", "head"),
            P("seq", "head"),
            P("head", None, None, None),
            P("head", None, "seq", None),
            P("seq", "head"),
        ),
        out_specs=(P("seq", "head"), P("head", None, "seq", None)),
        check_vma=False,
    )
```

```python
import functools
import math

import jax
import jax.numpy as jnp
import numpy as np
from jax import lax
from jax.experimental import pallas as pl
from jax.experimental.pallas import tpu as pltpu
from jax.sharding import PartitionSpec as P

HD = 512
WINDOW = 512

MOMENTUM_DECAY = 0.9
NORM_EPS = 1e-06
NEG_LARGE = -1e30
MIB = 1024 * 1024
ORIGINS = 4
BRIEF = pl.CostEstimate(flops=1, bytes_accessed=1, transcendentals=0)


def times_transposed(left, right):
    return lax.dot_general(
        left, right, (((1,), (1,)), ((), ())), preferred_element_type=jnp.float32
    )


def contract_rows(left, right):
    return lax.dot_general(
        left, right, (((0,), (0,)), ((), ())), preferred_element_type=jnp.float32
    )


def matmul(left, right):
    return jnp.dot(left, right, preferred_element_type=jnp.float32)


def swap(array, axis, mask):
    devices = lax.axis_size(axis)
    return lax.ppermute(array, axis, [(i, i ^ mask) for i in range(devices)])


def params(mib):
    return pltpu.CompilerParams(vmem_limit_bytes=mib * MIB)


def whole_spec():
    return pl.BlockSpec(memory_space=pltpu.VMEM)


def gradient_rows(outer, side, k, e, w, eye, hg_s, hu_s, err_s, dg_s, du_s):
    tokens, hidden = k.shape
    own = hidden // (2 * outer)
    hg = times_transposed(w[0], k)
    hu = times_transposed(w[1], k)
    hg_s[...] = hg
    hu_s[...] = hu
    gated = (hg * jax.nn.sigmoid(hg) * hu).astype(jnp.bfloat16)
    err_s[...] = times_transposed(eye, e).astype(jnp.bfloat16)
    down_t = times_transposed(eye, w[2]).astype(jnp.bfloat16)
    back = matmul(down_t, err_s[...])
    dg_s[2] = back
    errors = []
    for z in range(outer):
        rows = pl.ds(pl.multiple_of((2 * z + side) * own, own), own)
        to = pl.ds(z * own, own)
        g, u, b = hg_s[rows], hu_s[rows], dg_s[2, rows]
        s = jax.nn.sigmoid(g)
        du_s[0, to] = (b * u * s * (1.0 + g * (1.0 - s))).astype(jnp.bfloat16)
        du_s[1, to] = (b * g * s).astype(jnp.bfloat16)
        du_s[2, to] = err_s[rows]
    return (
        matmul(du_s[0], k),
        matmul(du_s[1], k),
        times_transposed(du_s[2], gated),
    )


def identity(size):
    rows = lax.broadcasted_iota(jnp.int32, (size, size), 0)
    columns = lax.broadcasted_iota(jnp.int32, (size, size), 1)
    return jnp.where(rows == columns, 1.0, 0.0).astype(jnp.bfloat16)


def own_kernel(outer, place, k, e, w, acc, *scratch):
    eye = identity(e.shape[1])
    parts = gradient_rows(outer, place[0], k[...], e[...], w[0], eye, *scratch)
    own = acc.shape[2]
    for i, part in enumerate(parts):
        acc[:, i] = part.reshape(outer, own, part.shape[1])


def both_kernel(outer, place, k, e, w, acc, mine, *rest):
    sent, scratch = rest[: outer - 1], rest[outer - 1 :]
    eye = identity(e.shape[1])
    parts = gradient_rows(outer, place[0], k[...], e[...], w[0], eye, *scratch)
    own = acc.shape[2]
    total = scratch[1]
    for i, part in enumerate(parts):
        total[pl.ds(0, outer * own), :] = part + acc[:, i].reshape(outer * own, part.shape[1])
        mine[i] = total[pl.ds(pl.multiple_of(place[1] * own, own), own), :]
        for step in range(1, outer):
            other = place[1] ^ step
            block = total[pl.ds(pl.multiple_of(other * own, own), own), :]
            sent[step - 1][i] = block.astype(jnp.bfloat16)


def gradient_scratch(tokens, hidden):
    return [
        pltpu.VMEM((hidden, tokens), jnp.float32),
        pltpu.VMEM((hidden, tokens), jnp.float32),
        pltpu.VMEM((hidden, tokens), jnp.bfloat16),
        pltpu.VMEM((3, hidden, tokens), jnp.float32),
        pltpu.VMEM((3, hidden // 2, tokens), jnp.bfloat16),
    ]


def own_gradients(place, k, e, w, outer):
    tokens, hidden = k.shape
    own = hidden // (2 * outer)
    return pl.pallas_call(
        functools.partial(own_kernel, outer),
        out_shape=jax.ShapeDtypeStruct((outer, 3, own, hidden), jnp.float32),
        in_specs=[pl.BlockSpec(memory_space=pltpu.SMEM)] + [whole_spec()] * 3,
        out_specs=whole_spec(),
        scratch_shapes=gradient_scratch(tokens, hidden),
        compiler_params=params(12),
        cost_estimate=BRIEF,
        name="own_gradients",
    )(place, k, e, w)


def both_gradients(place, k, e, w, acc, outer):
    tokens, hidden = k.shape
    own = hidden // (2 * outer)
    return pl.pallas_call(
        functools.partial(both_kernel, outer),
        out_shape=[jax.ShapeDtypeStruct((3, own, hidden), jnp.float32)]
        + [jax.ShapeDtypeStruct((3, own, hidden), jnp.bfloat16)] * (outer - 1),
        in_specs=[pl.BlockSpec(memory_space=pltpu.SMEM)] + [whole_spec()] * 4,
        out_specs=[whole_spec()] * outer,
        scratch_shapes=gradient_scratch(tokens, hidden),
        compiler_params=params(12),
        cost_estimate=BRIEF,
        name="both_gradients",
    )(place, k, e, w, acc)


def attend_kernel(blocks, place, q, k, v, pair_k, up_k, early_v, out):
    early_k = jnp.where(place[0] == 0, up_k[...], pair_k[...])
    early_v = early_v[: v.shape[0]]
    early_v = jnp.where(place[2] > 0, early_v, jnp.zeros_like(early_v))
    tokens = q.shape[0]
    rows = tokens // blocks
    scale = 1.0 / math.sqrt(q.shape[1])
    for b in range(blocks):
        first, last = b * rows, (b + 1) * rows
        own = times_transposed(q[first:last], k[:last]) * scale
        old = times_transposed(q[first:last], early_k[first:]) * scale
        row = first + lax.broadcasted_iota(jnp.int32, own.shape, 0)
        column = lax.broadcasted_iota(jnp.int32, own.shape, 1)
        own = jnp.where(column <= row, own, NEG_LARGE)
        row = first + lax.broadcasted_iota(jnp.int32, old.shape, 0)
        column = first + lax.broadcasted_iota(jnp.int32, old.shape, 1)
        old = jnp.where((column > row) & (place[2] > 0), old, NEG_LARGE)
        highest = jnp.maximum(
            jnp.max(own, axis=1, keepdims=True), jnp.max(old, axis=1, keepdims=True)
        )
        own, old = jnp.exp(own - highest), jnp.exp(old - highest)
        total = jnp.sum(own, axis=1, keepdims=True) + jnp.sum(old, axis=1, keepdims=True)
        own = (own / total).astype(jnp.bfloat16)
        old = (old / total).astype(jnp.bfloat16)
        out[first:last] = matmul(own, v[:last]) + matmul(old, early_v[first:])


def window_attention(place, q, k, v, *early):
    tokens, hidden = q.shape
    return pl.pallas_call(
        functools.partial(attend_kernel, 2),
        out_shape=jax.ShapeDtypeStruct((tokens, hidden), jnp.float32),
        in_specs=[pl.BlockSpec(memory_space=pltpu.SMEM)] + [whole_spec()] * 6,
        out_specs=whole_spec(),
        compiler_params=params(12),
        cost_estimate=BRIEF,
        name="window_attention",
    )(place, q, k, v, *early)


def crossing_kernel(place, even, odd, rows, out):
    tokens = even.shape[0]

    @pl.when(place[0] == 0)
    def _():
        out[:tokens] = even[...]

    @pl.when(place[0] == 1)
    def _():
        out[:tokens] = odd[...]

    out[tokens:] = rows[...]


def crossing(place, even, odd, rows):
    shape = (even.shape[0] + rows.shape[0], even.shape[1])
    return pl.pallas_call(
        crossing_kernel,
        out_shape=jax.ShapeDtypeStruct(shape, even.dtype),
        in_specs=[pl.BlockSpec(memory_space=pltpu.SMEM)] + [whole_spec()] * 3,
        out_specs=whole_spec(),
        compiler_params=params(12),
        cost_estimate=BRIEF,
        name="crossing",
    )(place, even, odd, rows)


def renew_kernel(place, w, momentum, mine, *rest):
    pieces, renewed = rest[:-1], rest[-1]
    own = mine.shape[1]
    total = mine[...]
    for piece in pieces:
        total = total + piece[...].astype(jnp.float32)
    new = MOMENTUM_DECAY * momentum[0] + total
    rows = pl.ds(pl.multiple_of(place[2] * own, own), own)
    for i in range(w.shape[1]):
        base = w[0, i, rows, :].astype(jnp.float32)
        renewed[i] = renormalize(base, new[i])


def renew(place, w, momentum, mine, pieces):
    return pl.pallas_call(
        renew_kernel,
        out_shape=jax.ShapeDtypeStruct(mine.shape, jnp.bfloat16),
        in_specs=[pl.BlockSpec(memory_space=pltpu.SMEM)] + [whole_spec()] * (3 + len(pieces)),
        out_specs=whole_spec(),
        compiler_params=params(12),
        cost_estimate=BRIEF,
        name="renew",
    )(place, w, momentum, mine, *pieces)


def apply_kernel(count, place, q, attended, *rest):
    units, combined, full = rest[:count], rest[count], rest[count + 1]
    own = units[0].shape[1]
    for i in range(count):
        step, across = i % (count // 2), i // (count // 2)
        rows = pl.ds(pl.multiple_of((place[2] ^ (2 * step + across)) * own, own), own)
        full[:, rows, :] = units[i][...]
    b1 = times_transposed(q[...], full[0])
    b3 = times_transposed(q[...], full[1])
    fast_in = (b1 * jax.nn.sigmoid(b1) * b3).astype(jnp.bfloat16)
    out = times_transposed(fast_in, full[2])
    combined[...] = (attended[...] + out).astype(jnp.bfloat16)


def apply_fast(place, q, attended, units):
    tokens, hidden = q.shape
    return pl.pallas_call(
        functools.partial(apply_kernel, len(units)),
        out_shape=jax.ShapeDtypeStruct((tokens, hidden), jnp.bfloat16),
        in_specs=[pl.BlockSpec(memory_space=pltpu.SMEM)] + [whole_spec()] * (2 + len(units)),
        out_specs=whole_spec(),
        scratch_shapes=[pltpu.VMEM((3, hidden, hidden), jnp.bfloat16)],
        compiler_params=params(12),
        cost_estimate=BRIEF,
        name="apply_fast",
    )(place, q, attended, *units)


def most_kernel(tags, last, rows_in, offsets, place, *rest):
    blocks, units = rest[: len(tags)], rest[len(tags) : -3]
    partial, last_rows, full = rest[-3:]
    for at, (unit, first) in enumerate(offsets):
        rows = pl.ds(pl.multiple_of(place[ORIGINS + at] * rows_in, rows_in), rows_in)
        full[rows, :] = units[unit][first : first + rows_in, :]
    width = blocks[0].shape[1]
    value = None
    for block, tag in zip(blocks, tags):
        rows = pl.ds(pl.multiple_of((place[3] ^ tag) * width, width), width)
        part = matmul(block[...], full[rows, :])
        value = part if value is None else value + part
    partial[...] = value
    rows = pl.ds(pl.multiple_of((place[3] ^ last) * width, width), width)
    last_rows[...] = full[rows, :]


def project_most(place, blocks, tags, last, near, far, rows_in):
    tokens, width = blocks[0].shape
    units = near + far
    offsets = [(i, 0) for i in range(len(near))]
    for i, unit in enumerate(far, len(near)):
        firsts = range(0, unit.shape[0], rows_in)
        offsets += [(i, first) for first in (firsts if i > len(near) else firsts[-1:])]
    columns = near[0].shape[1]
    return pl.pallas_call(
        functools.partial(most_kernel, tags, last, rows_in, offsets),
        out_shape=[
            jax.ShapeDtypeStruct((tokens, columns), jnp.float32),
            jax.ShapeDtypeStruct((width, columns), jnp.bfloat16),
        ],
        in_specs=[pl.BlockSpec(memory_space=pltpu.SMEM)]
        + [whole_spec()] * (len(units) + len(blocks)),
        out_specs=[whole_spec()] * 2,
        scratch_shapes=[pltpu.VMEM((rows_in * len(offsets), columns), jnp.bfloat16)],
        compiler_params=params(12),
        cost_estimate=BRIEF,
        name="project_most",
    )(place, *blocks, *units)


def last_kernel(partial, block, rows, mixed):
    mixed[...] = (partial[...] + matmul(block[...], rows[...])).astype(mixed.dtype)


def project_last(partial, block, rows):
    return pl.pallas_call(
        last_kernel,
        out_shape=jax.ShapeDtypeStruct(partial.shape, jnp.bfloat16),
        in_specs=[whole_spec()] * 3,
        out_specs=whole_spec(),
        compiler_params=params(12),
        cost_estimate=BRIEF,
        name="project_last",
    )(partial, block, rows)


def ring_order(outer):
    return [0] + list(range(1, outer, 2)) + list(range(outer - 2 + outer % 2, 0, -2))


def ring_step(unit, outer):
    order = ring_order(outer)
    pairs = []
    for place, z in enumerate(order):
        to = order[(place + 1) % outer]
        pairs += [(2 * z + y, 2 * to + y) for y in range(2)]
    return lax.ppermute(unit, "seq", pairs)


def after(array, *others):
    return lax.optimization_barrier((array,) + others)[0]


def place_table(outer, heads):
    order = ring_order(outer)
    table = []
    for s in range(2 * outer):
        place = order.index(s // 2)
        sources = [order[(place - step) % outer] for step in range(outer)]
        near = [2 * z + s % 2 for z in sources]
        far = [2 * z + 1 - s % 2 for z in sources]
        table += [[s % 2, s // 2, s, head] + near + far for head in range(heads)]
    return np.array(table, np.int32)


def renormalize(base, moment):
    updated = base - moment
    base_rms = jnp.sqrt(jnp.mean(base * base, axis=-1, keepdims=True) + NORM_EPS)
    new_rms = jnp.sqrt(jnp.mean(updated * updated, axis=-1, keepdims=True) + NORM_EPS)
    return (updated * (base_rms / new_rms)).astype(jnp.bfloat16)


def attention(queries, keys, values, early_keys, early_values, position):
    tok_rows = queries.shape[0]
    all_keys = jnp.concatenate([early_keys, keys], axis=0)
    all_values = jnp.concatenate([early_values, values], axis=0)
    key_pos = (position - 1) * tok_rows + jnp.arange(all_keys.shape[0])
    query_pos = position * tok_rows + jnp.arange(tok_rows)
    spacing = query_pos[:, None] - key_pos[None, :]
    allowed = (spacing >= 0) & (spacing < WINDOW) & (key_pos[None, :] >= 0)
    scores = times_transposed(queries, all_keys) * (1.0 / math.sqrt(HD))
    scores = jnp.where(allowed, scores, NEG_LARGE)
    highest = jnp.max(scores, axis=1, keepdims=True)
    expo = jnp.exp(scores - highest)
    probs = (expo / jnp.sum(expo, axis=1, keepdims=True)).astype(jnp.bfloat16)
    return jnp.dot(probs, all_values, preferred_element_type=jnp.float32)


def shards(queries, keys, values, rates, fast, momentum, out_proj):
    tok_rows = queries.shape[0]
    ranks = lax.axis_size("seq")
    heads = lax.axis_size("head")
    own_rows = momentum.shape[2]
    if own_rows % 16 or ranks != 8 or heads != 4 or tok_rows != WINDOW:
        return plain(queries, keys, values, rates, fast, momentum, out_proj)
    outer = ranks // 2
    grad_scale = 1.0 / math.sqrt(tok_rows * ranks)
    index = lax.axis_index("seq") * heads + lax.axis_index("head")
    place = lax.dynamic_index_in_dim(jnp.asarray(place_table(outer, heads)), index, 0, False)

    pair_keys = swap(keys, "seq", 1)
    errors = (-grad_scale * rates * values.astype(jnp.float32)).astype(jnp.bfloat16)
    pair_errors = swap(errors, "seq", 1)

    wide = [out_proj]
    for _ in range(2):
        wide.append(ring_step(wide[-1], outer))

    up_values = after(values, wide[1])
    up_values = lax.ppermute(up_values, "seq", [(s, s + 2) for s in range(1, ranks - 2, 2)])
    up_keys = after(pair_keys, wide[2])
    up_keys = lax.ppermute(up_keys, "seq", [(s, s + 2) for s in range(0, ranks - 2, 2)])

    acc = own_gradients(place, keys, errors, fast, outer)
    across = crossing(place, values, up_values, wide[0])
    pair_errors = after(pair_errors, up_keys, across)
    summed = both_gradients(place, pair_keys, pair_errors, fast, acc, outer)
    pieces = [swap(summed[step], "seq", step * 2) for step in range(1, outer)]
    crossed = swap(after(across, summed[1]), "seq", 1)
    pieces[2] = after(pieces[2], crossed)
    renewed = renew(place, fast, momentum, summed[0], pieces)

    near = [renewed]
    for step in range(1, outer):
        near.append(swap(renewed, "seq", step * 2))
    far = [swap(renewed, "seq", 1)]
    wide_far = [crossed, swap(after(wide[1], renewed), "seq", 1)]
    near[1] = after(near[1], far[0])
    far += [swap(unit, "seq", 1) for unit in near[1:]]
    attended = window_attention(
        place, queries, keys, values, pair_keys, up_keys, after(crossed, near[1])
    )
    wide.append(ring_step(after(wide[2], far[1], near[2], near[3], wide_far[1]), outer))
    rest = jnp.concatenate(wide[2:])
    far[-1] = after(far[-1], attended, rest)
    wide_far.append(swap(after(rest, far[1]), "seq", 1))

    total = after(summed[0], near[1])
    for piece in pieces:
        total = total + piece.astype(jnp.float32)
    moment = MOMENTUM_DECAY * momentum + total[None]

    combined = apply_fast(place, queries, attended, near + far)

    crossed_x = swap(combined, "head", 2)
    other_core = swap(combined, "head", 1)
    crossed_x = after(crossed_x, wide_far[2])
    last = swap(crossed_x, "head", 3 ^ 2)
    held = [out_proj] + wide[1:]
    partial, rows = project_most(
        place, [combined, other_core, crossed_x], [0, 1, 2], 3, held, wide_far, out_proj.shape[0]
    )
    mixed = project_last(partial, last, rows)
    return (mixed, moment)


def plain(queries, keys, values, rates, fast, momentum, out_proj):
    tok_rows = queries.shape[0]
    ranks = lax.axis_size("seq")
    position = lax.axis_index("seq")
    own_rows = momentum.shape[2]
    grad_scale = 1.0 / math.sqrt(tok_rows * ranks)
    weights = fast[0]
    h_gate = times_transposed(keys, weights[0])
    h_up = times_transposed(keys, weights[1])
    sigma = jax.nn.sigmoid(h_gate)
    gated = (h_gate * sigma * h_up).astype(jnp.bfloat16)
    errors = (-grad_scale * rates * values.astype(jnp.float32)).astype(jnp.bfloat16)
    grad_down = contract_rows(errors, gated)
    back = matmul(errors, weights[2])
    d_gate = (back * h_up * sigma * (1.0 + h_gate * (1.0 - sigma))).astype(jnp.bfloat16)
    d_up = (back * h_gate * sigma).astype(jnp.bfloat16)
    grads = jnp.stack([contract_rows(d_gate, keys), contract_rows(d_up, keys), grad_down])
    summed_rows = lax.psum_scatter(grads, "seq", scatter_dimension=1, tiled=True)
    moment_own = MOMENTUM_DECAY * momentum[0] + summed_rows
    base_rows = lax.dynamic_slice_in_dim(weights, position * own_rows, own_rows, 1).astype(jnp.float32)
    renewed = lax.all_gather(renormalize(base_rows, moment_own), "seq", axis=1, tiled=True)
    q_gate = times_transposed(queries, renewed[0])
    q_up = times_transposed(queries, renewed[1])
    fast_in = (q_gate * jax.nn.sigmoid(q_gate) * q_up).astype(jnp.bfloat16)
    fast_out = times_transposed(fast_in, renewed[2])
    behind = [(i, i + 1) for i in range(ranks - 1)]
    early_keys = lax.ppermute(keys, "seq", behind)
    early_values = lax.ppermute(values, "seq", behind)
    attended = attention(queries, keys, values, early_keys, early_values, position)
    combined = (attended + fast_out).astype(jnp.bfloat16)
    all_heads = lax.all_gather(combined, "head", axis=1, tiled=True)
    projection = lax.all_gather(out_proj, "seq", axis=0, tiled=True)
    return (matmul(all_heads, projection).astype(jnp.bfloat16), moment_own[None])


def solution(mesh):
    return jax.shard_map(
        shards,
        mesh=mesh,
        in_specs=(
            P("seq", "head"),
            P("seq", "head"),
            P("seq", "head"),
            P("seq", "head"),
            P("head", None, None, None),
            P("head", None, "seq", None),
            P("seq", "head"),
        ),
        out_specs=(P("seq", "head"), P("head", None, "seq", None)),
        check_vma=False,
    )
```

```python
import functools
import math

import jax
import jax.numpy as jnp
import numpy as np
from jax import lax
from jax.experimental import pallas as pl
from jax.experimental.pallas import tpu as pltpu
from jax.sharding import PartitionSpec as P

HD = 512
WINDOW = 512

MOMENTUM_DECAY = 0.9
NORM_EPS = 1e-06
NEG_LARGE = -1e30
MIB = 1024 * 1024
ORIGINS = 4
BRIEF = pl.CostEstimate(flops=1, bytes_accessed=1, transcendentals=0)


def times_transposed(left, right):
    return lax.dot_general(
        left, right, (((1,), (1,)), ((), ())), preferred_element_type=jnp.float32
    )


def contract_rows(left, right):
    return lax.dot_general(
        left, right, (((0,), (0,)), ((), ())), preferred_element_type=jnp.float32
    )


def matmul(left, right):
    return jnp.dot(left, right, preferred_element_type=jnp.float32)


def swap(array, axis, mask):
    devices = lax.axis_size(axis)
    return lax.ppermute(array, axis, [(i, i ^ mask) for i in range(devices)])


def params(mib):
    return pltpu.CompilerParams(vmem_limit_bytes=mib * MIB)


def whole_spec():
    return pl.BlockSpec(memory_space=pltpu.VMEM)


def gradient_rows(outer, side, k, e, w, eye, hg_s, hu_s, err_s, dg_s, du_s):
    tokens, hidden = k.shape
    own = hidden // (2 * outer)
    hg = times_transposed(w[0], k)
    hu = times_transposed(w[1], k)
    hg_s[...] = hg
    hu_s[...] = hu
    gated = (hg * jax.nn.sigmoid(hg) * hu).astype(jnp.bfloat16)
    err_s[...] = times_transposed(eye, e).astype(jnp.bfloat16)
    down_t = times_transposed(eye, w[2]).astype(jnp.bfloat16)
    back = matmul(down_t, err_s[...])
    dg_s[2] = back
    errors = []
    for z in range(outer):
        rows = pl.ds(pl.multiple_of((2 * z + side) * own, own), own)
        to = pl.ds(z * own, own)
        g, u, b = hg_s[rows], hu_s[rows], dg_s[2, rows]
        s = jax.nn.sigmoid(g)
        du_s[0, to] = (b * u * s * (1.0 + g * (1.0 - s))).astype(jnp.bfloat16)
        du_s[1, to] = (b * g * s).astype(jnp.bfloat16)
        du_s[2, to] = err_s[rows]
    return (
        matmul(du_s[0], k),
        matmul(du_s[1], k),
        times_transposed(du_s[2], gated),
    )


def identity(size):
    rows = lax.broadcasted_iota(jnp.int32, (size, size), 0)
    columns = lax.broadcasted_iota(jnp.int32, (size, size), 1)
    return jnp.where(rows == columns, 1.0, 0.0).astype(jnp.bfloat16)


def own_kernel(outer, place, k, e, w, acc, *scratch):
    eye = identity(e.shape[1])
    parts = gradient_rows(outer, place[0], k[...], e[...], w[0], eye, *scratch)
    own = acc.shape[2]
    for i, part in enumerate(parts):
        acc[:, i] = part.reshape(outer, own, part.shape[1])


def both_kernel(outer, place, k, e, w, acc, mine, *rest):
    sent, scratch = rest[: outer - 1], rest[outer - 1 :]
    eye = identity(e.shape[1])
    parts = gradient_rows(outer, place[0], k[...], e[...], w[0], eye, *scratch)
    own = acc.shape[2]
    total = scratch[1]
    for i, part in enumerate(parts):
        total[pl.ds(0, outer * own), :] = part + acc[:, i].reshape(outer * own, part.shape[1])
        mine[i] = total[pl.ds(pl.multiple_of(place[1] * own, own), own), :]
        for step in range(1, outer):
            other = place[1] ^ step
            block = total[pl.ds(pl.multiple_of(other * own, own), own), :]
            sent[step - 1][i] = block.astype(jnp.bfloat16)


def gradient_scratch(tokens, hidden):
    return [
        pltpu.VMEM((hidden, tokens), jnp.float32),
        pltpu.VMEM((hidden, tokens), jnp.float32),
        pltpu.VMEM((hidden, tokens), jnp.bfloat16),
        pltpu.VMEM((3, hidden, tokens), jnp.float32),
        pltpu.VMEM((3, hidden // 2, tokens), jnp.bfloat16),
    ]


def own_gradients(place, k, e, w, outer):
    tokens, hidden = k.shape
    own = hidden // (2 * outer)
    return pl.pallas_call(
        functools.partial(own_kernel, outer),
        out_shape=jax.ShapeDtypeStruct((outer, 3, own, hidden), jnp.float32),
        in_specs=[pl.BlockSpec(memory_space=pltpu.SMEM)] + [whole_spec()] * 3,
        out_specs=whole_spec(),
        scratch_shapes=gradient_scratch(tokens, hidden),
        compiler_params=params(12),
        cost_estimate=BRIEF,
        name="own_gradients",
    )(place, k, e, w)


def both_gradients(place, k, e, w, acc, outer):
    tokens, hidden = k.shape
    own = hidden // (2 * outer)
    return pl.pallas_call(
        functools.partial(both_kernel, outer),
        out_shape=[jax.ShapeDtypeStruct((3, own, hidden), jnp.float32)]
        + [jax.ShapeDtypeStruct((3, own, hidden), jnp.bfloat16)] * (outer - 1),
        in_specs=[pl.BlockSpec(memory_space=pltpu.SMEM)] + [whole_spec()] * 4,
        out_specs=[whole_spec()] * outer,
        scratch_shapes=gradient_scratch(tokens, hidden),
        compiler_params=params(12),
        cost_estimate=BRIEF,
        name="both_gradients",
    )(place, k, e, w, acc)


def attend_kernel(blocks, place, q, k, v, pair_k, up_k, early_v, out):
    early_k = jnp.where(place[0] == 0, up_k[...], pair_k[...])
    early_v = early_v[: v.shape[0]]
    early_v = jnp.where(place[2] > 0, early_v, jnp.zeros_like(early_v))
    tokens = q.shape[0]
    rows = tokens // blocks
    scale = 1.0 / math.sqrt(q.shape[1])
    for b in range(blocks):
        first, last = b * rows, (b + 1) * rows
        own = times_transposed(q[first:last], k[:last]) * scale
        old = times_transposed(q[first:last], early_k[first:]) * scale
        row = first + lax.broadcasted_iota(jnp.int32, own.shape, 0)
        column = lax.broadcasted_iota(jnp.int32, own.shape, 1)
        own = jnp.where(column <= row, own, NEG_LARGE)
        row = first + lax.broadcasted_iota(jnp.int32, old.shape, 0)
        column = first + lax.broadcasted_iota(jnp.int32, old.shape, 1)
        old = jnp.where((column > row) & (place[2] > 0), old, NEG_LARGE)
        highest = jnp.maximum(
            jnp.max(own, axis=1, keepdims=True), jnp.max(old, axis=1, keepdims=True)
        )
        own, old = jnp.exp(own - highest), jnp.exp(old - highest)
        total = jnp.sum(own, axis=1, keepdims=True) + jnp.sum(old, axis=1, keepdims=True)
        own = (own / total).astype(jnp.bfloat16)
        old = (old / total).astype(jnp.bfloat16)
        out[first:last] = matmul(own, v[:last]) + matmul(old, early_v[first:])


def window_attention(place, q, k, v, *early):
    tokens, hidden = q.shape
    return pl.pallas_call(
        functools.partial(attend_kernel, 2),
        out_shape=jax.ShapeDtypeStruct((tokens, hidden), jnp.float32),
        in_specs=[pl.BlockSpec(memory_space=pltpu.SMEM)] + [whole_spec()] * 6,
        out_specs=whole_spec(),
        compiler_params=params(12),
        cost_estimate=BRIEF,
        name="window_attention",
    )(place, q, k, v, *early)


def crossing_kernel(place, even, odd, rows, out):
    tokens = even.shape[0]

    @pl.when(place[0] == 0)
    def _():
        out[:tokens] = even[...]

    @pl.when(place[0] == 1)
    def _():
        out[:tokens] = odd[...]

    out[tokens:] = rows[...]


def crossing(place, even, odd, rows):
    shape = (even.shape[0] + rows.shape[0], even.shape[1])
    return pl.pallas_call(
        crossing_kernel,
        out_shape=jax.ShapeDtypeStruct(shape, even.dtype),
        in_specs=[pl.BlockSpec(memory_space=pltpu.SMEM)] + [whole_spec()] * 3,
        out_specs=whole_spec(),
        compiler_params=params(12),
        cost_estimate=BRIEF,
        name="crossing",
    )(place, even, odd, rows)


def renew_kernel(place, w, momentum, mine, *rest):
    pieces, renewed = rest[:-1], rest[-1]
    own = mine.shape[1]
    total = mine[...]
    for piece in pieces:
        total = total + piece[...].astype(jnp.float32)
    new = MOMENTUM_DECAY * momentum[0] + total
    rows = pl.ds(pl.multiple_of(place[2] * own, own), own)
    for i in range(w.shape[1]):
        base = w[0, i, rows, :].astype(jnp.float32)
        renewed[i] = renormalize(base, new[i])


def renew(place, w, momentum, mine, pieces):
    return pl.pallas_call(
        renew_kernel,
        out_shape=jax.ShapeDtypeStruct(mine.shape, jnp.bfloat16),
        in_specs=[pl.BlockSpec(memory_space=pltpu.SMEM)] + [whole_spec()] * (3 + len(pieces)),
        out_specs=whole_spec(),
        compiler_params=params(12),
        cost_estimate=BRIEF,
        name="renew",
    )(place, w, momentum, mine, *pieces)


def apply_kernel(count, place, q, attended, *rest):
    units, combined, full = rest[:count], rest[count], rest[count + 1]
    own = units[0].shape[1]
    for i in range(count):
        step, across = i % (count // 2), i // (count // 2)
        rows = pl.ds(pl.multiple_of((place[2] ^ (2 * step + across)) * own, own), own)
        full[:, rows, :] = units[i][...]
    b1 = times_transposed(q[...], full[0])
    b3 = times_transposed(q[...], full[1])
    fast_in = (b1 * jax.nn.sigmoid(b1) * b3).astype(jnp.bfloat16)
    out = times_transposed(fast_in, full[2])
    combined[...] = (attended[...] + out).astype(jnp.bfloat16)


def apply_fast(place, q, attended, units):
    tokens, hidden = q.shape
    return pl.pallas_call(
        functools.partial(apply_kernel, len(units)),
        out_shape=jax.ShapeDtypeStruct((tokens, hidden), jnp.bfloat16),
        in_specs=[pl.BlockSpec(memory_space=pltpu.SMEM)] + [whole_spec()] * (2 + len(units)),
        out_specs=whole_spec(),
        scratch_shapes=[pltpu.VMEM((3, hidden, hidden), jnp.bfloat16)],
        compiler_params=params(12),
        cost_estimate=BRIEF,
        name="apply_fast",
    )(place, q, attended, *units)


def most_kernel(tags, last, rows_in, offsets, place, *rest):
    blocks, units = rest[: len(tags)], rest[len(tags) : -3]
    partial, last_rows, full = rest[-3:]
    for at, (unit, first) in enumerate(offsets):
        rows = pl.ds(pl.multiple_of(place[ORIGINS + at] * rows_in, rows_in), rows_in)
        full[rows, :] = units[unit][first : first + rows_in, :]
    width = blocks[0].shape[1]
    value = None
    for block, tag in zip(blocks, tags):
        rows = pl.ds(pl.multiple_of((place[3] ^ tag) * width, width), width)
        part = matmul(block[...], full[rows, :])
        value = part if value is None else value + part
    partial[...] = value
    rows = pl.ds(pl.multiple_of((place[3] ^ last) * width, width), width)
    last_rows[...] = full[rows, :]


def project_most(place, blocks, tags, last, near, far, rows_in):
    tokens, width = blocks[0].shape
    units = near + far
    offsets = [(i, 0) for i in range(len(near))]
    for i, unit in enumerate(far, len(near)):
        firsts = range(0, unit.shape[0], rows_in)
        offsets += [(i, first) for first in (firsts if i > len(near) else firsts[-1:])]
    columns = near[0].shape[1]
    return pl.pallas_call(
        functools.partial(most_kernel, tags, last, rows_in, offsets),
        out_shape=[
            jax.ShapeDtypeStruct((tokens, columns), jnp.float32),
            jax.ShapeDtypeStruct((width, columns), jnp.bfloat16),
        ],
        in_specs=[pl.BlockSpec(memory_space=pltpu.SMEM)]
        + [whole_spec()] * (len(units) + len(blocks)),
        out_specs=[whole_spec()] * 2,
        scratch_shapes=[pltpu.VMEM((rows_in * len(offsets), columns), jnp.bfloat16)],
        compiler_params=params(12),
        cost_estimate=BRIEF,
        name="project_most",
    )(place, *blocks, *units)


def last_kernel(partial, block, rows, mixed):
    mixed[...] = (partial[...] + matmul(block[...], rows[...])).astype(mixed.dtype)


def project_last(partial, block, rows):
    return pl.pallas_call(
        last_kernel,
        out_shape=jax.ShapeDtypeStruct(partial.shape, jnp.bfloat16),
        in_specs=[whole_spec()] * 3,
        out_specs=whole_spec(),
        compiler_params=params(12),
        cost_estimate=BRIEF,
        name="project_last",
    )(partial, block, rows)


def ring_order(outer):
    return [0] + list(range(1, outer, 2)) + list(range(outer - 2 + outer % 2, 0, -2))


def ring_step(unit, outer):
    order = ring_order(outer)
    pairs = []
    for place, z in enumerate(order):
        to = order[(place + 1) % outer]
        pairs += [(2 * z + y, 2 * to + y) for y in range(2)]
    return lax.ppermute(unit, "seq", pairs)


def after(array, *others):
    return lax.optimization_barrier((array,) + others)[0]


def place_table(outer, heads):
    order = ring_order(outer)
    table = []
    for s in range(2 * outer):
        place = order.index(s // 2)
        sources = [order[(place - step) % outer] for step in range(outer)]
        near = [2 * z + s % 2 for z in sources]
        far = [2 * z + 1 - s % 2 for z in sources]
        table += [[s % 2, s // 2, s, head] + near + far for head in range(heads)]
    return np.array(table, np.int32)


def renormalize(base, moment):
    updated = base - moment
    base_rms = jnp.sqrt(jnp.mean(base * base, axis=-1, keepdims=True) + NORM_EPS)
    new_rms = jnp.sqrt(jnp.mean(updated * updated, axis=-1, keepdims=True) + NORM_EPS)
    return (updated * (base_rms / new_rms)).astype(jnp.bfloat16)


def attention(queries, keys, values, early_keys, early_values, position):
    tok_rows = queries.shape[0]
    all_keys = jnp.concatenate([early_keys, keys], axis=0)
    all_values = jnp.concatenate([early_values, values], axis=0)
    key_pos = (position - 1) * tok_rows + jnp.arange(all_keys.shape[0])
    query_pos = position * tok_rows + jnp.arange(tok_rows)
    spacing = query_pos[:, None] - key_pos[None, :]
    allowed = (spacing >= 0) & (spacing < WINDOW) & (key_pos[None, :] >= 0)
    scores = times_transposed(queries, all_keys) * (1.0 / math.sqrt(HD))
    scores = jnp.where(allowed, scores, NEG_LARGE)
    highest = jnp.max(scores, axis=1, keepdims=True)
    expo = jnp.exp(scores - highest)
    probs = (expo / jnp.sum(expo, axis=1, keepdims=True)).astype(jnp.bfloat16)
    return jnp.dot(probs, all_values, preferred_element_type=jnp.float32)


def shards(queries, keys, values, rates, fast, momentum, out_proj):
    tok_rows = queries.shape[0]
    ranks = lax.axis_size("seq")
    heads = lax.axis_size("head")
    own_rows = momentum.shape[2]
    if own_rows % 16 or ranks != 8 or heads != 4 or tok_rows != WINDOW:
        return plain(queries, keys, values, rates, fast, momentum, out_proj)
    outer = ranks // 2
    grad_scale = 1.0 / math.sqrt(tok_rows * ranks)
    index = lax.axis_index("seq") * heads + lax.axis_index("head")
    place = lax.dynamic_index_in_dim(jnp.asarray(place_table(outer, heads)), index, 0, False)

    pair_keys = swap(keys, "seq", 1)
    errors = (-grad_scale * rates * values.astype(jnp.float32)).astype(jnp.bfloat16)
    pair_errors = swap(errors, "seq", 1)

    wide = [out_proj]
    for _ in range(2):
        wide.append(ring_step(wide[-1], outer))

    up_values = after(values, wide[1])
    up_values = lax.ppermute(up_values, "seq", [(s, s + 2) for s in range(1, ranks - 2, 2)])
    up_keys = after(pair_keys, wide[2])
    up_keys = lax.ppermute(up_keys, "seq", [(s, s + 2) for s in range(0, ranks - 2, 2)])

    acc = own_gradients(place, keys, errors, fast, outer)
    across = crossing(place, values, up_values, wide[0])
    pair_errors = after(pair_errors, up_keys, across)
    summed = both_gradients(place, pair_keys, pair_errors, fast, acc, outer)
    pieces = [swap(summed[step], "seq", step * 2) for step in range(1, outer)]
    crossed = swap(after(across, summed[1]), "seq", 1)
    pieces[2] = after(pieces[2], crossed)
    renewed = renew(place, fast, momentum, summed[0], pieces)

    near = [renewed]
    for step in range(1, outer):
        near.append(swap(renewed, "seq", step * 2))
    far = [swap(renewed, "seq", 1)]
    wide_far = [crossed, swap(after(wide[1], near[1]), "seq", 1)]
    near[1] = after(near[1], far[0])
    far += [swap(unit, "seq", 1) for unit in near[1:]]
    attended = window_attention(
        place, queries, keys, values, pair_keys, up_keys, after(crossed, near[1])
    )
    wide.append(ring_step(after(wide[2], far[1], near[2], near[3]), outer))
    rest = jnp.concatenate(wide[2:])

    total = after(summed[0], near[1])
    for piece in pieces:
        total = total + piece.astype(jnp.float32)
    moment = MOMENTUM_DECAY * momentum + total[None]

    far[-1] = after(far[-1], attended, rest, wide_far[1], moment)
    wide_far.append(swap(after(rest, far[1]), "seq", 1))

    combined = apply_fast(place, queries, attended, near + far)

    crossed_x = swap(combined, "head", 2)
    other_core = swap(combined, "head", 1)
    crossed_x = after(crossed_x, wide_far[2])
    last = swap(crossed_x, "head", 3 ^ 2)
    held = [out_proj] + wide[1:]
    partial, rows = project_most(
        place, [combined, other_core, crossed_x], [0, 1, 2], 3, held, wide_far, out_proj.shape[0]
    )
    mixed = project_last(partial, last, rows)
    return (mixed, moment)


def plain(queries, keys, values, rates, fast, momentum, out_proj):
    tok_rows = queries.shape[0]
    ranks = lax.axis_size("seq")
    position = lax.axis_index("seq")
    own_rows = momentum.shape[2]
    grad_scale = 1.0 / math.sqrt(tok_rows * ranks)
    weights = fast[0]
    h_gate = times_transposed(keys, weights[0])
    h_up = times_transposed(keys, weights[1])
    sigma = jax.nn.sigmoid(h_gate)
    gated = (h_gate * sigma * h_up).astype(jnp.bfloat16)
    errors = (-grad_scale * rates * values.astype(jnp.float32)).astype(jnp.bfloat16)
    grad_down = contract_rows(errors, gated)
    back = matmul(errors, weights[2])
    d_gate = (back * h_up * sigma * (1.0 + h_gate * (1.0 - sigma))).astype(jnp.bfloat16)
    d_up = (back * h_gate * sigma).astype(jnp.bfloat16)
    grads = jnp.stack([contract_rows(d_gate, keys), contract_rows(d_up, keys), grad_down])
    summed_rows = lax.psum_scatter(grads, "seq", scatter_dimension=1, tiled=True)
    moment_own = MOMENTUM_DECAY * momentum[0] + summed_rows
    base_rows = lax.dynamic_slice_in_dim(weights, position * own_rows, own_rows, 1).astype(jnp.float32)
    renewed = lax.all_gather(renormalize(base_rows, moment_own), "seq", axis=1, tiled=True)
    q_gate = times_transposed(queries, renewed[0])
    q_up = times_transposed(queries, renewed[1])
    fast_in = (q_gate * jax.nn.sigmoid(q_gate) * q_up).astype(jnp.bfloat16)
    fast_out = times_transposed(fast_in, renewed[2])
    behind = [(i, i + 1) for i in range(ranks - 1)]
    early_keys = lax.ppermute(keys, "seq", behind)
    early_values = lax.ppermute(values, "seq", behind)
    attended = attention(queries, keys, values, early_keys, early_values, position)
    combined = (attended + fast_out).astype(jnp.bfloat16)
    all_heads = lax.all_gather(combined, "head", axis=1, tiled=True)
    projection = lax.all_gather(out_proj, "seq", axis=0, tiled=True)
    return (matmul(all_heads, projection).astype(jnp.bfloat16), moment_own[None])


def solution(mesh):
    return jax.shard_map(
        shards,
        mesh=mesh,
        in_specs=(
            P("seq", "head"),
            P("seq", "head"),
            P("seq", "head"),
            P("seq", "head"),
            P("head", None, None, None),
            P("head", None, "seq", None),
            P("seq", "head"),
        ),
        out_specs=(P("seq", "head"), P("head", None, "seq", None)),
        check_vma=False,
    )
```

```python
import functools
import math

import jax
import jax.numpy as jnp
import numpy as np
from jax import lax
from jax.experimental import pallas as pl
from jax.experimental.pallas import tpu as pltpu
from jax.sharding import PartitionSpec as P

HD = 512
WINDOW = 512

MOMENTUM_DECAY = 0.9
NORM_EPS = 1e-06
NEG_LARGE = -1e30
MIB = 1024 * 1024
ORIGINS = 4
BRIEF = pl.CostEstimate(flops=1, bytes_accessed=1, transcendentals=0)


def times_transposed(left, right):
    return lax.dot_general(
        left, right, (((1,), (1,)), ((), ())), preferred_element_type=jnp.float32
    )


def contract_rows(left, right):
    return lax.dot_general(
        left, right, (((0,), (0,)), ((), ())), preferred_element_type=jnp.float32
    )


def matmul(left, right):
    return jnp.dot(left, right, preferred_element_type=jnp.float32)


def swap(array, axis, mask):
    devices = lax.axis_size(axis)
    return lax.ppermute(array, axis, [(i, i ^ mask) for i in range(devices)])


def params(mib):
    return pltpu.CompilerParams(vmem_limit_bytes=mib * MIB)


def whole_spec():
    return pl.BlockSpec(memory_space=pltpu.VMEM)


def gradient_rows(outer, side, k, e, w, eye, hg_s, hu_s, err_s, dg_s, du_s):
    tokens, hidden = k.shape
    own = hidden // (2 * outer)
    hg = times_transposed(w[0], k)
    hu = times_transposed(w[1], k)
    hg_s[...] = hg
    hu_s[...] = hu
    gated = (hg * jax.nn.sigmoid(hg) * hu).astype(jnp.bfloat16)
    err_s[...] = times_transposed(eye, e).astype(jnp.bfloat16)
    down_t = times_transposed(eye, w[2]).astype(jnp.bfloat16)
    back = matmul(down_t, err_s[...])
    dg_s[2] = back
    errors = []
    for z in range(outer):
        rows = pl.ds(pl.multiple_of((2 * z + side) * own, own), own)
        to = pl.ds(z * own, own)
        g, u, b = hg_s[rows], hu_s[rows], dg_s[2, rows]
        s = jax.nn.sigmoid(g)
        du_s[0, to] = (b * u * s * (1.0 + g * (1.0 - s))).astype(jnp.bfloat16)
        du_s[1, to] = (b * g * s).astype(jnp.bfloat16)
        du_s[2, to] = err_s[rows]
    return (
        matmul(du_s[0], k),
        matmul(du_s[1], k),
        times_transposed(du_s[2], gated),
    )


def identity(size):
    rows = lax.broadcasted_iota(jnp.int32, (size, size), 0)
    columns = lax.broadcasted_iota(jnp.int32, (size, size), 1)
    return jnp.where(rows == columns, 1.0, 0.0).astype(jnp.bfloat16)


def own_kernel(outer, place, k, e, w, acc, *scratch):
    eye = identity(e.shape[1])
    parts = gradient_rows(outer, place[0], k[...], e[...], w[0], eye, *scratch)
    own = acc.shape[2]
    for i, part in enumerate(parts):
        acc[:, i] = part.reshape(outer, own, part.shape[1])


def both_kernel(outer, place, k, e, w, acc, mine, *rest):
    sent, scratch = rest[: outer - 1], rest[outer - 1 :]
    eye = identity(e.shape[1])
    parts = gradient_rows(outer, place[0], k[...], e[...], w[0], eye, *scratch)
    own = acc.shape[2]
    total = scratch[1]
    for i, part in enumerate(parts):
        total[pl.ds(0, outer * own), :] = part + acc[:, i].reshape(outer * own, part.shape[1])
        mine[i] = total[pl.ds(pl.multiple_of(place[1] * own, own), own), :]
        for step in range(1, outer):
            other = place[1] ^ step
            block = total[pl.ds(pl.multiple_of(other * own, own), own), :]
            sent[step - 1][i] = block.astype(jnp.bfloat16)


def gradient_scratch(tokens, hidden):
    return [
        pltpu.VMEM((hidden, tokens), jnp.float32),
        pltpu.VMEM((hidden, tokens), jnp.float32),
        pltpu.VMEM((hidden, tokens), jnp.bfloat16),
        pltpu.VMEM((3, hidden, tokens), jnp.float32),
        pltpu.VMEM((3, hidden // 2, tokens), jnp.bfloat16),
    ]


def own_gradients(place, k, e, w, outer):
    tokens, hidden = k.shape
    own = hidden // (2 * outer)
    return pl.pallas_call(
        functools.partial(own_kernel, outer),
        out_shape=jax.ShapeDtypeStruct((outer, 3, own, hidden), jnp.float32),
        in_specs=[pl.BlockSpec(memory_space=pltpu.SMEM)] + [whole_spec()] * 3,
        out_specs=whole_spec(),
        scratch_shapes=gradient_scratch(tokens, hidden),
        compiler_params=params(12),
        cost_estimate=BRIEF,
        name="own_gradients",
    )(place, k, e, w)


def both_gradients(place, k, e, w, acc, outer):
    tokens, hidden = k.shape
    own = hidden // (2 * outer)
    return pl.pallas_call(
        functools.partial(both_kernel, outer),
        out_shape=[jax.ShapeDtypeStruct((3, own, hidden), jnp.float32)]
        + [jax.ShapeDtypeStruct((3, own, hidden), jnp.bfloat16)] * (outer - 1),
        in_specs=[pl.BlockSpec(memory_space=pltpu.SMEM)] + [whole_spec()] * 4,
        out_specs=[whole_spec()] * outer,
        scratch_shapes=gradient_scratch(tokens, hidden),
        compiler_params=params(12),
        cost_estimate=BRIEF,
        name="both_gradients",
    )(place, k, e, w, acc)


def attend_kernel(blocks, place, q, k, v, pair_k, up_k, early_v, out):
    early_k = jnp.where(place[0] == 0, up_k[...], pair_k[...])
    early_v = early_v[: v.shape[0]]
    early_v = jnp.where(place[2] > 0, early_v, jnp.zeros_like(early_v))
    tokens = q.shape[0]
    rows = tokens // blocks
    scale = 1.0 / math.sqrt(q.shape[1])
    for b in range(blocks):
        first, last = b * rows, (b + 1) * rows
        own = times_transposed(q[first:last], k[:last]) * scale
        old = times_transposed(q[first:last], early_k[first:]) * scale
        row = first + lax.broadcasted_iota(jnp.int32, own.shape, 0)
        column = lax.broadcasted_iota(jnp.int32, own.shape, 1)
        own = jnp.where(column <= row, own, NEG_LARGE)
        row = first + lax.broadcasted_iota(jnp.int32, old.shape, 0)
        column = first + lax.broadcasted_iota(jnp.int32, old.shape, 1)
        old = jnp.where((column > row) & (place[2] > 0), old, NEG_LARGE)
        highest = jnp.maximum(
            jnp.max(own, axis=1, keepdims=True), jnp.max(old, axis=1, keepdims=True)
        )
        own, old = jnp.exp(own - highest), jnp.exp(old - highest)
        total = jnp.sum(own, axis=1, keepdims=True) + jnp.sum(old, axis=1, keepdims=True)
        own = (own / total).astype(jnp.bfloat16)
        old = (old / total).astype(jnp.bfloat16)
        out[first:last] = matmul(own, v[:last]) + matmul(old, early_v[first:])


def window_attention(place, q, k, v, *early):
    tokens, hidden = q.shape
    return pl.pallas_call(
        functools.partial(attend_kernel, 2),
        out_shape=jax.ShapeDtypeStruct((tokens, hidden), jnp.float32),
        in_specs=[pl.BlockSpec(memory_space=pltpu.SMEM)] + [whole_spec()] * 6,
        out_specs=whole_spec(),
        compiler_params=params(12),
        cost_estimate=BRIEF,
        name="window_attention",
    )(place, q, k, v, *early)


def crossing_kernel(place, even, odd, rows, out):
    tokens = even.shape[0]

    @pl.when(place[0] == 0)
    def _():
        out[:tokens] = even[...]

    @pl.when(place[0] == 1)
    def _():
        out[:tokens] = odd[...]

    out[tokens:] = rows[...]


def crossing(place, even, odd, rows):
    shape = (even.shape[0] + rows.shape[0], even.shape[1])
    return pl.pallas_call(
        crossing_kernel,
        out_shape=jax.ShapeDtypeStruct(shape, even.dtype),
        in_specs=[pl.BlockSpec(memory_space=pltpu.SMEM)] + [whole_spec()] * 3,
        out_specs=whole_spec(),
        compiler_params=params(12),
        cost_estimate=BRIEF,
        name="crossing",
    )(place, even, odd, rows)


def renew_kernel(place, w, momentum, mine, *rest):
    pieces, renewed = rest[:-1], rest[-1]
    own = mine.shape[1]
    total = mine[...]
    for piece in pieces:
        total = total + piece[...].astype(jnp.float32)
    new = MOMENTUM_DECAY * momentum[0] + total
    rows = pl.ds(pl.multiple_of(place[2] * own, own), own)
    for i in range(w.shape[1]):
        base = w[0, i, rows, :].astype(jnp.float32)
        renewed[i] = renormalize(base, new[i])


def renew(place, w, momentum, mine, pieces):
    return pl.pallas_call(
        renew_kernel,
        out_shape=jax.ShapeDtypeStruct(mine.shape, jnp.bfloat16),
        in_specs=[pl.BlockSpec(memory_space=pltpu.SMEM)] + [whole_spec()] * (3 + len(pieces)),
        out_specs=whole_spec(),
        compiler_params=params(12),
        cost_estimate=BRIEF,
        name="renew",
    )(place, w, momentum, mine, *pieces)


def apply_kernel(count, place, q, attended, *rest):
    units, combined, full = rest[:count], rest[count], rest[count + 1]
    own = units[0].shape[1]
    for i in range(count):
        step, across = i % (count // 2), i // (count // 2)
        rows = pl.ds(pl.multiple_of((place[2] ^ (2 * step + across)) * own, own), own)
        full[:, rows, :] = units[i][...]
    b1 = times_transposed(q[...], full[0])
    b3 = times_transposed(q[...], full[1])
    fast_in = (b1 * jax.nn.sigmoid(b1) * b3).astype(jnp.bfloat16)
    out = times_transposed(fast_in, full[2])
    combined[...] = (attended[...] + out).astype(jnp.bfloat16)


def apply_fast(place, q, attended, units):
    tokens, hidden = q.shape
    return pl.pallas_call(
        functools.partial(apply_kernel, len(units)),
        out_shape=jax.ShapeDtypeStruct((tokens, hidden), jnp.bfloat16),
        in_specs=[pl.BlockSpec(memory_space=pltpu.SMEM)] + [whole_spec()] * (2 + len(units)),
        out_specs=whole_spec(),
        scratch_shapes=[pltpu.VMEM((3, hidden, hidden), jnp.bfloat16)],
        compiler_params=params(12),
        cost_estimate=BRIEF,
        name="apply_fast",
    )(place, q, attended, *units)


def most_kernel(tags, last, rows_in, offsets, place, *rest):
    blocks, units = rest[: len(tags)], rest[len(tags) : -3]
    partial, last_rows, full = rest[-3:]
    for at, (unit, first) in enumerate(offsets):
        rows = pl.ds(pl.multiple_of(place[ORIGINS + at] * rows_in, rows_in), rows_in)
        full[rows, :] = units[unit][first : first + rows_in, :]
    width = blocks[0].shape[1]
    value = None
    for block, tag in zip(blocks, tags):
        rows = pl.ds(pl.multiple_of((place[3] ^ tag) * width, width), width)
        part = matmul(block[...], full[rows, :])
        value = part if value is None else value + part
    partial[...] = value
    rows = pl.ds(pl.multiple_of((place[3] ^ last) * width, width), width)
    last_rows[...] = full[rows, :]


def project_most(place, blocks, tags, last, near, far, rows_in):
    tokens, width = blocks[0].shape
    units = near + far
    offsets = [(i, 0) for i in range(len(near))]
    for i, unit in enumerate(far, len(near)):
        offsets.append((i, unit.shape[0] - rows_in))
    columns = near[0].shape[1]
    return pl.pallas_call(
        functools.partial(most_kernel, tags, last, rows_in, offsets),
        out_shape=[
            jax.ShapeDtypeStruct((tokens, columns), jnp.float32),
            jax.ShapeDtypeStruct((width, columns), jnp.bfloat16),
        ],
        in_specs=[pl.BlockSpec(memory_space=pltpu.SMEM)]
        + [whole_spec()] * (len(units) + len(blocks)),
        out_specs=[whole_spec()] * 2,
        scratch_shapes=[pltpu.VMEM((rows_in * len(offsets), columns), jnp.bfloat16)],
        compiler_params=params(12),
        cost_estimate=BRIEF,
        name="project_most",
    )(place, *blocks, *units)


def last_kernel(partial, block, rows, mixed):
    mixed[...] = (partial[...] + matmul(block[...], rows[...])).astype(mixed.dtype)


def project_last(partial, block, rows):
    return pl.pallas_call(
        last_kernel,
        out_shape=jax.ShapeDtypeStruct(partial.shape, jnp.bfloat16),
        in_specs=[whole_spec()] * 3,
        out_specs=whole_spec(),
        compiler_params=params(12),
        cost_estimate=BRIEF,
        name="project_last",
    )(partial, block, rows)


def ring_order(outer):
    return [0] + list(range(1, outer, 2)) + list(range(outer - 2 + outer % 2, 0, -2))


def ring_step(unit, outer):
    order = ring_order(outer)
    pairs = []
    for place, z in enumerate(order):
        to = order[(place + 1) % outer]
        pairs += [(2 * z + y, 2 * to + y) for y in range(2)]
    return lax.ppermute(unit, "seq", pairs)


def after(array, *others):
    return lax.optimization_barrier((array,) + others)[0]


def place_table(outer, heads):
    order = ring_order(outer)
    table = []
    for s in range(2 * outer):
        place = order.index(s // 2)
        sources = [order[(place - step) % outer] for step in range(outer)]
        near = [2 * z + s % 2 for z in sources]
        far = [2 * z + 1 - s % 2 for z in sources]
        table += [[s % 2, s // 2, s, head] + near + far for head in range(heads)]
    return np.array(table, np.int32)


def renormalize(base, moment):
    updated = base - moment
    base_rms = jnp.sqrt(jnp.mean(base * base, axis=-1, keepdims=True) + NORM_EPS)
    new_rms = jnp.sqrt(jnp.mean(updated * updated, axis=-1, keepdims=True) + NORM_EPS)
    return (updated * (base_rms / new_rms)).astype(jnp.bfloat16)


def attention(queries, keys, values, early_keys, early_values, position):
    tok_rows = queries.shape[0]
    all_keys = jnp.concatenate([early_keys, keys], axis=0)
    all_values = jnp.concatenate([early_values, values], axis=0)
    key_pos = (position - 1) * tok_rows + jnp.arange(all_keys.shape[0])
    query_pos = position * tok_rows + jnp.arange(tok_rows)
    spacing = query_pos[:, None] - key_pos[None, :]
    allowed = (spacing >= 0) & (spacing < WINDOW) & (key_pos[None, :] >= 0)
    scores = times_transposed(queries, all_keys) * (1.0 / math.sqrt(HD))
    scores = jnp.where(allowed, scores, NEG_LARGE)
    highest = jnp.max(scores, axis=1, keepdims=True)
    expo = jnp.exp(scores - highest)
    probs = (expo / jnp.sum(expo, axis=1, keepdims=True)).astype(jnp.bfloat16)
    return jnp.dot(probs, all_values, preferred_element_type=jnp.float32)


def shards(queries, keys, values, rates, fast, momentum, out_proj):
    tok_rows = queries.shape[0]
    ranks = lax.axis_size("seq")
    heads = lax.axis_size("head")
    own_rows = momentum.shape[2]
    if own_rows % 16 or ranks != 8 or heads != 4 or tok_rows != WINDOW:
        return plain(queries, keys, values, rates, fast, momentum, out_proj)
    outer = ranks // 2
    grad_scale = 1.0 / math.sqrt(tok_rows * ranks)
    index = lax.axis_index("seq") * heads + lax.axis_index("head")
    place = lax.dynamic_index_in_dim(jnp.asarray(place_table(outer, heads)), index, 0, False)

    pair_keys = swap(keys, "seq", 1)
    errors = (-grad_scale * rates * values.astype(jnp.float32)).astype(jnp.bfloat16)
    pair_errors = swap(errors, "seq", 1)

    wide = [out_proj]
    for _ in range(2):
        wide.append(ring_step(wide[-1], outer))

    up_values = after(values, wide[1])
    up_values = lax.ppermute(up_values, "seq", [(s, s + 2) for s in range(1, ranks - 2, 2)])
    up_keys = after(pair_keys, wide[2])
    up_keys = lax.ppermute(up_keys, "seq", [(s, s + 2) for s in range(0, ranks - 2, 2)])

    acc = own_gradients(place, keys, errors, fast, outer)
    across = crossing(place, values, up_values, wide[0])
    pair_errors = after(pair_errors, up_keys, across)
    summed = both_gradients(place, pair_keys, pair_errors, fast, acc, outer)
    pieces = [swap(summed[step], "seq", step * 2) for step in range(1, outer)]
    crossed = swap(after(across, summed[1]), "seq", 1)
    pieces[2] = after(pieces[2], crossed)
    renewed = renew(place, fast, momentum, summed[0], pieces)

    near = [renewed]
    for step in range(1, outer):
        near.append(swap(renewed, "seq", step * 2))
    far = [swap(renewed, "seq", 1)]
    wide_far = [crossed, swap(after(wide[1], near[1]), "seq", 1)]
    near[1] = after(near[1], far[0])
    far += [swap(unit, "seq", 1) for unit in near[1:]]
    attended = window_attention(
        place, queries, keys, values, pair_keys, up_keys, after(crossed, near[1])
    )
    wide.append(ring_step(after(wide[2], far[1], near[2], near[3]), outer))

    total = after(summed[0], near[1])
    for piece in pieces:
        total = total + piece.astype(jnp.float32)
    moment = MOMENTUM_DECAY * momentum + total[None]

    far[-1] = after(far[-1], attended, wide_far[1], moment)
    wide_far += [swap(after(wide[2], far[1]), "seq", 1), swap(wide[3], "seq", 1)]

    combined = apply_fast(place, queries, attended, near + far)

    crossed_x = swap(combined, "head", 2)
    other_core = swap(combined, "head", 1)
    crossed_x = after(crossed_x, *wide_far[2:])
    last = swap(crossed_x, "head", 3 ^ 2)
    held = [out_proj] + wide[1:]
    partial, rows = project_most(
        place, [combined, other_core, crossed_x], [0, 1, 2], 3, held, wide_far, out_proj.shape[0]
    )
    mixed = project_last(partial, last, rows)
    return (mixed, moment)


def plain(queries, keys, values, rates, fast, momentum, out_proj):
    tok_rows = queries.shape[0]
    ranks = lax.axis_size("seq")
    position = lax.axis_index("seq")
    own_rows = momentum.shape[2]
    grad_scale = 1.0 / math.sqrt(tok_rows * ranks)
    weights = fast[0]
    h_gate = times_transposed(keys, weights[0])
    h_up = times_transposed(keys, weights[1])
    sigma = jax.nn.sigmoid(h_gate)
    gated = (h_gate * sigma * h_up).astype(jnp.bfloat16)
    errors = (-grad_scale * rates * values.astype(jnp.float32)).astype(jnp.bfloat16)
    grad_down = contract_rows(errors, gated)
    back = matmul(errors, weights[2])
    d_gate = (back * h_up * sigma * (1.0 + h_gate * (1.0 - sigma))).astype(jnp.bfloat16)
    d_up = (back * h_gate * sigma).astype(jnp.bfloat16)
    grads = jnp.stack([contract_rows(d_gate, keys), contract_rows(d_up, keys), grad_down])
    summed_rows = lax.psum_scatter(grads, "seq", scatter_dimension=1, tiled=True)
    moment_own = MOMENTUM_DECAY * momentum[0] + summed_rows
    base_rows = lax.dynamic_slice_in_dim(weights, position * own_rows, own_rows, 1).astype(jnp.float32)
    renewed = lax.all_gather(renormalize(base_rows, moment_own), "seq", axis=1, tiled=True)
    q_gate = times_transposed(queries, renewed[0])
    q_up = times_transposed(queries, renewed[1])
    fast_in = (q_gate * jax.nn.sigmoid(q_gate) * q_up).astype(jnp.bfloat16)
    fast_out = times_transposed(fast_in, renewed[2])
    behind = [(i, i + 1) for i in range(ranks - 1)]
    early_keys = lax.ppermute(keys, "seq", behind)
    early_values = lax.ppermute(values, "seq", behind)
    attended = attention(queries, keys, values, early_keys, early_values, position)
    combined = (attended + fast_out).astype(jnp.bfloat16)
    all_heads = lax.all_gather(combined, "head", axis=1, tiled=True)
    projection = lax.all_gather(out_proj, "seq", axis=0, tiled=True)
    return (matmul(all_heads, projection).astype(jnp.bfloat16), moment_own[None])


def solution(mesh):
    return jax.shard_map(
        shards,
        mesh=mesh,
        in_specs=(
            P("seq", "head"),
            P("seq", "head"),
            P("seq", "head"),
            P("seq", "head"),
            P("head", None, None, None),
            P("head", None, "seq", None),
            P("seq", "head"),
        ),
        out_specs=(P("seq", "head"), P("head", None, "seq", None)),
        check_vma=False,
    )
```

```python
import functools
import math

import jax
import jax.numpy as jnp
import numpy as np
from jax import lax
from jax.experimental import pallas as pl
from jax.experimental.pallas import tpu as pltpu
from jax.sharding import PartitionSpec as P

HD = 512
WINDOW = 512

MOMENTUM_DECAY = 0.9
NORM_EPS = 1e-06
NEG_LARGE = -1e30
MIB = 1024 * 1024
ORIGINS = 4
BRIEF = pl.CostEstimate(flops=1, bytes_accessed=1, transcendentals=0)


def times_transposed(left, right):
    return lax.dot_general(
        left, right, (((1,), (1,)), ((), ())), preferred_element_type=jnp.float32
    )


def contract_rows(left, right):
    return lax.dot_general(
        left, right, (((0,), (0,)), ((), ())), preferred_element_type=jnp.float32
    )


def matmul(left, right):
    return jnp.dot(left, right, preferred_element_type=jnp.float32)


def swap(array, axis, mask):
    devices = lax.axis_size(axis)
    return lax.ppermute(array, axis, [(i, i ^ mask) for i in range(devices)])


def params(mib):
    return pltpu.CompilerParams(vmem_limit_bytes=mib * MIB)


def whole_spec():
    return pl.BlockSpec(memory_space=pltpu.VMEM)


def gradient_rows(outer, side, k, e, w, eye, hg_s, hu_s, err_s, dg_s, du_s):
    tokens, hidden = k.shape
    own = hidden // (2 * outer)
    hg = times_transposed(w[0], k)
    hu = times_transposed(w[1], k)
    hg_s[...] = hg
    hu_s[...] = hu
    gated = (hg * jax.nn.sigmoid(hg) * hu).astype(jnp.bfloat16)
    err_s[...] = times_transposed(eye, e).astype(jnp.bfloat16)
    down_t = times_transposed(eye, w[2]).astype(jnp.bfloat16)
    back = matmul(down_t, err_s[...])
    dg_s[2] = back
    errors = []
    for z in range(outer):
        rows = pl.ds(pl.multiple_of((2 * z + side) * own, own), own)
        to = pl.ds(z * own, own)
        g, u, b = hg_s[rows], hu_s[rows], dg_s[2, rows]
        s = jax.nn.sigmoid(g)
        du_s[0, to] = (b * u * s * (1.0 + g * (1.0 - s))).astype(jnp.bfloat16)
        du_s[1, to] = (b * g * s).astype(jnp.bfloat16)
        du_s[2, to] = err_s[rows]
    return (
        matmul(du_s[0], k),
        matmul(du_s[1], k),
        times_transposed(du_s[2], gated),
    )


def identity(size):
    rows = lax.broadcasted_iota(jnp.int32, (size, size), 0)
    columns = lax.broadcasted_iota(jnp.int32, (size, size), 1)
    return jnp.where(rows == columns, 1.0, 0.0).astype(jnp.bfloat16)


def own_kernel(outer, place, k, e, w, acc, *scratch):
    eye = identity(e.shape[1])
    parts = gradient_rows(outer, place[0], k[...], e[...], w[0], eye, *scratch)
    own = acc.shape[2]
    for i, part in enumerate(parts):
        acc[:, i] = part.reshape(outer, own, part.shape[1])


def both_kernel(outer, place, k, e, w, acc, mine, *rest):
    sent, scratch = rest[: outer - 1], rest[outer - 1 :]
    eye = identity(e.shape[1])
    parts = gradient_rows(outer, place[0], k[...], e[...], w[0], eye, *scratch)
    own = acc.shape[2]
    total = scratch[1]
    for i, part in enumerate(parts):
        total[pl.ds(0, outer * own), :] = part + acc[:, i].reshape(outer * own, part.shape[1])
        mine[i] = total[pl.ds(pl.multiple_of(place[1] * own, own), own), :]
        for step in range(1, outer):
            other = place[1] ^ step
            block = total[pl.ds(pl.multiple_of(other * own, own), own), :]
            sent[step - 1][i] = block.astype(jnp.bfloat16)


def gradient_scratch(tokens, hidden):
    return [
        pltpu.VMEM((hidden, tokens), jnp.float32),
        pltpu.VMEM((hidden, tokens), jnp.float32),
        pltpu.VMEM((hidden, tokens), jnp.bfloat16),
        pltpu.VMEM((3, hidden, tokens), jnp.float32),
        pltpu.VMEM((3, hidden // 2, tokens), jnp.bfloat16),
    ]


def own_gradients(place, k, e, w, outer):
    tokens, hidden = k.shape
    own = hidden // (2 * outer)
    return pl.pallas_call(
        functools.partial(own_kernel, outer),
        out_shape=jax.ShapeDtypeStruct((outer, 3, own, hidden), jnp.float32),
        in_specs=[pl.BlockSpec(memory_space=pltpu.SMEM)] + [whole_spec()] * 3,
        out_specs=whole_spec(),
        scratch_shapes=gradient_scratch(tokens, hidden),
        compiler_params=params(12),
        cost_estimate=BRIEF,
        name="own_gradients",
    )(place, k, e, w)


def both_gradients(place, k, e, w, acc, outer):
    tokens, hidden = k.shape
    own = hidden // (2 * outer)
    return pl.pallas_call(
        functools.partial(both_kernel, outer),
        out_shape=[jax.ShapeDtypeStruct((3, own, hidden), jnp.float32)]
        + [jax.ShapeDtypeStruct((3, own, hidden), jnp.bfloat16)] * (outer - 1),
        in_specs=[pl.BlockSpec(memory_space=pltpu.SMEM)] + [whole_spec()] * 4,
        out_specs=[whole_spec()] * outer,
        scratch_shapes=gradient_scratch(tokens, hidden),
        compiler_params=params(12),
        cost_estimate=BRIEF,
        name="both_gradients",
    )(place, k, e, w, acc)


def attend_kernel(blocks, place, q, k, v, pair_k, up_k, early_v, out):
    early_k = jnp.where(place[0] == 0, up_k[...], pair_k[...])
    early_v = early_v[: v.shape[0]]
    early_v = jnp.where(place[2] > 0, early_v, jnp.zeros_like(early_v))
    tokens = q.shape[0]
    rows = tokens // blocks
    scale = 1.0 / math.sqrt(q.shape[1])
    for b in range(blocks):
        first, last = b * rows, (b + 1) * rows
        own = times_transposed(q[first:last], k[:last]) * scale
        old = times_transposed(q[first:last], early_k[first:]) * scale
        row = first + lax.broadcasted_iota(jnp.int32, own.shape, 0)
        column = lax.broadcasted_iota(jnp.int32, own.shape, 1)
        own = jnp.where(column <= row, own, NEG_LARGE)
        row = first + lax.broadcasted_iota(jnp.int32, old.shape, 0)
        column = first + lax.broadcasted_iota(jnp.int32, old.shape, 1)
        old = jnp.where((column > row) & (place[2] > 0), old, NEG_LARGE)
        highest = jnp.maximum(
            jnp.max(own, axis=1, keepdims=True), jnp.max(old, axis=1, keepdims=True)
        )
        own, old = jnp.exp(own - highest), jnp.exp(old - highest)
        total = jnp.sum(own, axis=1, keepdims=True) + jnp.sum(old, axis=1, keepdims=True)
        own = (own / total).astype(jnp.bfloat16)
        old = (old / total).astype(jnp.bfloat16)
        out[first:last] = matmul(own, v[:last]) + matmul(old, early_v[first:])


def window_attention(place, q, k, v, *early):
    tokens, hidden = q.shape
    return pl.pallas_call(
        functools.partial(attend_kernel, 2),
        out_shape=jax.ShapeDtypeStruct((tokens, hidden), jnp.float32),
        in_specs=[pl.BlockSpec(memory_space=pltpu.SMEM)] + [whole_spec()] * 6,
        out_specs=whole_spec(),
        compiler_params=params(12),
        cost_estimate=BRIEF,
        name="window_attention",
    )(place, q, k, v, *early)


def crossing_kernel(place, even, odd, rows, out):
    tokens = even.shape[0]

    @pl.when(place[0] == 0)
    def _():
        out[:tokens] = even[...]

    @pl.when(place[0] == 1)
    def _():
        out[:tokens] = odd[...]

    out[tokens:] = rows[...]


def crossing(place, even, odd, rows):
    shape = (even.shape[0] + rows.shape[0], even.shape[1])
    return pl.pallas_call(
        crossing_kernel,
        out_shape=jax.ShapeDtypeStruct(shape, even.dtype),
        in_specs=[pl.BlockSpec(memory_space=pltpu.SMEM)] + [whole_spec()] * 3,
        out_specs=whole_spec(),
        compiler_params=params(12),
        cost_estimate=BRIEF,
        name="crossing",
    )(place, even, odd, rows)


def renew_kernel(place, w, momentum, mine, *rest):
    pieces, renewed = rest[:-1], rest[-1]
    own = mine.shape[1]
    total = mine[...]
    for piece in pieces:
        total = total + piece[...].astype(jnp.float32)
    new = MOMENTUM_DECAY * momentum[0] + total
    rows = pl.ds(pl.multiple_of(place[2] * own, own), own)
    for i in range(w.shape[1]):
        base = w[0, i, rows, :].astype(jnp.float32)
        renewed[i] = renormalize(base, new[i])


def renew(place, w, momentum, mine, pieces):
    return pl.pallas_call(
        renew_kernel,
        out_shape=jax.ShapeDtypeStruct(mine.shape, jnp.bfloat16),
        in_specs=[pl.BlockSpec(memory_space=pltpu.SMEM)] + [whole_spec()] * (3 + len(pieces)),
        out_specs=whole_spec(),
        compiler_params=params(12),
        cost_estimate=BRIEF,
        name="renew",
    )(place, w, momentum, mine, *pieces)


def apply_kernel(count, place, q, attended, *rest):
    units, combined, full = rest[:count], rest[count], rest[count + 1]
    own = units[0].shape[1]
    for i in range(count):
        step, across = i % (count // 2), i // (count // 2)
        rows = pl.ds(pl.multiple_of((place[2] ^ (2 * step + across)) * own, own), own)
        full[:, rows, :] = units[i][...]
    b1 = times_transposed(q[...], full[0])
    b3 = times_transposed(q[...], full[1])
    fast_in = (b1 * jax.nn.sigmoid(b1) * b3).astype(jnp.bfloat16)
    out = times_transposed(fast_in, full[2])
    combined[...] = (attended[...] + out).astype(jnp.bfloat16)


def apply_fast(place, q, attended, units):
    tokens, hidden = q.shape
    return pl.pallas_call(
        functools.partial(apply_kernel, len(units)),
        out_shape=jax.ShapeDtypeStruct((tokens, hidden), jnp.bfloat16),
        in_specs=[pl.BlockSpec(memory_space=pltpu.SMEM)] + [whole_spec()] * (2 + len(units)),
        out_specs=whole_spec(),
        scratch_shapes=[pltpu.VMEM((3, hidden, hidden), jnp.bfloat16)],
        compiler_params=params(12),
        cost_estimate=BRIEF,
        name="apply_fast",
    )(place, q, attended, *units)


def most_kernel(tags, last, rows_in, offsets, place, *rest):
    blocks, units = rest[: len(tags)], rest[len(tags) : -3]
    partial, last_rows, full = rest[-3:]
    for at, (unit, first) in enumerate(offsets):
        rows = pl.ds(pl.multiple_of(place[ORIGINS + at] * rows_in, rows_in), rows_in)
        full[rows, :] = units[unit][first : first + rows_in, :]
    width = blocks[0].shape[1]
    value = None
    for block, tag in zip(blocks, tags):
        rows = pl.ds(pl.multiple_of((place[3] ^ tag) * width, width), width)
        part = matmul(block[...], full[rows, :])
        value = part if value is None else value + part
    partial[...] = value
    rows = pl.ds(pl.multiple_of((place[3] ^ last) * width, width), width)
    last_rows[...] = full[rows, :]


def project_most(place, blocks, tags, last, near, far, rows_in):
    tokens, width = blocks[0].shape
    units = near + far
    offsets = [(i, 0) for i in range(len(near))]
    for i, unit in enumerate(far, len(near)):
        offsets.append((i, unit.shape[0] - rows_in))
    columns = near[0].shape[1]
    return pl.pallas_call(
        functools.partial(most_kernel, tags, last, rows_in, offsets),
        out_shape=[
            jax.ShapeDtypeStruct((tokens, columns), jnp.float32),
            jax.ShapeDtypeStruct((width, columns), jnp.bfloat16),
        ],
        in_specs=[pl.BlockSpec(memory_space=pltpu.SMEM)]
        + [whole_spec()] * (len(units) + len(blocks)),
        out_specs=[whole_spec()] * 2,
        scratch_shapes=[pltpu.VMEM((rows_in * len(offsets), columns), jnp.bfloat16)],
        compiler_params=params(12),
        cost_estimate=BRIEF,
        name="project_most",
    )(place, *blocks, *units)


def last_kernel(partial, block, rows, mixed):
    mixed[...] = (partial[...] + matmul(block[...], rows[...])).astype(mixed.dtype)


def project_last(partial, block, rows):
    return pl.pallas_call(
        last_kernel,
        out_shape=jax.ShapeDtypeStruct(partial.shape, jnp.bfloat16),
        in_specs=[whole_spec()] * 3,
        out_specs=whole_spec(),
        compiler_params=params(12),
        cost_estimate=BRIEF,
        name="project_last",
    )(partial, block, rows)


def ring_order(outer):
    return [0] + list(range(1, outer, 2)) + list(range(outer - 2 + outer % 2, 0, -2))


def ring_step(unit, outer):
    order = ring_order(outer)
    pairs = []
    for place, z in enumerate(order):
        to = order[(place + 1) % outer]
        pairs += [(2 * z + y, 2 * to + y) for y in range(2)]
    return lax.ppermute(unit, "seq", pairs)


def after(array, *others):
    return lax.optimization_barrier((array,) + others)[0]


def place_table(outer, heads):
    order = ring_order(outer)
    table = []
    for s in range(2 * outer):
        place = order.index(s // 2)
        sources = [order[(place - step) % outer] for step in range(outer)]
        near = [2 * z + s % 2 for z in sources]
        far = [2 * z + 1 - s % 2 for z in sources]
        table += [[s % 2, s // 2, s, head] + near + far for head in range(heads)]
    return np.array(table, np.int32)


def renormalize(base, moment):
    updated = base - moment
    base_rms = jnp.sqrt(jnp.mean(base * base, axis=-1, keepdims=True) + NORM_EPS)
    new_rms = jnp.sqrt(jnp.mean(updated * updated, axis=-1, keepdims=True) + NORM_EPS)
    return (updated * (base_rms / new_rms)).astype(jnp.bfloat16)


def attention(queries, keys, values, early_keys, early_values, position):
    tok_rows = queries.shape[0]
    all_keys = jnp.concatenate([early_keys, keys], axis=0)
    all_values = jnp.concatenate([early_values, values], axis=0)
    key_pos = (position - 1) * tok_rows + jnp.arange(all_keys.shape[0])
    query_pos = position * tok_rows + jnp.arange(tok_rows)
    spacing = query_pos[:, None] - key_pos[None, :]
    allowed = (spacing >= 0) & (spacing < WINDOW) & (key_pos[None, :] >= 0)
    scores = times_transposed(queries, all_keys) * (1.0 / math.sqrt(HD))
    scores = jnp.where(allowed, scores, NEG_LARGE)
    highest = jnp.max(scores, axis=1, keepdims=True)
    expo = jnp.exp(scores - highest)
    probs = (expo / jnp.sum(expo, axis=1, keepdims=True)).astype(jnp.bfloat16)
    return jnp.dot(probs, all_values, preferred_element_type=jnp.float32)


def shards(queries, keys, values, rates, fast, momentum, out_proj):
    tok_rows = queries.shape[0]
    ranks = lax.axis_size("seq")
    heads = lax.axis_size("head")
    own_rows = momentum.shape[2]
    if own_rows % 16 or ranks != 8 or heads != 4 or tok_rows != WINDOW:
        return plain(queries, keys, values, rates, fast, momentum, out_proj)
    outer = ranks // 2
    grad_scale = 1.0 / math.sqrt(tok_rows * ranks)
    index = lax.axis_index("seq") * heads + lax.axis_index("head")
    place = lax.dynamic_index_in_dim(jnp.asarray(place_table(outer, heads)), index, 0, False)

    pair_keys = swap(keys, "seq", 1)
    errors = (-grad_scale * rates * values.astype(jnp.float32)).astype(jnp.bfloat16)
    pair_errors = swap(errors, "seq", 1)

    wide = [out_proj]
    for _ in range(2):
        wide.append(ring_step(wide[-1], outer))

    up_values = after(values, wide[1])
    up_values = lax.ppermute(up_values, "seq", [(s, s + 2) for s in range(1, ranks - 2, 2)])
    up_keys = after(pair_keys, wide[2])
    up_keys = lax.ppermute(up_keys, "seq", [(s, s + 2) for s in range(0, ranks - 2, 2)])

    acc = own_gradients(place, keys, errors, fast, outer)
    across = crossing(place, values, up_values, wide[0])
    pair_errors = after(pair_errors, up_keys, across)
    summed = both_gradients(place, pair_keys, pair_errors, fast, acc, outer)
    pieces = [swap(summed[step], "seq", step * 2) for step in range(1, outer)]
    crossed = swap(after(across, summed[1]), "seq", 1)
    pieces[2] = after(pieces[2], crossed)
    renewed = renew(place, fast, momentum, summed[0], pieces)

    near = [renewed]
    for step in range(1, outer):
        near.append(swap(renewed, "seq", step * 2))
    far = [swap(renewed, "seq", 1)]
    wide_far = [crossed, swap(after(wide[1], near[1]), "seq", 1)]
    near[1] = after(near[1], far[0])
    far += [swap(unit, "seq", 1) for unit in near[1:]]
    attended = window_attention(
        place, queries, keys, values, pair_keys, up_keys, after(crossed, far[1])
    )
    wide.append(ring_step(after(wide[2], far[1], near[2], near[3]), outer))

    total = after(summed[0], far[1])
    for piece in pieces:
        total = total + piece.astype(jnp.float32)
    moment = MOMENTUM_DECAY * momentum + total[None]

    far[-1] = after(far[-1], attended, wide_far[1], moment)
    wide_far.append(swap(after(wide[2], far[1]), "seq", 1))
    wide_far.append(swap(after(wide[3], wide_far[2]), "seq", 1))

    combined = apply_fast(place, queries, attended, near + far)

    crossed_x = swap(combined, "head", 2)
    other_core = swap(combined, "head", 1)
    crossed_x = after(crossed_x, *wide_far[2:])
    last = swap(crossed_x, "head", 3 ^ 2)
    held = [out_proj] + wide[1:]
    partial, rows = project_most(
        place, [combined, other_core, crossed_x], [0, 1, 2], 3, held, wide_far, out_proj.shape[0]
    )
    mixed = project_last(partial, last, rows)
    return (mixed, moment)


def plain(queries, keys, values, rates, fast, momentum, out_proj):
    tok_rows = queries.shape[0]
    ranks = lax.axis_size("seq")
    position = lax.axis_index("seq")
    own_rows = momentum.shape[2]
    grad_scale = 1.0 / math.sqrt(tok_rows * ranks)
    weights = fast[0]
    h_gate = times_transposed(keys, weights[0])
    h_up = times_transposed(keys, weights[1])
    sigma = jax.nn.sigmoid(h_gate)
    gated = (h_gate * sigma * h_up).astype(jnp.bfloat16)
    errors = (-grad_scale * rates * values.astype(jnp.float32)).astype(jnp.bfloat16)
    grad_down = contract_rows(errors, gated)
    back = matmul(errors, weights[2])
    d_gate = (back * h_up * sigma * (1.0 + h_gate * (1.0 - sigma))).astype(jnp.bfloat16)
    d_up = (back * h_gate * sigma).astype(jnp.bfloat16)
    grads = jnp.stack([contract_rows(d_gate, keys), contract_rows(d_up, keys), grad_down])
    summed_rows = lax.psum_scatter(grads, "seq", scatter_dimension=1, tiled=True)
    moment_own = MOMENTUM_DECAY * momentum[0] + summed_rows
    base_rows = lax.dynamic_slice_in_dim(weights, position * own_rows, own_rows, 1).astype(jnp.float32)
    renewed = lax.all_gather(renormalize(base_rows, moment_own), "seq", axis=1, tiled=True)
    q_gate = times_transposed(queries, renewed[0])
    q_up = times_transposed(queries, renewed[1])
    fast_in = (q_gate * jax.nn.sigmoid(q_gate) * q_up).astype(jnp.bfloat16)
    fast_out = times_transposed(fast_in, renewed[2])
    behind = [(i, i + 1) for i in range(ranks - 1)]
    early_keys = lax.ppermute(keys, "seq", behind)
    early_values = lax.ppermute(values, "seq", behind)
    attended = attention(queries, keys, values, early_keys, early_values, position)
    combined = (attended + fast_out).astype(jnp.bfloat16)
    all_heads = lax.all_gather(combined, "head", axis=1, tiled=True)
    projection = lax.all_gather(out_proj, "seq", axis=0, tiled=True)
    return (matmul(all_heads, projection).astype(jnp.bfloat16), moment_own[None])


def solution(mesh):
    return jax.shard_map(
        shards,
        mesh=mesh,
        in_specs=(
            P("seq", "head"),
            P("seq", "head"),
            P("seq", "head"),
            P("seq", "head"),
            P("head", None, None, None),
            P("head", None, "seq", None),
            P("seq", "head"),
        ),
        out_specs=(P("seq", "head"), P("head", None, "seq", None)),
        check_vma=False,
    )
```

```python
import functools
import math

import jax
import jax.numpy as jnp
import numpy as np
from jax import lax
from jax.experimental import pallas as pl
from jax.experimental.pallas import tpu as pltpu
from jax.sharding import PartitionSpec as P

HD = 512
WINDOW = 512

MOMENTUM_DECAY = 0.9
NORM_EPS = 1e-06
NEG_LARGE = -1e30
MIB = 1024 * 1024
ORIGINS = 4
BRIEF = pl.CostEstimate(flops=1, bytes_accessed=1, transcendentals=0)


def times_transposed(left, right):
    return lax.dot_general(
        left, right, (((1,), (1,)), ((), ())), preferred_element_type=jnp.float32
    )


def contract_rows(left, right):
    return lax.dot_general(
        left, right, (((0,), (0,)), ((), ())), preferred_element_type=jnp.float32
    )


def matmul(left, right):
    return jnp.dot(left, right, preferred_element_type=jnp.float32)


def swap(array, axis, mask):
    devices = lax.axis_size(axis)
    return lax.ppermute(array, axis, [(i, i ^ mask) for i in range(devices)])


def params(mib):
    return pltpu.CompilerParams(vmem_limit_bytes=mib * MIB)


def whole_spec():
    return pl.BlockSpec(memory_space=pltpu.VMEM)


def gradient_rows(outer, side, k, e, w, eye, hg_s, hu_s, err_s, dg_s, du_s):
    tokens, hidden = k.shape
    own = hidden // (2 * outer)
    hg = times_transposed(w[0], k)
    hu = times_transposed(w[1], k)
    hg_s[...] = hg
    hu_s[...] = hu
    gated = (hg * jax.nn.sigmoid(hg) * hu).astype(jnp.bfloat16)
    err_s[...] = times_transposed(eye, e).astype(jnp.bfloat16)
    down_t = times_transposed(eye, w[2]).astype(jnp.bfloat16)
    back = matmul(down_t, err_s[...])
    dg_s[2] = back
    errors = []
    for z in range(outer):
        rows = pl.ds(pl.multiple_of((2 * z + side) * own, own), own)
        to = pl.ds(z * own, own)
        g, u, b = hg_s[rows], hu_s[rows], dg_s[2, rows]
        s = jax.nn.sigmoid(g)
        du_s[0, to] = (b * u * s * (1.0 + g * (1.0 - s))).astype(jnp.bfloat16)
        du_s[1, to] = (b * g * s).astype(jnp.bfloat16)
        du_s[2, to] = err_s[rows]
    return (
        matmul(du_s[0], k),
        matmul(du_s[1], k),
        times_transposed(du_s[2], gated),
    )


def identity(size):
    rows = lax.broadcasted_iota(jnp.int32, (size, size), 0)
    columns = lax.broadcasted_iota(jnp.int32, (size, size), 1)
    return jnp.where(rows == columns, 1.0, 0.0).astype(jnp.bfloat16)


def own_kernel(outer, place, k, e, w, acc, *scratch):
    eye = identity(e.shape[1])
    parts = gradient_rows(outer, place[0], k[...], e[...], w[0], eye, *scratch)
    own = acc.shape[2]
    for i, part in enumerate(parts):
        acc[:, i] = part.reshape(outer, own, part.shape[1])


def both_kernel(outer, place, k, e, w, acc, mine, *rest):
    sent, scratch = rest[: outer - 1], rest[outer - 1 :]
    eye = identity(e.shape[1])
    parts = gradient_rows(outer, place[0], k[...], e[...], w[0], eye, *scratch)
    own = acc.shape[2]
    total = scratch[1]
    for i, part in enumerate(parts):
        total[pl.ds(0, outer * own), :] = part + acc[:, i].reshape(outer * own, part.shape[1])
        mine[i] = total[pl.ds(pl.multiple_of(place[1] * own, own), own), :]
        for step in range(1, outer):
            other = place[1] ^ step
            block = total[pl.ds(pl.multiple_of(other * own, own), own), :]
            sent[step - 1][i] = block.astype(jnp.bfloat16)


def gradient_scratch(tokens, hidden):
    return [
        pltpu.VMEM((hidden, tokens), jnp.float32),
        pltpu.VMEM((hidden, tokens), jnp.float32),
        pltpu.VMEM((hidden, tokens), jnp.bfloat16),
        pltpu.VMEM((3, hidden, tokens), jnp.float32),
        pltpu.VMEM((3, hidden // 2, tokens), jnp.bfloat16),
    ]


def own_gradients(place, k, e, w, outer):
    tokens, hidden = k.shape
    own = hidden // (2 * outer)
    return pl.pallas_call(
        functools.partial(own_kernel, outer),
        out_shape=jax.ShapeDtypeStruct((outer, 3, own, hidden), jnp.float32),
        in_specs=[pl.BlockSpec(memory_space=pltpu.SMEM)] + [whole_spec()] * 3,
        out_specs=whole_spec(),
        scratch_shapes=gradient_scratch(tokens, hidden),
        compiler_params=params(12),
        cost_estimate=BRIEF,
        name="own_gradients",
    )(place, k, e, w)


def both_gradients(place, k, e, w, acc, outer):
    tokens, hidden = k.shape
    own = hidden // (2 * outer)
    return pl.pallas_call(
        functools.partial(both_kernel, outer),
        out_shape=[jax.ShapeDtypeStruct((3, own, hidden), jnp.float32)]
        + [jax.ShapeDtypeStruct((3, own, hidden), jnp.bfloat16)] * (outer - 1),
        in_specs=[pl.BlockSpec(memory_space=pltpu.SMEM)] + [whole_spec()] * 4,
        out_specs=[whole_spec()] * outer,
        scratch_shapes=gradient_scratch(tokens, hidden),
        compiler_params=params(12),
        cost_estimate=BRIEF,
        name="both_gradients",
    )(place, k, e, w, acc)


def attend_kernel(blocks, place, q, k, v, pair_k, up_k, early_v, out):
    early_k = jnp.where(place[0] == 0, up_k[...], pair_k[...])
    early_v = early_v[: v.shape[0]]
    early_v = jnp.where(place[2] > 0, early_v, jnp.zeros_like(early_v))
    tokens = q.shape[0]
    rows = tokens // blocks
    scale = 1.0 / math.sqrt(q.shape[1])
    for b in range(blocks):
        first, last = b * rows, (b + 1) * rows
        own = times_transposed(q[first:last], k[:last]) * scale
        old = times_transposed(q[first:last], early_k[first:]) * scale
        row = first + lax.broadcasted_iota(jnp.int32, own.shape, 0)
        column = lax.broadcasted_iota(jnp.int32, own.shape, 1)
        own = jnp.where(column <= row, own, NEG_LARGE)
        row = first + lax.broadcasted_iota(jnp.int32, old.shape, 0)
        column = first + lax.broadcasted_iota(jnp.int32, old.shape, 1)
        old = jnp.where((column > row) & (place[2] > 0), old, NEG_LARGE)
        highest = jnp.maximum(
            jnp.max(own, axis=1, keepdims=True), jnp.max(old, axis=1, keepdims=True)
        )
        own, old = jnp.exp(own - highest), jnp.exp(old - highest)
        total = jnp.sum(own, axis=1, keepdims=True) + jnp.sum(old, axis=1, keepdims=True)
        own = (own / total).astype(jnp.bfloat16)
        old = (old / total).astype(jnp.bfloat16)
        out[first:last] = matmul(own, v[:last]) + matmul(old, early_v[first:])


def window_attention(place, q, k, v, *early):
    tokens, hidden = q.shape
    return pl.pallas_call(
        functools.partial(attend_kernel, 2),
        out_shape=jax.ShapeDtypeStruct((tokens, hidden), jnp.float32),
        in_specs=[pl.BlockSpec(memory_space=pltpu.SMEM)] + [whole_spec()] * 6,
        out_specs=whole_spec(),
        compiler_params=params(12),
        cost_estimate=BRIEF,
        name="window_attention",
    )(place, q, k, v, *early)


def crossing_kernel(place, even, odd, *rest):
    units, out = rest[:-1], rest[-1]
    tokens, rows_in = even.shape[0], units[0].shape[0]

    @pl.when(place[0] == 0)
    def _():
        out[:tokens] = even[...]

    @pl.when(place[0] == 1)
    def _():
        out[:tokens] = odd[...]

    for i, unit in enumerate(units):
        out[tokens + i * rows_in : tokens + (i + 1) * rows_in] = unit[...]


def crossing(place, even, odd, units):
    shape = (even.shape[0] + sum(unit.shape[0] for unit in units), even.shape[1])
    return pl.pallas_call(
        crossing_kernel,
        out_shape=jax.ShapeDtypeStruct(shape, even.dtype),
        in_specs=[pl.BlockSpec(memory_space=pltpu.SMEM)] + [whole_spec()] * (2 + len(units)),
        out_specs=whole_spec(),
        compiler_params=params(12),
        cost_estimate=BRIEF,
        name="crossing",
    )(place, even, odd, *units)


def renew_kernel(place, w, momentum, mine, *rest):
    pieces, renewed = rest[:-1], rest[-1]
    own = mine.shape[1]
    total = mine[...]
    for piece in pieces:
        total = total + piece[...].astype(jnp.float32)
    new = MOMENTUM_DECAY * momentum[0] + total
    rows = pl.ds(pl.multiple_of(place[2] * own, own), own)
    for i in range(w.shape[1]):
        base = w[0, i, rows, :].astype(jnp.float32)
        renewed[i] = renormalize(base, new[i])


def renew(place, w, momentum, mine, pieces):
    return pl.pallas_call(
        renew_kernel,
        out_shape=jax.ShapeDtypeStruct(mine.shape, jnp.bfloat16),
        in_specs=[pl.BlockSpec(memory_space=pltpu.SMEM)] + [whole_spec()] * (3 + len(pieces)),
        out_specs=whole_spec(),
        compiler_params=params(12),
        cost_estimate=BRIEF,
        name="renew",
    )(place, w, momentum, mine, *pieces)


def apply_kernel(count, place, q, attended, *rest):
    units, combined, full = rest[:count], rest[count], rest[count + 1]
    own = units[0].shape[1]
    for i in range(count):
        step, across = i % (count // 2), i // (count // 2)
        rows = pl.ds(pl.multiple_of((place[2] ^ (2 * step + across)) * own, own), own)
        full[:, rows, :] = units[i][...]
    b1 = times_transposed(q[...], full[0])
    b3 = times_transposed(q[...], full[1])
    fast_in = (b1 * jax.nn.sigmoid(b1) * b3).astype(jnp.bfloat16)
    out = times_transposed(fast_in, full[2])
    combined[...] = (attended[...] + out).astype(jnp.bfloat16)


def apply_fast(place, q, attended, units):
    tokens, hidden = q.shape
    return pl.pallas_call(
        functools.partial(apply_kernel, len(units)),
        out_shape=jax.ShapeDtypeStruct((tokens, hidden), jnp.bfloat16),
        in_specs=[pl.BlockSpec(memory_space=pltpu.SMEM)] + [whole_spec()] * (2 + len(units)),
        out_specs=whole_spec(),
        scratch_shapes=[pltpu.VMEM((3, hidden, hidden), jnp.bfloat16)],
        compiler_params=params(12),
        cost_estimate=BRIEF,
        name="apply_fast",
    )(place, q, attended, *units)


def most_kernel(tags, last, rows_in, offsets, place, *rest):
    blocks, units = rest[: len(tags)], rest[len(tags) : -3]
    partial, last_rows, full = rest[-3:]
    for at, (unit, first) in enumerate(offsets):
        rows = pl.ds(pl.multiple_of(place[ORIGINS + at] * rows_in, rows_in), rows_in)
        full[rows, :] = units[unit][first : first + rows_in, :]
    width = blocks[0].shape[1]
    value = None
    for block, tag in zip(blocks, tags):
        rows = pl.ds(pl.multiple_of((place[3] ^ tag) * width, width), width)
        part = matmul(block[...], full[rows, :])
        value = part if value is None else value + part
    partial[...] = value
    rows = pl.ds(pl.multiple_of((place[3] ^ last) * width, width), width)
    last_rows[...] = full[rows, :]


def project_most(place, blocks, tags, last, near, far, rows_in):
    tokens, width = blocks[0].shape
    units = near + far
    offsets = [(i, 0) for i in range(len(near))]
    for i, unit in enumerate(far, len(near)):
        firsts = [tokens, tokens + rows_in] if i == len(near) else [0]
        offsets += [(i, first) for first in firsts]
    columns = near[0].shape[1]
    return pl.pallas_call(
        functools.partial(most_kernel, tags, last, rows_in, offsets),
        out_shape=[
            jax.ShapeDtypeStruct((tokens, columns), jnp.float32),
            jax.ShapeDtypeStruct((width, columns), jnp.bfloat16),
        ],
        in_specs=[pl.BlockSpec(memory_space=pltpu.SMEM)]
        + [whole_spec()] * (len(units) + len(blocks)),
        out_specs=[whole_spec()] * 2,
        scratch_shapes=[pltpu.VMEM((rows_in * len(offsets), columns), jnp.bfloat16)],
        compiler_params=params(12),
        cost_estimate=BRIEF,
        name="project_most",
    )(place, *blocks, *units)


def last_kernel(partial, block, rows, mixed):
    mixed[...] = (partial[...] + matmul(block[...], rows[...])).astype(mixed.dtype)


def project_last(partial, block, rows):
    return pl.pallas_call(
        last_kernel,
        out_shape=jax.ShapeDtypeStruct(partial.shape, jnp.bfloat16),
        in_specs=[whole_spec()] * 3,
        out_specs=whole_spec(),
        compiler_params=params(12),
        cost_estimate=BRIEF,
        name="project_last",
    )(partial, block, rows)


def ring_order(outer):
    return [0] + list(range(1, outer, 2)) + list(range(outer - 2 + outer % 2, 0, -2))


def ring_step(unit, outer):
    order = ring_order(outer)
    pairs = []
    for place, z in enumerate(order):
        to = order[(place + 1) % outer]
        pairs += [(2 * z + y, 2 * to + y) for y in range(2)]
    return lax.ppermute(unit, "seq", pairs)


def after(array, *others):
    return lax.optimization_barrier((array,) + others)[0]


def place_table(outer, heads):
    order = ring_order(outer)
    table = []
    for s in range(2 * outer):
        place = order.index(s // 2)
        sources = [order[(place - step) % outer] for step in range(outer)]
        near = [2 * z + s % 2 for z in sources]
        far = [2 * z + 1 - s % 2 for z in sources]
        table += [[s % 2, s // 2, s, head] + near + far for head in range(heads)]
    return np.array(table, np.int32)


def renormalize(base, moment):
    updated = base - moment
    base_rms = jnp.sqrt(jnp.mean(base * base, axis=-1, keepdims=True) + NORM_EPS)
    new_rms = jnp.sqrt(jnp.mean(updated * updated, axis=-1, keepdims=True) + NORM_EPS)
    return (updated * (base_rms / new_rms)).astype(jnp.bfloat16)


def attention(queries, keys, values, early_keys, early_values, position):
    tok_rows = queries.shape[0]
    all_keys = jnp.concatenate([early_keys, keys], axis=0)
    all_values = jnp.concatenate([early_values, values], axis=0)
    key_pos = (position - 1) * tok_rows + jnp.arange(all_keys.shape[0])
    query_pos = position * tok_rows + jnp.arange(tok_rows)
    spacing = query_pos[:, None] - key_pos[None, :]
    allowed = (spacing >= 0) & (spacing < WINDOW) & (key_pos[None, :] >= 0)
    scores = times_transposed(queries, all_keys) * (1.0 / math.sqrt(HD))
    scores = jnp.where(allowed, scores, NEG_LARGE)
    highest = jnp.max(scores, axis=1, keepdims=True)
    expo = jnp.exp(scores - highest)
    probs = (expo / jnp.sum(expo, axis=1, keepdims=True)).astype(jnp.bfloat16)
    return jnp.dot(probs, all_values, preferred_element_type=jnp.float32)


def shards(queries, keys, values, rates, fast, momentum, out_proj):
    tok_rows = queries.shape[0]
    ranks = lax.axis_size("seq")
    heads = lax.axis_size("head")
    own_rows = momentum.shape[2]
    if own_rows % 16 or ranks != 8 or heads != 4 or tok_rows != WINDOW:
        return plain(queries, keys, values, rates, fast, momentum, out_proj)
    outer = ranks // 2
    grad_scale = 1.0 / math.sqrt(tok_rows * ranks)
    index = lax.axis_index("seq") * heads + lax.axis_index("head")
    place = lax.dynamic_index_in_dim(jnp.asarray(place_table(outer, heads)), index, 0, False)

    pair_keys = swap(keys, "seq", 1)
    errors = (-grad_scale * rates * values.astype(jnp.float32)).astype(jnp.bfloat16)
    pair_errors = swap(errors, "seq", 1)

    wide = [out_proj]
    for _ in range(2):
        wide.append(ring_step(wide[-1], outer))

    up_values = after(values, wide[1])
    up_values = lax.ppermute(up_values, "seq", [(s, s + 2) for s in range(1, ranks - 2, 2)])
    up_keys = after(pair_keys, wide[2])
    up_keys = lax.ppermute(up_keys, "seq", [(s, s + 2) for s in range(0, ranks - 2, 2)])

    acc = own_gradients(place, keys, errors, fast, outer)
    across = crossing(place, values, up_values, wide[:2])
    pair_errors = after(pair_errors, up_keys, across)
    summed = both_gradients(place, pair_keys, pair_errors, fast, acc, outer)
    pieces = [swap(summed[step], "seq", step * 2) for step in range(1, outer)]
    crossed = swap(after(across, summed[1]), "seq", 1)
    pieces[2] = after(pieces[2], crossed)
    renewed = renew(place, fast, momentum, summed[0], pieces)

    near = [renewed]
    for step in range(1, outer):
        near.append(swap(renewed, "seq", step * 2))
    far = [swap(renewed, "seq", 1)]
    wide_far = [crossed, swap(after(wide[2], near[1]), "seq", 1)]
    near[1] = after(near[1], far[0])
    far += [swap(unit, "seq", 1) for unit in near[1:]]
    attended = window_attention(
        place, queries, keys, values, pair_keys, up_keys, after(crossed, near[1])
    )
    wide.append(ring_step(after(wide[2], far[1], near[2], near[3]), outer))

    total = after(summed[0], near[1])
    for piece in pieces:
        total = total + piece.astype(jnp.float32)
    moment = MOMENTUM_DECAY * momentum + total[None]

    far[-1] = after(far[-1], attended, wide_far[1], moment)
    wide_far.append(swap(wide[3], "seq", 1))

    combined = apply_fast(place, queries, attended, near + far)

    crossed_x = swap(combined, "head", 2)
    other_core = swap(combined, "head", 1)
    crossed_x = after(crossed_x, wide_far[2])
    last = swap(crossed_x, "head", 3 ^ 2)
    held = [out_proj] + wide[1:]
    partial, rows = project_most(
        place, [combined, other_core, crossed_x], [0, 1, 2], 3, held, wide_far, out_proj.shape[0]
    )
    mixed = project_last(partial, last, rows)
    return (mixed, moment)


def plain(queries, keys, values, rates, fast, momentum, out_proj):
    tok_rows = queries.shape[0]
    ranks = lax.axis_size("seq")
    position = lax.axis_index("seq")
    own_rows = momentum.shape[2]
    grad_scale = 1.0 / math.sqrt(tok_rows * ranks)
    weights = fast[0]
    h_gate = times_transposed(keys, weights[0])
    h_up = times_transposed(keys, weights[1])
    sigma = jax.nn.sigmoid(h_gate)
    gated = (h_gate * sigma * h_up).astype(jnp.bfloat16)
    errors = (-grad_scale * rates * values.astype(jnp.float32)).astype(jnp.bfloat16)
    grad_down = contract_rows(errors, gated)
    back = matmul(errors, weights[2])
    d_gate = (back * h_up * sigma * (1.0 + h_gate * (1.0 - sigma))).astype(jnp.bfloat16)
    d_up = (back * h_gate * sigma).astype(jnp.bfloat16)
    grads = jnp.stack([contract_rows(d_gate, keys), contract_rows(d_up, keys), grad_down])
    summed_rows = lax.psum_scatter(grads, "seq", scatter_dimension=1, tiled=True)
    moment_own = MOMENTUM_DECAY * momentum[0] + summed_rows
    base_rows = lax.dynamic_slice_in_dim(weights, position * own_rows, own_rows, 1).astype(jnp.float32)
    renewed = lax.all_gather(renormalize(base_rows, moment_own), "seq", axis=1, tiled=True)
    q_gate = times_transposed(queries, renewed[0])
    q_up = times_transposed(queries, renewed[1])
    fast_in = (q_gate * jax.nn.sigmoid(q_gate) * q_up).astype(jnp.bfloat16)
    fast_out = times_transposed(fast_in, renewed[2])
    behind = [(i, i + 1) for i in range(ranks - 1)]
    early_keys = lax.ppermute(keys, "seq", behind)
    early_values = lax.ppermute(values, "seq", behind)
    attended = attention(queries, keys, values, early_keys, early_values, position)
    combined = (attended + fast_out).astype(jnp.bfloat16)
    all_heads = lax.all_gather(combined, "head", axis=1, tiled=True)
    projection = lax.all_gather(out_proj, "seq", axis=0, tiled=True)
    return (matmul(all_heads, projection).astype(jnp.bfloat16), moment_own[None])


def solution(mesh):
    return jax.shard_map(
        shards,
        mesh=mesh,
        in_specs=(
            P("seq", "head"),
            P("seq", "head"),
            P("seq", "head"),
            P("seq", "head"),
            P("head", None, None, None),
            P("head", None, "seq", None),
            P("seq", "head"),
        ),
        out_specs=(P("seq", "head"), P("head", None, "seq", None)),
        check_vma=False,
    )
```

```python
import functools
import math

import jax
import jax.numpy as jnp
import numpy as np
from jax import lax
from jax.experimental import pallas as pl
from jax.experimental.pallas import tpu as pltpu
from jax.sharding import PartitionSpec as P

HD = 512
WINDOW = 512

MOMENTUM_DECAY = 0.9
NORM_EPS = 1e-06
NEG_LARGE = -1e30
MIB = 1024 * 1024
ORIGINS = 4
BRIEF = pl.CostEstimate(flops=1, bytes_accessed=1, transcendentals=0)


def times_transposed(left, right):
    return lax.dot_general(
        left, right, (((1,), (1,)), ((), ())), preferred_element_type=jnp.float32
    )


def contract_rows(left, right):
    return lax.dot_general(
        left, right, (((0,), (0,)), ((), ())), preferred_element_type=jnp.float32
    )


def matmul(left, right):
    return jnp.dot(left, right, preferred_element_type=jnp.float32)


def swap(array, axis, mask):
    devices = lax.axis_size(axis)
    return lax.ppermute(array, axis, [(i, i ^ mask) for i in range(devices)])


def params(mib):
    return pltpu.CompilerParams(vmem_limit_bytes=mib * MIB)


def whole_spec():
    return pl.BlockSpec(memory_space=pltpu.VMEM)


def identity(size):
    rows = lax.broadcasted_iota(jnp.int32, (size, size), 0)
    columns = lax.broadcasted_iota(jnp.int32, (size, size), 1)
    return jnp.where(rows == columns, 1.0, 0.0).astype(jnp.bfloat16)


def parity_rows(place, z, own):
    return pl.ds(pl.multiple_of((2 * z + place[0]) * own, own), own)


def keys_kernel(outer, place, k, w, gated, gate, up, down, hg_s, hu_s, down_s):
    own = gate.shape[0] // outer
    hg = times_transposed(w[0, 0], k[...])
    hu = times_transposed(w[0, 1], k[...])
    hg_s[...] = hg
    hu_s[...] = hu
    gated[...] = (hg * jax.nn.sigmoid(hg) * hu).astype(jnp.bfloat16)
    down_s[...] = times_transposed(identity(w.shape[3]), w[0, 2]).astype(jnp.bfloat16)
    for z in range(outer):
        rows, to = parity_rows(place, z, own), pl.ds(z * own, own)
        g, u = hg_s[rows], hu_s[rows]
        s = jax.nn.sigmoid(g)
        gate[to] = u * s * (1.0 + g * (1.0 - s))
        up[to] = g * s
        down[to] = down_s[rows]


def keys_part(place, k, w, outer):
    tokens, hidden = k.shape
    half = jax.ShapeDtypeStruct((hidden // 2, tokens), jnp.float32)
    return pl.pallas_call(
        functools.partial(keys_kernel, outer),
        out_shape=[
            jax.ShapeDtypeStruct((hidden, tokens), jnp.bfloat16),
            half,
            half,
            jax.ShapeDtypeStruct((hidden // 2, hidden), jnp.bfloat16),
        ],
        in_specs=[pl.BlockSpec(memory_space=pltpu.SMEM)] + [whole_spec()] * 2,
        out_specs=[whole_spec()] * 4,
        scratch_shapes=[
            pltpu.VMEM((hidden, tokens), jnp.float32),
            pltpu.VMEM((hidden, tokens), jnp.float32),
            pltpu.VMEM((hidden, hidden), jnp.bfloat16),
        ],
        compiler_params=params(12),
        cost_estimate=BRIEF,
        name="keys_part",
    )(place, k, w)


def gradient_rows(outer, place, k, e, gated, gate, up, down, err_s, er_s):
    own = gate.shape[0] // outer
    err_s[...] = times_transposed(identity(e.shape[1]), e[...]).astype(jnp.bfloat16)
    for z in range(outer):
        er_s[pl.ds(z * own, own)] = err_s[parity_rows(place, z, own)]
    back = matmul(down[...], err_s[...])
    return (
        matmul((back * gate[...]).astype(jnp.bfloat16), k[...]),
        matmul((back * up[...]).astype(jnp.bfloat16), k[...]),
        times_transposed(er_s[...], gated[...]),
    )


def own_kernel(outer, place, k, e, gated, gate, up, down, acc, *scratch):
    parts = gradient_rows(outer, place, k, e, gated, gate, up, down, *scratch)
    for i, part in enumerate(parts):
        acc[i] = part


def both_kernel(outer, place, k, e, gated, gate, up, down, acc, mine, *rest):
    sent, (total, *scratch) = rest[: outer - 1], rest[outer - 1 :]
    parts = gradient_rows(outer, place, k, e, gated, gate, up, down, *scratch)
    own = mine.shape[1]
    for i, part in enumerate(parts):
        total[i] = part + acc[i]
        mine[i] = total[i, pl.ds(pl.multiple_of(place[1] * own, own), own), :]
        for step in range(1, outer):
            other = place[1] ^ step
            block = total[i, pl.ds(pl.multiple_of(other * own, own), own), :]
            sent[step - 1][i] = block.astype(jnp.bfloat16)


def gradient_scratch(tokens, hidden):
    return [
        pltpu.VMEM((hidden, tokens), jnp.bfloat16),
        pltpu.VMEM((hidden // 2, tokens), jnp.bfloat16),
    ]


def own_gradients(place, k, e, factors, outer):
    tokens, hidden = k.shape
    return pl.pallas_call(
        functools.partial(own_kernel, outer),
        out_shape=jax.ShapeDtypeStruct((3, hidden // 2, hidden), jnp.float32),
        in_specs=[pl.BlockSpec(memory_space=pltpu.SMEM)] + [whole_spec()] * 6,
        out_specs=whole_spec(),
        scratch_shapes=gradient_scratch(tokens, hidden),
        compiler_params=params(12),
        cost_estimate=BRIEF,
        name="own_gradients",
    )(place, k, e, *factors)


def both_gradients(place, k, e, factors, acc, outer):
    tokens, hidden = k.shape
    own = hidden // (2 * outer)
    return pl.pallas_call(
        functools.partial(both_kernel, outer),
        out_shape=[jax.ShapeDtypeStruct((3, own, hidden), jnp.float32)]
        + [jax.ShapeDtypeStruct((3, own, hidden), jnp.bfloat16)] * (outer - 1),
        in_specs=[pl.BlockSpec(memory_space=pltpu.SMEM)] + [whole_spec()] * 7,
        out_specs=[whole_spec()] * outer,
        scratch_shapes=[pltpu.VMEM(acc.shape, jnp.float32)] + gradient_scratch(tokens, hidden),
        compiler_params=params(12),
        cost_estimate=BRIEF,
        name="both_gradients",
    )(place, k, e, *factors, acc)


def attend_kernel(blocks, place, q, k, v, pair_k, up_k, early_v, out):
    early_k = jnp.where(place[0] == 0, up_k[...], pair_k[...])
    early_v = early_v[: v.shape[0]]
    early_v = jnp.where(place[2] > 0, early_v, jnp.zeros_like(early_v))
    tokens = q.shape[0]
    rows = tokens // blocks
    scale = 1.0 / math.sqrt(q.shape[1])
    for b in range(blocks):
        first, last = b * rows, (b + 1) * rows
        own = times_transposed(q[first:last], k[:last]) * scale
        old = times_transposed(q[first:last], early_k[first:]) * scale
        row = first + lax.broadcasted_iota(jnp.int32, own.shape, 0)
        column = lax.broadcasted_iota(jnp.int32, own.shape, 1)
        own = jnp.where(column <= row, own, NEG_LARGE)
        row = first + lax.broadcasted_iota(jnp.int32, old.shape, 0)
        column = first + lax.broadcasted_iota(jnp.int32, old.shape, 1)
        old = jnp.where((column > row) & (place[2] > 0), old, NEG_LARGE)
        highest = jnp.maximum(
            jnp.max(own, axis=1, keepdims=True), jnp.max(old, axis=1, keepdims=True)
        )
        own, old = jnp.exp(own - highest), jnp.exp(old - highest)
        total = jnp.sum(own, axis=1, keepdims=True) + jnp.sum(old, axis=1, keepdims=True)
        own = (own / total).astype(jnp.bfloat16)
        old = (old / total).astype(jnp.bfloat16)
        out[first:last] = matmul(own, v[:last]) + matmul(old, early_v[first:])


def window_attention(place, q, k, v, *early):
    tokens, hidden = q.shape
    return pl.pallas_call(
        functools.partial(attend_kernel, 2),
        out_shape=jax.ShapeDtypeStruct((tokens, hidden), jnp.float32),
        in_specs=[pl.BlockSpec(memory_space=pltpu.SMEM)] + [whole_spec()] * 6,
        out_specs=whole_spec(),
        compiler_params=params(12),
        cost_estimate=BRIEF,
        name="window_attention",
    )(place, q, k, v, *early)


def crossing_kernel(place, even, odd, rows, out):
    tokens = even.shape[0]

    @pl.when(place[0] == 0)
    def _():
        out[:tokens] = even[...]

    @pl.when(place[0] == 1)
    def _():
        out[:tokens] = odd[...]

    out[tokens:] = rows[...]


def crossing(place, even, odd, rows):
    shape = (even.shape[0] + rows.shape[0], even.shape[1])
    return pl.pallas_call(
        crossing_kernel,
        out_shape=jax.ShapeDtypeStruct(shape, even.dtype),
        in_specs=[pl.BlockSpec(memory_space=pltpu.SMEM)] + [whole_spec()] * 3,
        out_specs=whole_spec(),
        compiler_params=params(12),
        cost_estimate=BRIEF,
        name="crossing",
    )(place, even, odd, rows)


def renew_kernel(place, w, momentum, mine, *rest):
    pieces, renewed = rest[:-1], rest[-1]
    own = mine.shape[1]
    total = mine[...]
    for piece in pieces:
        total = total + piece[...].astype(jnp.float32)
    new = MOMENTUM_DECAY * momentum[0] + total
    rows = pl.ds(pl.multiple_of(place[2] * own, own), own)
    for i in range(w.shape[1]):
        base = w[0, i, rows, :].astype(jnp.float32)
        renewed[i] = renormalize(base, new[i])


def renew(place, w, momentum, mine, pieces):
    return pl.pallas_call(
        renew_kernel,
        out_shape=jax.ShapeDtypeStruct(mine.shape, jnp.bfloat16),
        in_specs=[pl.BlockSpec(memory_space=pltpu.SMEM)] + [whole_spec()] * (3 + len(pieces)),
        out_specs=whole_spec(),
        compiler_params=params(12),
        cost_estimate=BRIEF,
        name="renew",
    )(place, w, momentum, mine, *pieces)


def apply_kernel(count, place, q, attended, *rest):
    units, combined, full = rest[:count], rest[count], rest[count + 1]
    own = units[0].shape[1]
    for i in range(count):
        step, across = i % (count // 2), i // (count // 2)
        rows = pl.ds(pl.multiple_of((place[2] ^ (2 * step + across)) * own, own), own)
        full[:, rows, :] = units[i][...]
    b1 = times_transposed(q[...], full[0])
    b3 = times_transposed(q[...], full[1])
    fast_in = (b1 * jax.nn.sigmoid(b1) * b3).astype(jnp.bfloat16)
    out = times_transposed(fast_in, full[2])
    combined[...] = (attended[...] + out).astype(jnp.bfloat16)


def apply_fast(place, q, attended, units):
    tokens, hidden = q.shape
    return pl.pallas_call(
        functools.partial(apply_kernel, len(units)),
        out_shape=jax.ShapeDtypeStruct((tokens, hidden), jnp.bfloat16),
        in_specs=[pl.BlockSpec(memory_space=pltpu.SMEM)] + [whole_spec()] * (2 + len(units)),
        out_specs=whole_spec(),
        scratch_shapes=[pltpu.VMEM((3, hidden, hidden), jnp.bfloat16)],
        compiler_params=params(12),
        cost_estimate=BRIEF,
        name="apply_fast",
    )(place, q, attended, *units)


def most_kernel(tags, last, rows_in, offsets, place, *rest):
    blocks, units = rest[: len(tags)], rest[len(tags) : -3]
    partial, last_rows, full = rest[-3:]
    for at, (unit, first) in enumerate(offsets):
        rows = pl.ds(pl.multiple_of(place[ORIGINS + at] * rows_in, rows_in), rows_in)
        full[rows, :] = units[unit][first : first + rows_in, :]
    width = blocks[0].shape[1]
    value = None
    for block, tag in zip(blocks, tags):
        rows = pl.ds(pl.multiple_of((place[3] ^ tag) * width, width), width)
        part = matmul(block[...], full[rows, :])
        value = part if value is None else value + part
    partial[...] = value
    rows = pl.ds(pl.multiple_of((place[3] ^ last) * width, width), width)
    last_rows[...] = full[rows, :]


def project_most(place, blocks, tags, last, near, far, rows_in):
    tokens, width = blocks[0].shape
    units = near + far
    offsets = [(i, 0) for i in range(len(near))]
    for i, unit in enumerate(far, len(near)):
        offsets.append((i, unit.shape[0] - rows_in))
    columns = near[0].shape[1]
    return pl.pallas_call(
        functools.partial(most_kernel, tags, last, rows_in, offsets),
        out_shape=[
            jax.ShapeDtypeStruct((tokens, columns), jnp.float32),
            jax.ShapeDtypeStruct((width, columns), jnp.bfloat16),
        ],
        in_specs=[pl.BlockSpec(memory_space=pltpu.SMEM)]
        + [whole_spec()] * (len(units) + len(blocks)),
        out_specs=[whole_spec()] * 2,
        scratch_shapes=[pltpu.VMEM((rows_in * len(offsets), columns), jnp.bfloat16)],
        compiler_params=params(12),
        cost_estimate=BRIEF,
        name="project_most",
    )(place, *blocks, *units)


def last_kernel(partial, block, rows, mixed):
    mixed[...] = (partial[...] + matmul(block[...], rows[...])).astype(mixed.dtype)


def project_last(partial, block, rows):
    return pl.pallas_call(
        last_kernel,
        out_shape=jax.ShapeDtypeStruct(partial.shape, jnp.bfloat16),
        in_specs=[whole_spec()] * 3,
        out_specs=whole_spec(),
        compiler_params=params(12),
        cost_estimate=BRIEF,
        name="project_last",
    )(partial, block, rows)


def ring_order(outer):
    return [0] + list(range(1, outer, 2)) + list(range(outer - 2 + outer % 2, 0, -2))


def ring_step(unit, outer):
    order = ring_order(outer)
    pairs = []
    for place, z in enumerate(order):
        to = order[(place + 1) % outer]
        pairs += [(2 * z + y, 2 * to + y) for y in range(2)]
    return lax.ppermute(unit, "seq", pairs)


def after(array, *others):
    return lax.optimization_barrier((array,) + others)[0]


def place_table(outer, heads):
    order = ring_order(outer)
    table = []
    for s in range(2 * outer):
        place = order.index(s // 2)
        sources = [order[(place - step) % outer] for step in range(outer)]
        near = [2 * z + s % 2 for z in sources]
        far = [2 * z + 1 - s % 2 for z in sources]
        table += [[s % 2, s // 2, s, head] + near + far for head in range(heads)]
    return np.array(table, np.int32)


def renormalize(base, moment):
    updated = base - moment
    base_rms = jnp.sqrt(jnp.mean(base * base, axis=-1, keepdims=True) + NORM_EPS)
    new_rms = jnp.sqrt(jnp.mean(updated * updated, axis=-1, keepdims=True) + NORM_EPS)
    return (updated * (base_rms / new_rms)).astype(jnp.bfloat16)


def attention(queries, keys, values, early_keys, early_values, position):
    tok_rows = queries.shape[0]
    all_keys = jnp.concatenate([early_keys, keys], axis=0)
    all_values = jnp.concatenate([early_values, values], axis=0)
    key_pos = (position - 1) * tok_rows + jnp.arange(all_keys.shape[0])
    query_pos = position * tok_rows + jnp.arange(tok_rows)
    spacing = query_pos[:, None] - key_pos[None, :]
    allowed = (spacing >= 0) & (spacing < WINDOW) & (key_pos[None, :] >= 0)
    scores = times_transposed(queries, all_keys) * (1.0 / math.sqrt(HD))
    scores = jnp.where(allowed, scores, NEG_LARGE)
    highest = jnp.max(scores, axis=1, keepdims=True)
    expo = jnp.exp(scores - highest)
    probs = (expo / jnp.sum(expo, axis=1, keepdims=True)).astype(jnp.bfloat16)
    return jnp.dot(probs, all_values, preferred_element_type=jnp.float32)


def shards(queries, keys, values, rates, fast, momentum, out_proj):
    tok_rows = queries.shape[0]
    ranks = lax.axis_size("seq")
    heads = lax.axis_size("head")
    own_rows = momentum.shape[2]
    if own_rows % 16 or ranks != 8 or heads != 4 or tok_rows != WINDOW:
        return plain(queries, keys, values, rates, fast, momentum, out_proj)
    outer = ranks // 2
    grad_scale = 1.0 / math.sqrt(tok_rows * ranks)
    index = lax.axis_index("seq") * heads + lax.axis_index("head")
    place = lax.dynamic_index_in_dim(jnp.asarray(place_table(outer, heads)), index, 0, False)

    pair_keys = swap(keys, "seq", 1)
    errors = (-grad_scale * rates * values.astype(jnp.float32)).astype(jnp.bfloat16)
    pair_errors = swap(errors, "seq", 1)

    wide = [out_proj, ring_step(out_proj, outer)]
    own_factors = keys_part(place, keys, fast, outer)
    wide.append(ring_step(after(wide[1], own_factors[0]), outer))

    up_values = after(values, wide[1])
    up_values = lax.ppermute(up_values, "seq", [(s, s + 2) for s in range(1, ranks - 2, 2)])
    up_keys = after(pair_keys, wide[2])
    up_keys = lax.ppermute(up_keys, "seq", [(s, s + 2) for s in range(0, ranks - 2, 2)])

    acc = own_gradients(place, keys, errors, own_factors, outer)
    pair_factors = keys_part(place, pair_keys, fast, outer)
    across = crossing(place, values, up_values, wide[0])
    pair_errors = after(pair_errors, up_keys, across)
    summed = both_gradients(place, pair_keys, pair_errors, pair_factors, acc, outer)
    pieces = [swap(summed[step], "seq", step * 2) for step in range(1, outer)]
    crossed = swap(after(across, summed[1]), "seq", 1)
    pieces[2] = after(pieces[2], crossed)
    renewed = renew(place, fast, momentum, summed[0], pieces)

    near = [renewed]
    for step in range(1, outer):
        near.append(swap(renewed, "seq", step * 2))
    far = [swap(renewed, "seq", 1)]
    wide_far = [crossed, swap(after(wide[1], near[1]), "seq", 1)]
    near[1] = after(near[1], far[0])
    far += [swap(unit, "seq", 1) for unit in near[1:]]
    attended = window_attention(
        place, queries, keys, values, pair_keys, up_keys, after(crossed, near[1])
    )
    wide.append(ring_step(after(wide[2], far[1], near[2], near[3]), outer))

    total = after(summed[0], near[1])
    for piece in pieces:
        total = total + piece.astype(jnp.float32)
    moment = MOMENTUM_DECAY * momentum + total[None]

    far[-1] = after(far[-1], attended, wide_far[1], moment)
    wide_far += [swap(after(wide[2], far[1]), "seq", 1), swap(wide[3], "seq", 1)]

    combined = apply_fast(place, queries, attended, near + far)

    crossed_x = swap(combined, "head", 2)
    other_core = swap(combined, "head", 1)
    crossed_x = after(crossed_x, *wide_far[2:])
    last = swap(crossed_x, "head", 3 ^ 2)
    held = [out_proj] + wide[1:]
    partial, rows = project_most(
        place, [combined, other_core, crossed_x], [0, 1, 2], 3, held, wide_far, out_proj.shape[0]
    )
    mixed = project_last(partial, last, rows)
    return (mixed, moment)


def plain(queries, keys, values, rates, fast, momentum, out_proj):
    tok_rows = queries.shape[0]
    ranks = lax.axis_size("seq")
    position = lax.axis_index("seq")
    own_rows = momentum.shape[2]
    grad_scale = 1.0 / math.sqrt(tok_rows * ranks)
    weights = fast[0]
    h_gate = times_transposed(keys, weights[0])
    h_up = times_transposed(keys, weights[1])
    sigma = jax.nn.sigmoid(h_gate)
    gated = (h_gate * sigma * h_up).astype(jnp.bfloat16)
    errors = (-grad_scale * rates * values.astype(jnp.float32)).astype(jnp.bfloat16)
    grad_down = contract_rows(errors, gated)
    back = matmul(errors, weights[2])
    d_gate = (back * h_up * sigma * (1.0 + h_gate * (1.0 - sigma))).astype(jnp.bfloat16)
    d_up = (back * h_gate * sigma).astype(jnp.bfloat16)
    grads = jnp.stack([contract_rows(d_gate, keys), contract_rows(d_up, keys), grad_down])
    summed_rows = lax.psum_scatter(grads, "seq", scatter_dimension=1, tiled=True)
    moment_own = MOMENTUM_DECAY * momentum[0] + summed_rows
    base_rows = lax.dynamic_slice_in_dim(weights, position * own_rows, own_rows, 1).astype(jnp.float32)
    renewed = lax.all_gather(renormalize(base_rows, moment_own), "seq", axis=1, tiled=True)
    q_gate = times_transposed(queries, renewed[0])
    q_up = times_transposed(queries, renewed[1])
    fast_in = (q_gate * jax.nn.sigmoid(q_gate) * q_up).astype(jnp.bfloat16)
    fast_out = times_transposed(fast_in, renewed[2])
    behind = [(i, i + 1) for i in range(ranks - 1)]
    early_keys = lax.ppermute(keys, "seq", behind)
    early_values = lax.ppermute(values, "seq", behind)
    attended = attention(queries, keys, values, early_keys, early_values, position)
    combined = (attended + fast_out).astype(jnp.bfloat16)
    all_heads = lax.all_gather(combined, "head", axis=1, tiled=True)
    projection = lax.all_gather(out_proj, "seq", axis=0, tiled=True)
    return (matmul(all_heads, projection).astype(jnp.bfloat16), moment_own[None])


def solution(mesh):
    return jax.shard_map(
        shards,
        mesh=mesh,
        in_specs=(
            P("seq", "head"),
            P("seq", "head"),
            P("seq", "head"),
            P("seq", "head"),
            P("head", None, None, None),
            P("head", None, "seq", None),
            P("seq", "head"),
        ),
        out_specs=(P("seq", "head"), P("head", None, "seq", None)),
        check_vma=False,
    )
```

```python
import functools
import math

import jax
import jax.numpy as jnp
import numpy as np
from jax import lax
from jax.experimental import pallas as pl
from jax.experimental.pallas import tpu as pltpu
from jax.sharding import PartitionSpec as P

HD = 512
WINDOW = 512

MOMENTUM_DECAY = 0.9
NORM_EPS = 1e-06
NEG_LARGE = -1e30
MIB = 1024 * 1024
ORIGINS = 4
BRIEF = pl.CostEstimate(flops=1, bytes_accessed=1, transcendentals=0)


def times_transposed(left, right):
    return lax.dot_general(
        left, right, (((1,), (1,)), ((), ())), preferred_element_type=jnp.float32
    )


def contract_rows(left, right):
    return lax.dot_general(
        left, right, (((0,), (0,)), ((), ())), preferred_element_type=jnp.float32
    )


def matmul(left, right):
    return jnp.dot(left, right, preferred_element_type=jnp.float32)


def swap(array, axis, mask):
    devices = lax.axis_size(axis)
    return lax.ppermute(array, axis, [(i, i ^ mask) for i in range(devices)])


def params(mib):
    return pltpu.CompilerParams(vmem_limit_bytes=mib * MIB)


def whole_spec():
    return pl.BlockSpec(memory_space=pltpu.VMEM)


def identity(size):
    rows = lax.broadcasted_iota(jnp.int32, (size, size), 0)
    columns = lax.broadcasted_iota(jnp.int32, (size, size), 1)
    return jnp.where(rows == columns, 1.0, 0.0).astype(jnp.bfloat16)


def parity_rows(place, z, own):
    return pl.ds(pl.multiple_of((2 * z + place[0]) * own, own), own)


def keys_kernel(outer, place, k, w, gated, gate, up, down, hg_s, hu_s, down_s):
    own = gate.shape[0] // outer
    hg = times_transposed(w[0, 0], k[...])
    hu = times_transposed(w[0, 1], k[...])
    hg_s[...] = hg
    hu_s[...] = hu
    gated[...] = (hg * jax.nn.sigmoid(hg) * hu).astype(jnp.bfloat16)
    down_s[...] = times_transposed(identity(w.shape[3]), w[0, 2]).astype(jnp.bfloat16)
    for z in range(outer):
        rows, to = parity_rows(place, z, own), pl.ds(z * own, own)
        g, u = hg_s[rows], hu_s[rows]
        s = jax.nn.sigmoid(g)
        gate[to] = u * s * (1.0 + g * (1.0 - s))
        up[to] = g * s
        down[to] = down_s[rows]


def keys_part(place, k, w, outer):
    tokens, hidden = k.shape
    half = jax.ShapeDtypeStruct((hidden // 2, tokens), jnp.float32)
    return pl.pallas_call(
        functools.partial(keys_kernel, outer),
        out_shape=[
            jax.ShapeDtypeStruct((hidden, tokens), jnp.bfloat16),
            half,
            half,
            jax.ShapeDtypeStruct((hidden // 2, hidden), jnp.bfloat16),
        ],
        in_specs=[pl.BlockSpec(memory_space=pltpu.SMEM)] + [whole_spec()] * 2,
        out_specs=[whole_spec()] * 4,
        scratch_shapes=[
            pltpu.VMEM((hidden, tokens), jnp.float32),
            pltpu.VMEM((hidden, tokens), jnp.float32),
            pltpu.VMEM((hidden, hidden), jnp.bfloat16),
        ],
        compiler_params=params(12),
        cost_estimate=BRIEF,
        name="keys_part",
    )(place, k, w)


def gradient_rows(outer, place, k, e, gated, gate, up, down, err_s, er_s):
    own = gate.shape[0] // outer
    err_s[...] = times_transposed(identity(e.shape[1]), e[...]).astype(jnp.bfloat16)
    for z in range(outer):
        er_s[pl.ds(z * own, own)] = err_s[parity_rows(place, z, own)]
    back = matmul(down[...], err_s[...])
    return (
        matmul((back * gate[...]).astype(jnp.bfloat16), k[...]),
        matmul((back * up[...]).astype(jnp.bfloat16), k[...]),
        times_transposed(er_s[...], gated[...]),
    )


def own_kernel(outer, place, k, e, gated, gate, up, down, acc, *scratch):
    parts = gradient_rows(outer, place, k, e, gated, gate, up, down, *scratch)
    for i, part in enumerate(parts):
        acc[i] = part


def both_kernel(outer, place, k, e, gated, gate, up, down, acc, mine, *rest):
    sent, (total, *scratch) = rest[: outer - 1], rest[outer - 1 :]
    parts = gradient_rows(outer, place, k, e, gated, gate, up, down, *scratch)
    own = mine.shape[1]
    for i, part in enumerate(parts):
        total[i] = part + acc[i]
        mine[i] = total[i, pl.ds(pl.multiple_of(place[1] * own, own), own), :]
        for step in range(1, outer):
            other = place[1] ^ step
            block = total[i, pl.ds(pl.multiple_of(other * own, own), own), :]
            sent[step - 1][i] = block.astype(jnp.bfloat16)


def gradient_scratch(tokens, hidden):
    return [
        pltpu.VMEM((hidden, tokens), jnp.bfloat16),
        pltpu.VMEM((hidden // 2, tokens), jnp.bfloat16),
    ]


def own_gradients(place, k, e, factors, outer):
    tokens, hidden = k.shape
    return pl.pallas_call(
        functools.partial(own_kernel, outer),
        out_shape=jax.ShapeDtypeStruct((3, hidden // 2, hidden), jnp.float32),
        in_specs=[pl.BlockSpec(memory_space=pltpu.SMEM)] + [whole_spec()] * 6,
        out_specs=whole_spec(),
        scratch_shapes=gradient_scratch(tokens, hidden),
        compiler_params=params(12),
        cost_estimate=BRIEF,
        name="own_gradients",
    )(place, k, e, *factors)


def both_gradients(place, k, e, factors, acc, outer):
    tokens, hidden = k.shape
    own = hidden // (2 * outer)
    return pl.pallas_call(
        functools.partial(both_kernel, outer),
        out_shape=[jax.ShapeDtypeStruct((3, own, hidden), jnp.float32)]
        + [jax.ShapeDtypeStruct((3, own, hidden), jnp.bfloat16)] * (outer - 1),
        in_specs=[pl.BlockSpec(memory_space=pltpu.SMEM)] + [whole_spec()] * 7,
        out_specs=[whole_spec()] * outer,
        scratch_shapes=[pltpu.VMEM(acc.shape, jnp.float32)] + gradient_scratch(tokens, hidden),
        compiler_params=params(12),
        cost_estimate=BRIEF,
        name="both_gradients",
    )(place, k, e, *factors, acc)


def attend_kernel(blocks, place, q, k, v, pair_k, up_k, early_v, out):
    early_k = jnp.where(place[0] == 0, up_k[...], pair_k[...])
    early_v = early_v[: v.shape[0]]
    early_v = jnp.where(place[2] > 0, early_v, jnp.zeros_like(early_v))
    tokens = q.shape[0]
    rows = tokens // blocks
    scale = 1.0 / math.sqrt(q.shape[1])
    for b in range(blocks):
        first, last = b * rows, (b + 1) * rows
        own = times_transposed(q[first:last], k[:last]) * scale
        old = times_transposed(q[first:last], early_k[first:]) * scale
        row = first + lax.broadcasted_iota(jnp.int32, own.shape, 0)
        column = lax.broadcasted_iota(jnp.int32, own.shape, 1)
        own = jnp.where(column <= row, own, NEG_LARGE)
        row = first + lax.broadcasted_iota(jnp.int32, old.shape, 0)
        column = first + lax.broadcasted_iota(jnp.int32, old.shape, 1)
        old = jnp.where((column > row) & (place[2] > 0), old, NEG_LARGE)
        highest = jnp.maximum(
            jnp.max(own, axis=1, keepdims=True), jnp.max(old, axis=1, keepdims=True)
        )
        own, old = jnp.exp(own - highest), jnp.exp(old - highest)
        total = jnp.sum(own, axis=1, keepdims=True) + jnp.sum(old, axis=1, keepdims=True)
        own = (own / total).astype(jnp.bfloat16)
        old = (old / total).astype(jnp.bfloat16)
        out[first:last] = matmul(own, v[:last]) + matmul(old, early_v[first:])


def window_attention(place, q, k, v, *early):
    tokens, hidden = q.shape
    return pl.pallas_call(
        functools.partial(attend_kernel, 2),
        out_shape=jax.ShapeDtypeStruct((tokens, hidden), jnp.float32),
        in_specs=[pl.BlockSpec(memory_space=pltpu.SMEM)] + [whole_spec()] * 6,
        out_specs=whole_spec(),
        compiler_params=params(12),
        cost_estimate=BRIEF,
        name="window_attention",
    )(place, q, k, v, *early)


def crossing_kernel(place, even, odd, rows, out):
    tokens = even.shape[0]

    @pl.when(place[0] == 0)
    def _():
        out[:tokens] = even[...]

    @pl.when(place[0] == 1)
    def _():
        out[:tokens] = odd[...]

    out[tokens:] = rows[...]


def crossing(place, even, odd, rows):
    shape = (even.shape[0] + rows.shape[0], even.shape[1])
    return pl.pallas_call(
        crossing_kernel,
        out_shape=jax.ShapeDtypeStruct(shape, even.dtype),
        in_specs=[pl.BlockSpec(memory_space=pltpu.SMEM)] + [whole_spec()] * 3,
        out_specs=whole_spec(),
        compiler_params=params(12),
        cost_estimate=BRIEF,
        name="crossing",
    )(place, even, odd, rows)


def renew_kernel(place, w, momentum, mine, *rest):
    pieces, renewed = rest[:-1], rest[-1]
    own = mine.shape[1]
    total = mine[...]
    for piece in pieces:
        total = total + piece[...].astype(jnp.float32)
    new = MOMENTUM_DECAY * momentum[0] + total
    rows = pl.ds(pl.multiple_of(place[2] * own, own), own)
    for i in range(w.shape[1]):
        base = w[0, i, rows, :].astype(jnp.float32)
        renewed[i] = renormalize(base, new[i])


def renew(place, w, momentum, mine, pieces):
    return pl.pallas_call(
        renew_kernel,
        out_shape=jax.ShapeDtypeStruct(mine.shape, jnp.bfloat16),
        in_specs=[pl.BlockSpec(memory_space=pltpu.SMEM)] + [whole_spec()] * (3 + len(pieces)),
        out_specs=whole_spec(),
        compiler_params=params(12),
        cost_estimate=BRIEF,
        name="renew",
    )(place, w, momentum, mine, *pieces)


def apply_kernel(count, place, q, attended, *rest):
    units, combined, full = rest[:count], rest[count], rest[count + 1]
    own = units[0].shape[1]
    for i in range(count):
        step, across = i % (count // 2), i // (count // 2)
        rows = pl.ds(pl.multiple_of((place[2] ^ (2 * step + across)) * own, own), own)
        full[:, rows, :] = units[i][...]
    b1 = times_transposed(q[...], full[0])
    b3 = times_transposed(q[...], full[1])
    fast_in = (b1 * jax.nn.sigmoid(b1) * b3).astype(jnp.bfloat16)
    out = times_transposed(fast_in, full[2])
    combined[...] = (attended[...] + out).astype(jnp.bfloat16)


def apply_fast(place, q, attended, units):
    tokens, hidden = q.shape
    return pl.pallas_call(
        functools.partial(apply_kernel, len(units)),
        out_shape=jax.ShapeDtypeStruct((tokens, hidden), jnp.bfloat16),
        in_specs=[pl.BlockSpec(memory_space=pltpu.SMEM)] + [whole_spec()] * (2 + len(units)),
        out_specs=whole_spec(),
        scratch_shapes=[pltpu.VMEM((3, hidden, hidden), jnp.bfloat16)],
        compiler_params=params(12),
        cost_estimate=BRIEF,
        name="apply_fast",
    )(place, q, attended, *units)


def most_kernel(tags, last, rows_in, offsets, place, *rest):
    blocks, units = rest[: len(tags)], rest[len(tags) : -3]
    partial, last_rows, full = rest[-3:]
    for at, (unit, first) in enumerate(offsets):
        rows = pl.ds(pl.multiple_of(place[ORIGINS + at] * rows_in, rows_in), rows_in)
        full[rows, :] = units[unit][first : first + rows_in, :]
    width = blocks[0].shape[1]
    value = None
    for block, tag in zip(blocks, tags):
        rows = pl.ds(pl.multiple_of((place[3] ^ tag) * width, width), width)
        part = matmul(block[...], full[rows, :])
        value = part if value is None else value + part
    partial[...] = value
    rows = pl.ds(pl.multiple_of((place[3] ^ last) * width, width), width)
    last_rows[...] = full[rows, :]


def project_most(place, blocks, tags, last, near, far, rows_in):
    tokens, width = blocks[0].shape
    units = near + far
    offsets = [(i, 0) for i in range(len(near))]
    for i, unit in enumerate(far, len(near)):
        offsets.append((i, unit.shape[0] - rows_in))
    columns = near[0].shape[1]
    return pl.pallas_call(
        functools.partial(most_kernel, tags, last, rows_in, offsets),
        out_shape=[
            jax.ShapeDtypeStruct((tokens, columns), jnp.float32),
            jax.ShapeDtypeStruct((width, columns), jnp.bfloat16),
        ],
        in_specs=[pl.BlockSpec(memory_space=pltpu.SMEM)]
        + [whole_spec()] * (len(units) + len(blocks)),
        out_specs=[whole_spec()] * 2,
        scratch_shapes=[pltpu.VMEM((rows_in * len(offsets), columns), jnp.bfloat16)],
        compiler_params=params(12),
        cost_estimate=BRIEF,
        name="project_most",
    )(place, *blocks, *units)


def last_kernel(partial, block, rows, mixed):
    mixed[...] = (partial[...] + matmul(block[...], rows[...])).astype(mixed.dtype)


def project_last(partial, block, rows):
    return pl.pallas_call(
        last_kernel,
        out_shape=jax.ShapeDtypeStruct(partial.shape, jnp.bfloat16),
        in_specs=[whole_spec()] * 3,
        out_specs=whole_spec(),
        compiler_params=params(12),
        cost_estimate=BRIEF,
        name="project_last",
    )(partial, block, rows)


def ring_order(outer):
    return [0] + list(range(1, outer, 2)) + list(range(outer - 2 + outer % 2, 0, -2))


def ring_step(unit, outer):
    order = ring_order(outer)
    pairs = []
    for place, z in enumerate(order):
        to = order[(place + 1) % outer]
        pairs += [(2 * z + y, 2 * to + y) for y in range(2)]
    return lax.ppermute(unit, "seq", pairs)


def after(array, *others):
    return lax.optimization_barrier((array,) + others)[0]


def place_table(outer, heads):
    order = ring_order(outer)
    table = []
    for s in range(2 * outer):
        place = order.index(s // 2)
        sources = [order[(place - step) % outer] for step in range(outer)]
        near = [2 * z + s % 2 for z in sources]
        far = [2 * z + 1 - s % 2 for z in sources]
        table += [[s % 2, s // 2, s, head] + near + far for head in range(heads)]
    return np.array(table, np.int32)


def renormalize(base, moment):
    updated = base - moment
    base_rms = jnp.sqrt(jnp.mean(base * base, axis=-1, keepdims=True) + NORM_EPS)
    new_rms = jnp.sqrt(jnp.mean(updated * updated, axis=-1, keepdims=True) + NORM_EPS)
    return (updated * (base_rms / new_rms)).astype(jnp.bfloat16)


def attention(queries, keys, values, early_keys, early_values, position):
    tok_rows = queries.shape[0]
    all_keys = jnp.concatenate([early_keys, keys], axis=0)
    all_values = jnp.concatenate([early_values, values], axis=0)
    key_pos = (position - 1) * tok_rows + jnp.arange(all_keys.shape[0])
    query_pos = position * tok_rows + jnp.arange(tok_rows)
    spacing = query_pos[:, None] - key_pos[None, :]
    allowed = (spacing >= 0) & (spacing < WINDOW) & (key_pos[None, :] >= 0)
    scores = times_transposed(queries, all_keys) * (1.0 / math.sqrt(HD))
    scores = jnp.where(allowed, scores, NEG_LARGE)
    highest = jnp.max(scores, axis=1, keepdims=True)
    expo = jnp.exp(scores - highest)
    probs = (expo / jnp.sum(expo, axis=1, keepdims=True)).astype(jnp.bfloat16)
    return jnp.dot(probs, all_values, preferred_element_type=jnp.float32)


def shards(queries, keys, values, rates, fast, momentum, out_proj):
    tok_rows = queries.shape[0]
    ranks = lax.axis_size("seq")
    heads = lax.axis_size("head")
    own_rows = momentum.shape[2]
    if own_rows % 16 or ranks != 8 or heads != 4 or tok_rows != WINDOW:
        return plain(queries, keys, values, rates, fast, momentum, out_proj)
    outer = ranks // 2
    grad_scale = 1.0 / math.sqrt(tok_rows * ranks)
    index = lax.axis_index("seq") * heads + lax.axis_index("head")
    place = lax.dynamic_index_in_dim(jnp.asarray(place_table(outer, heads)), index, 0, False)

    pair_keys = swap(keys, "seq", 1)
    errors = (-grad_scale * rates * values.astype(jnp.float32)).astype(jnp.bfloat16)
    pair_errors = swap(errors, "seq", 1)

    wide = [out_proj, ring_step(out_proj, outer)]
    own_factors = keys_part(place, keys, fast, outer)
    wide.append(ring_step(after(wide[1], own_factors[0]), outer))

    up_values = after(values, wide[1])
    up_values = lax.ppermute(up_values, "seq", [(s, s + 2) for s in range(1, ranks - 2, 2)])
    up_keys = after(pair_keys, wide[2])
    up_keys = lax.ppermute(up_keys, "seq", [(s, s + 2) for s in range(0, ranks - 2, 2)])

    acc = own_gradients(place, keys, errors, own_factors, outer)
    pair_factors = keys_part(place, pair_keys, fast, outer)
    across = crossing(place, values, up_values, wide[0])
    pair_errors = after(pair_errors, up_keys, across)
    summed = both_gradients(place, pair_keys, pair_errors, pair_factors, acc, outer)
    pieces = [swap(summed[step], "seq", step * 2) for step in range(1, outer)]
    crossed = swap(after(across, summed[1]), "seq", 1)
    pieces[2] = after(pieces[2], crossed)
    renewed = renew(place, fast, momentum, summed[0], pieces)

    near = [renewed]
    for step in range(1, outer):
        near.append(swap(renewed, "seq", step * 2))
    far = [swap(renewed, "seq", 1)]
    wide_far = [crossed, swap(after(wide[1], near[1]), "seq", 1)]
    near[1] = after(near[1], far[0])
    far += [swap(unit, "seq", 1) for unit in near[1:]]
    attended = window_attention(
        place, queries, keys, values, pair_keys, up_keys, after(crossed, near[1])
    )
    wide.append(ring_step(after(wide[2], far[1], near[2], near[3]), outer))

    total = after(summed[0], near[1])
    for piece in pieces:
        total = total + piece.astype(jnp.float32)
    moment = MOMENTUM_DECAY * momentum + total[None]

    forwarded = far[-1]
    far[-1] = after(far[-1], attended, wide_far[1], moment)
    wide_far.append(swap(after(wide[2], forwarded), "seq", 1))
    wide_far.append(swap(after(wide[3], wide_far[2]), "seq", 1))

    combined = apply_fast(place, queries, attended, near + far)

    crossed_x = swap(combined, "head", 2)
    other_core = swap(combined, "head", 1)
    crossed_x = after(crossed_x, *wide_far[2:])
    last = swap(crossed_x, "head", 3 ^ 2)
    held = [out_proj] + wide[1:]
    partial, rows = project_most(
        place, [combined, other_core, crossed_x], [0, 1, 2], 3, held, wide_far, out_proj.shape[0]
    )
    mixed = project_last(partial, last, rows)
    return (mixed, moment)


def plain(queries, keys, values, rates, fast, momentum, out_proj):
    tok_rows = queries.shape[0]
    ranks = lax.axis_size("seq")
    position = lax.axis_index("seq")
    own_rows = momentum.shape[2]
    grad_scale = 1.0 / math.sqrt(tok_rows * ranks)
    weights = fast[0]
    h_gate = times_transposed(keys, weights[0])
    h_up = times_transposed(keys, weights[1])
    sigma = jax.nn.sigmoid(h_gate)
    gated = (h_gate * sigma * h_up).astype(jnp.bfloat16)
    errors = (-grad_scale * rates * values.astype(jnp.float32)).astype(jnp.bfloat16)
    grad_down = contract_rows(errors, gated)
    back = matmul(errors, weights[2])
    d_gate = (back * h_up * sigma * (1.0 + h_gate * (1.0 - sigma))).astype(jnp.bfloat16)
    d_up = (back * h_gate * sigma).astype(jnp.bfloat16)
    grads = jnp.stack([contract_rows(d_gate, keys), contract_rows(d_up, keys), grad_down])
    summed_rows = lax.psum_scatter(grads, "seq", scatter_dimension=1, tiled=True)
    moment_own = MOMENTUM_DECAY * momentum[0] + summed_rows
    base_rows = lax.dynamic_slice_in_dim(weights, position * own_rows, own_rows, 1).astype(jnp.float32)
    renewed = lax.all_gather(renormalize(base_rows, moment_own), "seq", axis=1, tiled=True)
    q_gate = times_transposed(queries, renewed[0])
    q_up = times_transposed(queries, renewed[1])
    fast_in = (q_gate * jax.nn.sigmoid(q_gate) * q_up).astype(jnp.bfloat16)
    fast_out = times_transposed(fast_in, renewed[2])
    behind = [(i, i + 1) for i in range(ranks - 1)]
    early_keys = lax.ppermute(keys, "seq", behind)
    early_values = lax.ppermute(values, "seq", behind)
    attended = attention(queries, keys, values, early_keys, early_values, position)
    combined = (attended + fast_out).astype(jnp.bfloat16)
    all_heads = lax.all_gather(combined, "head", axis=1, tiled=True)
    projection = lax.all_gather(out_proj, "seq", axis=0, tiled=True)
    return (matmul(all_heads, projection).astype(jnp.bfloat16), moment_own[None])


def solution(mesh):
    return jax.shard_map(
        shards,
        mesh=mesh,
        in_specs=(
            P("seq", "head"),
            P("seq", "head"),
            P("seq", "head"),
            P("seq", "head"),
            P("head", None, None, None),
            P("head", None, "seq", None),
            P("seq", "head"),
        ),
        out_specs=(P("seq", "head"), P("head", None, "seq", None)),
        check_vma=False,
    )
```

```python
import functools
import math

import jax
import jax.numpy as jnp
import numpy as np
from jax import lax
from jax.experimental import pallas as pl
from jax.experimental.pallas import tpu as pltpu
from jax.sharding import PartitionSpec as P

HD = 512
WINDOW = 512

MOMENTUM_DECAY = 0.9
NORM_EPS = 1e-06
NEG_LARGE = -1e30
MIB = 1024 * 1024
ORIGINS = 4
BRIEF = pl.CostEstimate(flops=1, bytes_accessed=1, transcendentals=0)


def times_transposed(left, right):
    return lax.dot_general(
        left, right, (((1,), (1,)), ((), ())), preferred_element_type=jnp.float32
    )


def contract_rows(left, right):
    return lax.dot_general(
        left, right, (((0,), (0,)), ((), ())), preferred_element_type=jnp.float32
    )


def matmul(left, right):
    return jnp.dot(left, right, preferred_element_type=jnp.float32)


def swap(array, axis, mask):
    devices = lax.axis_size(axis)
    return lax.ppermute(array, axis, [(i, i ^ mask) for i in range(devices)])


def params(mib):
    return pltpu.CompilerParams(vmem_limit_bytes=mib * MIB)


def whole_spec():
    return pl.BlockSpec(memory_space=pltpu.VMEM)


def identity(size):
    rows = lax.broadcasted_iota(jnp.int32, (size, size), 0)
    columns = lax.broadcasted_iota(jnp.int32, (size, size), 1)
    return jnp.where(rows == columns, 1.0, 0.0).astype(jnp.bfloat16)


def parity_rows(place, z, own):
    return pl.ds(pl.multiple_of((2 * z + place[0]) * own, own), own)


def keys_kernel(outer, place, k, w, gated, gate, up, down, hg_s, hu_s, down_s):
    own = gate.shape[0] // outer
    hg = times_transposed(w[0, 0], k[...])
    hu = times_transposed(w[0, 1], k[...])
    hg_s[...] = hg
    hu_s[...] = hu
    gated[...] = (hg * jax.nn.sigmoid(hg) * hu).astype(jnp.bfloat16)
    down_s[...] = times_transposed(identity(w.shape[3]), w[0, 2]).astype(jnp.bfloat16)
    for z in range(outer):
        rows, to = parity_rows(place, z, own), pl.ds(z * own, own)
        g, u = hg_s[rows], hu_s[rows]
        s = jax.nn.sigmoid(g)
        gate[to] = u * s * (1.0 + g * (1.0 - s))
        up[to] = g * s
        down[to] = down_s[rows]


def keys_part(place, k, w, outer):
    tokens, hidden = k.shape
    half = jax.ShapeDtypeStruct((hidden // 2, tokens), jnp.float32)
    return pl.pallas_call(
        functools.partial(keys_kernel, outer),
        out_shape=[
            jax.ShapeDtypeStruct((hidden, tokens), jnp.bfloat16),
            half,
            half,
            jax.ShapeDtypeStruct((hidden // 2, hidden), jnp.bfloat16),
        ],
        in_specs=[pl.BlockSpec(memory_space=pltpu.SMEM)] + [whole_spec()] * 2,
        out_specs=[whole_spec()] * 4,
        scratch_shapes=[
            pltpu.VMEM((hidden, tokens), jnp.float32),
            pltpu.VMEM((hidden, tokens), jnp.float32),
            pltpu.VMEM((hidden, hidden), jnp.bfloat16),
        ],
        compiler_params=params(12),
        cost_estimate=BRIEF,
        name="keys_part",
    )(place, k, w)


def gradient_rows(outer, place, k, e, gated, gate, up, down, err_s, er_s):
    own = gate.shape[0] // outer
    err_s[...] = times_transposed(identity(e.shape[1]), e[...]).astype(jnp.bfloat16)
    for z in range(outer):
        er_s[pl.ds(z * own, own)] = err_s[parity_rows(place, z, own)]
    back = matmul(down[...], err_s[...])
    return (
        matmul((back * gate[...]).astype(jnp.bfloat16), k[...]),
        matmul((back * up[...]).astype(jnp.bfloat16), k[...]),
        times_transposed(er_s[...], gated[...]),
    )


def own_kernel(outer, place, k, e, gated, gate, up, down, acc, *scratch):
    parts = gradient_rows(outer, place, k, e, gated, gate, up, down, *scratch)
    for i, part in enumerate(parts):
        acc[i] = part


def both_kernel(outer, place, k, e, gated, gate, up, down, acc, mine, *rest):
    sent, (total, *scratch) = rest[: outer - 1], rest[outer - 1 :]
    parts = gradient_rows(outer, place, k, e, gated, gate, up, down, *scratch)
    own = mine.shape[1]
    for i, part in enumerate(parts):
        total[i] = part + acc[i]
        mine[i] = total[i, pl.ds(pl.multiple_of(place[1] * own, own), own), :]
        for step in range(1, outer):
            other = place[1] ^ step
            block = total[i, pl.ds(pl.multiple_of(other * own, own), own), :]
            sent[step - 1][i] = block.astype(jnp.bfloat16)


def gradient_scratch(tokens, hidden):
    return [
        pltpu.VMEM((hidden, tokens), jnp.bfloat16),
        pltpu.VMEM((hidden // 2, tokens), jnp.bfloat16),
    ]


def own_gradients(place, k, e, factors, outer):
    tokens, hidden = k.shape
    return pl.pallas_call(
        functools.partial(own_kernel, outer),
        out_shape=jax.ShapeDtypeStruct((3, hidden // 2, hidden), jnp.float32),
        in_specs=[pl.BlockSpec(memory_space=pltpu.SMEM)] + [whole_spec()] * 6,
        out_specs=whole_spec(),
        scratch_shapes=gradient_scratch(tokens, hidden),
        compiler_params=params(12),
        cost_estimate=BRIEF,
        name="own_gradients",
    )(place, k, e, *factors)


def both_gradients(place, k, e, factors, acc, outer):
    tokens, hidden = k.shape
    own = hidden // (2 * outer)
    return pl.pallas_call(
        functools.partial(both_kernel, outer),
        out_shape=[jax.ShapeDtypeStruct((3, own, hidden), jnp.float32)]
        + [jax.ShapeDtypeStruct((3, own, hidden), jnp.bfloat16)] * (outer - 1),
        in_specs=[pl.BlockSpec(memory_space=pltpu.SMEM)] + [whole_spec()] * 7,
        out_specs=[whole_spec()] * outer,
        scratch_shapes=[pltpu.VMEM(acc.shape, jnp.float32)] + gradient_scratch(tokens, hidden),
        compiler_params=params(12),
        cost_estimate=BRIEF,
        name="both_gradients",
    )(place, k, e, *factors, acc)


def attend_kernel(blocks, place, q, k, v, pair_k, up_k, early_v, out):
    early_k = jnp.where(place[0] == 0, up_k[...], pair_k[...])
    early_v = early_v[: v.shape[0]]
    early_v = jnp.where(place[2] > 0, early_v, jnp.zeros_like(early_v))
    tokens = q.shape[0]
    rows = tokens // blocks
    scale = 1.0 / math.sqrt(q.shape[1])
    for b in range(blocks):
        first, last = b * rows, (b + 1) * rows
        own = times_transposed(q[first:last], k[:last]) * scale
        old = times_transposed(q[first:last], early_k[first:]) * scale
        row = first + lax.broadcasted_iota(jnp.int32, own.shape, 0)
        column = lax.broadcasted_iota(jnp.int32, own.shape, 1)
        own = jnp.where(column <= row, own, NEG_LARGE)
        row = first + lax.broadcasted_iota(jnp.int32, old.shape, 0)
        column = first + lax.broadcasted_iota(jnp.int32, old.shape, 1)
        old = jnp.where((column > row) & (place[2] > 0), old, NEG_LARGE)
        highest = jnp.maximum(
            jnp.max(own, axis=1, keepdims=True), jnp.max(old, axis=1, keepdims=True)
        )
        own, old = jnp.exp(own - highest), jnp.exp(old - highest)
        total = jnp.sum(own, axis=1, keepdims=True) + jnp.sum(old, axis=1, keepdims=True)
        own = (own / total).astype(jnp.bfloat16)
        old = (old / total).astype(jnp.bfloat16)
        out[first:last] = matmul(own, v[:last]) + matmul(old, early_v[first:])


def window_attention(place, q, k, v, *early):
    tokens, hidden = q.shape
    return pl.pallas_call(
        functools.partial(attend_kernel, 2),
        out_shape=jax.ShapeDtypeStruct((tokens, hidden), jnp.float32),
        in_specs=[pl.BlockSpec(memory_space=pltpu.SMEM)] + [whole_spec()] * 6,
        out_specs=whole_spec(),
        compiler_params=params(12),
        cost_estimate=BRIEF,
        name="window_attention",
    )(place, q, k, v, *early)


def crossing_kernel(place, even, odd, rows, out):
    tokens = even.shape[0]

    @pl.when(place[0] == 0)
    def _():
        out[:tokens] = even[...]

    @pl.when(place[0] == 1)
    def _():
        out[:tokens] = odd[...]

    out[tokens:] = rows[...]


def crossing(place, even, odd, rows):
    shape = (even.shape[0] + rows.shape[0], even.shape[1])
    return pl.pallas_call(
        crossing_kernel,
        out_shape=jax.ShapeDtypeStruct(shape, even.dtype),
        in_specs=[pl.BlockSpec(memory_space=pltpu.SMEM)] + [whole_spec()] * 3,
        out_specs=whole_spec(),
        compiler_params=params(12),
        cost_estimate=BRIEF,
        name="crossing",
    )(place, even, odd, rows)


def renew_kernel(place, w, momentum, mine, *rest):
    pieces, renewed = rest[:-1], rest[-1]
    own = mine.shape[1]
    total = mine[...]
    for piece in pieces:
        total = total + piece[...].astype(jnp.float32)
    new = MOMENTUM_DECAY * momentum[0] + total
    rows = pl.ds(pl.multiple_of(place[2] * own, own), own)
    for i in range(w.shape[1]):
        base = w[0, i, rows, :].astype(jnp.float32)
        renewed[i] = renormalize(base, new[i])


def renew(place, w, momentum, mine, pieces):
    return pl.pallas_call(
        renew_kernel,
        out_shape=jax.ShapeDtypeStruct(mine.shape, jnp.bfloat16),
        in_specs=[pl.BlockSpec(memory_space=pltpu.SMEM)] + [whole_spec()] * (3 + len(pieces)),
        out_specs=whole_spec(),
        compiler_params=params(12),
        cost_estimate=BRIEF,
        name="renew",
    )(place, w, momentum, mine, *pieces)


def apply_kernel(count, place, q, attended, *rest):
    units, combined, full = rest[:count], rest[count], rest[count + 1]
    own = units[0].shape[1]
    for i in range(count):
        step, across = i % (count // 2), i // (count // 2)
        rows = pl.ds(pl.multiple_of((place[2] ^ (2 * step + across)) * own, own), own)
        full[:, rows, :] = units[i][...]
    b1 = times_transposed(q[...], full[0])
    b3 = times_transposed(q[...], full[1])
    fast_in = (b1 * jax.nn.sigmoid(b1) * b3).astype(jnp.bfloat16)
    out = times_transposed(fast_in, full[2])
    combined[...] = (attended[...] + out).astype(jnp.bfloat16)


def apply_fast(place, q, attended, units):
    tokens, hidden = q.shape
    return pl.pallas_call(
        functools.partial(apply_kernel, len(units)),
        out_shape=jax.ShapeDtypeStruct((tokens, hidden), jnp.bfloat16),
        in_specs=[pl.BlockSpec(memory_space=pltpu.SMEM)] + [whole_spec()] * (2 + len(units)),
        out_specs=whole_spec(),
        scratch_shapes=[pltpu.VMEM((3, hidden, hidden), jnp.bfloat16)],
        compiler_params=params(12),
        cost_estimate=BRIEF,
        name="apply_fast",
    )(place, q, attended, *units)


def most_kernel(tags, last, rows_in, offsets, place, *rest):
    blocks, units = rest[: len(tags)], rest[len(tags) : -3]
    partial, last_rows, full = rest[-3:]
    for at, (unit, first) in enumerate(offsets):
        rows = pl.ds(pl.multiple_of(place[ORIGINS + at] * rows_in, rows_in), rows_in)
        full[rows, :] = units[unit][first : first + rows_in, :]
    width = blocks[0].shape[1]
    value = None
    for block, tag in zip(blocks, tags):
        rows = pl.ds(pl.multiple_of((place[3] ^ tag) * width, width), width)
        part = matmul(block[...], full[rows, :])
        value = part if value is None else value + part
    partial[...] = value
    rows = pl.ds(pl.multiple_of((place[3] ^ last) * width, width), width)
    last_rows[...] = full[rows, :]


def project_most(place, blocks, tags, last, near, far, rows_in):
    tokens, width = blocks[0].shape
    units = near + far
    offsets = [(i, 0) for i in range(len(near))]
    for i, unit in enumerate(far, len(near)):
        offsets.append((i, unit.shape[0] - rows_in))
    columns = near[0].shape[1]
    return pl.pallas_call(
        functools.partial(most_kernel, tags, last, rows_in, offsets),
        out_shape=[
            jax.ShapeDtypeStruct((tokens, columns), jnp.float32),
            jax.ShapeDtypeStruct((width, columns), jnp.bfloat16),
        ],
        in_specs=[pl.BlockSpec(memory_space=pltpu.SMEM)]
        + [whole_spec()] * (len(units) + len(blocks)),
        out_specs=[whole_spec()] * 2,
        scratch_shapes=[pltpu.VMEM((rows_in * len(offsets), columns), jnp.bfloat16)],
        compiler_params=params(12),
        cost_estimate=BRIEF,
        name="project_most",
    )(place, *blocks, *units)


def last_kernel(partial, block, rows, mixed):
    mixed[...] = (partial[...] + matmul(block[...], rows[...])).astype(mixed.dtype)


def project_last(partial, block, rows):
    return pl.pallas_call(
        last_kernel,
        out_shape=jax.ShapeDtypeStruct(partial.shape, jnp.bfloat16),
        in_specs=[whole_spec()] * 3,
        out_specs=whole_spec(),
        compiler_params=params(12),
        cost_estimate=BRIEF,
        name="project_last",
    )(partial, block, rows)


def ring_order(outer):
    return [0] + list(range(1, outer, 2)) + list(range(outer - 2 + outer % 2, 0, -2))


def ring_step(unit, outer):
    order = ring_order(outer)
    pairs = []
    for place, z in enumerate(order):
        to = order[(place + 1) % outer]
        pairs += [(2 * z + y, 2 * to + y) for y in range(2)]
    return lax.ppermute(unit, "seq", pairs)


def after(array, *others):
    return lax.optimization_barrier((array,) + others)[0]


def place_table(outer, heads):
    order = ring_order(outer)
    table = []
    for s in range(2 * outer):
        place = order.index(s // 2)
        sources = [order[(place - step) % outer] for step in range(outer)]
        near = [2 * z + s % 2 for z in sources]
        far = [2 * z + 1 - s % 2 for z in sources]
        table += [[s % 2, s // 2, s, head] + near + far for head in range(heads)]
    return np.array(table, np.int32)


def renormalize(base, moment):
    updated = base - moment
    base_rms = jnp.sqrt(jnp.mean(base * base, axis=-1, keepdims=True) + NORM_EPS)
    new_rms = jnp.sqrt(jnp.mean(updated * updated, axis=-1, keepdims=True) + NORM_EPS)
    return (updated * (base_rms / new_rms)).astype(jnp.bfloat16)


def attention(queries, keys, values, early_keys, early_values, position):
    tok_rows = queries.shape[0]
    all_keys = jnp.concatenate([early_keys, keys], axis=0)
    all_values = jnp.concatenate([early_values, values], axis=0)
    key_pos = (position - 1) * tok_rows + jnp.arange(all_keys.shape[0])
    query_pos = position * tok_rows + jnp.arange(tok_rows)
    spacing = query_pos[:, None] - key_pos[None, :]
    allowed = (spacing >= 0) & (spacing < WINDOW) & (key_pos[None, :] >= 0)
    scores = times_transposed(queries, all_keys) * (1.0 / math.sqrt(HD))
    scores = jnp.where(allowed, scores, NEG_LARGE)
    highest = jnp.max(scores, axis=1, keepdims=True)
    expo = jnp.exp(scores - highest)
    probs = (expo / jnp.sum(expo, axis=1, keepdims=True)).astype(jnp.bfloat16)
    return jnp.dot(probs, all_values, preferred_element_type=jnp.float32)


def shards(queries, keys, values, rates, fast, momentum, out_proj):
    tok_rows = queries.shape[0]
    ranks = lax.axis_size("seq")
    heads = lax.axis_size("head")
    own_rows = momentum.shape[2]
    if own_rows % 16 or ranks != 8 or heads != 4 or tok_rows != WINDOW:
        return plain(queries, keys, values, rates, fast, momentum, out_proj)
    outer = ranks // 2
    grad_scale = 1.0 / math.sqrt(tok_rows * ranks)
    index = lax.axis_index("seq") * heads + lax.axis_index("head")
    place = lax.dynamic_index_in_dim(jnp.asarray(place_table(outer, heads)), index, 0, False)

    pair_keys = swap(keys, "seq", 1)
    errors = (-grad_scale * rates * values.astype(jnp.float32)).astype(jnp.bfloat16)
    pair_errors = swap(errors, "seq", 1)

    wide = [out_proj, ring_step(out_proj, outer)]
    own_factors = keys_part(place, keys, fast, outer)
    wide.append(ring_step(after(wide[1], own_factors[0]), outer))

    up_values = after(values, wide[1])
    up_values = lax.ppermute(up_values, "seq", [(s, s + 2) for s in range(1, ranks - 2, 2)])
    up_keys = after(pair_keys, wide[2])
    up_keys = lax.ppermute(up_keys, "seq", [(s, s + 2) for s in range(0, ranks - 2, 2)])

    acc = own_gradients(place, keys, errors, own_factors, outer)
    pair_factors = keys_part(place, pair_keys, fast, outer)
    across = crossing(place, values, up_values, wide[0])
    pair_errors = after(pair_errors, up_keys, across)
    summed = both_gradients(place, pair_keys, pair_errors, pair_factors, acc, outer)
    pieces = [swap(summed[step], "seq", step * 2) for step in range(1, outer)]
    crossed = swap(after(across, summed[1]), "seq", 1)
    pieces[2] = after(pieces[2], crossed)
    renewed = renew(place, fast, momentum, summed[0], pieces)

    near = [renewed]
    for step in range(1, outer):
        near.append(swap(renewed, "seq", step * 2))
    far = [swap(renewed, "seq", 1)]
    wide_far = [crossed, swap(after(wide[1], near[1]), "seq", 1)]
    near[1] = after(near[1], far[0])
    attended = window_attention(
        place, queries, keys, values, pair_keys, up_keys, after(crossed, near[1])
    )

    total = after(summed[0], near[1])
    for piece in pieces:
        total = total + piece.astype(jnp.float32)
    moment = MOMENTUM_DECAY * momentum + total[None]

    near[3] = after(near[3], attended, moment)
    far += [swap(unit, "seq", 1) for unit in near[1:]]
    wide.append(ring_step(after(wide[2], far[1], near[2], near[3]), outer))
    forwarded = far[-1]
    far[-1] = after(far[-1], wide_far[1])
    wide_far.append(swap(after(wide[2], forwarded), "seq", 1))
    wide_far.append(swap(after(wide[3], wide_far[2]), "seq", 1))
    combined = apply_fast(place, queries, attended, near + far)

    crossed_x = swap(combined, "head", 2)
    other_core = swap(combined, "head", 1)
    crossed_x = after(crossed_x, *wide_far[2:])
    last = swap(crossed_x, "head", 3 ^ 2)
    held = [out_proj] + wide[1:]
    partial, rows = project_most(
        place, [combined, other_core, crossed_x], [0, 1, 2], 3, held, wide_far, out_proj.shape[0]
    )
    mixed = project_last(partial, last, rows)
    return (mixed, moment)


def plain(queries, keys, values, rates, fast, momentum, out_proj):
    tok_rows = queries.shape[0]
    ranks = lax.axis_size("seq")
    position = lax.axis_index("seq")
    own_rows = momentum.shape[2]
    grad_scale = 1.0 / math.sqrt(tok_rows * ranks)
    weights = fast[0]
    h_gate = times_transposed(keys, weights[0])
    h_up = times_transposed(keys, weights[1])
    sigma = jax.nn.sigmoid(h_gate)
    gated = (h_gate * sigma * h_up).astype(jnp.bfloat16)
    errors = (-grad_scale * rates * values.astype(jnp.float32)).astype(jnp.bfloat16)
    grad_down = contract_rows(errors, gated)
    back = matmul(errors, weights[2])
    d_gate = (back * h_up * sigma * (1.0 + h_gate * (1.0 - sigma))).astype(jnp.bfloat16)
    d_up = (back * h_gate * sigma).astype(jnp.bfloat16)
    grads = jnp.stack([contract_rows(d_gate, keys), contract_rows(d_up, keys), grad_down])
    summed_rows = lax.psum_scatter(grads, "seq", scatter_dimension=1, tiled=True)
    moment_own = MOMENTUM_DECAY * momentum[0] + summed_rows
    base_rows = lax.dynamic_slice_in_dim(weights, position * own_rows, own_rows, 1).astype(jnp.float32)
    renewed = lax.all_gather(renormalize(base_rows, moment_own), "seq", axis=1, tiled=True)
    q_gate = times_transposed(queries, renewed[0])
    q_up = times_transposed(queries, renewed[1])
    fast_in = (q_gate * jax.nn.sigmoid(q_gate) * q_up).astype(jnp.bfloat16)
    fast_out = times_transposed(fast_in, renewed[2])
    behind = [(i, i + 1) for i in range(ranks - 1)]
    early_keys = lax.ppermute(keys, "seq", behind)
    early_values = lax.ppermute(values, "seq", behind)
    attended = attention(queries, keys, values, early_keys, early_values, position)
    combined = (attended + fast_out).astype(jnp.bfloat16)
    all_heads = lax.all_gather(combined, "head", axis=1, tiled=True)
    projection = lax.all_gather(out_proj, "seq", axis=0, tiled=True)
    return (matmul(all_heads, projection).astype(jnp.bfloat16), moment_own[None])


def solution(mesh):
    return jax.shard_map(
        shards,
        mesh=mesh,
        in_specs=(
            P("seq", "head"),
            P("seq", "head"),
            P("seq", "head"),
            P("seq", "head"),
            P("head", None, None, None),
            P("head", None, "seq", None),
            P("seq", "head"),
        ),
        out_specs=(P("seq", "head"), P("head", None, "seq", None)),
        check_vma=False,
    )
```

```python
import functools
import math

import jax
import jax.numpy as jnp
import numpy as np
from jax import lax
from jax.experimental import pallas as pl
from jax.experimental.pallas import tpu as pltpu
from jax.sharding import PartitionSpec as P

HD = 512
WINDOW = 512

MOMENTUM_DECAY = 0.9
NORM_EPS = 1e-06
NEG_LARGE = -1e30
MIB = 1024 * 1024
ORIGINS = 4
BRIEF = pl.CostEstimate(flops=1, bytes_accessed=1, transcendentals=0)


def times_transposed(left, right):
    return lax.dot_general(
        left, right, (((1,), (1,)), ((), ())), preferred_element_type=jnp.float32
    )


def contract_rows(left, right):
    return lax.dot_general(
        left, right, (((0,), (0,)), ((), ())), preferred_element_type=jnp.float32
    )


def matmul(left, right):
    return jnp.dot(left, right, preferred_element_type=jnp.float32)


def swap(array, axis, mask):
    devices = lax.axis_size(axis)
    return lax.ppermute(array, axis, [(i, i ^ mask) for i in range(devices)])


def params(mib):
    return pltpu.CompilerParams(vmem_limit_bytes=mib * MIB)


def whole_spec():
    return pl.BlockSpec(memory_space=pltpu.VMEM)


def identity(size):
    rows = lax.broadcasted_iota(jnp.int32, (size, size), 0)
    columns = lax.broadcasted_iota(jnp.int32, (size, size), 1)
    return jnp.where(rows == columns, 1.0, 0.0).astype(jnp.bfloat16)


def parity_rows(place, z, own):
    return pl.ds(pl.multiple_of((2 * z + place[0]) * own, own), own)


def keys_kernel(outer, place, k, w, gated, gate, up, down, hg_s, hu_s, down_s):
    own = gate.shape[0] // outer
    hg = times_transposed(w[0, 0], k[...])
    hu = times_transposed(w[0, 1], k[...])
    hg_s[...] = hg
    hu_s[...] = hu
    gated[...] = (hg * jax.nn.sigmoid(hg) * hu).astype(jnp.bfloat16)
    down_s[...] = times_transposed(identity(w.shape[3]), w[0, 2]).astype(jnp.bfloat16)
    for z in range(outer):
        rows, to = parity_rows(place, z, own), pl.ds(z * own, own)
        g, u = hg_s[rows], hu_s[rows]
        s = jax.nn.sigmoid(g)
        gate[to] = u * s * (1.0 + g * (1.0 - s))
        up[to] = g * s
        down[to] = down_s[rows]


def keys_part(place, k, w, outer):
    tokens, hidden = k.shape
    half = jax.ShapeDtypeStruct((hidden // 2, tokens), jnp.float32)
    return pl.pallas_call(
        functools.partial(keys_kernel, outer),
        out_shape=[
            jax.ShapeDtypeStruct((hidden, tokens), jnp.bfloat16),
            half,
            half,
            jax.ShapeDtypeStruct((hidden // 2, hidden), jnp.bfloat16),
        ],
        in_specs=[pl.BlockSpec(memory_space=pltpu.SMEM)] + [whole_spec()] * 2,
        out_specs=[whole_spec()] * 4,
        scratch_shapes=[
            pltpu.VMEM((hidden, tokens), jnp.float32),
            pltpu.VMEM((hidden, tokens), jnp.float32),
            pltpu.VMEM((hidden, hidden), jnp.bfloat16),
        ],
        compiler_params=params(12),
        cost_estimate=BRIEF,
        name="keys_part",
    )(place, k, w)


def gradient_rows(outer, place, k, e, gated, gate, up, down, err_s, er_s):
    own = gate.shape[0] // outer
    err_s[...] = times_transposed(identity(e.shape[1]), e[...]).astype(jnp.bfloat16)
    for z in range(outer):
        er_s[pl.ds(z * own, own)] = err_s[parity_rows(place, z, own)]
    back = matmul(down[...], err_s[...])
    return (
        matmul((back * gate[...]).astype(jnp.bfloat16), k[...]),
        matmul((back * up[...]).astype(jnp.bfloat16), k[...]),
        times_transposed(er_s[...], gated[...]),
    )


def own_kernel(outer, place, k, e, gated, gate, up, down, acc, *scratch):
    parts = gradient_rows(outer, place, k, e, gated, gate, up, down, *scratch)
    for i, part in enumerate(parts):
        acc[i] = part


def both_kernel(outer, place, k, e, gated, gate, up, down, acc, mine, *rest):
    sent, (total, *scratch) = rest[: outer - 1], rest[outer - 1 :]
    parts = gradient_rows(outer, place, k, e, gated, gate, up, down, *scratch)
    own = mine.shape[1]
    for i, part in enumerate(parts):
        total[i] = part + acc[i]
        mine[i] = total[i, pl.ds(pl.multiple_of(place[1] * own, own), own), :]
        for step in range(1, outer):
            other = place[1] ^ step
            block = total[i, pl.ds(pl.multiple_of(other * own, own), own), :]
            sent[step - 1][i] = block.astype(jnp.bfloat16)


def gradient_scratch(tokens, hidden):
    return [
        pltpu.VMEM((hidden, tokens), jnp.bfloat16),
        pltpu.VMEM((hidden // 2, tokens), jnp.bfloat16),
    ]


def own_gradients(place, k, e, factors, outer):
    tokens, hidden = k.shape
    return pl.pallas_call(
        functools.partial(own_kernel, outer),
        out_shape=jax.ShapeDtypeStruct((3, hidden // 2, hidden), jnp.float32),
        in_specs=[pl.BlockSpec(memory_space=pltpu.SMEM)] + [whole_spec()] * 6,
        out_specs=whole_spec(),
        scratch_shapes=gradient_scratch(tokens, hidden),
        compiler_params=params(12),
        cost_estimate=BRIEF,
        name="own_gradients",
    )(place, k, e, *factors)


def both_gradients(place, k, e, factors, acc, outer):
    tokens, hidden = k.shape
    own = hidden // (2 * outer)
    return pl.pallas_call(
        functools.partial(both_kernel, outer),
        out_shape=[jax.ShapeDtypeStruct((3, own, hidden), jnp.float32)]
        + [jax.ShapeDtypeStruct((3, own, hidden), jnp.bfloat16)] * (outer - 1),
        in_specs=[pl.BlockSpec(memory_space=pltpu.SMEM)] + [whole_spec()] * 7,
        out_specs=[whole_spec()] * outer,
        scratch_shapes=[pltpu.VMEM(acc.shape, jnp.float32)] + gradient_scratch(tokens, hidden),
        compiler_params=params(12),
        cost_estimate=BRIEF,
        name="both_gradients",
    )(place, k, e, *factors, acc)


def attend_kernel(blocks, place, q, k, v, pair_k, up_k, early_v, out):
    early_k = jnp.where(place[0] == 0, up_k[...], pair_k[...])
    early_v = early_v[: v.shape[0]]
    early_v = jnp.where(place[2] > 0, early_v, jnp.zeros_like(early_v))
    tokens = q.shape[0]
    rows = tokens // blocks
    scale = 1.0 / math.sqrt(q.shape[1])
    for b in range(blocks):
        first, last = b * rows, (b + 1) * rows
        own = times_transposed(q[first:last], k[:last]) * scale
        old = times_transposed(q[first:last], early_k[first:]) * scale
        row = first + lax.broadcasted_iota(jnp.int32, own.shape, 0)
        column = lax.broadcasted_iota(jnp.int32, own.shape, 1)
        own = jnp.where(column <= row, own, NEG_LARGE)
        row = first + lax.broadcasted_iota(jnp.int32, old.shape, 0)
        column = first + lax.broadcasted_iota(jnp.int32, old.shape, 1)
        old = jnp.where((column > row) & (place[2] > 0), old, NEG_LARGE)
        highest = jnp.maximum(
            jnp.max(own, axis=1, keepdims=True), jnp.max(old, axis=1, keepdims=True)
        )
        own, old = jnp.exp(own - highest), jnp.exp(old - highest)
        total = jnp.sum(own, axis=1, keepdims=True) + jnp.sum(old, axis=1, keepdims=True)
        own = (own / total).astype(jnp.bfloat16)
        old = (old / total).astype(jnp.bfloat16)
        out[first:last] = matmul(own, v[:last]) + matmul(old, early_v[first:])


def window_attention(place, q, k, v, *early):
    tokens, hidden = q.shape
    return pl.pallas_call(
        functools.partial(attend_kernel, 2),
        out_shape=jax.ShapeDtypeStruct((tokens, hidden), jnp.float32),
        in_specs=[pl.BlockSpec(memory_space=pltpu.SMEM)] + [whole_spec()] * 6,
        out_specs=whole_spec(),
        compiler_params=params(12),
        cost_estimate=BRIEF,
        name="window_attention",
    )(place, q, k, v, *early)


def crossing_kernel(place, even, odd, rows, out):
    tokens = even.shape[0]

    @pl.when(place[0] == 0)
    def _():
        out[:tokens] = even[...]

    @pl.when(place[0] == 1)
    def _():
        out[:tokens] = odd[...]

    out[tokens:] = rows[...]


def crossing(place, even, odd, rows):
    shape = (even.shape[0] + rows.shape[0], even.shape[1])
    return pl.pallas_call(
        crossing_kernel,
        out_shape=jax.ShapeDtypeStruct(shape, even.dtype),
        in_specs=[pl.BlockSpec(memory_space=pltpu.SMEM)] + [whole_spec()] * 3,
        out_specs=whole_spec(),
        compiler_params=params(12),
        cost_estimate=BRIEF,
        name="crossing",
    )(place, even, odd, rows)


def renew_kernel(place, w, momentum, mine, *rest):
    pieces, renewed = rest[:-1], rest[-1]
    own = mine.shape[1]
    total = mine[...]
    for piece in pieces:
        total = total + piece[...].astype(jnp.float32)
    new = MOMENTUM_DECAY * momentum[0] + total
    rows = pl.ds(pl.multiple_of(place[2] * own, own), own)
    for i in range(w.shape[1]):
        base = w[0, i, rows, :].astype(jnp.float32)
        renewed[i] = renormalize(base, new[i])


def renew(place, w, momentum, mine, pieces):
    return pl.pallas_call(
        renew_kernel,
        out_shape=jax.ShapeDtypeStruct(mine.shape, jnp.bfloat16),
        in_specs=[pl.BlockSpec(memory_space=pltpu.SMEM)] + [whole_spec()] * (3 + len(pieces)),
        out_specs=whole_spec(),
        compiler_params=params(12),
        cost_estimate=BRIEF,
        name="renew",
    )(place, w, momentum, mine, *pieces)


def apply_kernel(count, place, q, attended, *rest):
    units, combined, full = rest[:count], rest[count], rest[count + 1]
    own = units[0].shape[1]
    for i in range(count):
        step, across = i % (count // 2), i // (count // 2)
        rows = pl.ds(pl.multiple_of((place[2] ^ (2 * step + across)) * own, own), own)
        full[:, rows, :] = units[i][...]
    b1 = times_transposed(q[...], full[0])
    b3 = times_transposed(q[...], full[1])
    fast_in = (b1 * jax.nn.sigmoid(b1) * b3).astype(jnp.bfloat16)
    out = times_transposed(fast_in, full[2])
    combined[...] = (attended[...] + out).astype(jnp.bfloat16)


def apply_fast(place, q, attended, units):
    tokens, hidden = q.shape
    return pl.pallas_call(
        functools.partial(apply_kernel, len(units)),
        out_shape=jax.ShapeDtypeStruct((tokens, hidden), jnp.bfloat16),
        in_specs=[pl.BlockSpec(memory_space=pltpu.SMEM)] + [whole_spec()] * (2 + len(units)),
        out_specs=whole_spec(),
        scratch_shapes=[pltpu.VMEM((3, hidden, hidden), jnp.bfloat16)],
        compiler_params=params(12),
        cost_estimate=BRIEF,
        name="apply_fast",
    )(place, q, attended, *units)


def most_kernel(tags, last, rows_in, offsets, place, *rest):
    blocks, units = rest[: len(tags)], rest[len(tags) : -3]
    partial, last_rows, full = rest[-3:]
    for at, (unit, first) in enumerate(offsets):
        rows = pl.ds(pl.multiple_of(place[ORIGINS + at] * rows_in, rows_in), rows_in)
        full[rows, :] = units[unit][first : first + rows_in, :]
    width = blocks[0].shape[1]
    value = None
    for block, tag in zip(blocks, tags):
        rows = pl.ds(pl.multiple_of((place[3] ^ tag) * width, width), width)
        part = matmul(block[...], full[rows, :])
        value = part if value is None else value + part
    partial[...] = value
    rows = pl.ds(pl.multiple_of((place[3] ^ last) * width, width), width)
    last_rows[...] = full[rows, :]


def project_most(place, blocks, tags, last, near, far, rows_in):
    tokens, width = blocks[0].shape
    units = near + far
    offsets = [(i, 0) for i in range(len(near))]
    for i, unit in enumerate(far, len(near)):
        offsets.append((i, unit.shape[0] - rows_in))
    columns = near[0].shape[1]
    return pl.pallas_call(
        functools.partial(most_kernel, tags, last, rows_in, offsets),
        out_shape=[
            jax.ShapeDtypeStruct((tokens, columns), jnp.float32),
            jax.ShapeDtypeStruct((width, columns), jnp.bfloat16),
        ],
        in_specs=[pl.BlockSpec(memory_space=pltpu.SMEM)]
        + [whole_spec()] * (len(units) + len(blocks)),
        out_specs=[whole_spec()] * 2,
        scratch_shapes=[pltpu.VMEM((rows_in * len(offsets), columns), jnp.bfloat16)],
        compiler_params=params(12),
        cost_estimate=BRIEF,
        name="project_most",
    )(place, *blocks, *units)


def last_kernel(partial, block, rows, mixed):
    mixed[...] = (partial[...] + matmul(block[...], rows[...])).astype(mixed.dtype)


def project_last(partial, block, rows):
    return pl.pallas_call(
        last_kernel,
        out_shape=jax.ShapeDtypeStruct(partial.shape, jnp.bfloat16),
        in_specs=[whole_spec()] * 3,
        out_specs=whole_spec(),
        compiler_params=params(12),
        cost_estimate=BRIEF,
        name="project_last",
    )(partial, block, rows)


def ring_order(outer):
    return [0] + list(range(1, outer, 2)) + list(range(outer - 2 + outer % 2, 0, -2))


def ring_step(unit, outer):
    order = ring_order(outer)
    pairs = []
    for place, z in enumerate(order):
        to = order[(place + 1) % outer]
        pairs += [(2 * z + y, 2 * to + y) for y in range(2)]
    return lax.ppermute(unit, "seq", pairs)


def after(array, *others):
    return lax.optimization_barrier((array,) + others)[0]


def place_table(outer, heads):
    order = ring_order(outer)
    table = []
    for s in range(2 * outer):
        place = order.index(s // 2)
        sources = [order[(place - step) % outer] for step in range(outer)]
        near = [2 * z + s % 2 for z in sources]
        far = [2 * z + 1 - s % 2 for z in sources]
        table += [[s % 2, s // 2, s, head] + near + far for head in range(heads)]
    return np.array(table, np.int32)


def renormalize(base, moment):
    updated = base - moment
    base_rms = jnp.sqrt(jnp.mean(base * base, axis=-1, keepdims=True) + NORM_EPS)
    new_rms = jnp.sqrt(jnp.mean(updated * updated, axis=-1, keepdims=True) + NORM_EPS)
    return (updated * (base_rms / new_rms)).astype(jnp.bfloat16)


def attention(queries, keys, values, early_keys, early_values, position):
    tok_rows = queries.shape[0]
    all_keys = jnp.concatenate([early_keys, keys], axis=0)
    all_values = jnp.concatenate([early_values, values], axis=0)
    key_pos = (position - 1) * tok_rows + jnp.arange(all_keys.shape[0])
    query_pos = position * tok_rows + jnp.arange(tok_rows)
    spacing = query_pos[:, None] - key_pos[None, :]
    allowed = (spacing >= 0) & (spacing < WINDOW) & (key_pos[None, :] >= 0)
    scores = times_transposed(queries, all_keys) * (1.0 / math.sqrt(HD))
    scores = jnp.where(allowed, scores, NEG_LARGE)
    highest = jnp.max(scores, axis=1, keepdims=True)
    expo = jnp.exp(scores - highest)
    probs = (expo / jnp.sum(expo, axis=1, keepdims=True)).astype(jnp.bfloat16)
    return jnp.dot(probs, all_values, preferred_element_type=jnp.float32)


def shards(queries, keys, values, rates, fast, momentum, out_proj):
    tok_rows = queries.shape[0]
    ranks = lax.axis_size("seq")
    heads = lax.axis_size("head")
    own_rows = momentum.shape[2]
    if own_rows % 16 or ranks != 8 or heads != 4 or tok_rows != WINDOW:
        return plain(queries, keys, values, rates, fast, momentum, out_proj)
    outer = ranks // 2
    grad_scale = 1.0 / math.sqrt(tok_rows * ranks)
    index = lax.axis_index("seq") * heads + lax.axis_index("head")
    place = lax.dynamic_index_in_dim(jnp.asarray(place_table(outer, heads)), index, 0, False)

    pair_keys = swap(keys, "seq", 1)
    errors = (-grad_scale * rates * values.astype(jnp.float32)).astype(jnp.bfloat16)
    pair_errors = swap(errors, "seq", 1)

    wide = [out_proj, ring_step(out_proj, outer)]
    own_factors = keys_part(place, keys, fast, outer)
    wide.append(ring_step(after(wide[1], own_factors[0]), outer))

    up_values = after(values, wide[1])
    up_values = lax.ppermute(up_values, "seq", [(s, s + 2) for s in range(1, ranks - 2, 2)])
    up_keys = after(pair_keys, wide[2])
    up_keys = lax.ppermute(up_keys, "seq", [(s, s + 2) for s in range(0, ranks - 2, 2)])

    acc = own_gradients(place, keys, errors, own_factors, outer)
    pair_factors = keys_part(place, pair_keys, fast, outer)
    across = crossing(place, values, up_values, wide[0])
    pair_errors = after(pair_errors, up_keys, across)
    summed = both_gradients(place, pair_keys, pair_errors, pair_factors, acc, outer)
    pieces = [swap(summed[step], "seq", step * 2) for step in range(1, outer)]
    crossed = swap(after(across, summed[1]), "seq", 1)
    pieces[2] = after(pieces[2], crossed)
    renewed = renew(place, fast, momentum, summed[0], pieces)

    near = [renewed]
    for step in range(1, outer):
        near.append(swap(renewed, "seq", step * 2))
    far = [swap(renewed, "seq", 1)]
    wide_far = [crossed, swap(after(wide[1], near[1]), "seq", 1)]
    near[1] = after(near[1], far[0])
    attended = window_attention(
        place, queries, keys, values, pair_keys, up_keys, after(crossed, near[1])
    )

    total = after(summed[0], near[1])
    for piece in pieces:
        total = total + piece.astype(jnp.float32)
    moment = MOMENTUM_DECAY * momentum + total[None]

    near[3] = after(near[3], attended, moment)
    far += [swap(unit, "seq", 1) for unit in near[1:]]
    wide.append(ring_step(after(wide[2], far[1], near[2], near[3]), outer))
    forwarded = far[-1]
    far[-1] = after(far[-1], wide_far[1])
    wide_far.append(swap(after(wide[2], forwarded, far[2]), "seq", 1))
    wide_far.append(swap(after(wide[3], wide_far[2]), "seq", 1))
    combined = apply_fast(place, queries, attended, near + far)

    crossed_x = swap(combined, "head", 2)
    other_core = swap(combined, "head", 1)
    crossed_x = after(crossed_x, *wide_far[2:])
    last = swap(crossed_x, "head", 3 ^ 2)
    held = [out_proj] + wide[1:]
    partial, rows = project_most(
        place, [combined, other_core, crossed_x], [0, 1, 2], 3, held, wide_far, out_proj.shape[0]
    )
    mixed = project_last(partial, last, rows)
    return (mixed, moment)


def plain(queries, keys, values, rates, fast, momentum, out_proj):
    tok_rows = queries.shape[0]
    ranks = lax.axis_size("seq")
    position = lax.axis_index("seq")
    own_rows = momentum.shape[2]
    grad_scale = 1.0 / math.sqrt(tok_rows * ranks)
    weights = fast[0]
    h_gate = times_transposed(keys, weights[0])
    h_up = times_transposed(keys, weights[1])
    sigma = jax.nn.sigmoid(h_gate)
    gated = (h_gate * sigma * h_up).astype(jnp.bfloat16)
    errors = (-grad_scale * rates * values.astype(jnp.float32)).astype(jnp.bfloat16)
    grad_down = contract_rows(errors, gated)
    back = matmul(errors, weights[2])
    d_gate = (back * h_up * sigma * (1.0 + h_gate * (1.0 - sigma))).astype(jnp.bfloat16)
    d_up = (back * h_gate * sigma).astype(jnp.bfloat16)
    grads = jnp.stack([contract_rows(d_gate, keys), contract_rows(d_up, keys), grad_down])
    summed_rows = lax.psum_scatter(grads, "seq", scatter_dimension=1, tiled=True)
    moment_own = MOMENTUM_DECAY * momentum[0] + summed_rows
    base_rows = lax.dynamic_slice_in_dim(weights, position * own_rows, own_rows, 1).astype(jnp.float32)
    renewed = lax.all_gather(renormalize(base_rows, moment_own), "seq", axis=1, tiled=True)
    q_gate = times_transposed(queries, renewed[0])
    q_up = times_transposed(queries, renewed[1])
    fast_in = (q_gate * jax.nn.sigmoid(q_gate) * q_up).astype(jnp.bfloat16)
    fast_out = times_transposed(fast_in, renewed[2])
    behind = [(i, i + 1) for i in range(ranks - 1)]
    early_keys = lax.ppermute(keys, "seq", behind)
    early_values = lax.ppermute(values, "seq", behind)
    attended = attention(queries, keys, values, early_keys, early_values, position)
    combined = (attended + fast_out).astype(jnp.bfloat16)
    all_heads = lax.all_gather(combined, "head", axis=1, tiled=True)
    projection = lax.all_gather(out_proj, "seq", axis=0, tiled=True)
    return (matmul(all_heads, projection).astype(jnp.bfloat16), moment_own[None])


def solution(mesh):
    return jax.shard_map(
        shards,
        mesh=mesh,
        in_specs=(
            P("seq", "head"),
            P("seq", "head"),
            P("seq", "head"),
            P("seq", "head"),
            P("head", None, None, None),
            P("head", None, "seq", None),
            P("seq", "head"),
        ),
        out_specs=(P("seq", "head"), P("head", None, "seq", None)),
        check_vma=False,
    )
```

```python
import functools
import math

import jax
import jax.numpy as jnp
import numpy as np
from jax import lax
from jax.experimental import pallas as pl
from jax.experimental.pallas import tpu as pltpu
from jax.sharding import PartitionSpec as P

HD = 512
WINDOW = 512

MOMENTUM_DECAY = 0.9
NORM_EPS = 1e-06
NEG_LARGE = -1e30
MIB = 1024 * 1024
ORIGINS = 4
BRIEF = pl.CostEstimate(flops=1, bytes_accessed=1, transcendentals=0)


def times_transposed(left, right):
    return lax.dot_general(
        left, right, (((1,), (1,)), ((), ())), preferred_element_type=jnp.float32
    )


def contract_rows(left, right):
    return lax.dot_general(
        left, right, (((0,), (0,)), ((), ())), preferred_element_type=jnp.float32
    )


def matmul(left, right):
    return jnp.dot(left, right, preferred_element_type=jnp.float32)


def swap(array, axis, mask):
    devices = lax.axis_size(axis)
    return lax.ppermute(array, axis, [(i, i ^ mask) for i in range(devices)])


def params(mib):
    return pltpu.CompilerParams(vmem_limit_bytes=mib * MIB)


def whole_spec():
    return pl.BlockSpec(memory_space=pltpu.VMEM)


def identity(size):
    rows = lax.broadcasted_iota(jnp.int32, (size, size), 0)
    columns = lax.broadcasted_iota(jnp.int32, (size, size), 1)
    return jnp.where(rows == columns, 1.0, 0.0).astype(jnp.bfloat16)


def parity_rows(place, z, own):
    return pl.ds(pl.multiple_of((2 * z + place[0]) * own, own), own)


def keys_kernel(outer, place, k, w, gated, gate, up, down, hg_s, hu_s, down_s):
    own = gate.shape[0] // outer
    hg = times_transposed(w[0, 0], k[...])
    hu = times_transposed(w[0, 1], k[...])
    hg_s[...] = hg
    hu_s[...] = hu
    gated[...] = (hg * jax.nn.sigmoid(hg) * hu).astype(jnp.bfloat16)
    down_s[...] = times_transposed(identity(w.shape[3]), w[0, 2]).astype(jnp.bfloat16)
    for z in range(outer):
        rows, to = parity_rows(place, z, own), pl.ds(z * own, own)
        g, u = hg_s[rows], hu_s[rows]
        s = jax.nn.sigmoid(g)
        gate[to] = u * s * (1.0 + g * (1.0 - s))
        up[to] = g * s
        down[to] = down_s[rows]


def keys_part(place, k, w, outer):
    tokens, hidden = k.shape
    half = jax.ShapeDtypeStruct((hidden // 2, tokens), jnp.float32)
    return pl.pallas_call(
        functools.partial(keys_kernel, outer),
        out_shape=[
            jax.ShapeDtypeStruct((hidden, tokens), jnp.bfloat16),
            half,
            half,
            jax.ShapeDtypeStruct((hidden // 2, hidden), jnp.bfloat16),
        ],
        in_specs=[pl.BlockSpec(memory_space=pltpu.SMEM)] + [whole_spec()] * 2,
        out_specs=[whole_spec()] * 4,
        scratch_shapes=[
            pltpu.VMEM((hidden, tokens), jnp.float32),
            pltpu.VMEM((hidden, tokens), jnp.float32),
            pltpu.VMEM((hidden, hidden), jnp.bfloat16),
        ],
        compiler_params=params(12),
        cost_estimate=BRIEF,
        name="keys_part",
    )(place, k, w)


def gradient_rows(outer, place, k, e, gated, gate, up, down, err_s, er_s):
    own = gate.shape[0] // outer
    err_s[...] = times_transposed(identity(e.shape[1]), e[...]).astype(jnp.bfloat16)
    for z in range(outer):
        er_s[pl.ds(z * own, own)] = err_s[parity_rows(place, z, own)]
    back = matmul(down[...], err_s[...])
    return (
        matmul((back * gate[...]).astype(jnp.bfloat16), k[...]),
        matmul((back * up[...]).astype(jnp.bfloat16), k[...]),
        times_transposed(er_s[...], gated[...]),
    )


def own_kernel(outer, place, k, e, gated, gate, up, down, acc, *scratch):
    parts = gradient_rows(outer, place, k, e, gated, gate, up, down, *scratch)
    for i, part in enumerate(parts):
        acc[i] = part


def both_kernel(outer, place, k, e, gated, gate, up, down, acc, mine, *rest):
    sent, (total, *scratch) = rest[: outer - 1], rest[outer - 1 :]
    parts = gradient_rows(outer, place, k, e, gated, gate, up, down, *scratch)
    own = mine.shape[1]
    for i, part in enumerate(parts):
        total[i] = part + acc[i]
        mine[i] = total[i, pl.ds(pl.multiple_of(place[1] * own, own), own), :]
        for step in range(1, outer):
            other = place[1] ^ step
            block = total[i, pl.ds(pl.multiple_of(other * own, own), own), :]
            sent[step - 1][i] = block.astype(jnp.bfloat16)


def gradient_scratch(tokens, hidden):
    return [
        pltpu.VMEM((hidden, tokens), jnp.bfloat16),
        pltpu.VMEM((hidden // 2, tokens), jnp.bfloat16),
    ]


def own_gradients(place, k, e, factors, outer):
    tokens, hidden = k.shape
    return pl.pallas_call(
        functools.partial(own_kernel, outer),
        out_shape=jax.ShapeDtypeStruct((3, hidden // 2, hidden), jnp.float32),
        in_specs=[pl.BlockSpec(memory_space=pltpu.SMEM)] + [whole_spec()] * 6,
        out_specs=whole_spec(),
        scratch_shapes=gradient_scratch(tokens, hidden),
        compiler_params=params(12),
        cost_estimate=BRIEF,
        name="own_gradients",
    )(place, k, e, *factors)


def both_gradients(place, k, e, factors, acc, outer):
    tokens, hidden = k.shape
    own = hidden // (2 * outer)
    return pl.pallas_call(
        functools.partial(both_kernel, outer),
        out_shape=[jax.ShapeDtypeStruct((3, own, hidden), jnp.float32)]
        + [jax.ShapeDtypeStruct((3, own, hidden), jnp.bfloat16)] * (outer - 1),
        in_specs=[pl.BlockSpec(memory_space=pltpu.SMEM)] + [whole_spec()] * 7,
        out_specs=[whole_spec()] * outer,
        scratch_shapes=[pltpu.VMEM(acc.shape, jnp.float32)] + gradient_scratch(tokens, hidden),
        compiler_params=params(12),
        cost_estimate=BRIEF,
        name="both_gradients",
    )(place, k, e, *factors, acc)


def attend_kernel(blocks, place, q, k, v, pair_k, up_k, early_v, out):
    early_k = jnp.where(place[0] == 0, up_k[...], pair_k[...])
    early_v = early_v[: v.shape[0]]
    early_v = jnp.where(place[2] > 0, early_v, jnp.zeros_like(early_v))
    tokens = q.shape[0]
    rows = tokens // blocks
    scale = 1.0 / math.sqrt(q.shape[1])
    for b in range(blocks):
        first, last = b * rows, (b + 1) * rows
        own = times_transposed(q[first:last], k[:last]) * scale
        old = times_transposed(q[first:last], early_k[first:]) * scale
        row = first + lax.broadcasted_iota(jnp.int32, own.shape, 0)
        column = lax.broadcasted_iota(jnp.int32, own.shape, 1)
        own = jnp.where(column <= row, own, NEG_LARGE)
        row = first + lax.broadcasted_iota(jnp.int32, old.shape, 0)
        column = first + lax.broadcasted_iota(jnp.int32, old.shape, 1)
        old = jnp.where((column > row) & (place[2] > 0), old, NEG_LARGE)
        highest = jnp.maximum(
            jnp.max(own, axis=1, keepdims=True), jnp.max(old, axis=1, keepdims=True)
        )
        own, old = jnp.exp(own - highest), jnp.exp(old - highest)
        total = jnp.sum(own, axis=1, keepdims=True) + jnp.sum(old, axis=1, keepdims=True)
        own = (own / total).astype(jnp.bfloat16)
        old = (old / total).astype(jnp.bfloat16)
        out[first:last] = matmul(own, v[:last]) + matmul(old, early_v[first:])


def window_attention(place, q, k, v, *early):
    tokens, hidden = q.shape
    return pl.pallas_call(
        functools.partial(attend_kernel, 2),
        out_shape=jax.ShapeDtypeStruct((tokens, hidden), jnp.float32),
        in_specs=[pl.BlockSpec(memory_space=pltpu.SMEM)] + [whole_spec()] * 6,
        out_specs=whole_spec(),
        compiler_params=params(12),
        cost_estimate=BRIEF,
        name="window_attention",
    )(place, q, k, v, *early)


def crossing_kernel(place, even, odd, rows, out):
    tokens = even.shape[0]

    @pl.when(place[0] == 0)
    def _():
        out[:tokens] = even[...]

    @pl.when(place[0] == 1)
    def _():
        out[:tokens] = odd[...]

    out[tokens:] = rows[...]


def crossing(place, even, odd, rows):
    shape = (even.shape[0] + rows.shape[0], even.shape[1])
    return pl.pallas_call(
        crossing_kernel,
        out_shape=jax.ShapeDtypeStruct(shape, even.dtype),
        in_specs=[pl.BlockSpec(memory_space=pltpu.SMEM)] + [whole_spec()] * 3,
        out_specs=whole_spec(),
        compiler_params=params(12),
        cost_estimate=BRIEF,
        name="crossing",
    )(place, even, odd, rows)


def renew_kernel(place, w, momentum, mine, *rest):
    pieces, renewed = rest[:-1], rest[-1]
    own = mine.shape[1]
    total = mine[...]
    for piece in pieces:
        total = total + piece[...].astype(jnp.float32)
    new = MOMENTUM_DECAY * momentum[0] + total
    rows = pl.ds(pl.multiple_of(place[2] * own, own), own)
    for i in range(w.shape[1]):
        base = w[0, i, rows, :].astype(jnp.float32)
        renewed[i] = renormalize(base, new[i])


def renew(place, w, momentum, mine, pieces):
    return pl.pallas_call(
        renew_kernel,
        out_shape=jax.ShapeDtypeStruct(mine.shape, jnp.bfloat16),
        in_specs=[pl.BlockSpec(memory_space=pltpu.SMEM)] + [whole_spec()] * (3 + len(pieces)),
        out_specs=whole_spec(),
        compiler_params=params(12),
        cost_estimate=BRIEF,
        name="renew",
    )(place, w, momentum, mine, *pieces)


def apply_kernel(count, place, q, attended, *rest):
    units, combined, full = rest[:count], rest[count], rest[count + 1]
    own = units[0].shape[1]
    for i in range(count):
        step, across = i % (count // 2), i // (count // 2)
        rows = pl.ds(pl.multiple_of((place[2] ^ (2 * step + across)) * own, own), own)
        full[:, rows, :] = units[i][...]
    b1 = times_transposed(q[...], full[0])
    b3 = times_transposed(q[...], full[1])
    fast_in = (b1 * jax.nn.sigmoid(b1) * b3).astype(jnp.bfloat16)
    out = times_transposed(fast_in, full[2])
    combined[...] = (attended[...] + out).astype(jnp.bfloat16)


def apply_fast(place, q, attended, units):
    tokens, hidden = q.shape
    return pl.pallas_call(
        functools.partial(apply_kernel, len(units)),
        out_shape=jax.ShapeDtypeStruct((tokens, hidden), jnp.bfloat16),
        in_specs=[pl.BlockSpec(memory_space=pltpu.SMEM)] + [whole_spec()] * (2 + len(units)),
        out_specs=whole_spec(),
        scratch_shapes=[pltpu.VMEM((3, hidden, hidden), jnp.bfloat16)],
        compiler_params=params(12),
        cost_estimate=BRIEF,
        name="apply_fast",
    )(place, q, attended, *units)


def most_kernel(tags, last, rows_in, offsets, place, *rest):
    blocks, units = rest[: len(tags)], rest[len(tags) : -3]
    partial, last_rows, full = rest[-3:]
    for at, (unit, first) in enumerate(offsets):
        rows = pl.ds(pl.multiple_of(place[ORIGINS + at] * rows_in, rows_in), rows_in)
        full[rows, :] = units[unit][first : first + rows_in, :]
    width = blocks[0].shape[1]
    value = None
    for block, tag in zip(blocks, tags):
        rows = pl.ds(pl.multiple_of((place[3] ^ tag) * width, width), width)
        part = matmul(block[...], full[rows, :])
        value = part if value is None else value + part
    partial[...] = value
    rows = pl.ds(pl.multiple_of((place[3] ^ last) * width, width), width)
    last_rows[...] = full[rows, :]


def project_most(place, blocks, tags, last, near, far, rows_in):
    tokens, width = blocks[0].shape
    units = near + far
    offsets = [(i, 0) for i in range(len(near))]
    for i, unit in enumerate(far, len(near)):
        offsets.append((i, unit.shape[0] - rows_in))
    columns = near[0].shape[1]
    return pl.pallas_call(
        functools.partial(most_kernel, tags, last, rows_in, offsets),
        out_shape=[
            jax.ShapeDtypeStruct((tokens, columns), jnp.float32),
            jax.ShapeDtypeStruct((width, columns), jnp.bfloat16),
        ],
        in_specs=[pl.BlockSpec(memory_space=pltpu.SMEM)]
        + [whole_spec()] * (len(units) + len(blocks)),
        out_specs=[whole_spec()] * 2,
        scratch_shapes=[pltpu.VMEM((rows_in * len(offsets), columns), jnp.bfloat16)],
        compiler_params=params(12),
        cost_estimate=BRIEF,
        name="project_most",
    )(place, *blocks, *units)


def last_kernel(partial, block, rows, mixed):
    mixed[...] = (partial[...] + matmul(block[...], rows[...])).astype(mixed.dtype)


def project_last(partial, block, rows):
    return pl.pallas_call(
        last_kernel,
        out_shape=jax.ShapeDtypeStruct(partial.shape, jnp.bfloat16),
        in_specs=[whole_spec()] * 3,
        out_specs=whole_spec(),
        compiler_params=params(12),
        cost_estimate=BRIEF,
        name="project_last",
    )(partial, block, rows)


def ring_order(outer):
    return [0] + list(range(1, outer, 2)) + list(range(outer - 2 + outer % 2, 0, -2))


def ring_step(unit, outer):
    order = ring_order(outer)
    pairs = []
    for place, z in enumerate(order):
        to = order[(place + 1) % outer]
        pairs += [(2 * z + y, 2 * to + y) for y in range(2)]
    return lax.ppermute(unit, "seq", pairs)


def after(array, *others):
    return lax.optimization_barrier((array,) + others)[0]


def place_table(outer, heads):
    order = ring_order(outer)
    table = []
    for s in range(2 * outer):
        place = order.index(s // 2)
        sources = [order[(place - step) % outer] for step in range(outer)]
        near = [2 * z + s % 2 for z in sources]
        far = [2 * z + 1 - s % 2 for z in sources]
        table += [[s % 2, s // 2, s, head] + near + far for head in range(heads)]
    return np.array(table, np.int32)


def renormalize(base, moment):
    updated = base - moment
    base_rms = jnp.sqrt(jnp.mean(base * base, axis=-1, keepdims=True) + NORM_EPS)
    new_rms = jnp.sqrt(jnp.mean(updated * updated, axis=-1, keepdims=True) + NORM_EPS)
    return (updated * (base_rms / new_rms)).astype(jnp.bfloat16)


def attention(queries, keys, values, early_keys, early_values, position):
    tok_rows = queries.shape[0]
    all_keys = jnp.concatenate([early_keys, keys], axis=0)
    all_values = jnp.concatenate([early_values, values], axis=0)
    key_pos = (position - 1) * tok_rows + jnp.arange(all_keys.shape[0])
    query_pos = position * tok_rows + jnp.arange(tok_rows)
    spacing = query_pos[:, None] - key_pos[None, :]
    allowed = (spacing >= 0) & (spacing < WINDOW) & (key_pos[None, :] >= 0)
    scores = times_transposed(queries, all_keys) * (1.0 / math.sqrt(HD))
    scores = jnp.where(allowed, scores, NEG_LARGE)
    highest = jnp.max(scores, axis=1, keepdims=True)
    expo = jnp.exp(scores - highest)
    probs = (expo / jnp.sum(expo, axis=1, keepdims=True)).astype(jnp.bfloat16)
    return jnp.dot(probs, all_values, preferred_element_type=jnp.float32)


def shards(queries, keys, values, rates, fast, momentum, out_proj):
    tok_rows = queries.shape[0]
    ranks = lax.axis_size("seq")
    heads = lax.axis_size("head")
    own_rows = momentum.shape[2]
    if own_rows % 16 or ranks != 8 or heads != 4 or tok_rows != WINDOW:
        return plain(queries, keys, values, rates, fast, momentum, out_proj)
    outer = ranks // 2
    grad_scale = 1.0 / math.sqrt(tok_rows * ranks)
    index = lax.axis_index("seq") * heads + lax.axis_index("head")
    place = lax.dynamic_index_in_dim(jnp.asarray(place_table(outer, heads)), index, 0, False)

    pair_keys = swap(keys, "seq", 1)
    errors = (-grad_scale * rates * values.astype(jnp.float32)).astype(jnp.bfloat16)
    pair_errors = swap(errors, "seq", 1)

    wide = [out_proj, ring_step(out_proj, outer)]
    own_factors = keys_part(place, keys, fast, outer)
    wide.append(ring_step(after(wide[1], own_factors[0]), outer))

    up_values = after(values, wide[1])
    up_values = lax.ppermute(up_values, "seq", [(s, s + 2) for s in range(1, ranks - 2, 2)])
    up_keys = after(pair_keys, wide[2])
    up_keys = lax.ppermute(up_keys, "seq", [(s, s + 2) for s in range(0, ranks - 2, 2)])

    acc = own_gradients(place, keys, errors, own_factors, outer)
    pair_factors = keys_part(place, pair_keys, fast, outer)
    across = crossing(place, values, up_values, wide[0])
    pair_errors = after(pair_errors, up_keys, across)
    summed = both_gradients(place, pair_keys, pair_errors, pair_factors, acc, outer)
    pieces = [swap(summed[step], "seq", step * 2) for step in range(1, outer)]
    crossed = swap(after(across, summed[1]), "seq", 1)
    pieces[2] = after(pieces[2], crossed)
    renewed = renew(place, fast, momentum, summed[0], pieces)

    near = [renewed]
    for step in range(1, outer):
        near.append(swap(renewed, "seq", step * 2))
    far = [swap(renewed, "seq", 1)]
    wide_far = [crossed, swap(after(wide[1], near[1]), "seq", 1)]
    near[1] = after(near[1], far[0])
    total = after(summed[0], near[1])
    for piece in pieces:
        total = total + piece.astype(jnp.float32)
    moment = MOMENTUM_DECAY * momentum + total[None]
    near[3] = after(near[3], moment)
    far += [swap(unit, "seq", 1) for unit in near[1:]]
    attended = window_attention(
        place, queries, keys, values, pair_keys, up_keys, after(crossed, near[1])
    )
    wide.append(ring_step(after(wide[2], far[1], near[2], near[3]), outer))

    forwarded = far[-1]
    far[-1] = after(far[-1], attended, wide_far[1])
    wide_far.append(swap(after(wide[2], forwarded), "seq", 1))
    wide_far.append(swap(after(wide[3], wide_far[2]), "seq", 1))

    combined = apply_fast(place, queries, attended, near + far)

    crossed_x = swap(combined, "head", 2)
    other_core = swap(combined, "head", 1)
    crossed_x = after(crossed_x, *wide_far[2:])
    last = swap(crossed_x, "head", 3 ^ 2)
    held = [out_proj] + wide[1:]
    partial, rows = project_most(
        place, [combined, other_core, crossed_x], [0, 1, 2], 3, held, wide_far, out_proj.shape[0]
    )
    mixed = project_last(partial, last, rows)
    return (mixed, moment)


def plain(queries, keys, values, rates, fast, momentum, out_proj):
    tok_rows = queries.shape[0]
    ranks = lax.axis_size("seq")
    position = lax.axis_index("seq")
    own_rows = momentum.shape[2]
    grad_scale = 1.0 / math.sqrt(tok_rows * ranks)
    weights = fast[0]
    h_gate = times_transposed(keys, weights[0])
    h_up = times_transposed(keys, weights[1])
    sigma = jax.nn.sigmoid(h_gate)
    gated = (h_gate * sigma * h_up).astype(jnp.bfloat16)
    errors = (-grad_scale * rates * values.astype(jnp.float32)).astype(jnp.bfloat16)
    grad_down = contract_rows(errors, gated)
    back = matmul(errors, weights[2])
    d_gate = (back * h_up * sigma * (1.0 + h_gate * (1.0 - sigma))).astype(jnp.bfloat16)
    d_up = (back * h_gate * sigma).astype(jnp.bfloat16)
    grads = jnp.stack([contract_rows(d_gate, keys), contract_rows(d_up, keys), grad_down])
    summed_rows = lax.psum_scatter(grads, "seq", scatter_dimension=1, tiled=True)
    moment_own = MOMENTUM_DECAY * momentum[0] + summed_rows
    base_rows = lax.dynamic_slice_in_dim(weights, position * own_rows, own_rows, 1).astype(jnp.float32)
    renewed = lax.all_gather(renormalize(base_rows, moment_own), "seq", axis=1, tiled=True)
    q_gate = times_transposed(queries, renewed[0])
    q_up = times_transposed(queries, renewed[1])
    fast_in = (q_gate * jax.nn.sigmoid(q_gate) * q_up).astype(jnp.bfloat16)
    fast_out = times_transposed(fast_in, renewed[2])
    behind = [(i, i + 1) for i in range(ranks - 1)]
    early_keys = lax.ppermute(keys, "seq", behind)
    early_values = lax.ppermute(values, "seq", behind)
    attended = attention(queries, keys, values, early_keys, early_values, position)
    combined = (attended + fast_out).astype(jnp.bfloat16)
    all_heads = lax.all_gather(combined, "head", axis=1, tiled=True)
    projection = lax.all_gather(out_proj, "seq", axis=0, tiled=True)
    return (matmul(all_heads, projection).astype(jnp.bfloat16), moment_own[None])


def solution(mesh):
    return jax.shard_map(
        shards,
        mesh=mesh,
        in_specs=(
            P("seq", "head"),
            P("seq", "head"),
            P("seq", "head"),
            P("seq", "head"),
            P("head", None, None, None),
            P("head", None, "seq", None),
            P("seq", "head"),
        ),
        out_specs=(P("seq", "head"), P("head", None, "seq", None)),
        check_vma=False,
    )
```
